32 devices in a mesh: groups: 1, gx: 8 (over z, y), gy: 2 (over core), segment: 2 (over x).
Axes of the slice: x: 2, y: 2, z: 4, core: 2. Of those that a mesh axis runs over, the one named last changes fastest.
Arguments:
- activations: bfloat16 [2, 8, 128, 128, 128], P('segment', 'groups', 'gx', 'gy'), may hold values from -6 to 6
- cotangent: bfloat16 [8, 128, 128, 128], P('groups', 'gx', 'gy'), may hold values from -6 to 6
- spectral_weights: float32 [2, 32, 32, 8, 8, 32], P('segment', 'gy', 'gx'), may hold values from -6 to 6
- pointwise: float32 [2, 8, 8], P('segment'), may hold values from -2 to 2
- channel_bias: float32 [2, 8], P('segment'), may hold values from -3 to 3
Outputs:
- input_grads: bfloat16 [2, 8, 128, 128, 128], P('segment', 'groups', 'gx', 'gy')
- spectral_grads: float32 [2, 32, 32, 8, 8, 32], P('segment', 'gy', 'gx', 'groups')
The draws below stay inside these ranges and needn't reach their ends.
All inputs are finite; a program needn't handle non-finite values.
Results may differ from the reference program's by a relative error of at most 0.0042.
Values may be sent and summed in bfloat16 or wider, within the bound.
A program may use at most 64 MiB of HBM per device.

```python
import math
import jax
import jax.numpy as jnp
from jax import lax

C = 8
NX = 128
NY = 128
NZ = 128
MODES = 32
SEGMENTS = 2


def levels(key, extent, split, low, high):
    loudness, own = 1.0, jax.random.fold_in(key, 6)
    for axis_at, shards_of in split:
        heights = jnp.exp(jax.random.uniform(jax.random.fold_in(own, axis_at), (shards_of,), jnp.float32, low / len(split), high / len(split)))
        loudness = loudness * jnp.repeat(heights, extent[axis_at] // shards_of).reshape([-1 if axis == axis_at else 1 for axis in range(len(extent))])
    return loudness


def scatter_about(own_key, extent, spread, most, pieces=(), kind=jnp.bfloat16):
    level = levels(own_key, extent, pieces, -0.22, 0.18) if pieces else 1.0
    result = jax.random.normal(own_key, extent, jnp.float32) * spread * level
    return jnp.minimum(jnp.maximum(result, -most), most).astype(kind)


def setup_inputs(seed: int = 0, part: int = 0) -> dict:
    arg_keys = jax.random.split(jax.random.key(seed), 6)
    own_keys = jax.random.split(jax.random.fold_in(arg_keys[5], part), 6)
    activations = scatter_about(own_keys[0], (SEGMENTS, C, NX, NY, NZ), 1.0, 6.0, ((0, 2), (2, 8), (3, 2)))
    cotangent = scatter_about(own_keys[1], (C, NX, NY, NZ), 1.0, 6.0, ((1, 8), (2, 2)))
    spectral_weights = scatter_about(arg_keys[2], (SEGMENTS, MODES, MODES, C, C, MODES), 1.0, 6.0, ((0, 2), (1, 2), (2, 8)), jnp.float32)
    pointwise = scatter_about(arg_keys[3], (SEGMENTS, C, C), C ** -0.5, 2.0, ((0, 2),), jnp.float32)
    channel_bias = scatter_about(arg_keys[4], (SEGMENTS, C), 0.7, 3.0, ((0, 2),), jnp.float32)
    return dict(activations=activations, cotangent=cotangent, spectral_weights=spectral_weights, pointwise=pointwise, channel_bias=channel_bias)


highest = lax.Precision.HIGHEST

def trig_basis(length, mode_count):
    half = mode_count // 2
    freqs = jnp.arange(half, dtype=jnp.int32)[:, None]
    points = jnp.arange(length, dtype=jnp.int32)[None, :]
    step_angle = 2.0 * math.pi / length
    cosine = jnp.cos((freqs * points % length).astype(jnp.float32) * step_angle)
    sine = jnp.sin(((freqs + 1) * points % length).astype(jnp.float32) * step_angle)
    rows_all = jnp.concatenate([cosine, sine], axis=0)
    scales = jnp.where(jnp.arange(mode_count) == 0, 1.0 / math.sqrt(length), math.sqrt(2.0 / length)).astype(jnp.float32)
    return rows_all * scales[:, None]

def to_modes(field, along_x, along_y, along_z):
    inner = jnp.einsum('ixyz,cz->cixy', field, along_z, precision=highest)
    inner = jnp.einsum('cixy,ax->ciay', inner, along_x, precision=highest)
    return jnp.einsum('ciay,jy->jcia', inner, along_y, precision=highest)

def to_field(spectrum, along_x, along_y, along_z):
    inner = jnp.einsum('jcia,jy->ciay', spectrum, along_y, precision=highest)
    inner = jnp.einsum('ciay,ax->cixy', inner, along_x, precision=highest)
    return jnp.einsum('cixy,cz->ixyz', inner, along_z, precision=highest)

def gelu_slope(value):
    normal_cdf = 0.5 * (1.0 + jax.scipy.special.erf(value * 0.7071067811865476))
    return normal_cdf + value * jnp.exp(-0.5 * value * value) * 0.3989422804014327

def reference(activations, cotangent, spectral_weights, pointwise, channel_bias):
    along_x = trig_basis(NX, MODES)
    along_y = trig_basis(NY, MODES)
    along_z = trig_basis(NZ, MODES)
    incoming = cotangent
    grad_fields = []
    weight_grads = []
    for segment_index in range(SEGMENTS - 1, -1, -1):
        inputs = activations[segment_index].astype(jnp.float32)
        weights = spectral_weights[segment_index]
        mixing = pointwise[segment_index]
        input_modes = to_modes(inputs, along_x, along_y, along_z)
        mixed = jnp.einsum('jcioa,jcia->jcoa', weights, input_modes, precision=highest)
        pre_act = jnp.einsum('oi,ixyz->oxyz', mixing, inputs, precision=highest)
        pre_act = pre_act + channel_bias[segment_index][:, None, None, None] + to_field(mixed, along_x, along_y, along_z)
        signal = incoming.astype(jnp.float32) * gelu_slope(pre_act)
        grad_modes = to_modes(signal, along_x, along_y, along_z)
        back = jnp.einsum('jcioa,jcoa->jcia', weights, grad_modes, precision=highest)
        input_grad = jnp.einsum('oi,oxyz->ixyz', mixing, signal, precision=highest) + to_field(back, along_x, along_y, along_z)
        input_grad = input_grad.astype(jnp.bfloat16)
        grad_fields.append(input_grad)
        weight_grads.append(jnp.einsum('jcia,jcoa->jcioa', input_modes, grad_modes, precision=highest))
        incoming = input_grad
    ordered_fields = grad_fields[::-1]
    ordered_weights = weight_grads[::-1]
    return (jnp.stack(ordered_fields), jnp.stack(ordered_weights))
```

```python
import functools
import math

import jax
import jax.numpy as jnp
import ml_dtypes
import numpy as np
from jax import lax
from jax.experimental import pallas as pl
from jax.experimental.pallas import tpu as pltpu
from jax.sharding import PartitionSpec as P

MODES = 32
f32, bf16 = jnp.float32, jnp.bfloat16


def from_behind(block, axis, distance):
    devices = range(lax.axis_size(axis))
    route = [(i - distance, i) for i in devices if i - distance in devices]
    return lax.ppermute(block, axis, route)


def trig_basis(length):
    half = MODES // 2
    freqs = np.arange(half)[:, None]
    points = np.arange(length)[None, :]
    step = 2.0 * math.pi / length
    rows = np.concatenate(
        [np.cos((freqs * points % length) * step), np.sin(((freqs + 1) * points % length) * step)]
    )
    scales = np.where(np.arange(MODES) == 0, 1.0 / math.sqrt(length), math.sqrt(2.0 / length))
    return rows * scales[:, None]


def halves(matrix):
    matrix = np.asarray(matrix, np.float32)
    top = matrix.astype(ml_dtypes.bfloat16)
    rest = (matrix - top.astype(np.float32)).astype(ml_dtypes.bfloat16)
    return np.stack([top, rest])


def split(value):
    top = value.astype(bf16)
    return top, (value - top.astype(f32)).astype(bf16)


def dot(a, b, ca=1, cb=0):
    return lax.dot_general(a, b, (((ca,), (cb,)), ((), ())), preferred_element_type=f32)


def kernel(
    back, nx, ny, xr, *refs
):
    if back:
        (inc_ref, slope_ref, w_hbm, mix_ref, bz_ref, bzs_ref, ky_ref, kyt_ref, bx_ref, bxr_ref,
         out_ref, modes_ref, got_ref, *scratch) = refs
    else:
        (inc_ref, w_hbm, mix_ref, bias_ref, bz_ref, bzs_ref, ky_ref, kyt_ref, bx_ref, bxr_ref,
         out_ref, modes_ref, got_ref, *scratch) = refs
    (w_ref, sig_ref, ghi_ref, glo_ref, s_ref, r_ref, m_ref, p_ref, q_ref, qs_ref,
     send1, recv1, send2, recv2, wsem) = scratch
    channels, _, yr, zr = inc_ref.shape
    cl, jl, xp = MODES // nx, MODES // ny, r_ref.shape[2]
    n = nx * ny
    lanes = jl * channels
    gx, gy = lax.axis_index("gx"), lax.axis_index("gy")
    me = gx * ny + gy

    wcopy = pltpu.make_async_copy(w_hbm, w_ref, wsem)
    wcopy.start()

    barrier = pltpu.get_barrier_semaphore()

    def greet(k, carry):
        peer = lax.rem(me + k, n)
        pl.semaphore_signal(
            barrier, inc=1,
            device_id={"gx": peer // ny, "gy": lax.rem(peer, ny)},
            device_id_type=pl.DeviceIdType.MESH,
        )
        return carry

    lax.fori_loop(1, n, greet, 0)

    def along_z(x, carry):
        if back:
            signal = inc_ref[:, x].astype(f32) * slope_ref[:, x]
            sig_ref[:, x] = signal
            block = signal.astype(bf16)
        else:
            block = inc_ref[:, x]
        block = block.reshape(channels * yr, zr)
        g = dot(bz_ref[0], block, 1, 1) + dot(bz_ref[1], block, 1, 1)
        ghi, glo = split(g)
        rows = pl.ds(pl.multiple_of(x * MODES, MODES), MODES)
        ghi_ref[rows, :] = ghi
        glo_ref[rows, :] = glo
        return carry

    lax.fori_loop(0, xr, along_z, 0)
    ghi = ghi_ref[...]
    t = dot(ghi, ky_ref[0]) + dot(ghi, ky_ref[1]) + dot(glo_ref[...], ky_ref[0])
    t = jnp.swapaxes(t.reshape(xr, MODES, ny * lanes), 0, 1)
    if xp > xr:
        t = jnp.concatenate([t, jnp.zeros((MODES, xp - xr, ny * lanes), f32)], axis=1)
    t = t.astype(bf16)
    for h in range(ny):
        s_ref[h] = t[:, :, h * lanes : (h + 1) * lanes].reshape(nx, cl, xp, lanes)

    pl.semaphore_wait(barrier, n - 1)

    def exchange(source, target, send, recv):
        def copy_to(peer, slot_of):
            return pltpu.make_async_remote_copy(
                src_ref=source(peer // ny, lax.rem(peer, ny)),
                dst_ref=target.at[lax.rem(slot_of, ny) * nx + slot_of // ny],
                send_sem=send.at[peer],
                recv_sem=recv.at[slot_of],
                device_id={"gx": peer // ny, "gy": lax.rem(peer, ny)},
                device_id_type=pl.DeviceIdType.MESH,
            )

        def begin(k, carry):
            copy_to(lax.rem(me + k, n), me).start()
            return carry

        def finish(k, carry):
            copy_to(lax.rem(me + k, n), me).wait_send()
            peer = lax.rem(me + n - k, n)
            copy_to(peer, peer).wait_recv()
            return carry

        lax.fori_loop(1, n, begin, 0)
        target[gy * nx + gx] = source(gx, gy)[...]
        lax.fori_loop(1, n, finish, 0)

    exchange(lambda d, h: s_ref.at[h, d], r_ref, send1, recv1)

    for c in range(cl):
        part = r_ref[:, c].reshape(n * xp, lanes)
        own = dot(bx_ref[0], part) + dot(bx_ref[1], part)
        modes_ref[c] = own.T.reshape(jl, channels, MODES)
    wcopy.wait()

    def mix(j, carry):
        for c in range(cl):
            own = modes_ref[c, j]
            weight = w_ref[j, c]
            if back:
                m_ref[c, j] = jnp.sum(weight * own[None], axis=1)
            else:
                m_ref[c, j] = jnp.sum(weight * own[:, None, :], axis=0)
        return carry

    lax.fori_loop(0, jl, mix, 0)
    for c in range(cl):
        top, rest = split(m_ref[c].reshape(lanes, MODES))
        spread = (
            dot(bxr_ref[0], top, 1, 1) + dot(bxr_ref[1], top, 1, 1) + dot(bxr_ref[0], rest, 1, 1)
        )
        p_ref[:, c] = spread.astype(bf16).reshape(nx, xp, lanes)

    exchange(lambda d, h: p_ref.at[d], q_ref, send2, recv2)

    got = [q_ref[h * nx : (h + 1) * nx].reshape(MODES, xp, lanes) for h in range(ny)]
    got = jnp.concatenate(got, axis=2).astype(f32)
    got = jnp.swapaxes(got, 0, 1)[:xr].reshape(xr * MODES, ny * lanes).astype(bf16)
    got_ref[...] = got
    qs_ref[...] = dot(got, kyt_ref[0]) + dot(got, kyt_ref[1])

    def finish_field(x, carry):
        rows = pl.ds(pl.multiple_of(x * MODES, MODES), MODES)
        top, rest = split(qs_ref[rows, :])
        stack = jnp.concatenate([top, rest, top], axis=0)
        field = dot(stack, bzs_ref[...], 0, 0).reshape(channels, yr, zr)
        if back:
            values = [sig_ref[i, x] for i in range(channels)]
        else:
            values = [inc_ref[i, x].astype(f32) for i in range(channels)]
        for o in range(channels):
            total = field[o]
            for i in range(channels):
                total = total + (mix_ref[i, o] if back else mix_ref[o, i]) * values[i]
            if back:
                out_ref[o, x] = total.astype(bf16)
            else:
                total = total + bias_ref[0, o]
                cdf = 0.5 * (1.0 + lax.erf(total * 0.7071067811865476))
                out_ref[o, x] = cdf + total * jnp.exp(-0.5 * total * total) * 0.3989422804014327
        return carry

    lax.fori_loop(0, xr, finish_field, 0)


def ahead_kernel(
    act_ref, cot_ref, got_ref, got_back_ref, mix_ref, bias_ref, bzs_ref, kyt_ref, out_ref,
    pre_ref, back_ref,
):
    channels, xr, yr, zr = act_ref.shape
    pre_ref[...] = dot(got_ref[...], kyt_ref[0]) + dot(got_ref[...], kyt_ref[1])
    back_ref[...] = dot(got_back_ref[...], kyt_ref[0]) + dot(got_back_ref[...], kyt_ref[1])

    def field_of(ref, x):
        rows = pl.ds(pl.multiple_of(x * MODES, MODES), MODES)
        top, rest = split(ref[rows, :])
        stack = jnp.concatenate([top, rest, top], axis=0)
        return dot(stack, bzs_ref[...], 0, 0).reshape(channels, yr, zr)

    def step(x, carry):
        field = field_of(pre_ref, x)
        values = [act_ref[i, x].astype(f32) for i in range(channels)]
        signals = []
        for o in range(channels):
            total = field[o]
            for i in range(channels):
                total = total + mix_ref[o, i] * values[i]
            total = total + bias_ref[0, o]
            cdf = 0.5 * (1.0 + lax.erf(total * 0.7071067811865476))
            slope = cdf + total * jnp.exp(-0.5 * total * total) * 0.3989422804014327
            signals.append(cot_ref[o, x].astype(f32) * slope)
        field = field_of(back_ref, x)
        for o in range(channels):
            total = field[o]
            for i in range(channels):
                total = total + mix_ref[i, o] * signals[i]
            out_ref[o, x] = total.astype(bf16)
        return carry

    lax.fori_loop(0, xr, step, 0)


def ahead(activations, cotangent, got, got_back, mixing, bias, bzs, kyt):
    channels, xr, yr, zr = activations.shape
    vmem = pl.BlockSpec(memory_space=pltpu.VMEM)
    smem = pl.BlockSpec(memory_space=pltpu.SMEM)
    return pl.pallas_call(
        ahead_kernel,
        out_shape=jax.ShapeDtypeStruct(activations.shape, bf16),
        in_specs=[vmem] * 4 + [smem] * 2 + [vmem] * 2,
        out_specs=vmem,
        scratch_shapes=[pltpu.VMEM((xr * MODES, channels * yr), f32)] * 2,
        compiler_params=pltpu.CompilerParams(vmem_limit_bytes=50 * 2**20),
        cost_estimate=pl.CostEstimate(flops=10**9, bytes_accessed=10**7, transcendentals=10**6),
    )(activations, cotangent, got, got_back, mixing, bias, bzs, kyt)


def block_turn(back, nx, ny, collective, field, slope, weights, mixing, bias, tables):
    channels, xr, yr, zr = field.shape
    xp = -(-xr // 16) * 16
    cl, jl, n = MODES // nx, MODES // ny, nx * ny
    lanes = jl * channels
    vmem = pl.BlockSpec(memory_space=pltpu.VMEM)
    smem = pl.BlockSpec(memory_space=pltpu.SMEM)
    hbm = pl.BlockSpec(memory_space=pl.ANY)
    if back:
        args = (field, slope, weights, mixing, *tables)
        specs = [vmem, vmem, hbm, smem] + [vmem] * len(tables)
    else:
        args = (field, weights, mixing, bias, *tables)
        specs = [vmem, hbm, smem, smem] + [vmem] * len(tables)
    dma = pltpu.SemaphoreType.DMA
    return pl.pallas_call(
        functools.partial(kernel, back, nx, ny, xr),
        out_shape=(
            jax.ShapeDtypeStruct(field.shape, bf16 if back else f32),
            jax.ShapeDtypeStruct((cl, jl, channels, MODES), f32),
            jax.ShapeDtypeStruct((xr * MODES, ny * lanes), bf16),
        ),
        in_specs=specs,
        out_specs=(vmem, vmem, vmem),
        scratch_shapes=[
            pltpu.VMEM(weights.shape, f32),
            pltpu.VMEM(field.shape if back else (8, 128), f32),
            pltpu.VMEM((xr * MODES, channels * yr), bf16),
            pltpu.VMEM((xr * MODES, channels * yr), bf16),
            pltpu.VMEM((ny, nx, cl, xp, lanes), bf16),
            pltpu.VMEM((n, cl, xp, lanes), bf16),
            pltpu.VMEM((cl, jl, channels, MODES), f32),
            pltpu.VMEM((nx, cl, xp, lanes), bf16),
            pltpu.VMEM((n, cl, xp, lanes), bf16),
            pltpu.VMEM((xr * MODES, channels * yr), f32),
            dma((n,)), dma((n,)), dma((n,)), dma((n,)), dma,
        ],
        compiler_params=pltpu.CompilerParams(
            collective_id=collective, has_side_effects=True, vmem_limit_bytes=50 * 2**20
        ),
        cost_estimate=pl.CostEstimate(flops=10**9, bytes_accessed=2 * 10**7, transcendentals=10**6),
    )(*args)


def body(activations, cotangent, spectral_weights, pointwise, channel_bias):
    inputs = activations[0]
    channels, xr, yr, zr = inputs.shape
    nx, ny = lax.axis_size("gx"), lax.axis_size("gy")
    xp = -(-xr // 16) * 16
    bz = trig_basis(zr)
    bx = trig_basis(xr * nx).reshape(MODES, nx, xr)
    bx = np.concatenate([bx, np.zeros((MODES, nx, xp - xr))], axis=2).reshape(MODES, nx * xp)
    by = trig_basis(yr * ny).reshape(MODES, ny, yr)
    kron = np.einsum("jgy,ik->giyjk", by, np.eye(channels)).reshape(
        ny, channels * yr, MODES * channels
    )
    bzh = halves(bz)
    kh = halves(kron)
    gy = lax.axis_index("gy")
    ky = lax.dynamic_index_in_dim(jnp.asarray(np.swapaxes(kh, 0, 1)), gy, 0, False)
    kyt = lax.dynamic_index_in_dim(
        jnp.asarray(np.ascontiguousarray(np.transpose(kh, (1, 0, 3, 2)))), gy, 0, False
    )
    tables = (
        jnp.asarray(bzh),
        jnp.asarray(np.concatenate([bzh[0], bzh[0], bzh[1]], axis=0)),
        ky,
        kyt,
        jnp.asarray(halves(np.concatenate([bx] * ny, axis=1))),
        jnp.asarray(halves(bx.T)),
    )
    weights = spectral_weights[0]
    mixing = pointwise[0]
    following = [from_behind(v, "segment", -1) for v in (inputs, mixing, channel_bias)]
    slope, input_modes, got = block_turn(
        False, nx, ny, 0, inputs, None, weights, mixing, channel_bias, tables
    )
    next_got = from_behind(got, "segment", -1)
    segment_index = lax.axis_index("segment")
    segment_count = lax.axis_size("segment")
    incoming = cotangent
    kept_grad = jnp.zeros(cotangent.shape, bf16)
    kept_modes = jnp.zeros(input_modes.shape, f32)
    for turn_index in range(segment_count):
        active = segment_index == segment_count - 1 - turn_index
        input_grad, grad_modes, got_back = block_turn(
            True, nx, ny, 1 + turn_index, incoming, slope, weights, mixing, None, tables
        )
        kept_grad = jnp.where(active, input_grad, kept_grad)
        kept_modes = jnp.where(active, grad_modes, kept_modes)
        if turn_index == 0 and segment_count > 1:
            next_back = from_behind(got_back, "segment", -1)
            incoming = ahead(
                following[0], cotangent, next_got, next_back, following[1], following[2],
                tables[1], tables[3],
            )
        elif turn_index + 1 < segment_count:
            incoming = from_behind(input_grad, "segment", -1)
    input_modes = jnp.swapaxes(input_modes, 0, 1)
    kept_modes = jnp.swapaxes(kept_modes, 0, 1)
    weight_grad = input_modes[:, :, :, None, :] * kept_modes[:, :, None, :, :]
    return (kept_grad[None], weight_grad[None])


def slope_of(value):
    cdf = 0.5 * (1.0 + lax.erf(value * 0.7071067811865476))
    return cdf + value * jnp.exp(-0.5 * value * value) * 0.3989422804014327


def relay_kernel(
    nx, ny, xq,
    act_hbm, cot_hbm, w_hbm, mix_ref, bias_ref, mixv_ref, biasv_ref,
    kyt_hbm, ky_hbm, bzf_hbm, bzi_hbm, bx_hbm, sp_hbm,
    grad_hbm, wgrad_hbm,
    act, act1, cot, w, wd, kyt, ky, bzf, bzi, bx, sp,
    u, v, slope, sig, out, wgrad, in_modes, grad_modes, m_ref, mt_send, mt_recv,
    mixv1, biasv1, mix1, bias1, s_ref, p_ref, r_ref,
    load_sem, send_sem, recv_sem, row_send, row_recv, small_send, small_recv, store_sem,
):
    channels, xr, yr, zr = act.shape
    n = nx * ny
    cl, jl = MODES // nx, MODES // ny
    nh, hq = r_ref.shape[1], r_ref.shape[3]
    lanes = jl * channels
    rows = channels * yr
    gx, gy, seg = lax.axis_index("gx"), lax.axis_index("gy"), lax.axis_index("segment")
    me = gx * ny + gy
    mine = gy * nx + gx
    first, last = seg == 0, seg == 1
    mesh_ids = pl.DeviceIdType.MESH

    loads = [
        pltpu.make_async_copy(source, target, load_sem.at[k])
        for k, (source, target) in enumerate(
            [
                (act_hbm, act), (bzf_hbm, bzf), (kyt_hbm.at[gy], kyt), (w_hbm, w), (bx_hbm, bx),
                (sp_hbm, sp), (ky_hbm.at[gy], ky), (bzi_hbm, bzi), (cot_hbm, cot),
            ]
        )
    ]
    for load in loads:
        load.start()

    barrier = pltpu.get_barrier_semaphore()

    def greet(k, carry):
        peer = lax.rem(me + k, n)
        pl.semaphore_signal(
            barrier, inc=1,
            device_id={"gx": peer // ny, "gy": lax.rem(peer, ny)},
            device_id_type=mesh_ids,
        )
        return carry

    lax.fori_loop(1, n, greet, 0)
    pl.semaphore_signal(
        barrier, inc=1, device_id={"segment": 1 - seg}, device_id_type=mesh_ids
    )

    def ahead(source, target, send, recv):
        return pltpu.make_async_remote_copy(
            src_ref=source, dst_ref=target, send_sem=send, recv_sem=recv,
            device_id={"segment": 1 - seg}, device_id_type=mesh_ids,
        )

    def rows_copy(q):
        part = pl.ds(q * xq, xq)
        return ahead(act_hbm.at[:, part], act1.at[:, part], row_send.at[q], row_recv.at[q])

    def modes_copy(k):
        return ahead(mt_send.at[k], mt_recv.at[k], small_send.at[k], small_recv.at[k])

    small = [
        ahead(mixv_ref, mixv1, small_send.at[2], small_recv.at[2]),
        ahead(biasv_ref, biasv1, small_send.at[3], small_recv.at[3]),
    ]

    def send(source, e, half):
        def begin(k, carry):
            peer = lax.rem(me + k, n)
            d, h = peer // ny, lax.rem(peer, ny)
            pltpu.make_async_remote_copy(
                src_ref=source(d, h), dst_ref=r_ref.at[e, half, mine],
                send_sem=send_sem.at[e, half], recv_sem=recv_sem.at[e, half],
                device_id={"gx": d, "gy": h}, device_id_type=mesh_ids,
            ).start()
            return carry

        lax.fori_loop(1, n, begin, 0)
        r_ref[e, half, mine] = source(gx, gy)[...]

    def arrive(e, half):
        block = r_ref.at[e, half, pl.ds(0, n - 1)]
        pltpu.make_async_copy(block, block, recv_sem.at[e, half]).wait()

    def sent(e):
        for half in range(nh):
            block = r_ref.at[e, half, pl.ds(0, n - 1)]
            pltpu.make_async_copy(block, block, send_sem.at[e, half]).wait()

    def to_modes(block, k, half, q):
        g = dot(block, bzf[...])
        g = g[:, : nx * 16] + g[:, nx * 16 :]
        top, rest = split(g)
        t = dot(kyt[0], top) + dot(kyt[1], top) + dot(kyt[0], rest)
        t = t.T.astype(bf16)
        for h in range(ny):
            s_ref[k, half, h * nx : (h + 1) * nx, q] = t[:, h * lanes : (h + 1) * lanes].reshape(
                nx, 16, lanes
            )

    def to_field(e, half, q):
        block = jnp.concatenate(
            [
                r_ref[e, half, h * nx : (h + 1) * nx, q].reshape(nx * 16, lanes)
                for h in range(ny)
            ],
            axis=1,
        )
        top, rest = split(dot(ky[0], block, 1, 1) + dot(ky[1], block, 1, 1))
        return dot(jnp.concatenate([top, rest, top], axis=1), bzi[...])

    def row(field, x):
        return field[:, x * zr : (x + 1) * zr].reshape(channels, yr, zr)

    def send_modes(k, e, half):
        send(lambda d, h: s_ref.at[k, half, h * nx + d], e, half)

    def own_modes(e):
        block = r_ref[e].reshape(nh * n * hq * 16, lanes)
        own = dot(bx[0], block) + dot(bx[1], block)
        return own.T.reshape(jl, channels, cl * MODES)

    def send_cells(mt, k, e):
        top, rest = split(mt)
        cells = dot(sp[0], top) + dot(sp[1], top) + dot(sp[0], rest)
        p_ref[k] = cells.astype(bf16).reshape(nh, nx, hq, 16, lanes)
        for half in range(nh):
            send(lambda d, h: p_ref.at[k, half, d], e, half)

    def mixed():
        return m_ref[...].reshape(lanes, cl * MODES).T

    def mix_back(e):
        for half in range(nh):
            arrive(e, half)
        grad_modes[...] = own_modes(e)

        def step(j, carry):
            m_ref[j] = jnp.sum(wd[j] * grad_modes[j][None], axis=1)
            return carry

        lax.fori_loop(0, jl, step, 0)

    def blend(mixing, values, o, back):
        total = (mixing[0, o] if back else mixing[o, 0]) * values[0]
        for i in range(1, channels):
            total = total + (mixing[i, o] if back else mixing[o, i]) * values[i]
        return total

    for load in loads[:3]:
        load.wait()
    for half in range(nh):
        def step(q, carry):
            x = (half * hq + q) * xq
            block = [act[:, x + k].reshape(rows, zr) for k in range(xq)]
            to_modes(jnp.concatenate(block, axis=1), 0, half, q)
            return carry

        lax.fori_loop(0, hq, step, 0)
        if half == 0:
            pl.semaphore_wait(barrier, n)

            @pl.when(last)
            def _():
                for copy in small:
                    copy.start()
                for q in range(xr // xq):
                    rows_copy(q).start()

        send_modes(0, 0, half)

    for load in loads[3:]:
        load.wait()

    def dense(j, carry):
        for i in range(channels):
            wd[j, i] = jnp.concatenate([w[j, c, i] for c in range(cl)], axis=1)
        return carry

    lax.fori_loop(0, jl, dense, 0)

    def pointwise(x, carry):
        values = [act[i, x].astype(f32) for i in range(channels)]
        for o in range(channels):
            u[o, x] = blend(mix_ref, values, o, False) + bias_ref[0, o]
        return carry

    lax.fori_loop(0, xr, pointwise, 0)

    for half in range(nh):
        arrive(0, half)
    in_modes[...] = own_modes(0)

    def mix(j, carry):
        own = in_modes[j]
        m_ref[j] = jnp.sum(wd[j] * own[:, None, :], axis=0)
        return carry

    lax.fori_loop(0, jl, mix, 0)
    mt_send[0] = mixed()

    @pl.when(last)
    def _():
        modes_copy(0).start()

    send_cells(mt_send[0], 0, 1)

    @pl.when(last)
    def _():
        for half in range(nh):
            arrive(1, half)

            def step(q, carry):
                field = to_field(1, half, q)
                x0 = (half * hq + q) * xq
                blocks = []
                for k in range(xq):
                    signal = cot[:, x0 + k].astype(f32) * slope_of(row(field, k) + u[:, x0 + k])
                    sig[:, x0 + k] = signal
                    blocks.append(signal.astype(bf16).reshape(rows, zr))
                to_modes(jnp.concatenate(blocks, axis=1), 1, half, q)
                return carry

            lax.fori_loop(0, hq, step, 0)
            send_modes(1, 2, half)
        mix_back(2)
        mt_send[1] = mixed()
        modes_copy(1).start()
        send_cells(mt_send[1], 1, 3)

    @pl.when(first)
    def _():
        modes_copy(0).wait_recv()
        send_cells(mt_recv[0], 1, 2)
        for copy in small:
            copy.wait_recv()
        for k, (source, target) in enumerate([(mixv1, mix1), (biasv1, bias1)]):
            copy = pltpu.make_async_copy(source, target, store_sem.at[k])
            copy.start()
            copy.wait()
        for half in range(nh):
            arrive(1, half)

            def step(q, carry):
                field = to_field(1, half, q)
                x0 = (half * hq + q) * xq
                for k in range(xq):
                    slope[:, x0 + k] = slope_of(row(field, k) + u[:, x0 + k])
                return carry

            lax.fori_loop(0, hq, step, 0)

        def ahead_quarter(half, q):
            rows_copy(half * hq + q).wait_recv()
            field = to_field(2, half, q)
            x0 = (half * hq + q) * xq
            for k in range(xq):
                values = [act1[i, x0 + k].astype(f32) for i in range(channels)]
                here = row(field, k)
                signals = []
                for o in range(channels):
                    pre = here[o] + blend(mix1, values, o, False) + bias1[0, o]
                    signals.append(cot[o, x0 + k].astype(f32) * slope_of(pre))
                for i in range(channels):
                    v[i, x0 + k] = blend(mix1, signals, i, True)

        def back_quarter(half, q):
            field = to_field(3, half, q)
            x0 = (half * hq + q) * xq
            blocks = []
            for k in range(xq):
                incoming = (row(field, k) + v[:, x0 + k]).astype(bf16).astype(f32)
                signal = incoming * slope[:, x0 + k]
                sig[:, x0 + k] = signal
                blocks.append(signal.astype(bf16).reshape(rows, zr))
            to_modes(jnp.concatenate(blocks, axis=1), 1, half, q)

        for half in range(nh):
            arrive(2, half)
        quarters = [(half, q) for half in range(nh) for q in range(hq)]
        for half, q in quarters[:-1]:
            ahead_quarter(half, q)
        modes_copy(1).wait_recv()
        send_cells(mt_recv[1], 2, 3)
        for half in range(nh):
            arrive(3, half)
        for half, q in quarters:
            if (half, q) == quarters[-1]:
                ahead_quarter(half, q)
            back_quarter(half, q)
            if q == hq - 1:
                send_modes(1, 4, half)
        mix_back(4)
        send_cells(mixed(), 3, 5)

    def pointwise_back(x, carry):
        values = [sig[i, x] for i in range(channels)]
        for o in range(channels):
            u[o, x] = blend(mix_ref, values, o, True)
        return carry

    lax.fori_loop(0, xr, pointwise_back, 0)

    def weight_grad(j, carry):
        for c in range(cl):
            part = slice(c * MODES, (c + 1) * MODES)
            wgrad[j, c] = in_modes[j][:, None, part] * grad_modes[j][None, :, part]
        return carry

    lax.fori_loop(0, jl, weight_grad, 0)
    stores = [pltpu.make_async_copy(wgrad, wgrad_hbm, store_sem.at[0])]
    stores[0].start()
    e = 3 + 2 * (1 - seg)
    for half in range(nh):
        arrive(e, half)

        def step(q, carry):
            field = to_field(e, half, q)
            x0 = (half * hq + q) * xq
            for k in range(xq):
                out[:, x0 + k] = (row(field, k) + u[:, x0 + k]).astype(bf16)
            return carry

        lax.fori_loop(0, hq, step, 0)
        part = pl.ds(half * hq * xq, hq * xq)
        store = pltpu.make_async_copy(out.at[:, part], grad_hbm.at[:, part], store_sem.at[1 + half])
        store.start()
        stores.append(store)
    for e in range(4):
        sent(e)

    @pl.when(first)
    def _():
        sent(4)
        sent(5)

    @pl.when(last)
    def _():
        for copy in small:
            copy.wait_send()
        for q in range(xr // xq):
            rows_copy(q).wait_send()
        for k in range(2):
            modes_copy(k).wait_send()

    for store in stores:
        store.wait()


def two_section_body(activations, cotangent, spectral_weights, pointwise, channel_bias):
    inputs = activations[0]
    channels, xr, yr, zr = inputs.shape
    nx, ny = lax.axis_size("gx"), lax.axis_size("gy")
    n = nx * ny
    cl, jl = MODES // nx, MODES // ny
    xq = 16 // cl
    nh = 2
    hq = xr // (nh * xq)
    lanes, rows = jl * channels, channels * yr
    bz = trig_basis(zr).reshape(nx, cl, zr)
    eye_x, eye_c = np.eye(xq), np.eye(cl)
    bzf = np.einsum("dcz,xX->xzdXc", bz, eye_x).reshape(xq * zr, nx * 16)
    bzi = halves(bzf.reshape(xq, zr, nx * 16).transpose(2, 0, 1).reshape(nx * 16, xq * zr))
    by = trig_basis(yr * ny).reshape(MODES, ny, yr)
    ky = np.einsum("jgy,ik->giyjk", by, np.eye(channels)).reshape(ny, rows, ny * lanes)
    ky = halves(ky)
    bx = trig_basis(xr * nx).reshape(MODES, nx, nh, hq, xq)
    sp = np.einsum("adtqx,cC->tdqxCca", bx, eye_c).reshape(nh * nx * hq * 16, cl * MODES)
    bxf = np.broadcast_to(
        sp.reshape(nh, 1, nx * hq * 16, cl * MODES), (nh, ny, nx * hq * 16, cl * MODES)
    )
    bxf = bxf.reshape(nh * n * hq * 16, cl * MODES).T
    bzf = halves(bzf)
    tables = [
        np.ascontiguousarray(ky.transpose(1, 0, 3, 2)),
        np.ascontiguousarray(ky.transpose(1, 0, 2, 3)),
        np.concatenate([bzf[0], bzf[1]], axis=1),
        np.concatenate([bzi[0], bzi[0], bzi[1]], axis=0),
        halves(bxf),
        halves(sp),
    ]
    weights, mixing = spectral_weights[0], pointwise[0]
    vmem = pl.BlockSpec(memory_space=pltpu.VMEM)
    smem = pl.BlockSpec(memory_space=pltpu.SMEM)
    hbm = pl.BlockSpec(memory_space=pl.ANY)
    dma = pltpu.SemaphoreType.DMA
    grid = inputs.shape
    scratch = [
        pltpu.VMEM(grid, bf16), pltpu.VMEM(grid, bf16), pltpu.VMEM(grid, bf16),
        pltpu.VMEM(weights.shape, f32),
        pltpu.VMEM((jl, channels, channels, cl * MODES), f32),
        pltpu.VMEM((2, ny * lanes, rows), bf16),
        pltpu.VMEM((2, rows, ny * lanes), bf16),
        pltpu.VMEM((xq * zr, 2 * nx * 16), bf16),
        pltpu.VMEM((3 * nx * 16, xq * zr), bf16),
        pltpu.VMEM((2, cl * MODES, nh * n * hq * 16), bf16),
        pltpu.VMEM((2, nh * nx * hq * 16, cl * MODES), bf16),
        pltpu.VMEM(grid, f32), pltpu.VMEM(grid, f32), pltpu.VMEM(grid, f32), pltpu.VMEM(grid, f32),
        pltpu.VMEM(grid, bf16),
        pltpu.VMEM(weights.shape, f32),
        pltpu.VMEM((jl, channels, cl * MODES), f32),
        pltpu.VMEM((jl, channels, cl * MODES), f32),
        pltpu.VMEM((jl, channels, cl * MODES), f32),
        pltpu.VMEM((2, cl * MODES, lanes), f32),
        pltpu.VMEM((2, cl * MODES, lanes), f32),
        pltpu.VMEM(mixing.shape, f32), pltpu.VMEM(channel_bias.shape, f32),
        pltpu.SMEM(mixing.shape, f32), pltpu.SMEM(channel_bias.shape, f32),
        pltpu.VMEM((2, nh, n, hq, 16, lanes), bf16),
        pltpu.VMEM((4, nh, nx, hq, 16, lanes), bf16),
        pltpu.VMEM((6, nh, n, hq, 16, lanes), bf16),
        dma((9,)), dma((6, nh)), dma((6, nh)),
        dma((xr // xq,)), dma((xr // xq,)), dma((4,)), dma((4,)), dma((1 + nh,)),
    ]
    input_grad, weight_grad = pl.pallas_call(
        functools.partial(relay_kernel, nx, ny, xq),
        out_shape=(
            jax.ShapeDtypeStruct(grid, bf16),
            jax.ShapeDtypeStruct(weights.shape, f32),
        ),
        in_specs=[hbm, hbm, hbm, smem, smem, vmem, vmem] + [hbm] * len(tables),
        out_specs=(hbm, hbm),
        scratch_shapes=scratch,
        compiler_params=pltpu.CompilerParams(
            collective_id=0, has_side_effects=True, vmem_limit_bytes=58 * 2**20
        ),
        cost_estimate=pl.CostEstimate(
            flops=4 * 10**9, bytes_accessed=2 * 10**7, transcendentals=10**7
        ),
    )(
        inputs, cotangent, weights, mixing, channel_bias, mixing, channel_bias,
        *[jnp.asarray(table) for table in tables],
    )
    return (input_grad[None], weight_grad[None])


def fits(mesh):
    nx = mesh.shape["gx"]
    return mesh.shape["segment"] == 2 and mesh.shape["gy"] == 2 and nx == 8


def solution(mesh):
    return jax.shard_map(
        two_section_body if fits(mesh) else body,
        mesh=mesh,
        in_specs=(
            P("segment", "groups", "gx", "gy", None),
            P("groups", "gx", "gy", None),
            P("segment", "gy", "gx", None, None, None),
            P("segment", None, None),
            P("segment", None),
        ),
        out_specs=(
            P("segment", "groups", "gx", "gy", None),
            P("segment", "gy", "gx", "groups", None, None),
        ),
        check_vma=False,
    )
```

```python
import functools
import math

import jax
import jax.numpy as jnp
import ml_dtypes
import numpy as np
from jax import lax
from jax.experimental import pallas as pl
from jax.experimental.pallas import tpu as pltpu
from jax.sharding import PartitionSpec as P

MODES = 32
f32, bf16 = jnp.float32, jnp.bfloat16


def from_behind(block, axis, distance):
    devices = range(lax.axis_size(axis))
    route = [(i - distance, i) for i in devices if i - distance in devices]
    return lax.ppermute(block, axis, route)


def trig_basis(length):
    half = MODES // 2
    freqs = np.arange(half)[:, None]
    points = np.arange(length)[None, :]
    step = 2.0 * math.pi / length
    rows = np.concatenate(
        [np.cos((freqs * points % length) * step), np.sin(((freqs + 1) * points % length) * step)]
    )
    scales = np.where(np.arange(MODES) == 0, 1.0 / math.sqrt(length), math.sqrt(2.0 / length))
    return rows * scales[:, None]


def halves(matrix):
    matrix = np.asarray(matrix, np.float32)
    top = matrix.astype(ml_dtypes.bfloat16)
    rest = (matrix - top.astype(np.float32)).astype(ml_dtypes.bfloat16)
    return np.stack([top, rest])


def split(value):
    top = value.astype(bf16)
    return top, (value - top.astype(f32)).astype(bf16)


def dot(a, b, ca=1, cb=0):
    return lax.dot_general(a, b, (((ca,), (cb,)), ((), ())), preferred_element_type=f32)


def kernel(
    back, nx, ny, xr, *refs
):
    if back:
        (inc_ref, slope_ref, w_hbm, mix_ref, bz_ref, bzs_ref, ky_ref, kyt_ref, bx_ref, bxr_ref,
         out_ref, modes_ref, got_ref, *scratch) = refs
    else:
        (inc_ref, w_hbm, mix_ref, bias_ref, bz_ref, bzs_ref, ky_ref, kyt_ref, bx_ref, bxr_ref,
         out_ref, modes_ref, got_ref, *scratch) = refs
    (w_ref, sig_ref, ghi_ref, glo_ref, s_ref, r_ref, m_ref, p_ref, q_ref, qs_ref,
     send1, recv1, send2, recv2, wsem) = scratch
    channels, _, yr, zr = inc_ref.shape
    cl, jl, xp = MODES // nx, MODES // ny, r_ref.shape[2]
    n = nx * ny
    lanes = jl * channels
    gx, gy = lax.axis_index("gx"), lax.axis_index("gy")
    me = gx * ny + gy

    wcopy = pltpu.make_async_copy(w_hbm, w_ref, wsem)
    wcopy.start()

    barrier = pltpu.get_barrier_semaphore()

    def greet(k, carry):
        peer = lax.rem(me + k, n)
        pl.semaphore_signal(
            barrier, inc=1,
            device_id={"gx": peer // ny, "gy": lax.rem(peer, ny)},
            device_id_type=pl.DeviceIdType.MESH,
        )
        return carry

    lax.fori_loop(1, n, greet, 0)

    def along_z(x, carry):
        if back:
            signal = inc_ref[:, x].astype(f32) * slope_ref[:, x]
            sig_ref[:, x] = signal
            block = signal.astype(bf16)
        else:
            block = inc_ref[:, x]
        block = block.reshape(channels * yr, zr)
        g = dot(bz_ref[0], block, 1, 1) + dot(bz_ref[1], block, 1, 1)
        ghi, glo = split(g)
        rows = pl.ds(pl.multiple_of(x * MODES, MODES), MODES)
        ghi_ref[rows, :] = ghi
        glo_ref[rows, :] = glo
        return carry

    lax.fori_loop(0, xr, along_z, 0)
    ghi = ghi_ref[...]
    t = dot(ghi, ky_ref[0]) + dot(ghi, ky_ref[1]) + dot(glo_ref[...], ky_ref[0])
    t = jnp.swapaxes(t.reshape(xr, MODES, ny * lanes), 0, 1)
    if xp > xr:
        t = jnp.concatenate([t, jnp.zeros((MODES, xp - xr, ny * lanes), f32)], axis=1)
    t = t.astype(bf16)
    for h in range(ny):
        s_ref[h] = t[:, :, h * lanes : (h + 1) * lanes].reshape(nx, cl, xp, lanes)

    pl.semaphore_wait(barrier, n - 1)

    def exchange(source, target, send, recv):
        def copy_to(peer, slot_of):
            return pltpu.make_async_remote_copy(
                src_ref=source(peer // ny, lax.rem(peer, ny)),
                dst_ref=target.at[lax.rem(slot_of, ny) * nx + slot_of // ny],
                send_sem=send.at[peer],
                recv_sem=recv.at[slot_of],
                device_id={"gx": peer // ny, "gy": lax.rem(peer, ny)},
                device_id_type=pl.DeviceIdType.MESH,
            )

        def begin(k, carry):
            copy_to(lax.rem(me + k, n), me).start()
            return carry

        def finish(k, carry):
            copy_to(lax.rem(me + k, n), me).wait_send()
            peer = lax.rem(me + n - k, n)
            copy_to(peer, peer).wait_recv()
            return carry

        lax.fori_loop(1, n, begin, 0)
        target[gy * nx + gx] = source(gx, gy)[...]
        lax.fori_loop(1, n, finish, 0)

    exchange(lambda d, h: s_ref.at[h, d], r_ref, send1, recv1)

    for c in range(cl):
        part = r_ref[:, c].reshape(n * xp, lanes)
        own = dot(bx_ref[0], part) + dot(bx_ref[1], part)
        modes_ref[c] = own.T.reshape(jl, channels, MODES)
    wcopy.wait()

    def mix(j, carry):
        for c in range(cl):
            own = modes_ref[c, j]
            weight = w_ref[j, c]
            if back:
                m_ref[c, j] = jnp.sum(weight * own[None], axis=1)
            else:
                m_ref[c, j] = jnp.sum(weight * own[:, None, :], axis=0)
        return carry

    lax.fori_loop(0, jl, mix, 0)
    for c in range(cl):
        top, rest = split(m_ref[c].reshape(lanes, MODES))
        spread = (
            dot(bxr_ref[0], top, 1, 1) + dot(bxr_ref[1], top, 1, 1) + dot(bxr_ref[0], rest, 1, 1)
        )
        p_ref[:, c] = spread.astype(bf16).reshape(nx, xp, lanes)

    exchange(lambda d, h: p_ref.at[d], q_ref, send2, recv2)

    got = [q_ref[h * nx : (h + 1) * nx].reshape(MODES, xp, lanes) for h in range(ny)]
    got = jnp.concatenate(got, axis=2).astype(f32)
    got = jnp.swapaxes(got, 0, 1)[:xr].reshape(xr * MODES, ny * lanes).astype(bf16)
    got_ref[...] = got
    qs_ref[...] = dot(got, kyt_ref[0]) + dot(got, kyt_ref[1])

    def finish_field(x, carry):
        rows = pl.ds(pl.multiple_of(x * MODES, MODES), MODES)
        top, rest = split(qs_ref[rows, :])
        stack = jnp.concatenate([top, rest, top], axis=0)
        field = dot(stack, bzs_ref[...], 0, 0).reshape(channels, yr, zr)
        if back:
            values = [sig_ref[i, x] for i in range(channels)]
        else:
            values = [inc_ref[i, x].astype(f32) for i in range(channels)]
        for o in range(channels):
            total = field[o]
            for i in range(channels):
                total = total + (mix_ref[i, o] if back else mix_ref[o, i]) * values[i]
            if back:
                out_ref[o, x] = total.astype(bf16)
            else:
                total = total + bias_ref[0, o]
                cdf = 0.5 * (1.0 + lax.erf(total * 0.7071067811865476))
                out_ref[o, x] = cdf + total * jnp.exp(-0.5 * total * total) * 0.3989422804014327
        return carry

    lax.fori_loop(0, xr, finish_field, 0)


def ahead_kernel(
    act_ref, cot_ref, got_ref, got_back_ref, mix_ref, bias_ref, bzs_ref, kyt_ref, out_ref,
    pre_ref, back_ref,
):
    channels, xr, yr, zr = act_ref.shape
    pre_ref[...] = dot(got_ref[...], kyt_ref[0]) + dot(got_ref[...], kyt_ref[1])
    back_ref[...] = dot(got_back_ref[...], kyt_ref[0]) + dot(got_back_ref[...], kyt_ref[1])

    def field_of(ref, x):
        rows = pl.ds(pl.multiple_of(x * MODES, MODES), MODES)
        top, rest = split(ref[rows, :])
        stack = jnp.concatenate([top, rest, top], axis=0)
        return dot(stack, bzs_ref[...], 0, 0).reshape(channels, yr, zr)

    def step(x, carry):
        field = field_of(pre_ref, x)
        values = [act_ref[i, x].astype(f32) for i in range(channels)]
        signals = []
        for o in range(channels):
            total = field[o]
            for i in range(channels):
                total = total + mix_ref[o, i] * values[i]
            total = total + bias_ref[0, o]
            cdf = 0.5 * (1.0 + lax.erf(total * 0.7071067811865476))
            slope = cdf + total * jnp.exp(-0.5 * total * total) * 0.3989422804014327
            signals.append(cot_ref[o, x].astype(f32) * slope)
        field = field_of(back_ref, x)
        for o in range(channels):
            total = field[o]
            for i in range(channels):
                total = total + mix_ref[i, o] * signals[i]
            out_ref[o, x] = total.astype(bf16)
        return carry

    lax.fori_loop(0, xr, step, 0)


def ahead(activations, cotangent, got, got_back, mixing, bias, bzs, kyt):
    channels, xr, yr, zr = activations.shape
    vmem = pl.BlockSpec(memory_space=pltpu.VMEM)
    smem = pl.BlockSpec(memory_space=pltpu.SMEM)
    return pl.pallas_call(
        ahead_kernel,
        out_shape=jax.ShapeDtypeStruct(activations.shape, bf16),
        in_specs=[vmem] * 4 + [smem] * 2 + [vmem] * 2,
        out_specs=vmem,
        scratch_shapes=[pltpu.VMEM((xr * MODES, channels * yr), f32)] * 2,
        compiler_params=pltpu.CompilerParams(vmem_limit_bytes=50 * 2**20),
        cost_estimate=pl.CostEstimate(flops=10**9, bytes_accessed=10**7, transcendentals=10**6),
    )(activations, cotangent, got, got_back, mixing, bias, bzs, kyt)


def block_turn(back, nx, ny, collective, field, slope, weights, mixing, bias, tables):
    channels, xr, yr, zr = field.shape
    xp = -(-xr // 16) * 16
    cl, jl, n = MODES // nx, MODES // ny, nx * ny
    lanes = jl * channels
    vmem = pl.BlockSpec(memory_space=pltpu.VMEM)
    smem = pl.BlockSpec(memory_space=pltpu.SMEM)
    hbm = pl.BlockSpec(memory_space=pl.ANY)
    if back:
        args = (field, slope, weights, mixing, *tables)
        specs = [vmem, vmem, hbm, smem] + [vmem] * len(tables)
    else:
        args = (field, weights, mixing, bias, *tables)
        specs = [vmem, hbm, smem, smem] + [vmem] * len(tables)
    dma = pltpu.SemaphoreType.DMA
    return pl.pallas_call(
        functools.partial(kernel, back, nx, ny, xr),
        out_shape=(
            jax.ShapeDtypeStruct(field.shape, bf16 if back else f32),
            jax.ShapeDtypeStruct((cl, jl, channels, MODES), f32),
            jax.ShapeDtypeStruct((xr * MODES, ny * lanes), bf16),
        ),
        in_specs=specs,
        out_specs=(vmem, vmem, vmem),
        scratch_shapes=[
            pltpu.VMEM(weights.shape, f32),
            pltpu.VMEM(field.shape if back else (8, 128), f32),
            pltpu.VMEM((xr * MODES, channels * yr), bf16),
            pltpu.VMEM((xr * MODES, channels * yr), bf16),
            pltpu.VMEM((ny, nx, cl, xp, lanes), bf16),
            pltpu.VMEM((n, cl, xp, lanes), bf16),
            pltpu.VMEM((cl, jl, channels, MODES), f32),
            pltpu.VMEM((nx, cl, xp, lanes), bf16),
            pltpu.VMEM((n, cl, xp, lanes), bf16),
            pltpu.VMEM((xr * MODES, channels * yr), f32),
            dma((n,)), dma((n,)), dma((n,)), dma((n,)), dma,
        ],
        compiler_params=pltpu.CompilerParams(
            collective_id=collective, has_side_effects=True, vmem_limit_bytes=50 * 2**20
        ),
        cost_estimate=pl.CostEstimate(flops=10**9, bytes_accessed=2 * 10**7, transcendentals=10**6),
    )(*args)


def body(activations, cotangent, spectral_weights, pointwise, channel_bias):
    inputs = activations[0]
    channels, xr, yr, zr = inputs.shape
    nx, ny = lax.axis_size("gx"), lax.axis_size("gy")
    xp = -(-xr // 16) * 16
    bz = trig_basis(zr)
    bx = trig_basis(xr * nx).reshape(MODES, nx, xr)
    bx = np.concatenate([bx, np.zeros((MODES, nx, xp - xr))], axis=2).reshape(MODES, nx * xp)
    by = trig_basis(yr * ny).reshape(MODES, ny, yr)
    kron = np.einsum("jgy,ik->giyjk", by, np.eye(channels)).reshape(
        ny, channels * yr, MODES * channels
    )
    bzh = halves(bz)
    kh = halves(kron)
    gy = lax.axis_index("gy")
    ky = lax.dynamic_index_in_dim(jnp.asarray(np.swapaxes(kh, 0, 1)), gy, 0, False)
    kyt = lax.dynamic_index_in_dim(
        jnp.asarray(np.ascontiguousarray(np.transpose(kh, (1, 0, 3, 2)))), gy, 0, False
    )
    tables = (
        jnp.asarray(bzh),
        jnp.asarray(np.concatenate([bzh[0], bzh[0], bzh[1]], axis=0)),
        ky,
        kyt,
        jnp.asarray(halves(np.concatenate([bx] * ny, axis=1))),
        jnp.asarray(halves(bx.T)),
    )
    weights = spectral_weights[0]
    mixing = pointwise[0]
    following = [from_behind(v, "segment", -1) for v in (inputs, mixing, channel_bias)]
    slope, input_modes, got = block_turn(
        False, nx, ny, 0, inputs, None, weights, mixing, channel_bias, tables
    )
    next_got = from_behind(got, "segment", -1)
    segment_index = lax.axis_index("segment")
    segment_count = lax.axis_size("segment")
    incoming = cotangent
    kept_grad = jnp.zeros(cotangent.shape, bf16)
    kept_modes = jnp.zeros(input_modes.shape, f32)
    for turn_index in range(segment_count):
        active = segment_index == segment_count - 1 - turn_index
        input_grad, grad_modes, got_back = block_turn(
            True, nx, ny, 1 + turn_index, incoming, slope, weights, mixing, None, tables
        )
        kept_grad = jnp.where(active, input_grad, kept_grad)
        kept_modes = jnp.where(active, grad_modes, kept_modes)
        if turn_index == 0 and segment_count > 1:
            next_back = from_behind(got_back, "segment", -1)
            incoming = ahead(
                following[0], cotangent, next_got, next_back, following[1], following[2],
                tables[1], tables[3],
            )
        elif turn_index + 1 < segment_count:
            incoming = from_behind(input_grad, "segment", -1)
    input_modes = jnp.swapaxes(input_modes, 0, 1)
    kept_modes = jnp.swapaxes(kept_modes, 0, 1)
    weight_grad = input_modes[:, :, :, None, :] * kept_modes[:, :, None, :, :]
    return (kept_grad[None], weight_grad[None])


def slope_of(value):
    cdf = 0.5 * (1.0 + lax.erf(value * 0.7071067811865476))
    return cdf + value * jnp.exp(-0.5 * value * value) * 0.3989422804014327


def field_of(cells, ny, ky, bzi):
    blocks = []
    for h in range(ny):
        block = cells(h)
        blocks.append(block.reshape(block.shape[0] * block.shape[1], block.shape[2]))
    block = jnp.concatenate(blocks, axis=1)
    top, rest = split(dot(ky[0], block, 1, 1) + dot(ky[1], block, 1, 1))
    return dot(jnp.concatenate([top, rest, top], axis=1), bzi[...])


def relay_kernel(
    nx, ny, xq, cuts,
    act_hbm, cot_hbm, w_hbm, mix_ref, bias_ref, mixv_ref, biasv_ref,
    kyt_hbm, ky_hbm, bzf_hbm, bzi_hbm, bx_hbm, sp_hbm,
    out, rest_ref, cells_ref, wgrad, ky, bzi,
    act, act1, cot, w, wd, kyt, bzf, bx, sp,
    u, v, slope, sig, in_modes, grad_modes, m_ref, mt_send, mt_recv,
    mixv1, biasv1, mix1, bias1, s_ref, p_ref, r_ref,
    load_sem, send_sem, recv_sem, row_send, row_recv, small_send, small_recv, store_sem,
):
    channels, xr, yr, zr = act.shape
    n = nx * ny
    cl, jl = MODES // nx, MODES // ny
    nh, hq = r_ref.shape[1], r_ref.shape[3]
    lanes = jl * channels
    rows = channels * yr
    gx, gy, seg = lax.axis_index("gx"), lax.axis_index("gy"), lax.axis_index("segment")
    me = gx * ny + gy
    mine = gy * nx + gx
    first, last = seg == 0, seg == 1
    mesh_ids = pl.DeviceIdType.MESH

    loads = [
        pltpu.make_async_copy(source, target, load_sem.at[k])
        for k, (source, target) in enumerate(
            [
                (act_hbm, act), (bzf_hbm, bzf), (kyt_hbm.at[gy], kyt), (w_hbm, w), (bx_hbm, bx),
                (sp_hbm, sp), (ky_hbm.at[gy], ky), (bzi_hbm, bzi), (cot_hbm, cot),
            ]
        )
    ]
    for load in loads:
        load.start()

    barrier = pltpu.get_barrier_semaphore()

    def greet(k, carry):
        peer = lax.rem(me + k, n)
        pl.semaphore_signal(
            barrier, inc=1,
            device_id={"gx": peer // ny, "gy": lax.rem(peer, ny)},
            device_id_type=mesh_ids,
        )
        return carry

    lax.fori_loop(1, n, greet, 0)
    pl.semaphore_signal(
        barrier, inc=1, device_id={"segment": 1 - seg}, device_id_type=mesh_ids
    )

    def ahead(source, target, send, recv):
        return pltpu.make_async_remote_copy(
            src_ref=source, dst_ref=target, send_sem=send, recv_sem=recv,
            device_id={"segment": 1 - seg}, device_id_type=mesh_ids,
        )

    def row_copy(x):
        return ahead(act_hbm.at[:, x], act1.at[:, x], row_send.at[x], row_recv.at[x])

    def send_rows(start, stop):
        @pl.when(last)
        def _():
            for x in range(start, stop):
                row_copy(x).start()

    def modes_copy(k):
        return ahead(mt_send.at[k], mt_recv.at[k], small_send.at[k], small_recv.at[k])

    small = [
        ahead(mixv_ref, mixv1, small_send.at[2], small_recv.at[2]),
        ahead(biasv_ref, biasv1, small_send.at[3], small_recv.at[3]),
    ]

    def send(source, e, half):
        def begin(k, carry):
            peer = lax.rem(me + k, n)
            d, h = peer // ny, lax.rem(peer, ny)
            pltpu.make_async_remote_copy(
                src_ref=source(d, h), dst_ref=r_ref.at[e, half, mine],
                send_sem=send_sem.at[e, half], recv_sem=recv_sem.at[e, half],
                device_id={"gx": d, "gy": h}, device_id_type=mesh_ids,
            ).start()
            return carry

        lax.fori_loop(1, n, begin, 0)
        r_ref[e, half, mine] = source(gx, gy)[...]

    def arrive(e, half):
        block = r_ref.at[e, half, pl.ds(0, n - 1)]
        pltpu.make_async_copy(block, block, recv_sem.at[e, half]).wait()

    def sent(e):
        for half in range(nh):
            block = r_ref.at[e, half, pl.ds(0, n - 1)]
            pltpu.make_async_copy(block, block, send_sem.at[e, half]).wait()

    def to_modes(blocks, k, half):
        parts = []
        for block in blocks:
            g = dot(block, bzf[...])
            parts.append(g[:, : nx * 16] + g[:, nx * 16 :])
        top, rest = split(jnp.concatenate(parts, axis=1))
        t = dot(kyt[0], top) + dot(kyt[1], top) + dot(kyt[0], rest)
        t = t.T.astype(bf16)
        for q in range(hq):
            for h in range(ny):
                part = t[q * nx * 16 : (q + 1) * nx * 16, h * lanes : (h + 1) * lanes]
                s_ref[k, half, h * nx : (h + 1) * nx, q] = part.reshape(nx, 16, lanes)

    def to_field(e, half, q):
        return field_of(lambda h: r_ref[e, half, h * nx : (h + 1) * nx, q], ny, ky, bzi)

    def row(field, x):
        return field[:, x * zr : (x + 1) * zr].reshape(channels, yr, zr)

    def send_modes(k, e, half):
        send(lambda d, h: s_ref.at[k, half, h * nx + d], e, half)

    def own_modes(e):
        block = r_ref[e].reshape(nh * n * hq * 16, lanes)
        own = dot(bx[0], block) + dot(bx[1], block)
        return own.T.reshape(jl, channels, cl * MODES)

    def send_cells(mt, k, e):
        top, rest = split(mt)
        cells = dot(sp[0], top) + dot(sp[1], top) + dot(sp[0], rest)
        p_ref[k] = cells.astype(bf16).reshape(nh, nx, hq, 16, lanes)
        for half in range(nh):
            send(lambda d, h: p_ref.at[k, half, d], e, half)

    def mixed():
        return m_ref[...].reshape(lanes, cl * MODES).T

    def mix_back(e):
        for half in range(nh):
            arrive(e, half)
        grad_modes[...] = own_modes(e)

        def step(j, carry):
            m_ref[j] = jnp.sum(wd[j] * grad_modes[j][None], axis=1)
            return carry

        lax.fori_loop(0, jl, step, 0)

    def blend(mixing, values, o, back):
        total = (mixing[0, o] if back else mixing[o, 0]) * values[0]
        for i in range(1, channels):
            total = total + (mixing[i, o] if back else mixing[o, i]) * values[i]
        return total

    pl.semaphore_wait(barrier, n)

    @pl.when(last)
    def _():
        for copy in small:
            copy.start()

    send_rows(0, cuts[0])
    for load in loads[:3]:
        load.wait()
    for half in range(nh):
        blocks = []
        for q in range(hq):
            x = (half * hq + q) * xq
            block = [act[:, x + k].reshape(rows, zr) for k in range(xq)]
            blocks.append(jnp.concatenate(block, axis=1))
        to_modes(blocks, 0, half)
        send_modes(0, 0, half)

    for load in loads[3:]:
        load.wait()

    def dense(j, carry):
        for i in range(channels):
            wd[j, i] = jnp.concatenate([w[j, c, i] for c in range(cl)], axis=1)
        return carry

    lax.fori_loop(0, jl, dense, 0)

    def pointwise(x, carry):
        values = [act[i, x].astype(f32) for i in range(channels)]
        for o in range(channels):
            u[o, x] = blend(mix_ref, values, o, False) + bias_ref[0, o]
        return carry

    lax.fori_loop(0, xr, pointwise, 0)

    for half in range(nh):
        arrive(0, half)
    in_modes[...] = own_modes(0)

    def mix(j, carry):
        own = in_modes[j]
        m_ref[j] = jnp.sum(wd[j] * own[:, None, :], axis=0)
        return carry

    lax.fori_loop(0, jl, mix, 0)
    mt_send[0] = mixed()

    @pl.when(last)
    def _():
        modes_copy(0).start()

    send_rows(cuts[0], cuts[1])
    send_cells(mt_send[0], 0, 1)

    @pl.when(last)
    def _():
        for half in range(nh):
            arrive(1, half)

            blocks = []
            for q in range(hq):
                field = to_field(1, half, q)
                x0 = (half * hq + q) * xq
                block = []
                for k in range(xq):
                    signal = cot[:, x0 + k].astype(f32) * slope_of(row(field, k) + u[:, x0 + k])
                    sig[:, x0 + k] = signal
                    block.append(signal.astype(bf16).reshape(rows, zr))
                blocks.append(jnp.concatenate(block, axis=1))
            to_modes(blocks, 1, half)
            send_modes(1, 2, half)
        mix_back(2)
        mt_send[1] = mixed()
        modes_copy(1).start()
        for x in range(cuts[1], xr):
            row_copy(x).start()
        send_cells(mt_send[1], 1, 3)

    @pl.when(first)
    def _():
        modes_copy(0).wait_recv()
        send_cells(mt_recv[0], 1, 2)
        for copy in small:
            copy.wait_recv()
        for k, (source, target) in enumerate([(mixv1, mix1), (biasv1, bias1)]):
            copy = pltpu.make_async_copy(source, target, store_sem.at[k])
            copy.start()
            copy.wait()
        for half in range(nh):
            arrive(1, half)

            def step(q, carry):
                field = to_field(1, half, q)
                x0 = (half * hq + q) * xq
                for k in range(xq):
                    slope[:, x0 + k] = slope_of(row(field, k) + u[:, x0 + k])
                return carry

            lax.fori_loop(0, hq, step, 0)

        def ahead_quarter(half, q):
            field = to_field(2, half, q)
            x0 = (half * hq + q) * xq
            for k in range(xq):
                row_copy(x0 + k).wait_recv()
                values = [act1[i, x0 + k].astype(f32) for i in range(channels)]
                here = row(field, k)
                signals = []
                for o in range(channels):
                    pre = here[o] + blend(mix1, values, o, False) + bias1[0, o]
                    signals.append(cot[o, x0 + k].astype(f32) * slope_of(pre))
                for i in range(channels):
                    v[i, x0 + k] = blend(mix1, signals, i, True)

        def back_half(half):
            blocks = []
            for q in range(hq):
                field = to_field(3, half, q)
                x0 = (half * hq + q) * xq
                block = []
                for k in range(xq):
                    incoming = (row(field, k) + v[:, x0 + k]).astype(bf16).astype(f32)
                    signal = incoming * slope[:, x0 + k]
                    sig[:, x0 + k] = signal
                    block.append(signal.astype(bf16).reshape(rows, zr))
                blocks.append(jnp.concatenate(block, axis=1))
            to_modes(blocks, 1, half)
            send_modes(1, 4, half)

        for half in range(nh):
            arrive(2, half)
        quarters = [(half, q) for half in range(nh) for q in range(hq)]
        early = cuts[1] // xq
        for half, q in quarters[:early]:
            ahead_quarter(half, q)
        modes_copy(1).wait_recv()
        send_cells(mt_recv[1], 2, 3)
        for half, q in quarters[early:]:
            ahead_quarter(half, q)
            if (half, q) == (nh - 1, 0):
                for back in range(nh):
                    arrive(3, back)
                for back in range(nh - 1):
                    back_half(back)
        back_half(nh - 1)
        mix_back(4)
        send_cells(mixed(), 3, 5)

    def pointwise_back(x, carry):
        values = [sig[i, x] for i in range(channels)]
        for o in range(channels):
            u[o, x] = blend(mix_ref, values, o, True)
        return carry

    lax.fori_loop(0, xr, pointwise_back, 0)

    def weight_grad(j, carry):
        for c in range(cl):
            part = slice(c * MODES, (c + 1) * MODES)
            wgrad[j, c] = in_modes[j][:, None, part] * grad_modes[j][None, :, part]
        return carry

    lax.fori_loop(0, jl, weight_grad, 0)
    e = 3 + 2 * (1 - seg)
    for half in range(nh - 1):
        arrive(e, half)
        for q in range(hq):
            field = to_field(e, half, q)
            x0 = (half * hq + q) * xq
            for k in range(xq):
                out[:, x0 + k] = (row(field, k) + u[:, x0 + k]).astype(bf16)
    done = (nh - 1) * hq * xq
    rest_ref[...] = u[:, done:]
    arrive(e, nh - 1)
    cells_ref[...] = r_ref[e, nh - 1]
    for e in range(4):
        sent(e)

    @pl.when(first)
    def _():
        sent(4)
        sent(5)

    @pl.when(last)
    def _():
        for copy in small:
            copy.wait_send()
        for x in range(xr):
            row_copy(x).wait_send()
        for k in range(2):
            modes_copy(k).wait_send()


def finish_kernel(
    nx, ny, xq, done_ref, rest_ref, cells_ref, wgrad, ky, bzi, grad_hbm, wgrad_hbm, out, sem
):
    channels, done, yr, zr = done_ref.shape
    hq = cells_ref.shape[1]
    stores = [
        pltpu.make_async_copy(wgrad, wgrad_hbm, sem.at[0]),
        pltpu.make_async_copy(done_ref, grad_hbm.at[:, pl.ds(0, done)], sem.at[1]),
    ]
    for store in stores:
        store.start()
    for q in range(hq):
        field = field_of(lambda h: cells_ref[h * nx : (h + 1) * nx, q], ny, ky, bzi)
        for k in range(xq):
            x = q * xq + k
            here = field[:, k * zr : (k + 1) * zr].reshape(channels, yr, zr)
            out[:, x] = (here + rest_ref[:, x]).astype(bf16)
        part = pl.ds(q * xq, xq)
        store = pltpu.make_async_copy(
            out.at[:, part], grad_hbm.at[:, pl.ds(done + q * xq, xq)], sem.at[2 + q]
        )
        store.start()
        stores.append(store)
    for store in stores:
        store.wait()


def two_section_body(activations, cotangent, spectral_weights, pointwise, channel_bias):
    inputs = activations[0]
    channels, xr, yr, zr = inputs.shape
    nx, ny = lax.axis_size("gx"), lax.axis_size("gy")
    n = nx * ny
    cl, jl = MODES // nx, MODES // ny
    xq = 16 // cl
    nh = 2
    hq = xr // (nh * xq)
    lanes, rows = jl * channels, channels * yr
    bz = trig_basis(zr).reshape(nx, cl, zr)
    eye_x, eye_c = np.eye(xq), np.eye(cl)
    bzf = np.einsum("dcz,xX->xzdXc", bz, eye_x).reshape(xq * zr, nx * 16)
    bzi = halves(bzf.reshape(xq, zr, nx * 16).transpose(2, 0, 1).reshape(nx * 16, xq * zr))
    by = trig_basis(yr * ny).reshape(MODES, ny, yr)
    ky = np.einsum("jgy,ik->giyjk", by, np.eye(channels)).reshape(ny, rows, ny * lanes)
    ky = halves(ky)
    bx = trig_basis(xr * nx).reshape(MODES, nx, nh, hq, xq)
    sp = np.einsum("adtqx,cC->tdqxCca", bx, eye_c).reshape(nh * nx * hq * 16, cl * MODES)
    bxf = np.broadcast_to(
        sp.reshape(nh, 1, nx * hq * 16, cl * MODES), (nh, ny, nx * hq * 16, cl * MODES)
    )
    bxf = bxf.reshape(nh * n * hq * 16, cl * MODES).T
    bzf = halves(bzf)
    tables = [
        np.ascontiguousarray(ky.transpose(1, 0, 3, 2)),
        np.ascontiguousarray(ky.transpose(1, 0, 2, 3)),
        np.concatenate([bzf[0], bzf[1]], axis=1),
        np.concatenate([bzi[0], bzi[0], bzi[1]], axis=0),
        halves(bxf),
        halves(sp),
    ]
    weights, mixing = spectral_weights[0], pointwise[0]
    vmem = pl.BlockSpec(memory_space=pltpu.VMEM)
    smem = pl.BlockSpec(memory_space=pltpu.SMEM)
    hbm = pl.BlockSpec(memory_space=pl.ANY)
    dma = pltpu.SemaphoreType.DMA
    grid = inputs.shape
    done = grid[:1] + ((nh - 1) * hq * xq,) + grid[2:]
    left = grid[:1] + (hq * xq,) + grid[2:]
    scratch = [
        pltpu.VMEM(grid, bf16), pltpu.VMEM(grid, bf16), pltpu.VMEM(grid, bf16),
        pltpu.VMEM(weights.shape, f32),
        pltpu.VMEM((jl, channels, channels, cl * MODES), f32),
        pltpu.VMEM((2, ny * lanes, rows), bf16),
        pltpu.VMEM((xq * zr, 2 * nx * 16), bf16),
        pltpu.VMEM((2, cl * MODES, nh * n * hq * 16), bf16),
        pltpu.VMEM((2, nh * nx * hq * 16, cl * MODES), bf16),
        pltpu.VMEM(grid, f32), pltpu.VMEM(grid, f32), pltpu.VMEM(grid, f32), pltpu.VMEM(grid, f32),
        pltpu.VMEM((jl, channels, cl * MODES), f32),
        pltpu.VMEM((jl, channels, cl * MODES), f32),
        pltpu.VMEM((jl, channels, cl * MODES), f32),
        pltpu.VMEM((2, cl * MODES, lanes), f32),
        pltpu.VMEM((2, cl * MODES, lanes), f32),
        pltpu.VMEM(mixing.shape, f32), pltpu.VMEM(channel_bias.shape, f32),
        pltpu.SMEM(mixing.shape, f32), pltpu.SMEM(channel_bias.shape, f32),
        pltpu.VMEM((2, nh, n, hq, 16, lanes), bf16),
        pltpu.VMEM((4, nh, nx, hq, 16, lanes), bf16),
        pltpu.VMEM((6, nh, n, hq, 16, lanes), bf16),
        dma((9,)), dma((6, nh)), dma((6, nh)),
        dma((xr,)), dma((xr,)), dma((4,)), dma((4,)), dma((2,)),
    ]
    parts = pl.pallas_call(
        functools.partial(relay_kernel, nx, ny, xq, (3, 9)),
        out_shape=(
            jax.ShapeDtypeStruct(done, bf16),
            jax.ShapeDtypeStruct(left, f32),
            jax.ShapeDtypeStruct((n, hq, 16, lanes), bf16),
            pltpu.VMEM(weights.shape, f32),
            jax.ShapeDtypeStruct((2, rows, ny * lanes), bf16),
            jax.ShapeDtypeStruct((3 * nx * 16, xq * zr), bf16),
        ),
        in_specs=[hbm, hbm, hbm, smem, smem, vmem, vmem] + [hbm] * len(tables),
        out_specs=[vmem] * 6,
        scratch_shapes=scratch,
        compiler_params=pltpu.CompilerParams(
            collective_id=0, has_side_effects=True, vmem_limit_bytes=46 * 2**20
        ),
        cost_estimate=pl.CostEstimate(
            flops=4 * 10**9, bytes_accessed=2 * 10**7, transcendentals=10**7
        ),
    )(
        inputs, cotangent, weights, mixing, channel_bias, mixing, channel_bias,
        *[pltpu.with_memory_space_constraint(jnp.asarray(table), pltpu.HBM) for table in tables],
    )
    input_grad, weight_grad = pl.pallas_call(
        functools.partial(finish_kernel, nx, ny, xq),
        out_shape=(
            jax.ShapeDtypeStruct(grid, bf16),
            jax.ShapeDtypeStruct(weights.shape, f32),
        ),
        in_specs=[vmem] * 6,
        out_specs=(hbm, hbm),
        scratch_shapes=[pltpu.VMEM(left, bf16), dma((2 + hq,))],
        compiler_params=pltpu.CompilerParams(vmem_limit_bytes=24 * 2**20),
        cost_estimate=pl.CostEstimate(flops=10**9, bytes_accessed=10**7, transcendentals=0),
    )(*parts)
    return (input_grad[None], weight_grad[None])


def fits(mesh):
    nx = mesh.shape["gx"]
    return mesh.shape["segment"] == 2 and mesh.shape["gy"] == 2 and nx == 8


def solution(mesh):
    return jax.shard_map(
        two_section_body if fits(mesh) else body,
        mesh=mesh,
        in_specs=(
            P("segment", "groups", "gx", "gy", None),
            P("groups", "gx", "gy", None),
            P("segment", "gy", "gx", None, None, None),
            P("segment", None, None),
            P("segment", None),
        ),
        out_specs=(
            P("segment", "groups", "gx", "gy", None),
            P("segment", "gy", "gx", "groups", None, None),
        ),
        check_vma=False,
    )
```

```python
import functools
import math

import jax
import jax.numpy as jnp
import ml_dtypes
import numpy as np
from jax import lax
from jax.experimental import pallas as pl
from jax.experimental.pallas import tpu as pltpu
from jax.sharding import PartitionSpec as P

MODES = 32
f32, bf16 = jnp.float32, jnp.bfloat16


def from_behind(block, axis, distance):
    devices = range(lax.axis_size(axis))
    route = [(i - distance, i) for i in devices if i - distance in devices]
    return lax.ppermute(block, axis, route)


def trig_basis(length):
    half = MODES // 2
    freqs = np.arange(half)[:, None]
    points = np.arange(length)[None, :]
    step = 2.0 * math.pi / length
    rows = np.concatenate(
        [np.cos((freqs * points % length) * step), np.sin(((freqs + 1) * points % length) * step)]
    )
    scales = np.where(np.arange(MODES) == 0, 1.0 / math.sqrt(length), math.sqrt(2.0 / length))
    return rows * scales[:, None]


def halves(matrix):
    matrix = np.asarray(matrix, np.float32)
    top = matrix.astype(ml_dtypes.bfloat16)
    rest = (matrix - top.astype(np.float32)).astype(ml_dtypes.bfloat16)
    return np.stack([top, rest])


def split(value):
    top = value.astype(bf16)
    return top, (value - top.astype(f32)).astype(bf16)


def dot(a, b, ca=1, cb=0):
    return lax.dot_general(a, b, (((ca,), (cb,)), ((), ())), preferred_element_type=f32)


def kernel(
    back, nx, ny, xr, *refs
):
    if back:
        (inc_ref, slope_ref, w_hbm, mix_ref, bz_ref, bzs_ref, ky_ref, kyt_ref, bx_ref, bxr_ref,
         out_ref, modes_ref, got_ref, *scratch) = refs
    else:
        (inc_ref, w_hbm, mix_ref, bias_ref, bz_ref, bzs_ref, ky_ref, kyt_ref, bx_ref, bxr_ref,
         out_ref, modes_ref, got_ref, *scratch) = refs
    (w_ref, sig_ref, ghi_ref, glo_ref, s_ref, r_ref, m_ref, p_ref, q_ref, qs_ref,
     send1, recv1, send2, recv2, wsem) = scratch
    channels, _, yr, zr = inc_ref.shape
    cl, jl, xp = MODES // nx, MODES // ny, r_ref.shape[2]
    n = nx * ny
    lanes = jl * channels
    gx, gy = lax.axis_index("gx"), lax.axis_index("gy")
    me = gx * ny + gy

    wcopy = pltpu.make_async_copy(w_hbm, w_ref, wsem)
    wcopy.start()

    barrier = pltpu.get_barrier_semaphore()

    def greet(k, carry):
        peer = lax.rem(me + k, n)
        pl.semaphore_signal(
            barrier, inc=1,
            device_id={"gx": peer // ny, "gy": lax.rem(peer, ny)},
            device_id_type=pl.DeviceIdType.MESH,
        )
        return carry

    lax.fori_loop(1, n, greet, 0)

    def along_z(x, carry):
        if back:
            signal = inc_ref[:, x].astype(f32) * slope_ref[:, x]
            sig_ref[:, x] = signal
            block = signal.astype(bf16)
        else:
            block = inc_ref[:, x]
        block = block.reshape(channels * yr, zr)
        g = dot(bz_ref[0], block, 1, 1) + dot(bz_ref[1], block, 1, 1)
        ghi, glo = split(g)
        rows = pl.ds(pl.multiple_of(x * MODES, MODES), MODES)
        ghi_ref[rows, :] = ghi
        glo_ref[rows, :] = glo
        return carry

    lax.fori_loop(0, xr, along_z, 0)
    ghi = ghi_ref[...]
    t = dot(ghi, ky_ref[0]) + dot(ghi, ky_ref[1]) + dot(glo_ref[...], ky_ref[0])
    t = jnp.swapaxes(t.reshape(xr, MODES, ny * lanes), 0, 1)
    if xp > xr:
        t = jnp.concatenate([t, jnp.zeros((MODES, xp - xr, ny * lanes), f32)], axis=1)
    t = t.astype(bf16)
    for h in range(ny):
        s_ref[h] = t[:, :, h * lanes : (h + 1) * lanes].reshape(nx, cl, xp, lanes)

    pl.semaphore_wait(barrier, n - 1)

    def exchange(source, target, send, recv):
        def copy_to(peer, slot_of):
            return pltpu.make_async_remote_copy(
                src_ref=source(peer // ny, lax.rem(peer, ny)),
                dst_ref=target.at[lax.rem(slot_of, ny) * nx + slot_of // ny],
                send_sem=send.at[peer],
                recv_sem=recv.at[slot_of],
                device_id={"gx": peer // ny, "gy": lax.rem(peer, ny)},
                device_id_type=pl.DeviceIdType.MESH,
            )

        def begin(k, carry):
            copy_to(lax.rem(me + k, n), me).start()
            return carry

        def finish(k, carry):
            copy_to(lax.rem(me + k, n), me).wait_send()
            peer = lax.rem(me + n - k, n)
            copy_to(peer, peer).wait_recv()
            return carry

        lax.fori_loop(1, n, begin, 0)
        target[gy * nx + gx] = source(gx, gy)[...]
        lax.fori_loop(1, n, finish, 0)

    exchange(lambda d, h: s_ref.at[h, d], r_ref, send1, recv1)

    for c in range(cl):
        part = r_ref[:, c].reshape(n * xp, lanes)
        own = dot(bx_ref[0], part) + dot(bx_ref[1], part)
        modes_ref[c] = own.T.reshape(jl, channels, MODES)
    wcopy.wait()

    def mix(j, carry):
        for c in range(cl):
            own = modes_ref[c, j]
            weight = w_ref[j, c]
            if back:
                m_ref[c, j] = jnp.sum(weight * own[None], axis=1)
            else:
                m_ref[c, j] = jnp.sum(weight * own[:, None, :], axis=0)
        return carry

    lax.fori_loop(0, jl, mix, 0)
    for c in range(cl):
        top, rest = split(m_ref[c].reshape(lanes, MODES))
        spread = (
            dot(bxr_ref[0], top, 1, 1) + dot(bxr_ref[1], top, 1, 1) + dot(bxr_ref[0], rest, 1, 1)
        )
        p_ref[:, c] = spread.astype(bf16).reshape(nx, xp, lanes)

    exchange(lambda d, h: p_ref.at[d], q_ref, send2, recv2)

    got = [q_ref[h * nx : (h + 1) * nx].reshape(MODES, xp, lanes) for h in range(ny)]
    got = jnp.concatenate(got, axis=2).astype(f32)
    got = jnp.swapaxes(got, 0, 1)[:xr].reshape(xr * MODES, ny * lanes).astype(bf16)
    got_ref[...] = got
    qs_ref[...] = dot(got, kyt_ref[0]) + dot(got, kyt_ref[1])

    def finish_field(x, carry):
        rows = pl.ds(pl.multiple_of(x * MODES, MODES), MODES)
        top, rest = split(qs_ref[rows, :])
        stack = jnp.concatenate([top, rest, top], axis=0)
        field = dot(stack, bzs_ref[...], 0, 0).reshape(channels, yr, zr)
        if back:
            values = [sig_ref[i, x] for i in range(channels)]
        else:
            values = [inc_ref[i, x].astype(f32) for i in range(channels)]
        for o in range(channels):
            total = field[o]
            for i in range(channels):
                total = total + (mix_ref[i, o] if back else mix_ref[o, i]) * values[i]
            if back:
                out_ref[o, x] = total.astype(bf16)
            else:
                total = total + bias_ref[0, o]
                cdf = 0.5 * (1.0 + lax.erf(total * 0.7071067811865476))
                out_ref[o, x] = cdf + total * jnp.exp(-0.5 * total * total) * 0.3989422804014327
        return carry

    lax.fori_loop(0, xr, finish_field, 0)


def ahead_kernel(
    act_ref, cot_ref, got_ref, got_back_ref, mix_ref, bias_ref, bzs_ref, kyt_ref, out_ref,
    pre_ref, back_ref,
):
    channels, xr, yr, zr = act_ref.shape
    pre_ref[...] = dot(got_ref[...], kyt_ref[0]) + dot(got_ref[...], kyt_ref[1])
    back_ref[...] = dot(got_back_ref[...], kyt_ref[0]) + dot(got_back_ref[...], kyt_ref[1])

    def field_of(ref, x):
        rows = pl.ds(pl.multiple_of(x * MODES, MODES), MODES)
        top, rest = split(ref[rows, :])
        stack = jnp.concatenate([top, rest, top], axis=0)
        return dot(stack, bzs_ref[...], 0, 0).reshape(channels, yr, zr)

    def step(x, carry):
        field = field_of(pre_ref, x)
        values = [act_ref[i, x].astype(f32) for i in range(channels)]
        signals = []
        for o in range(channels):
            total = field[o]
            for i in range(channels):
                total = total + mix_ref[o, i] * values[i]
            total = total + bias_ref[0, o]
            cdf = 0.5 * (1.0 + lax.erf(total * 0.7071067811865476))
            slope = cdf + total * jnp.exp(-0.5 * total * total) * 0.3989422804014327
            signals.append(cot_ref[o, x].astype(f32) * slope)
        field = field_of(back_ref, x)
        for o in range(channels):
            total = field[o]
            for i in range(channels):
                total = total + mix_ref[i, o] * signals[i]
            out_ref[o, x] = total.astype(bf16)
        return carry

    lax.fori_loop(0, xr, step, 0)


def ahead(activations, cotangent, got, got_back, mixing, bias, bzs, kyt):
    channels, xr, yr, zr = activations.shape
    vmem = pl.BlockSpec(memory_space=pltpu.VMEM)
    smem = pl.BlockSpec(memory_space=pltpu.SMEM)
    return pl.pallas_call(
        ahead_kernel,
        out_shape=jax.ShapeDtypeStruct(activations.shape, bf16),
        in_specs=[vmem] * 4 + [smem] * 2 + [vmem] * 2,
        out_specs=vmem,
        scratch_shapes=[pltpu.VMEM((xr * MODES, channels * yr), f32)] * 2,
        compiler_params=pltpu.CompilerParams(vmem_limit_bytes=50 * 2**20),
        cost_estimate=pl.CostEstimate(flops=10**9, bytes_accessed=10**7, transcendentals=10**6),
    )(activations, cotangent, got, got_back, mixing, bias, bzs, kyt)


def block_turn(back, nx, ny, collective, field, slope, weights, mixing, bias, tables):
    channels, xr, yr, zr = field.shape
    xp = -(-xr // 16) * 16
    cl, jl, n = MODES // nx, MODES // ny, nx * ny
    lanes = jl * channels
    vmem = pl.BlockSpec(memory_space=pltpu.VMEM)
    smem = pl.BlockSpec(memory_space=pltpu.SMEM)
    hbm = pl.BlockSpec(memory_space=pl.ANY)
    if back:
        args = (field, slope, weights, mixing, *tables)
        specs = [vmem, vmem, hbm, smem] + [vmem] * len(tables)
    else:
        args = (field, weights, mixing, bias, *tables)
        specs = [vmem, hbm, smem, smem] + [vmem] * len(tables)
    dma = pltpu.SemaphoreType.DMA
    return pl.pallas_call(
        functools.partial(kernel, back, nx, ny, xr),
        out_shape=(
            jax.ShapeDtypeStruct(field.shape, bf16 if back else f32),
            jax.ShapeDtypeStruct((cl, jl, channels, MODES), f32),
            jax.ShapeDtypeStruct((xr * MODES, ny * lanes), bf16),
        ),
        in_specs=specs,
        out_specs=(vmem, vmem, vmem),
        scratch_shapes=[
            pltpu.VMEM(weights.shape, f32),
            pltpu.VMEM(field.shape if back else (8, 128), f32),
            pltpu.VMEM((xr * MODES, channels * yr), bf16),
            pltpu.VMEM((xr * MODES, channels * yr), bf16),
            pltpu.VMEM((ny, nx, cl, xp, lanes), bf16),
            pltpu.VMEM((n, cl, xp, lanes), bf16),
            pltpu.VMEM((cl, jl, channels, MODES), f32),
            pltpu.VMEM((nx, cl, xp, lanes), bf16),
            pltpu.VMEM((n, cl, xp, lanes), bf16),
            pltpu.VMEM((xr * MODES, channels * yr), f32),
            dma((n,)), dma((n,)), dma((n,)), dma((n,)), dma,
        ],
        compiler_params=pltpu.CompilerParams(
            collective_id=collective, has_side_effects=True, vmem_limit_bytes=50 * 2**20
        ),
        cost_estimate=pl.CostEstimate(flops=10**9, bytes_accessed=2 * 10**7, transcendentals=10**6),
    )(*args)


def body(activations, cotangent, spectral_weights, pointwise, channel_bias):
    inputs = activations[0]
    channels, xr, yr, zr = inputs.shape
    nx, ny = lax.axis_size("gx"), lax.axis_size("gy")
    xp = -(-xr // 16) * 16
    bz = trig_basis(zr)
    bx = trig_basis(xr * nx).reshape(MODES, nx, xr)
    bx = np.concatenate([bx, np.zeros((MODES, nx, xp - xr))], axis=2).reshape(MODES, nx * xp)
    by = trig_basis(yr * ny).reshape(MODES, ny, yr)
    kron = np.einsum("jgy,ik->giyjk", by, np.eye(channels)).reshape(
        ny, channels * yr, MODES * channels
    )
    bzh = halves(bz)
    kh = halves(kron)
    gy = lax.axis_index("gy")
    ky = lax.dynamic_index_in_dim(jnp.asarray(np.swapaxes(kh, 0, 1)), gy, 0, False)
    kyt = lax.dynamic_index_in_dim(
        jnp.asarray(np.ascontiguousarray(np.transpose(kh, (1, 0, 3, 2)))), gy, 0, False
    )
    tables = (
        jnp.asarray(bzh),
        jnp.asarray(np.concatenate([bzh[0], bzh[0], bzh[1]], axis=0)),
        ky,
        kyt,
        jnp.asarray(halves(np.concatenate([bx] * ny, axis=1))),
        jnp.asarray(halves(bx.T)),
    )
    weights = spectral_weights[0]
    mixing = pointwise[0]
    following = [from_behind(v, "segment", -1) for v in (inputs, mixing, channel_bias)]
    slope, input_modes, got = block_turn(
        False, nx, ny, 0, inputs, None, weights, mixing, channel_bias, tables
    )
    next_got = from_behind(got, "segment", -1)
    segment_index = lax.axis_index("segment")
    segment_count = lax.axis_size("segment")
    incoming = cotangent
    kept_grad = jnp.zeros(cotangent.shape, bf16)
    kept_modes = jnp.zeros(input_modes.shape, f32)
    for turn_index in range(segment_count):
        active = segment_index == segment_count - 1 - turn_index
        input_grad, grad_modes, got_back = block_turn(
            True, nx, ny, 1 + turn_index, incoming, slope, weights, mixing, None, tables
        )
        kept_grad = jnp.where(active, input_grad, kept_grad)
        kept_modes = jnp.where(active, grad_modes, kept_modes)
        if turn_index == 0 and segment_count > 1:
            next_back = from_behind(got_back, "segment", -1)
            incoming = ahead(
                following[0], cotangent, next_got, next_back, following[1], following[2],
                tables[1], tables[3],
            )
        elif turn_index + 1 < segment_count:
            incoming = from_behind(input_grad, "segment", -1)
    input_modes = jnp.swapaxes(input_modes, 0, 1)
    kept_modes = jnp.swapaxes(kept_modes, 0, 1)
    weight_grad = input_modes[:, :, :, None, :] * kept_modes[:, :, None, :, :]
    return (kept_grad[None], weight_grad[None])


def slope_of(value):
    cdf = 0.5 * (1.0 + lax.erf(value * 0.7071067811865476))
    return cdf + value * jnp.exp(-0.5 * value * value) * 0.3989422804014327


def field_of(cells, ny, ky, bzi):
    blocks = []
    for h in range(ny):
        block = cells(h)
        blocks.append(block.reshape(block.shape[0] * block.shape[1], block.shape[2]))
    block = jnp.concatenate(blocks, axis=1)
    top, rest = split(dot(ky[0], block, 1, 1) + dot(ky[1], block, 1, 1))
    return dot(jnp.concatenate([top, rest, top], axis=1), bzi[...])


def relay_kernel(
    nx, ny, xq, cuts,
    act_hbm, cot_hbm, w_hbm, mix_ref, bias_ref, mix_hbm, bias_hbm,
    kyt_hbm, ky_hbm, bzf_hbm, bzi_hbm, bx_hbm, sp_hbm,
    out, rest_ref, cells_ref, wgrad, ky, bzi,
    act, act1, cot, w, wd, kyt, bzf, bx, sp,
    u, v, slope, sig, in_modes, grad_modes, m_ref, mt_send, mt_recv,
    mixv1, biasv1, mix1, bias1, s_ref, p_ref, r_ref,
    load_sem, send_sem, recv_sem, row_send, row_recv, small_send, small_recv, store_sem,
    tail_send, tail_recv,
):
    channels, xr, yr, zr = act.shape
    n = nx * ny
    cl, jl = MODES // nx, MODES // ny
    nh, hq = r_ref.shape[1], r_ref.shape[3]
    lanes = jl * channels
    rows = channels * yr
    tail = xr - xq
    gx, gy, seg = lax.axis_index("gx"), lax.axis_index("gy"), lax.axis_index("segment")
    me = gx * ny + gy
    mine = gy * nx + gx
    first, last = seg == 0, seg == 1
    mesh_ids = pl.DeviceIdType.MESH

    loads = [
        pltpu.make_async_copy(source, target, load_sem.at[k])
        for k, (source, target) in enumerate(
            [
                (act_hbm, act), (bzf_hbm, bzf), (kyt_hbm.at[gy], kyt), (w_hbm, w), (bx_hbm, bx),
                (sp_hbm, sp), (ky_hbm.at[gy], ky), (bzi_hbm, bzi), (cot_hbm, cot),
            ]
        )
    ]
    for load in loads:
        load.start()

    barrier = pltpu.get_barrier_semaphore()

    def greet(k, carry):
        other = lax.rem(seg * n + me + k, 2 * n)
        peer = lax.rem(other, n)
        pl.semaphore_signal(
            barrier, inc=1,
            device_id={"segment": other // n, "gx": peer // ny, "gy": lax.rem(peer, ny)},
            device_id_type=mesh_ids,
        )
        return carry

    lax.fori_loop(1, 2 * n, greet, 0)

    def ahead(source, target, send, recv):
        return pltpu.make_async_remote_copy(
            src_ref=source, dst_ref=target, send_sem=send, recv_sem=recv,
            device_id={"segment": 1 - seg}, device_id_type=mesh_ids,
        )

    def row_copy(x):
        return ahead(act_hbm.at[:, x], act1.at[:, x], row_send.at[x], row_recv.at[x])

    def send_rows(start, stop):
        for x in range(start, stop):
            row_copy(x).start()

    def modes_copy(k):
        return ahead(mt_send.at[k], mt_recv.at[k], small_send.at[k], small_recv.at[k])

    small = [
        ahead(mix_hbm, mixv1, small_send.at[2], small_recv.at[2]),
        ahead(bias_hbm, biasv1, small_send.at[3], small_recv.at[3]),
    ]

    def send(source, target, sends, receives):
        def begin(k, carry):
            peer = lax.rem(me + k, n)
            d, h = peer // ny, lax.rem(peer, ny)
            pltpu.make_async_remote_copy(
                src_ref=source(d, h), dst_ref=target, send_sem=sends, recv_sem=receives,
                device_id={"gx": d, "gy": h}, device_id_type=mesh_ids,
            ).start()
            return carry

        lax.fori_loop(1, n, begin, 0)
        target[...] = source(gx, gy)[...]

    def send_half(source, e, half):
        send(source, r_ref.at[e, half, mine], send_sem.at[e, half], recv_sem.at[e, half])

    def send_quarter(source, e, half, q):
        send(source, r_ref.at[e, half, mine, q], send_sem.at[e, half], recv_sem.at[e, half])

    def send_tail(k, carry):
        peer = lax.rem(me + k, n)
        d, h = peer // ny, lax.rem(peer, ny)
        pltpu.make_async_remote_copy(
            src_ref=s_ref.at[2, nh - 1, h * nx + d, hq - 1],
            dst_ref=r_ref.at[4, nh - 1, mine, hq - 1],
            send_sem=tail_send.at[0], recv_sem=tail_recv.at[0],
            device_id={"segment": 0, "gx": d, "gy": h}, device_id_type=mesh_ids,
        ).start()
        return carry

    def await_block(block, sem):
        pltpu.make_async_copy(block, block, sem).wait()

    def arrive(e, half):
        await_block(r_ref.at[e, half, pl.ds(0, n - 1)], recv_sem.at[e, half])

    def arrive_quarter(e, half, q):
        await_block(r_ref.at[e, half, pl.ds(0, n - 1), q], recv_sem.at[e, half])

    def sent(e, half):
        await_block(r_ref.at[e, half, pl.ds(0, n - 1)], send_sem.at[e, half])

    def sent_quarter(e, half, q):
        await_block(r_ref.at[e, half, pl.ds(0, n - 1), q], send_sem.at[e, half])

    def to_modes(blocks, k, half, q0):
        parts = []
        for block in blocks:
            g = dot(block, bzf[...])
            parts.append(g[:, : nx * 16] + g[:, nx * 16 :])
        top, rest = split(jnp.concatenate(parts, axis=1))
        t = dot(kyt[0], top) + dot(kyt[1], top) + dot(kyt[0], rest)
        t = t.T.astype(bf16)
        for q in range(len(blocks)):
            for h in range(ny):
                part = t[q * nx * 16 : (q + 1) * nx * 16, h * lanes : (h + 1) * lanes]
                s_ref[k, half, h * nx : (h + 1) * nx, q0 + q] = part.reshape(nx, 16, lanes)

    def to_field(e, half, q):
        return field_of(lambda h: r_ref[e, half, h * nx : (h + 1) * nx, q], ny, ky, bzi)

    def row(field, x):
        return field[:, x * zr : (x + 1) * zr].reshape(channels, yr, zr)

    def send_modes(k, e, half):
        send_half(lambda d, h: s_ref.at[k, half, h * nx + d], e, half)

    def own_modes(e):
        block = r_ref[e].reshape(nh * n * hq * 16, lanes)
        own = dot(bx[0], block) + dot(bx[1], block)
        return own.T.reshape(jl, channels, cl * MODES)

    def cells_of(table, mt):
        top, rest = split(mt)
        return (dot(table[0], top) + dot(table[1], top) + dot(table[0], rest)).astype(bf16)

    def send_cells(mt, k, e):
        table = [sp[i].reshape(nh * nx * hq * 16, cl * MODES) for i in range(2)]
        p_ref[k] = cells_of(table, mt).reshape(nh, nx, hq, 16, lanes)
        for half in range(nh):
            send_half(lambda d, h: p_ref.at[k, half, d], e, half)

    def mixed():
        return m_ref[...].reshape(lanes, cl * MODES).T

    def mix_back(e):
        grad_modes[...] = own_modes(e)

        def step(j, carry):
            m_ref[j] = jnp.sum(wd[j] * grad_modes[j][None], axis=1)
            return carry

        lax.fori_loop(0, jl, step, 0)

    def blend(mixing, values, o, back):
        total = (mixing[0, o] if back else mixing[o, 0]) * values[0]
        for i in range(1, channels):
            total = total + (mixing[i, o] if back else mixing[o, i]) * values[i]
        return total

    def fetch_small():
        for copy in small:
            copy.wait_recv()
        for k, (source, target) in enumerate([(mixv1, mix1), (biasv1, bias1)]):
            copy = pltpu.make_async_copy(source, target, store_sem.at[k])
            copy.start()
            copy.wait()

    def back_block(half, q, offset):
        field = to_field(3, half, q)
        x0 = (half * hq + q) * xq
        block = []
        for k in range(xq):
            incoming = (row(field, k) + offset[:, x0 + k]).astype(bf16).astype(f32)
            signal = incoming * slope[:, x0 + k]
            block.append((x0 + k, signal))
        return block

    def packed(block):
        return jnp.concatenate([s.astype(bf16).reshape(rows, zr) for _, s in block], axis=1)

    def blend_back(start, stop):
        def step(x, carry):
            values = [sig[i, x] for i in range(channels)]
            for o in range(channels):
                u[o, x] = blend(mix_ref, values, o, True)
            return carry

        lax.fori_loop(start, stop, step, 0)

    pl.semaphore_wait(barrier, 2 * n - 1)
    for copy in small:
        copy.start()

    @pl.when(last)
    def _():
        send_rows(0, cuts[0])

    @pl.when(first)
    def _():
        send_rows(tail, xr)

    for load in loads[:3]:
        load.wait()
    for half in range(nh):
        blocks = []
        for q in range(hq):
            x = (half * hq + q) * xq
            block = [act[:, x + k].reshape(rows, zr) for k in range(xq)]
            blocks.append(jnp.concatenate(block, axis=1))
        to_modes(blocks, 0, half, 0)
        send_modes(0, 0, half)

    for load in loads[3:]:
        load.wait()

    def dense(j, carry):
        for i in range(channels):
            wd[j, i] = jnp.concatenate([w[j, c, i] for c in range(cl)], axis=1)
        return carry

    lax.fori_loop(0, jl, dense, 0)

    def pointwise(x, carry):
        values = [act[i, x].astype(f32) for i in range(channels)]
        for o in range(channels):
            u[o, x] = blend(mix_ref, values, o, False) + bias_ref[0, o]
        return carry

    lax.fori_loop(0, xr, pointwise, 0)

    for half in range(nh):
        arrive(0, half)
    in_modes[...] = own_modes(0)

    def mix(j, carry):
        own = in_modes[j]
        m_ref[j] = jnp.sum(wd[j] * own[:, None, :], axis=0)
        return carry

    lax.fori_loop(0, jl, mix, 0)
    mt_send[0] = mixed()
    modes_copy(0).start()

    @pl.when(last)
    def _():
        send_rows(cuts[0], cuts[1])

    send_cells(mt_send[0], 0, 1)

    @pl.when(last)
    def _():
        for half in range(nh):
            arrive(1, half)
            blocks = []
            for q in range(hq):
                field = to_field(1, half, q)
                x0 = (half * hq + q) * xq
                block = []
                for k in range(xq):
                    signal = cot[:, x0 + k].astype(f32) * slope_of(row(field, k) + u[:, x0 + k])
                    sig[:, x0 + k] = signal
                    block.append(signal.astype(bf16).reshape(rows, zr))
                blocks.append(jnp.concatenate(block, axis=1))
            to_modes(blocks, 1, half, 0)
            send_modes(1, 2, half)

        modes_copy(0).wait_recv()
        table = [
            sp[i, nh - 1, :, hq - 1].reshape(nx * 16, cl * MODES) for i in range(2)
        ]
        p_ref[3, nh - 1, :, hq - 1] = cells_of(table, mt_recv[0]).reshape(nx, 16, lanes)
        send_quarter(lambda d, h: p_ref.at[3, nh - 1, d, hq - 1], 5, nh - 1, hq - 1)
        fetch_small()

        for half in range(nh):
            arrive(2, half)
        mix_back(2)
        mt_send[1] = mixed()
        modes_copy(1).start()
        send_rows(cuts[1], tail)
        send_cells(mt_send[1], 1, 3)

        blend_back(0, xr)
        arrive_quarter(5, nh - 1, hq - 1)
        for x in range(tail, xr):
            row_copy(x).wait_recv()
        field = to_field(5, nh - 1, hq - 1)
        for k in range(xq):
            values = [act1[i, tail + k].astype(f32) for i in range(channels)]
            here = row(field, k)
            for o in range(channels):
                slope[o, tail + k] = slope_of(here[o] + blend(mix1, values, o, False) + bias1[0, o])
        arrive(3, nh - 1)
        to_modes([packed(back_block(nh - 1, hq - 1, u))], 2, nh - 1, hq - 1)
        lax.fori_loop(0, n, send_tail, 0)
        send_rows(tail, xr)

    def ahead_quarter(half, q):
        field = to_field(2, half, q)
        x0 = (half * hq + q) * xq
        for k in range(xq):
            row_copy(x0 + k).wait_recv()
            values = [act1[i, x0 + k].astype(f32) for i in range(channels)]
            here = row(field, k)
            signals = []
            for o in range(channels):
                pre = here[o] + blend(mix1, values, o, False) + bias1[0, o]
                signals.append(cot[o, x0 + k].astype(f32) * slope_of(pre))
            for i in range(channels):
                v[i, x0 + k] = blend(mix1, signals, i, True)

    def kept(block):
        for x, signal in block:
            sig[:, x] = signal
        return block

    @pl.when(first)
    def _():
        modes_copy(0).wait_recv()
        send_cells(mt_recv[0], 1, 2)
        fetch_small()
        for half in range(nh):
            arrive(1, half)

            def step(q, carry):
                field = to_field(1, half, q)
                x0 = (half * hq + q) * xq
                for k in range(xq):
                    slope[:, x0 + k] = slope_of(row(field, k) + u[:, x0 + k])
                return carry

            lax.fori_loop(0, hq, step, 0)

        for half in range(nh):
            arrive(2, half)
        quarters = [(half, q) for half in range(nh) for q in range(hq)][:-1]
        early = cuts[1] // xq
        for half, q in quarters[:early]:
            ahead_quarter(half, q)
        modes_copy(1).wait_recv()
        send_cells(mt_recv[1], 2, 3)
        for half in range(nh):
            arrive(3, half)
        for half in range(nh - 1):
            to_modes([packed(kept(back_block(half, q, v))) for q in range(hq)], 1, half, 0)
            send_modes(1, 4, half)
        for half, q in quarters[early:]:
            ahead_quarter(half, q)
        for q in range(hq - 1):
            to_modes([packed(kept(back_block(nh - 1, q, v)))], 1, nh - 1, q)
            send_quarter(lambda d, h: s_ref.at[1, nh - 1, h * nx + d, q], 4, nh - 1, q)
        for half in range(nh - 1):
            arrive(4, half)
        for q in range(hq - 1):
            arrive_quarter(4, nh - 1, q)
        await_block(r_ref.at[4, nh - 1, :, hq - 1], tail_recv.at[0])
        mix_back(4)
        send_cells(mixed(), 3, 5)
        blend_back(0, tail)

    def weight_grad(j, carry):
        for c in range(cl):
            part = slice(c * MODES, (c + 1) * MODES)
            wgrad[j, c] = in_modes[j][:, None, part] * grad_modes[j][None, :, part]
        return carry

    lax.fori_loop(0, jl, weight_grad, 0)
    e = 3 + 2 * (1 - seg)

    @pl.when(last)
    def _():
        for half in range(nh - 1):
            arrive(3, half)

    @pl.when(first)
    def _():
        for half in range(nh - 1):
            arrive(5, half)

    for half in range(nh - 1):
        for q in range(hq):
            field = to_field(e, half, q)
            x0 = (half * hq + q) * xq
            for k in range(xq):
                out[:, x0 + k] = (row(field, k) + u[:, x0 + k]).astype(bf16)

    @pl.when(first)
    def _():
        ahead_quarter(nh - 1, hq - 1)
        kept(back_block(nh - 1, hq - 1, v))
        blend_back(tail, xr)
        arrive(5, nh - 1)

    rest_ref[...] = u[:, (nh - 1) * hq * xq :]
    cells_ref[...] = r_ref[e, nh - 1]
    for half in range(nh):
        for k in range(4):
            sent(k, half)
    for copy in small:
        copy.wait_send()
    modes_copy(0).wait_send()

    @pl.when(first)
    def _():
        for half in range(nh - 1):
            sent(4, half)
        for q in range(hq - 1):
            sent_quarter(4, nh - 1, q)
        for half in range(nh):
            sent(5, half)
        for x in range(tail, xr):
            row_copy(x).wait_send()

    @pl.when(last)
    def _():
        sent_quarter(5, nh - 1, hq - 1)
        modes_copy(1).wait_send()
        await_block(r_ref.at[4, nh - 1, :, hq - 1], tail_send.at[0])
        for x in range(xr):
            row_copy(x).wait_send()


def finish_kernel(
    nx, ny, xq, done_ref, rest_ref, cells_ref, wgrad, ky, bzi, grad_hbm, wgrad_hbm, out, sem
):
    channels, done, yr, zr = done_ref.shape
    hq = cells_ref.shape[1]
    stores = [
        pltpu.make_async_copy(wgrad, wgrad_hbm, sem.at[0]),
        pltpu.make_async_copy(done_ref, grad_hbm.at[:, pl.ds(0, done)], sem.at[1]),
    ]
    for store in stores:
        store.start()
    for q in range(hq):
        field = field_of(lambda h: cells_ref[h * nx : (h + 1) * nx, q], ny, ky, bzi)
        for k in range(xq):
            x = q * xq + k
            here = field[:, k * zr : (k + 1) * zr].reshape(channels, yr, zr)
            out[:, x] = (here + rest_ref[:, x]).astype(bf16)
        part = pl.ds(q * xq, xq)
        store = pltpu.make_async_copy(
            out.at[:, part], grad_hbm.at[:, pl.ds(done + q * xq, xq)], sem.at[2 + q]
        )
        store.start()
        stores.append(store)
    for store in stores:
        store.wait()


def two_section_body(activations, cotangent, spectral_weights, pointwise, channel_bias):
    inputs = activations[0]
    channels, xr, yr, zr = inputs.shape
    nx, ny = lax.axis_size("gx"), lax.axis_size("gy")
    n = nx * ny
    cl, jl = MODES // nx, MODES // ny
    xq = 16 // cl
    nh = 2
    hq = xr // (nh * xq)
    lanes, rows = jl * channels, channels * yr
    bz = trig_basis(zr).reshape(nx, cl, zr)
    eye_x, eye_c = np.eye(xq), np.eye(cl)
    bzf = np.einsum("dcz,xX->xzdXc", bz, eye_x).reshape(xq * zr, nx * 16)
    bzi = halves(bzf.reshape(xq, zr, nx * 16).transpose(2, 0, 1).reshape(nx * 16, xq * zr))
    by = trig_basis(yr * ny).reshape(MODES, ny, yr)
    ky = np.einsum("jgy,ik->giyjk", by, np.eye(channels)).reshape(ny, rows, ny * lanes)
    ky = halves(ky)
    bx = trig_basis(xr * nx).reshape(MODES, nx, nh, hq, xq)
    sp = np.einsum("adtqx,cC->tdqxCca", bx, eye_c).reshape(nh * nx * hq * 16, cl * MODES)
    bxf = np.broadcast_to(
        sp.reshape(nh, 1, nx * hq * 16, cl * MODES), (nh, ny, nx * hq * 16, cl * MODES)
    )
    bxf = bxf.reshape(nh * n * hq * 16, cl * MODES).T
    bzf = halves(bzf)
    tables = [
        np.ascontiguousarray(ky.transpose(1, 0, 3, 2)),
        np.ascontiguousarray(ky.transpose(1, 0, 2, 3)),
        np.concatenate([bzf[0], bzf[1]], axis=1),
        np.concatenate([bzi[0], bzi[0], bzi[1]], axis=0),
        halves(bxf),
        halves(sp).reshape(2, nh, nx, hq, 16, cl * MODES),
    ]
    weights, mixing = spectral_weights[0], pointwise[0]
    vmem = pl.BlockSpec(memory_space=pltpu.VMEM)
    smem = pl.BlockSpec(memory_space=pltpu.SMEM)
    hbm = pl.BlockSpec(memory_space=pl.ANY)
    dma = pltpu.SemaphoreType.DMA
    grid = inputs.shape
    done = grid[:1] + ((nh - 1) * hq * xq,) + grid[2:]
    left = grid[:1] + (hq * xq,) + grid[2:]
    scratch = [
        pltpu.VMEM(grid, bf16), pltpu.VMEM(grid, bf16), pltpu.VMEM(grid, bf16),
        pltpu.VMEM(weights.shape, f32),
        pltpu.VMEM((jl, channels, channels, cl * MODES), f32),
        pltpu.VMEM((2, ny * lanes, rows), bf16),
        pltpu.VMEM((xq * zr, 2 * nx * 16), bf16),
        pltpu.VMEM((2, cl * MODES, nh * n * hq * 16), bf16),
        pltpu.VMEM((2, nh, nx, hq, 16, cl * MODES), bf16),
        pltpu.VMEM(grid, f32), pltpu.VMEM(grid, f32), pltpu.VMEM(grid, f32), pltpu.VMEM(grid, f32),
        pltpu.VMEM((jl, channels, cl * MODES), f32),
        pltpu.VMEM((jl, channels, cl * MODES), f32),
        pltpu.VMEM((jl, channels, cl * MODES), f32),
        pltpu.VMEM((2, cl * MODES, lanes), f32),
        pltpu.VMEM((2, cl * MODES, lanes), f32),
        pltpu.VMEM(mixing.shape, f32), pltpu.VMEM(channel_bias.shape, f32),
        pltpu.SMEM(mixing.shape, f32), pltpu.SMEM(channel_bias.shape, f32),
        pltpu.VMEM((3, nh, n, hq, 16, lanes), bf16),
        pltpu.VMEM((4, nh, nx, hq, 16, lanes), bf16),
        pltpu.VMEM((6, nh, n, hq, 16, lanes), bf16),
        dma((9,)), dma((6, nh)), dma((6, nh)),
        dma((xr,)), dma((xr,)), dma((4,)), dma((4,)), dma((2,)), dma((1,)), dma((1,)),
    ]
    parts = pl.pallas_call(
        functools.partial(relay_kernel, nx, ny, xq, (3, 9)),
        out_shape=(
            jax.ShapeDtypeStruct(done, bf16),
            jax.ShapeDtypeStruct(left, f32),
            jax.ShapeDtypeStruct((n, hq, 16, lanes), bf16),
            pltpu.VMEM(weights.shape, f32),
            jax.ShapeDtypeStruct((2, rows, ny * lanes), bf16),
            jax.ShapeDtypeStruct((3 * nx * 16, xq * zr), bf16),
        ),
        in_specs=[hbm, hbm, hbm, smem, smem] + [hbm] * (2 + len(tables)),
        out_specs=[vmem] * 6,
        scratch_shapes=scratch,
        compiler_params=pltpu.CompilerParams(
            collective_id=0, has_side_effects=True, vmem_limit_bytes=46 * 2**20
        ),
        cost_estimate=pl.CostEstimate(
            flops=4 * 10**9, bytes_accessed=2 * 10**7, transcendentals=10**7
        ),
    )(
        inputs, cotangent, weights, mixing, channel_bias,
        *[
            pltpu.with_memory_space_constraint(jnp.asarray(table), pltpu.HBM)
            for table in [mixing, channel_bias] + tables
        ],
    )
    input_grad, weight_grad = pl.pallas_call(
        functools.partial(finish_kernel, nx, ny, xq),
        out_shape=(
            jax.ShapeDtypeStruct(grid, bf16),
            jax.ShapeDtypeStruct(weights.shape, f32),
        ),
        in_specs=[vmem] * 6,
        out_specs=(hbm, hbm),
        scratch_shapes=[pltpu.VMEM(left, bf16), dma((2 + hq,))],
        compiler_params=pltpu.CompilerParams(vmem_limit_bytes=24 * 2**20),
        cost_estimate=pl.CostEstimate(flops=10**9, bytes_accessed=10**7, transcendentals=0),
    )(*parts)
    return (input_grad[None], weight_grad[None])


def fits(mesh):
    nx = mesh.shape["gx"]
    return mesh.shape["segment"] == 2 and mesh.shape["gy"] == 2 and nx == 8


def solution(mesh):
    return jax.shard_map(
        two_section_body if fits(mesh) else body,
        mesh=mesh,
        in_specs=(
            P("segment", "groups", "gx", "gy", None),
            P("groups", "gx", "gy", None),
            P("segment", "gy", "gx", None, None, None),
            P("segment", None, None),
            P("segment", None),
        ),
        out_specs=(
            P("segment", "groups", "gx", "gy", None),
            P("segment", "gy", "gx", "groups", None, None),
        ),
        check_vma=False,
    )
```

```python
import functools
import math

import jax
import jax.numpy as jnp
import ml_dtypes
import numpy as np
from jax import lax
from jax.experimental import pallas as pl
from jax.experimental.pallas import tpu as pltpu
from jax.sharding import PartitionSpec as P

MODES = 32
f32, bf16 = jnp.float32, jnp.bfloat16


def from_behind(block, axis, distance):
    devices = range(lax.axis_size(axis))
    route = [(i - distance, i) for i in devices if i - distance in devices]
    return lax.ppermute(block, axis, route)


def trig_basis(length):
    half = MODES // 2
    freqs = np.arange(half)[:, None]
    points = np.arange(length)[None, :]
    step = 2.0 * math.pi / length
    rows = np.concatenate(
        [np.cos((freqs * points % length) * step), np.sin(((freqs + 1) * points % length) * step)]
    )
    scales = np.where(np.arange(MODES) == 0, 1.0 / math.sqrt(length), math.sqrt(2.0 / length))
    return rows * scales[:, None]


def halves(matrix):
    matrix = np.asarray(matrix, np.float32)
    top = matrix.astype(ml_dtypes.bfloat16)
    rest = (matrix - top.astype(np.float32)).astype(ml_dtypes.bfloat16)
    return np.stack([top, rest])


def split(value):
    top = value.astype(bf16)
    return top, (value - top.astype(f32)).astype(bf16)


def dot(a, b, ca=1, cb=0):
    return lax.dot_general(a, b, (((ca,), (cb,)), ((), ())), preferred_element_type=f32)


def kernel(
    back, nx, ny, xr, *refs
):
    if back:
        (inc_ref, slope_ref, w_hbm, mix_ref, bz_ref, bzs_ref, ky_ref, kyt_ref, bx_ref, bxr_ref,
         out_ref, modes_ref, got_ref, *scratch) = refs
    else:
        (inc_ref, w_hbm, mix_ref, bias_ref, bz_ref, bzs_ref, ky_ref, kyt_ref, bx_ref, bxr_ref,
         out_ref, modes_ref, got_ref, *scratch) = refs
    (w_ref, sig_ref, ghi_ref, glo_ref, s_ref, r_ref, m_ref, p_ref, q_ref, qs_ref,
     send1, recv1, send2, recv2, wsem) = scratch
    channels, _, yr, zr = inc_ref.shape
    cl, jl, xp = MODES // nx, MODES // ny, r_ref.shape[2]
    n = nx * ny
    lanes = jl * channels
    gx, gy = lax.axis_index("gx"), lax.axis_index("gy")
    me = gx * ny + gy

    wcopy = pltpu.make_async_copy(w_hbm, w_ref, wsem)
    wcopy.start()

    barrier = pltpu.get_barrier_semaphore()

    def greet(k, carry):
        peer = lax.rem(me + k, n)
        pl.semaphore_signal(
            barrier, inc=1,
            device_id={"gx": peer // ny, "gy": lax.rem(peer, ny)},
            device_id_type=pl.DeviceIdType.MESH,
        )
        return carry

    lax.fori_loop(1, n, greet, 0)

    def along_z(x, carry):
        if back:
            signal = inc_ref[:, x].astype(f32) * slope_ref[:, x]
            sig_ref[:, x] = signal
            block = signal.astype(bf16)
        else:
            block = inc_ref[:, x]
        block = block.reshape(channels * yr, zr)
        g = dot(bz_ref[0], block, 1, 1) + dot(bz_ref[1], block, 1, 1)
        ghi, glo = split(g)
        rows = pl.ds(pl.multiple_of(x * MODES, MODES), MODES)
        ghi_ref[rows, :] = ghi
        glo_ref[rows, :] = glo
        return carry

    lax.fori_loop(0, xr, along_z, 0)
    ghi = ghi_ref[...]
    t = dot(ghi, ky_ref[0]) + dot(ghi, ky_ref[1]) + dot(glo_ref[...], ky_ref[0])
    t = jnp.swapaxes(t.reshape(xr, MODES, ny * lanes), 0, 1)
    if xp > xr:
        t = jnp.concatenate([t, jnp.zeros((MODES, xp - xr, ny * lanes), f32)], axis=1)
    t = t.astype(bf16)
    for h in range(ny):
        s_ref[h] = t[:, :, h * lanes : (h + 1) * lanes].reshape(nx, cl, xp, lanes)

    pl.semaphore_wait(barrier, n - 1)

    def exchange(source, target, send, recv):
        def copy_to(peer, slot_of):
            return pltpu.make_async_remote_copy(
                src_ref=source(peer // ny, lax.rem(peer, ny)),
                dst_ref=target.at[lax.rem(slot_of, ny) * nx + slot_of // ny],
                send_sem=send.at[peer],
                recv_sem=recv.at[slot_of],
                device_id={"gx": peer // ny, "gy": lax.rem(peer, ny)},
                device_id_type=pl.DeviceIdType.MESH,
            )

        def begin(k, carry):
            copy_to(lax.rem(me + k, n), me).start()
            return carry

        def finish(k, carry):
            copy_to(lax.rem(me + k, n), me).wait_send()
            peer = lax.rem(me + n - k, n)
            copy_to(peer, peer).wait_recv()
            return carry

        lax.fori_loop(1, n, begin, 0)
        target[gy * nx + gx] = source(gx, gy)[...]
        lax.fori_loop(1, n, finish, 0)

    exchange(lambda d, h: s_ref.at[h, d], r_ref, send1, recv1)

    for c in range(cl):
        part = r_ref[:, c].reshape(n * xp, lanes)
        own = dot(bx_ref[0], part) + dot(bx_ref[1], part)
        modes_ref[c] = own.T.reshape(jl, channels, MODES)
    wcopy.wait()

    def mix(j, carry):
        for c in range(cl):
            own = modes_ref[c, j]
            weight = w_ref[j, c]
            if back:
                m_ref[c, j] = jnp.sum(weight * own[None], axis=1)
            else:
                m_ref[c, j] = jnp.sum(weight * own[:, None, :], axis=0)
        return carry

    lax.fori_loop(0, jl, mix, 0)
    for c in range(cl):
        top, rest = split(m_ref[c].reshape(lanes, MODES))
        spread = (
            dot(bxr_ref[0], top, 1, 1) + dot(bxr_ref[1], top, 1, 1) + dot(bxr_ref[0], rest, 1, 1)
        )
        p_ref[:, c] = spread.astype(bf16).reshape(nx, xp, lanes)

    exchange(lambda d, h: p_ref.at[d], q_ref, send2, recv2)

    got = [q_ref[h * nx : (h + 1) * nx].reshape(MODES, xp, lanes) for h in range(ny)]
    got = jnp.concatenate(got, axis=2).astype(f32)
    got = jnp.swapaxes(got, 0, 1)[:xr].reshape(xr * MODES, ny * lanes).astype(bf16)
    got_ref[...] = got
    qs_ref[...] = dot(got, kyt_ref[0]) + dot(got, kyt_ref[1])

    def finish_field(x, carry):
        rows = pl.ds(pl.multiple_of(x * MODES, MODES), MODES)
        top, rest = split(qs_ref[rows, :])
        stack = jnp.concatenate([top, rest, top], axis=0)
        field = dot(stack, bzs_ref[...], 0, 0).reshape(channels, yr, zr)
        if back:
            values = [sig_ref[i, x] for i in range(channels)]
        else:
            values = [inc_ref[i, x].astype(f32) for i in range(channels)]
        for o in range(channels):
            total = field[o]
            for i in range(channels):
                total = total + (mix_ref[i, o] if back else mix_ref[o, i]) * values[i]
            if back:
                out_ref[o, x] = total.astype(bf16)
            else:
                total = total + bias_ref[0, o]
                cdf = 0.5 * (1.0 + lax.erf(total * 0.7071067811865476))
                out_ref[o, x] = cdf + total * jnp.exp(-0.5 * total * total) * 0.3989422804014327
        return carry

    lax.fori_loop(0, xr, finish_field, 0)


def ahead_kernel(
    act_ref, cot_ref, got_ref, got_back_ref, mix_ref, bias_ref, bzs_ref, kyt_ref, out_ref,
    pre_ref, back_ref,
):
    channels, xr, yr, zr = act_ref.shape
    pre_ref[...] = dot(got_ref[...], kyt_ref[0]) + dot(got_ref[...], kyt_ref[1])
    back_ref[...] = dot(got_back_ref[...], kyt_ref[0]) + dot(got_back_ref[...], kyt_ref[1])

    def field_of(ref, x):
        rows = pl.ds(pl.multiple_of(x * MODES, MODES), MODES)
        top, rest = split(ref[rows, :])
        stack = jnp.concatenate([top, rest, top], axis=0)
        return dot(stack, bzs_ref[...], 0, 0).reshape(channels, yr, zr)

    def step(x, carry):
        field = field_of(pre_ref, x)
        values = [act_ref[i, x].astype(f32) for i in range(channels)]
        signals = []
        for o in range(channels):
            total = field[o]
            for i in range(channels):
                total = total + mix_ref[o, i] * values[i]
            total = total + bias_ref[0, o]
            cdf = 0.5 * (1.0 + lax.erf(total * 0.7071067811865476))
            slope = cdf + total * jnp.exp(-0.5 * total * total) * 0.3989422804014327
            signals.append(cot_ref[o, x].astype(f32) * slope)
        field = field_of(back_ref, x)
        for o in range(channels):
            total = field[o]
            for i in range(channels):
                total = total + mix_ref[i, o] * signals[i]
            out_ref[o, x] = total.astype(bf16)
        return carry

    lax.fori_loop(0, xr, step, 0)


def ahead(activations, cotangent, got, got_back, mixing, bias, bzs, kyt):
    channels, xr, yr, zr = activations.shape
    vmem = pl.BlockSpec(memory_space=pltpu.VMEM)
    smem = pl.BlockSpec(memory_space=pltpu.SMEM)
    return pl.pallas_call(
        ahead_kernel,
        out_shape=jax.ShapeDtypeStruct(activations.shape, bf16),
        in_specs=[vmem] * 4 + [smem] * 2 + [vmem] * 2,
        out_specs=vmem,
        scratch_shapes=[pltpu.VMEM((xr * MODES, channels * yr), f32)] * 2,
        compiler_params=pltpu.CompilerParams(vmem_limit_bytes=50 * 2**20),
        cost_estimate=pl.CostEstimate(flops=10**9, bytes_accessed=10**7, transcendentals=10**6),
    )(activations, cotangent, got, got_back, mixing, bias, bzs, kyt)


def block_turn(back, nx, ny, collective, field, slope, weights, mixing, bias, tables):
    channels, xr, yr, zr = field.shape
    xp = -(-xr // 16) * 16
    cl, jl, n = MODES // nx, MODES // ny, nx * ny
    lanes = jl * channels
    vmem = pl.BlockSpec(memory_space=pltpu.VMEM)
    smem = pl.BlockSpec(memory_space=pltpu.SMEM)
    hbm = pl.BlockSpec(memory_space=pl.ANY)
    if back:
        args = (field, slope, weights, mixing, *tables)
        specs = [vmem, vmem, hbm, smem] + [vmem] * len(tables)
    else:
        args = (field, weights, mixing, bias, *tables)
        specs = [vmem, hbm, smem, smem] + [vmem] * len(tables)
    dma = pltpu.SemaphoreType.DMA
    return pl.pallas_call(
        functools.partial(kernel, back, nx, ny, xr),
        out_shape=(
            jax.ShapeDtypeStruct(field.shape, bf16 if back else f32),
            jax.ShapeDtypeStruct((cl, jl, channels, MODES), f32),
            jax.ShapeDtypeStruct((xr * MODES, ny * lanes), bf16),
        ),
        in_specs=specs,
        out_specs=(vmem, vmem, vmem),
        scratch_shapes=[
            pltpu.VMEM(weights.shape, f32),
            pltpu.VMEM(field.shape if back else (8, 128), f32),
            pltpu.VMEM((xr * MODES, channels * yr), bf16),
            pltpu.VMEM((xr * MODES, channels * yr), bf16),
            pltpu.VMEM((ny, nx, cl, xp, lanes), bf16),
            pltpu.VMEM((n, cl, xp, lanes), bf16),
            pltpu.VMEM((cl, jl, channels, MODES), f32),
            pltpu.VMEM((nx, cl, xp, lanes), bf16),
            pltpu.VMEM((n, cl, xp, lanes), bf16),
            pltpu.VMEM((xr * MODES, channels * yr), f32),
            dma((n,)), dma((n,)), dma((n,)), dma((n,)), dma,
        ],
        compiler_params=pltpu.CompilerParams(
            collective_id=collective, has_side_effects=True, vmem_limit_bytes=50 * 2**20
        ),
        cost_estimate=pl.CostEstimate(flops=10**9, bytes_accessed=2 * 10**7, transcendentals=10**6),
    )(*args)


def body(activations, cotangent, spectral_weights, pointwise, channel_bias):
    inputs = activations[0]
    channels, xr, yr, zr = inputs.shape
    nx, ny = lax.axis_size("gx"), lax.axis_size("gy")
    xp = -(-xr // 16) * 16
    bz = trig_basis(zr)
    bx = trig_basis(xr * nx).reshape(MODES, nx, xr)
    bx = np.concatenate([bx, np.zeros((MODES, nx, xp - xr))], axis=2).reshape(MODES, nx * xp)
    by = trig_basis(yr * ny).reshape(MODES, ny, yr)
    kron = np.einsum("jgy,ik->giyjk", by, np.eye(channels)).reshape(
        ny, channels * yr, MODES * channels
    )
    bzh = halves(bz)
    kh = halves(kron)
    gy = lax.axis_index("gy")
    ky = lax.dynamic_index_in_dim(jnp.asarray(np.swapaxes(kh, 0, 1)), gy, 0, False)
    kyt = lax.dynamic_index_in_dim(
        jnp.asarray(np.ascontiguousarray(np.transpose(kh, (1, 0, 3, 2)))), gy, 0, False
    )
    tables = (
        jnp.asarray(bzh),
        jnp.asarray(np.concatenate([bzh[0], bzh[0], bzh[1]], axis=0)),
        ky,
        kyt,
        jnp.asarray(halves(np.concatenate([bx] * ny, axis=1))),
        jnp.asarray(halves(bx.T)),
    )
    weights = spectral_weights[0]
    mixing = pointwise[0]
    following = [from_behind(v, "segment", -1) for v in (inputs, mixing, channel_bias)]
    slope, input_modes, got = block_turn(
        False, nx, ny, 0, inputs, None, weights, mixing, channel_bias, tables
    )
    next_got = from_behind(got, "segment", -1)
    segment_index = lax.axis_index("segment")
    segment_count = lax.axis_size("segment")
    incoming = cotangent
    kept_grad = jnp.zeros(cotangent.shape, bf16)
    kept_modes = jnp.zeros(input_modes.shape, f32)
    for turn_index in range(segment_count):
        active = segment_index == segment_count - 1 - turn_index
        input_grad, grad_modes, got_back = block_turn(
            True, nx, ny, 1 + turn_index, incoming, slope, weights, mixing, None, tables
        )
        kept_grad = jnp.where(active, input_grad, kept_grad)
        kept_modes = jnp.where(active, grad_modes, kept_modes)
        if turn_index == 0 and segment_count > 1:
            next_back = from_behind(got_back, "segment", -1)
            incoming = ahead(
                following[0], cotangent, next_got, next_back, following[1], following[2],
                tables[1], tables[3],
            )
        elif turn_index + 1 < segment_count:
            incoming = from_behind(input_grad, "segment", -1)
    input_modes = jnp.swapaxes(input_modes, 0, 1)
    kept_modes = jnp.swapaxes(kept_modes, 0, 1)
    weight_grad = input_modes[:, :, :, None, :] * kept_modes[:, :, None, :, :]
    return (kept_grad[None], weight_grad[None])


def slope_of(value):
    cdf = 0.5 * (1.0 + lax.erf(value * 0.7071067811865476))
    return cdf + value * jnp.exp(-0.5 * value * value) * 0.3989422804014327


def field_of(cells, ny, ky, bzi):
    blocks = []
    for h in range(ny):
        block = cells(h)
        blocks.append(block.reshape(block.shape[0] * block.shape[1], block.shape[2]))
    block = jnp.concatenate(blocks, axis=1)
    top, rest = split(dot(ky[0], block, 1, 1) + dot(ky[1], block, 1, 1))
    return dot(jnp.concatenate([top, rest, top], axis=1), bzi[...])


def relay_kernel(
    nx, ny, xq, cuts,
    act_hbm, cot_hbm, w_hbm, mix_ref, bias_ref, mix_hbm, bias_hbm,
    kyt_hbm, ky_hbm, bzf_hbm, bzi_hbm, bx_hbm, sp_hbm,
    out, rest_ref, cells_ref, wgrad, ky, bzi,
    act, act1, cot, w, wd, kyt, bzf, bx, sp,
    u, v, slope, sig, in_modes, grad_modes, m_ref, mt_send, mt_recv,
    mixv1, biasv1, mix1, bias1, s_ref, p_ref, r_ref,
    load_sem, send_sem, recv_sem, row_send, row_recv, small_send, small_recv, store_sem,
    tail_send, tail_recv,
):
    channels, xr, yr, zr = act.shape
    n = nx * ny
    cl, jl = MODES // nx, MODES // ny
    nh, hq = r_ref.shape[1], r_ref.shape[3]
    lanes = jl * channels
    rows = channels * yr
    tail = xr - hq * xq
    gx, gy, seg = lax.axis_index("gx"), lax.axis_index("gy"), lax.axis_index("segment")
    me = gx * ny + gy
    mine = gy * nx + gx
    first, last = seg == 0, seg == 1
    mesh_ids = pl.DeviceIdType.MESH

    loads = [
        pltpu.make_async_copy(source, target, load_sem.at[k])
        for k, (source, target) in enumerate(
            [
                (act_hbm, act), (bzf_hbm, bzf), (kyt_hbm.at[gy], kyt), (w_hbm, w), (bx_hbm, bx),
                (sp_hbm, sp), (ky_hbm.at[gy], ky), (bzi_hbm, bzi), (cot_hbm, cot),
            ]
        )
    ]
    for load in loads:
        load.start()

    barrier = pltpu.get_barrier_semaphore()

    def greet(k, carry):
        other = lax.rem(seg * n + me + k, 2 * n)
        peer = lax.rem(other, n)
        pl.semaphore_signal(
            barrier, inc=1,
            device_id={"segment": other // n, "gx": peer // ny, "gy": lax.rem(peer, ny)},
            device_id_type=mesh_ids,
        )
        return carry

    lax.fori_loop(1, 2 * n, greet, 0)

    def ahead(source, target, send, recv):
        return pltpu.make_async_remote_copy(
            src_ref=source, dst_ref=target, send_sem=send, recv_sem=recv,
            device_id={"segment": 1 - seg}, device_id_type=mesh_ids,
        )

    def row_copy(x):
        return ahead(act_hbm.at[:, x], act1.at[:, x], row_send.at[x], row_recv.at[x])

    def send_rows(start, stop):
        for x in range(start, stop):
            row_copy(x).start()

    def modes_copy(k):
        return ahead(mt_send.at[k], mt_recv.at[k], small_send.at[k], small_recv.at[k])

    small = [
        ahead(mix_hbm, mixv1, small_send.at[2], small_recv.at[2]),
        ahead(bias_hbm, biasv1, small_send.at[3], small_recv.at[3]),
    ]

    def send(source, target, sends, receives):
        def begin(k, carry):
            peer = lax.rem(me + k, n)
            d, h = peer // ny, lax.rem(peer, ny)
            pltpu.make_async_remote_copy(
                src_ref=source(d, h), dst_ref=target, send_sem=sends, recv_sem=receives,
                device_id={"gx": d, "gy": h}, device_id_type=mesh_ids,
            ).start()
            return carry

        lax.fori_loop(1, n, begin, 0)
        target[...] = source(gx, gy)[...]

    def send_half(source, e, half):
        send(source, r_ref.at[e, half, mine], send_sem.at[e, half], recv_sem.at[e, half])

    def send_tail(k, carry):
        peer = lax.rem(me + k, n)
        d, h = peer // ny, lax.rem(peer, ny)
        pltpu.make_async_remote_copy(
            src_ref=s_ref.at[2, nh - 1, h * nx + d], dst_ref=r_ref.at[4, nh - 1, mine],
            send_sem=tail_send.at[0], recv_sem=tail_recv.at[0],
            device_id={"segment": 0, "gx": d, "gy": h}, device_id_type=mesh_ids,
        ).start()
        return carry

    def await_block(block, sem):
        pltpu.make_async_copy(block, block, sem).wait()

    def arrive(e, half):
        await_block(r_ref.at[e, half, pl.ds(0, n - 1)], recv_sem.at[e, half])

    def sent(e, half):
        await_block(r_ref.at[e, half, pl.ds(0, n - 1)], send_sem.at[e, half])

    def to_modes(blocks, k, half):
        parts = []
        for block in blocks:
            g = dot(block, bzf[...])
            parts.append(g[:, : nx * 16] + g[:, nx * 16 :])
        top, rest = split(jnp.concatenate(parts, axis=1))
        t = dot(kyt[0], top) + dot(kyt[1], top) + dot(kyt[0], rest)
        t = t.T.astype(bf16)
        for q in range(len(blocks)):
            for h in range(ny):
                part = t[q * nx * 16 : (q + 1) * nx * 16, h * lanes : (h + 1) * lanes]
                s_ref[k, half, h * nx : (h + 1) * nx, q] = part.reshape(nx, 16, lanes)

    def to_field(e, half, q):
        return field_of(lambda h: r_ref[e, half, h * nx : (h + 1) * nx, q], ny, ky, bzi)

    def row(field, x):
        return field[:, x * zr : (x + 1) * zr].reshape(channels, yr, zr)

    def send_modes(k, e, half):
        send_half(lambda d, h: s_ref.at[k, half, h * nx + d], e, half)

    def own_modes(e, await_half):
        own = None
        for half in range(nh):
            await_half(half)
            block = r_ref[e, half].reshape(n * hq * 16, lanes)
            part = slice(half * n * hq * 16, (half + 1) * n * hq * 16)
            term = dot(bx[0, :, part], block) + dot(bx[1, :, part], block)
            own = term if own is None else own + term
        return own.T.reshape(jl, channels, cl * MODES)

    def send_cells(mt, k, e, halves):
        top, rest = split(mt)
        for half in halves:
            table = [sp[i, half].reshape(nx * hq * 16, cl * MODES) for i in range(2)]
            cells = dot(table[0], top) + dot(table[1], top) + dot(table[0], rest)
            p_ref[k, half] = cells.astype(bf16).reshape(nx, hq, 16, lanes)
            send_half(lambda d, h: p_ref.at[k, half, d], e, half)

    def mixed():
        return m_ref[...].reshape(lanes, cl * MODES).T

    def mix_back(e, await_half):
        grad_modes[...] = own_modes(e, await_half)

        def step(j, carry):
            m_ref[j] = jnp.sum(wd[j] * grad_modes[j][None], axis=1)
            return carry

        lax.fori_loop(0, jl, step, 0)

    def blend(mixing, values, o, back):
        total = (mixing[0, o] if back else mixing[o, 0]) * values[0]
        for i in range(1, channels):
            total = total + (mixing[i, o] if back else mixing[o, i]) * values[i]
        return total

    def fetch_small():
        for copy in small:
            copy.wait_recv()
        for k, (source, target) in enumerate([(mixv1, mix1), (biasv1, bias1)]):
            copy = pltpu.make_async_copy(source, target, store_sem.at[k])
            copy.start()
            copy.wait()

    def back_block(half, q, offset):
        field = to_field(3, half, q)
        x0 = (half * hq + q) * xq
        block = []
        for k in range(xq):
            incoming = (row(field, k) + offset[:, x0 + k]).astype(bf16).astype(f32)
            signal = incoming * slope[:, x0 + k]
            block.append((x0 + k, signal))
        return block

    def packed(block):
        return jnp.concatenate([s.astype(bf16).reshape(rows, zr) for _, s in block], axis=1)

    def blend_back(start, stop):
        def step(x, carry):
            values = [sig[i, x] for i in range(channels)]
            for o in range(channels):
                u[o, x] = blend(mix_ref, values, o, True)
            return carry

        lax.fori_loop(start, stop, step, 0)

    for load in loads[:3]:
        load.wait()
    for half in range(nh):
        blocks = []
        for q in range(hq):
            x = (half * hq + q) * xq
            block = [act[:, x + k].reshape(rows, zr) for k in range(xq)]
            blocks.append(jnp.concatenate(block, axis=1))
        to_modes(blocks, 0, half)
        if half == 0:
            pl.semaphore_wait(barrier, 2 * n - 1)
            for copy in small:
                copy.start()

            @pl.when(last)
            def _():
                send_rows(0, cuts[0])

            @pl.when(first)
            def _():
                send_rows(tail, xr)

        send_modes(0, 0, half)

    for load in loads[3:]:
        load.wait()

    def dense(j, carry):
        for i in range(channels):
            wd[j, i] = jnp.concatenate([w[j, c, i] for c in range(cl)], axis=1)
        return carry

    lax.fori_loop(0, jl, dense, 0)

    def pointwise(x, carry):
        values = [act[i, x].astype(f32) for i in range(channels)]
        for o in range(channels):
            u[o, x] = blend(mix_ref, values, o, False) + bias_ref[0, o]
        return carry

    lax.fori_loop(0, xr, pointwise, 0)

    in_modes[...] = own_modes(0, lambda half: arrive(0, half))

    def mix(j, carry):
        own = in_modes[j]
        m_ref[j] = jnp.sum(wd[j] * own[:, None, :], axis=0)
        return carry

    lax.fori_loop(0, jl, mix, 0)
    mt_send[0] = mixed()
    modes_copy(0).start()

    @pl.when(last)
    def _():
        send_rows(cuts[0], cuts[1])

    send_cells(mt_send[0], 0, 1, range(nh))

    @pl.when(last)
    def _():
        for half in range(nh):
            arrive(1, half)
            blocks = []
            for q in range(hq):
                field = to_field(1, half, q)
                x0 = (half * hq + q) * xq
                block = []
                for k in range(xq):
                    signal = cot[:, x0 + k].astype(f32) * slope_of(row(field, k) + u[:, x0 + k])
                    sig[:, x0 + k] = signal
                    block.append(signal.astype(bf16).reshape(rows, zr))
                blocks.append(jnp.concatenate(block, axis=1))
            to_modes(blocks, 1, half)
            send_modes(1, 2, half)

        modes_copy(0).wait_recv()
        send_cells(mt_recv[0], 3, 5, [nh - 1])
        fetch_small()

        mix_back(2, lambda half: arrive(2, half))
        mt_send[1] = mixed()
        modes_copy(1).start()
        send_rows(cuts[1], cuts[2])
        send_cells(mt_send[1], 1, 3, reversed(range(nh)))

        blend_back(0, xr)
        for x in range(tail, xr):
            row_copy(x).wait_recv()
        arrive(5, nh - 1)
        for q in range(hq):
            field = to_field(5, nh - 1, q)
            x0 = tail + q * xq
            for k in range(xq):
                values = [act1[i, x0 + k].astype(f32) for i in range(channels)]
                here = row(field, k)
                for o in range(channels):
                    pre = here[o] + blend(mix1, values, o, False) + bias1[0, o]
                    slope[o, x0 + k] = slope_of(pre)
        arrive(3, nh - 1)
        to_modes([packed(back_block(nh - 1, q, u)) for q in range(hq)], 2, nh - 1)
        lax.fori_loop(0, n, send_tail, 0)
        send_rows(cuts[2], xr)

    def ahead_quarter(half, q):
        field = to_field(2, half, q)
        x0 = (half * hq + q) * xq
        for k in range(xq):
            row_copy(x0 + k).wait_recv()
            values = [act1[i, x0 + k].astype(f32) for i in range(channels)]
            here = row(field, k)
            signals = []
            for o in range(channels):
                pre = here[o] + blend(mix1, values, o, False) + bias1[0, o]
                signals.append(cot[o, x0 + k].astype(f32) * slope_of(pre))
            for i in range(channels):
                v[i, x0 + k] = blend(mix1, signals, i, True)

    def kept(block):
        for x, signal in block:
            sig[:, x] = signal
        return block

    @pl.when(first)
    def _():
        modes_copy(0).wait_recv()
        send_cells(mt_recv[0], 1, 2, range(nh))
        fetch_small()
        for half in range(nh):
            arrive(1, half)

            def step(q, carry):
                field = to_field(1, half, q)
                x0 = (half * hq + q) * xq
                for k in range(xq):
                    slope[:, x0 + k] = slope_of(row(field, k) + u[:, x0 + k])
                return carry

            lax.fori_loop(0, hq, step, 0)

        for half in range(nh):
            arrive(2, half)
        for half in range(nh - 1):
            for q in range(hq):
                ahead_quarter(half, q)
        modes_copy(1).wait_recv()
        send_cells(mt_recv[1], 2, 3, range(nh))
        for half in range(nh - 1):
            arrive(3, half)
            to_modes([packed(kept(back_block(half, q, v))) for q in range(hq)], 1, half)
            send_modes(1, 4, half)
        blend_back(0, tail)
        arrive(3, nh - 1)
        for q in range(hq - 1):
            ahead_quarter(nh - 1, q)
            kept(back_block(nh - 1, q, v))

        def await_half(half):
            if half < nh - 1:
                arrive(4, half)
            else:
                await_block(r_ref.at[4, half], tail_recv.at[0])

        mix_back(4, await_half)
        send_cells(mixed(), 3, 5, range(nh))

    def weight_grad(j, carry):
        for c in range(cl):
            part = slice(c * MODES, (c + 1) * MODES)
            wgrad[j, c] = in_modes[j][:, None, part] * grad_modes[j][None, :, part]
        return carry

    lax.fori_loop(0, jl, weight_grad, 0)
    e = 3 + 2 * (1 - seg)

    @pl.when(last)
    def _():
        for half in range(nh - 1):
            arrive(3, half)

    @pl.when(first)
    def _():
        for half in range(nh - 1):
            arrive(5, half)

    for half in range(nh - 1):
        for q in range(hq):
            field = to_field(e, half, q)
            x0 = (half * hq + q) * xq
            for k in range(xq):
                out[:, x0 + k] = (row(field, k) + u[:, x0 + k]).astype(bf16)

    @pl.when(first)
    def _():
        ahead_quarter(nh - 1, hq - 1)
        kept(back_block(nh - 1, hq - 1, v))
        blend_back(tail, xr)
        arrive(5, nh - 1)

    rest_ref[...] = u[:, (nh - 1) * hq * xq :]
    cells_ref[...] = r_ref[e, nh - 1]
    for half in range(nh):
        for k in range(4):
            sent(k, half)
    for copy in small:
        copy.wait_send()
    modes_copy(0).wait_send()

    @pl.when(first)
    def _():
        for half in range(nh - 1):
            sent(4, half)
        for half in range(nh):
            sent(5, half)
        for x in range(tail, xr):
            row_copy(x).wait_send()

    @pl.when(last)
    def _():
        sent(5, nh - 1)
        modes_copy(1).wait_send()
        await_block(r_ref.at[4, nh - 1], tail_send.at[0])
        for x in range(xr):
            row_copy(x).wait_send()


def finish_kernel(
    nx, ny, xq, done_ref, rest_ref, cells_ref, wgrad, ky, bzi, grad_hbm, wgrad_hbm, out, sem
):
    channels, done, yr, zr = done_ref.shape
    hq = cells_ref.shape[1]
    stores = [
        pltpu.make_async_copy(wgrad, wgrad_hbm, sem.at[0]),
        pltpu.make_async_copy(done_ref, grad_hbm.at[:, pl.ds(0, done)], sem.at[1]),
    ]
    for store in stores:
        store.start()
    for q in range(hq):
        field = field_of(lambda h: cells_ref[h * nx : (h + 1) * nx, q], ny, ky, bzi)
        for k in range(xq):
            x = q * xq + k
            here = field[:, k * zr : (k + 1) * zr].reshape(channels, yr, zr)
            out[:, x] = (here + rest_ref[:, x]).astype(bf16)
        part = pl.ds(q * xq, xq)
        store = pltpu.make_async_copy(
            out.at[:, part], grad_hbm.at[:, pl.ds(done + q * xq, xq)], sem.at[2 + q]
        )
        store.start()
        stores.append(store)
    for store in stores:
        store.wait()


def two_section_body(activations, cotangent, spectral_weights, pointwise, channel_bias):
    inputs = activations[0]
    channels, xr, yr, zr = inputs.shape
    nx, ny = lax.axis_size("gx"), lax.axis_size("gy")
    n = nx * ny
    cl, jl = MODES // nx, MODES // ny
    xq = 16 // cl
    nh = 2
    hq = xr // (nh * xq)
    lanes, rows = jl * channels, channels * yr
    bz = trig_basis(zr).reshape(nx, cl, zr)
    eye_x, eye_c = np.eye(xq), np.eye(cl)
    bzf = np.einsum("dcz,xX->xzdXc", bz, eye_x).reshape(xq * zr, nx * 16)
    bzi = halves(bzf.reshape(xq, zr, nx * 16).transpose(2, 0, 1).reshape(nx * 16, xq * zr))
    by = trig_basis(yr * ny).reshape(MODES, ny, yr)
    ky = np.einsum("jgy,ik->giyjk", by, np.eye(channels)).reshape(ny, rows, ny * lanes)
    ky = halves(ky)
    bx = trig_basis(xr * nx).reshape(MODES, nx, nh, hq, xq)
    sp = np.einsum("adtqx,cC->tdqxCca", bx, eye_c).reshape(nh * nx * hq * 16, cl * MODES)
    bxf = np.broadcast_to(
        sp.reshape(nh, 1, nx * hq * 16, cl * MODES), (nh, ny, nx * hq * 16, cl * MODES)
    )
    bxf = bxf.reshape(nh * n * hq * 16, cl * MODES).T
    bzf = halves(bzf)
    tables = [
        np.ascontiguousarray(ky.transpose(1, 0, 3, 2)),
        np.ascontiguousarray(ky.transpose(1, 0, 2, 3)),
        np.concatenate([bzf[0], bzf[1]], axis=1),
        np.concatenate([bzi[0], bzi[0], bzi[1]], axis=0),
        halves(bxf),
        halves(sp).reshape(2, nh, nx, hq, 16, cl * MODES),
    ]
    weights, mixing = spectral_weights[0], pointwise[0]
    vmem = pl.BlockSpec(memory_space=pltpu.VMEM)
    smem = pl.BlockSpec(memory_space=pltpu.SMEM)
    hbm = pl.BlockSpec(memory_space=pl.ANY)
    dma = pltpu.SemaphoreType.DMA
    grid = inputs.shape
    done = grid[:1] + ((nh - 1) * hq * xq,) + grid[2:]
    left = grid[:1] + (hq * xq,) + grid[2:]
    scratch = [
        pltpu.VMEM(grid, bf16), pltpu.VMEM(grid, bf16), pltpu.VMEM(grid, bf16),
        pltpu.VMEM(weights.shape, f32),
        pltpu.VMEM((jl, channels, channels, cl * MODES), f32),
        pltpu.VMEM((2, ny * lanes, rows), bf16),
        pltpu.VMEM((xq * zr, 2 * nx * 16), bf16),
        pltpu.VMEM((2, cl * MODES, nh * n * hq * 16), bf16),
        pltpu.VMEM((2, nh, nx, hq, 16, cl * MODES), bf16),
        pltpu.VMEM(grid, f32), pltpu.VMEM(grid, f32), pltpu.VMEM(grid, f32), pltpu.VMEM(grid, f32),
        pltpu.VMEM((jl, channels, cl * MODES), f32),
        pltpu.VMEM((jl, channels, cl * MODES), f32),
        pltpu.VMEM((jl, channels, cl * MODES), f32),
        pltpu.VMEM((2, cl * MODES, lanes), f32),
        pltpu.VMEM((2, cl * MODES, lanes), f32),
        pltpu.VMEM(mixing.shape, f32), pltpu.VMEM(channel_bias.shape, f32),
        pltpu.SMEM(mixing.shape, f32), pltpu.SMEM(channel_bias.shape, f32),
        pltpu.VMEM((3, nh, n, hq, 16, lanes), bf16),
        pltpu.VMEM((4, nh, nx, hq, 16, lanes), bf16),
        pltpu.VMEM((6, nh, n, hq, 16, lanes), bf16),
        dma((9,)), dma((6, nh)), dma((6, nh)),
        dma((xr,)), dma((xr,)), dma((4,)), dma((4,)), dma((2,)), dma((1,)), dma((1,)),
    ]
    parts = pl.pallas_call(
        functools.partial(relay_kernel, nx, ny, xq, (3, 9, 12)),
        out_shape=(
            jax.ShapeDtypeStruct(done, bf16),
            jax.ShapeDtypeStruct(left, f32),
            jax.ShapeDtypeStruct((n, hq, 16, lanes), bf16),
            pltpu.VMEM(weights.shape, f32),
            jax.ShapeDtypeStruct((2, rows, ny * lanes), bf16),
            jax.ShapeDtypeStruct((3 * nx * 16, xq * zr), bf16),
        ),
        in_specs=[hbm, hbm, hbm, smem, smem] + [hbm] * (2 + len(tables)),
        out_specs=[vmem] * 6,
        scratch_shapes=scratch,
        compiler_params=pltpu.CompilerParams(
            collective_id=0, has_side_effects=True, vmem_limit_bytes=46 * 2**20
        ),
        cost_estimate=pl.CostEstimate(
            flops=4 * 10**9, bytes_accessed=2 * 10**7, transcendentals=10**7
        ),
    )(
        inputs, cotangent, weights, mixing, channel_bias,
        *[
            pltpu.with_memory_space_constraint(jnp.asarray(table), pltpu.HBM)
            for table in [mixing, channel_bias] + tables
        ],
    )
    input_grad, weight_grad = pl.pallas_call(
        functools.partial(finish_kernel, nx, ny, xq),
        out_shape=(
            jax.ShapeDtypeStruct(grid, bf16),
            jax.ShapeDtypeStruct(weights.shape, f32),
        ),
        in_specs=[vmem] * 6,
        out_specs=(hbm, hbm),
        scratch_shapes=[pltpu.VMEM(left, bf16), dma((2 + hq,))],
        compiler_params=pltpu.CompilerParams(vmem_limit_bytes=24 * 2**20),
        cost_estimate=pl.CostEstimate(flops=10**9, bytes_accessed=10**7, transcendentals=0),
    )(*parts)
    return (input_grad[None], weight_grad[None])


def fits(mesh):
    nx = mesh.shape["gx"]
    return mesh.shape["segment"] == 2 and mesh.shape["gy"] == 2 and nx == 8


def solution(mesh):
    return jax.shard_map(
        two_section_body if fits(mesh) else body,
        mesh=mesh,
        in_specs=(
            P("segment", "groups", "gx", "gy", None),
            P("groups", "gx", "gy", None),
            P("segment", "gy", "gx", None, None, None),
            P("segment", None, None),
            P("segment", None),
        ),
        out_specs=(
            P("segment", "groups", "gx", "gy", None),
            P("segment", "gy", "gx", "groups", None, None),
        ),
        check_vma=False,
    )
```

```python
import functools
import math

import jax
import jax.numpy as jnp
import ml_dtypes
import numpy as np
from jax import lax
from jax.experimental import pallas as pl
from jax.experimental.pallas import tpu as pltpu
from jax.sharding import PartitionSpec as P

MODES = 32
f32, bf16 = jnp.float32, jnp.bfloat16


def from_behind(block, axis, distance):
    devices = range(lax.axis_size(axis))
    route = [(i - distance, i) for i in devices if i - distance in devices]
    return lax.ppermute(block, axis, route)


def trig_basis(length):
    half = MODES // 2
    freqs = np.arange(half)[:, None]
    points = np.arange(length)[None, :]
    step = 2.0 * math.pi / length
    rows = np.concatenate(
        [np.cos((freqs * points % length) * step), np.sin(((freqs + 1) * points % length) * step)]
    )
    scales = np.where(np.arange(MODES) == 0, 1.0 / math.sqrt(length), math.sqrt(2.0 / length))
    return rows * scales[:, None]


def halves(matrix):
    matrix = np.asarray(matrix, np.float32)
    top = matrix.astype(ml_dtypes.bfloat16)
    rest = (matrix - top.astype(np.float32)).astype(ml_dtypes.bfloat16)
    return np.stack([top, rest])


def split(value):
    top = value.astype(bf16)
    return top, (value - top.astype(f32)).astype(bf16)


def dot(a, b, ca=1, cb=0):
    return lax.dot_general(a, b, (((ca,), (cb,)), ((), ())), preferred_element_type=f32)


def kernel(
    back, nx, ny, xr, *refs
):
    if back:
        (inc_ref, slope_ref, w_hbm, mix_ref, bz_ref, bzs_ref, ky_ref, kyt_ref, bx_ref, bxr_ref,
         out_ref, modes_ref, got_ref, *scratch) = refs
    else:
        (inc_ref, w_hbm, mix_ref, bias_ref, bz_ref, bzs_ref, ky_ref, kyt_ref, bx_ref, bxr_ref,
         out_ref, modes_ref, got_ref, *scratch) = refs
    (w_ref, sig_ref, ghi_ref, glo_ref, s_ref, r_ref, m_ref, p_ref, q_ref, qs_ref,
     send1, recv1, send2, recv2, wsem) = scratch
    channels, _, yr, zr = inc_ref.shape
    cl, jl, xp = MODES // nx, MODES // ny, r_ref.shape[2]
    n = nx * ny
    lanes = jl * channels
    gx, gy = lax.axis_index("gx"), lax.axis_index("gy")
    me = gx * ny + gy

    wcopy = pltpu.make_async_copy(w_hbm, w_ref, wsem)
    wcopy.start()

    barrier = pltpu.get_barrier_semaphore()

    def greet(k, carry):
        peer = lax.rem(me + k, n)
        pl.semaphore_signal(
            barrier, inc=1,
            device_id={"gx": peer // ny, "gy": lax.rem(peer, ny)},
            device_id_type=pl.DeviceIdType.MESH,
        )
        return carry

    lax.fori_loop(1, n, greet, 0)

    def along_z(x, carry):
        if back:
            signal = inc_ref[:, x].astype(f32) * slope_ref[:, x]
            sig_ref[:, x] = signal
            block = signal.astype(bf16)
        else:
            block = inc_ref[:, x]
        block = block.reshape(channels * yr, zr)
        g = dot(bz_ref[0], block, 1, 1) + dot(bz_ref[1], block, 1, 1)
        ghi, glo = split(g)
        rows = pl.ds(pl.multiple_of(x * MODES, MODES), MODES)
        ghi_ref[rows, :] = ghi
        glo_ref[rows, :] = glo
        return carry

    lax.fori_loop(0, xr, along_z, 0)
    ghi = ghi_ref[...]
    t = dot(ghi, ky_ref[0]) + dot(ghi, ky_ref[1]) + dot(glo_ref[...], ky_ref[0])
    t = jnp.swapaxes(t.reshape(xr, MODES, ny * lanes), 0, 1)
    if xp > xr:
        t = jnp.concatenate([t, jnp.zeros((MODES, xp - xr, ny * lanes), f32)], axis=1)
    t = t.astype(bf16)
    for h in range(ny):
        s_ref[h] = t[:, :, h * lanes : (h + 1) * lanes].reshape(nx, cl, xp, lanes)

    pl.semaphore_wait(barrier, n - 1)

    def exchange(source, target, send, recv):
        def copy_to(peer, slot_of):
            return pltpu.make_async_remote_copy(
                src_ref=source(peer // ny, lax.rem(peer, ny)),
                dst_ref=target.at[lax.rem(slot_of, ny) * nx + slot_of // ny],
                send_sem=send.at[peer],
                recv_sem=recv.at[slot_of],
                device_id={"gx": peer // ny, "gy": lax.rem(peer, ny)},
                device_id_type=pl.DeviceIdType.MESH,
            )

        def begin(k, carry):
            copy_to(lax.rem(me + k, n), me).start()
            return carry

        def finish(k, carry):
            copy_to(lax.rem(me + k, n), me).wait_send()
            peer = lax.rem(me + n - k, n)
            copy_to(peer, peer).wait_recv()
            return carry

        lax.fori_loop(1, n, begin, 0)
        target[gy * nx + gx] = source(gx, gy)[...]
        lax.fori_loop(1, n, finish, 0)

    exchange(lambda d, h: s_ref.at[h, d], r_ref, send1, recv1)

    for c in range(cl):
        part = r_ref[:, c].reshape(n * xp, lanes)
        own = dot(bx_ref[0], part) + dot(bx_ref[1], part)
        modes_ref[c] = own.T.reshape(jl, channels, MODES)
    wcopy.wait()

    def mix(j, carry):
        for c in range(cl):
            own = modes_ref[c, j]
            weight = w_ref[j, c]
            if back:
                m_ref[c, j] = jnp.sum(weight * own[None], axis=1)
            else:
                m_ref[c, j] = jnp.sum(weight * own[:, None, :], axis=0)
        return carry

    lax.fori_loop(0, jl, mix, 0)
    for c in range(cl):
        top, rest = split(m_ref[c].reshape(lanes, MODES))
        spread = (
            dot(bxr_ref[0], top, 1, 1) + dot(bxr_ref[1], top, 1, 1) + dot(bxr_ref[0], rest, 1, 1)
        )
        p_ref[:, c] = spread.astype(bf16).reshape(nx, xp, lanes)

    exchange(lambda d, h: p_ref.at[d], q_ref, send2, recv2)

    got = [q_ref[h * nx : (h + 1) * nx].reshape(MODES, xp, lanes) for h in range(ny)]
    got = jnp.concatenate(got, axis=2).astype(f32)
    got = jnp.swapaxes(got, 0, 1)[:xr].reshape(xr * MODES, ny * lanes).astype(bf16)
    got_ref[...] = got
    qs_ref[...] = dot(got, kyt_ref[0]) + dot(got, kyt_ref[1])

    def finish_field(x, carry):
        rows = pl.ds(pl.multiple_of(x * MODES, MODES), MODES)
        top, rest = split(qs_ref[rows, :])
        stack = jnp.concatenate([top, rest, top], axis=0)
        field = dot(stack, bzs_ref[...], 0, 0).reshape(channels, yr, zr)
        if back:
            values = [sig_ref[i, x] for i in range(channels)]
        else:
            values = [inc_ref[i, x].astype(f32) for i in range(channels)]
        for o in range(channels):
            total = field[o]
            for i in range(channels):
                total = total + (mix_ref[i, o] if back else mix_ref[o, i]) * values[i]
            if back:
                out_ref[o, x] = total.astype(bf16)
            else:
                total = total + bias_ref[0, o]
                cdf = 0.5 * (1.0 + lax.erf(total * 0.7071067811865476))
                out_ref[o, x] = cdf + total * jnp.exp(-0.5 * total * total) * 0.3989422804014327
        return carry

    lax.fori_loop(0, xr, finish_field, 0)


def ahead_kernel(
    act_ref, cot_ref, got_ref, got_back_ref, mix_ref, bias_ref, bzs_ref, kyt_ref, out_ref,
    pre_ref, back_ref,
):
    channels, xr, yr, zr = act_ref.shape
    pre_ref[...] = dot(got_ref[...], kyt_ref[0]) + dot(got_ref[...], kyt_ref[1])
    back_ref[...] = dot(got_back_ref[...], kyt_ref[0]) + dot(got_back_ref[...], kyt_ref[1])

    def field_of(ref, x):
        rows = pl.ds(pl.multiple_of(x * MODES, MODES), MODES)
        top, rest = split(ref[rows, :])
        stack = jnp.concatenate([top, rest, top], axis=0)
        return dot(stack, bzs_ref[...], 0, 0).reshape(channels, yr, zr)

    def step(x, carry):
        field = field_of(pre_ref, x)
        values = [act_ref[i, x].astype(f32) for i in range(channels)]
        signals = []
        for o in range(channels):
            total = field[o]
            for i in range(channels):
                total = total + mix_ref[o, i] * values[i]
            total = total + bias_ref[0, o]
            cdf = 0.5 * (1.0 + lax.erf(total * 0.7071067811865476))
            slope = cdf + total * jnp.exp(-0.5 * total * total) * 0.3989422804014327
            signals.append(cot_ref[o, x].astype(f32) * slope)
        field = field_of(back_ref, x)
        for o in range(channels):
            total = field[o]
            for i in range(channels):
                total = total + mix_ref[i, o] * signals[i]
            out_ref[o, x] = total.astype(bf16)
        return carry

    lax.fori_loop(0, xr, step, 0)


def ahead(activations, cotangent, got, got_back, mixing, bias, bzs, kyt):
    channels, xr, yr, zr = activations.shape
    vmem = pl.BlockSpec(memory_space=pltpu.VMEM)
    smem = pl.BlockSpec(memory_space=pltpu.SMEM)
    return pl.pallas_call(
        ahead_kernel,
        out_shape=jax.ShapeDtypeStruct(activations.shape, bf16),
        in_specs=[vmem] * 4 + [smem] * 2 + [vmem] * 2,
        out_specs=vmem,
        scratch_shapes=[pltpu.VMEM((xr * MODES, channels * yr), f32)] * 2,
        compiler_params=pltpu.CompilerParams(vmem_limit_bytes=50 * 2**20),
        cost_estimate=pl.CostEstimate(flops=10**9, bytes_accessed=10**7, transcendentals=10**6),
    )(activations, cotangent, got, got_back, mixing, bias, bzs, kyt)


def block_turn(back, nx, ny, collective, field, slope, weights, mixing, bias, tables):
    channels, xr, yr, zr = field.shape
    xp = -(-xr // 16) * 16
    cl, jl, n = MODES // nx, MODES // ny, nx * ny
    lanes = jl * channels
    vmem = pl.BlockSpec(memory_space=pltpu.VMEM)
    smem = pl.BlockSpec(memory_space=pltpu.SMEM)
    hbm = pl.BlockSpec(memory_space=pl.ANY)
    if back:
        args = (field, slope, weights, mixing, *tables)
        specs = [vmem, vmem, hbm, smem] + [vmem] * len(tables)
    else:
        args = (field, weights, mixing, bias, *tables)
        specs = [vmem, hbm, smem, smem] + [vmem] * len(tables)
    dma = pltpu.SemaphoreType.DMA
    return pl.pallas_call(
        functools.partial(kernel, back, nx, ny, xr),
        out_shape=(
            jax.ShapeDtypeStruct(field.shape, bf16 if back else f32),
            jax.ShapeDtypeStruct((cl, jl, channels, MODES), f32),
            jax.ShapeDtypeStruct((xr * MODES, ny * lanes), bf16),
        ),
        in_specs=specs,
        out_specs=(vmem, vmem, vmem),
        scratch_shapes=[
            pltpu.VMEM(weights.shape, f32),
            pltpu.VMEM(field.shape if back else (8, 128), f32),
            pltpu.VMEM((xr * MODES, channels * yr), bf16),
            pltpu.VMEM((xr * MODES, channels * yr), bf16),
            pltpu.VMEM((ny, nx, cl, xp, lanes), bf16),
            pltpu.VMEM((n, cl, xp, lanes), bf16),
            pltpu.VMEM((cl, jl, channels, MODES), f32),
            pltpu.VMEM((nx, cl, xp, lanes), bf16),
            pltpu.VMEM((n, cl, xp, lanes), bf16),
            pltpu.VMEM((xr * MODES, channels * yr), f32),
            dma((n,)), dma((n,)), dma((n,)), dma((n,)), dma,
        ],
        compiler_params=pltpu.CompilerParams(
            collective_id=collective, has_side_effects=True, vmem_limit_bytes=50 * 2**20
        ),
        cost_estimate=pl.CostEstimate(flops=10**9, bytes_accessed=2 * 10**7, transcendentals=10**6),
    )(*args)


def body(activations, cotangent, spectral_weights, pointwise, channel_bias):
    inputs = activations[0]
    channels, xr, yr, zr = inputs.shape
    nx, ny = lax.axis_size("gx"), lax.axis_size("gy")
    xp = -(-xr // 16) * 16
    bz = trig_basis(zr)
    bx = trig_basis(xr * nx).reshape(MODES, nx, xr)
    bx = np.concatenate([bx, np.zeros((MODES, nx, xp - xr))], axis=2).reshape(MODES, nx * xp)
    by = trig_basis(yr * ny).reshape(MODES, ny, yr)
    kron = np.einsum("jgy,ik->giyjk", by, np.eye(channels)).reshape(
        ny, channels * yr, MODES * channels
    )
    bzh = halves(bz)
    kh = halves(kron)
    gy = lax.axis_index("gy")
    ky = lax.dynamic_index_in_dim(jnp.asarray(np.swapaxes(kh, 0, 1)), gy, 0, False)
    kyt = lax.dynamic_index_in_dim(
        jnp.asarray(np.ascontiguousarray(np.transpose(kh, (1, 0, 3, 2)))), gy, 0, False
    )
    tables = (
        jnp.asarray(bzh),
        jnp.asarray(np.concatenate([bzh[0], bzh[0], bzh[1]], axis=0)),
        ky,
        kyt,
        jnp.asarray(halves(np.concatenate([bx] * ny, axis=1))),
        jnp.asarray(halves(bx.T)),
    )
    weights = spectral_weights[0]
    mixing = pointwise[0]
    following = [from_behind(v, "segment", -1) for v in (inputs, mixing, channel_bias)]
    slope, input_modes, got = block_turn(
        False, nx, ny, 0, inputs, None, weights, mixing, channel_bias, tables
    )
    next_got = from_behind(got, "segment", -1)
    segment_index = lax.axis_index("segment")
    segment_count = lax.axis_size("segment")
    incoming = cotangent
    kept_grad = jnp.zeros(cotangent.shape, bf16)
    kept_modes = jnp.zeros(input_modes.shape, f32)
    for turn_index in range(segment_count):
        active = segment_index == segment_count - 1 - turn_index
        input_grad, grad_modes, got_back = block_turn(
            True, nx, ny, 1 + turn_index, incoming, slope, weights, mixing, None, tables
        )
        kept_grad = jnp.where(active, input_grad, kept_grad)
        kept_modes = jnp.where(active, grad_modes, kept_modes)
        if turn_index == 0 and segment_count > 1:
            next_back = from_behind(got_back, "segment", -1)
            incoming = ahead(
                following[0], cotangent, next_got, next_back, following[1], following[2],
                tables[1], tables[3],
            )
        elif turn_index + 1 < segment_count:
            incoming = from_behind(input_grad, "segment", -1)
    input_modes = jnp.swapaxes(input_modes, 0, 1)
    kept_modes = jnp.swapaxes(kept_modes, 0, 1)
    weight_grad = input_modes[:, :, :, None, :] * kept_modes[:, :, None, :, :]
    return (kept_grad[None], weight_grad[None])


def slope_of(value):
    cdf = 0.5 * (1.0 + lax.erf(value * 0.7071067811865476))
    return cdf + value * jnp.exp(-0.5 * value * value) * 0.3989422804014327


def field_of(cells, ny, ky, bzi):
    blocks = []
    for h in range(ny):
        block = cells(h)
        blocks.append(block.reshape(block.shape[0] * block.shape[1], block.shape[2]))
    block = jnp.concatenate(blocks, axis=1)
    top, rest = split(dot(ky[0], block, 1, 1) + dot(ky[1], block, 1, 1))
    return dot(jnp.concatenate([top, rest, top], axis=1), bzi[...])


def relay_kernel(
    nx, ny, xq, cuts,
    act_hbm, cot_hbm, w_hbm, mix_ref, bias_ref, mix_hbm, bias_hbm,
    kyt_hbm, ky_hbm, bzf_hbm, bzi_hbm, bx_hbm, sp_hbm,
    out, rest_ref, cells_ref, wgrad, ky, bzi,
    act, act1, cot, w, wd, kyt, bzf, bx, sp,
    u, v, slope, sig, in_modes, grad_modes, m_ref, mt_send, mt_recv,
    mixv1, biasv1, mix1, bias1, s_ref, p_ref, r_ref,
    load_sem, send_sem, recv_sem, row_send, row_recv, small_send, small_recv, store_sem,
    tail_send, tail_recv, pair_send, pair_recv,
):
    channels, xr, yr, zr = act.shape
    n = nx * ny
    cl, jl = MODES // nx, MODES // ny
    nh, hq = r_ref.shape[1], r_ref.shape[3]
    lanes = jl * channels
    rows = channels * yr
    tail = xr - hq * xq
    late = xr - xq
    gx, gy, seg = lax.axis_index("gx"), lax.axis_index("gy"), lax.axis_index("segment")
    me = gx * ny + gy
    mine = gy * nx + gx
    first, last = seg == 0, seg == 1
    mesh_ids = pl.DeviceIdType.MESH

    loads = [
        pltpu.make_async_copy(source, target, load_sem.at[k])
        for k, (source, target) in enumerate(
            [
                (act_hbm, act), (bzf_hbm, bzf), (kyt_hbm.at[gy], kyt), (w_hbm, w), (bx_hbm, bx),
                (sp_hbm, sp), (ky_hbm.at[gy], ky), (bzi_hbm, bzi), (cot_hbm, cot),
            ]
        )
    ]
    for load in loads:
        load.start()

    barrier = pltpu.get_barrier_semaphore()

    def greet(k, carry):
        other = lax.rem(seg * n + me + k, 2 * n)
        peer = lax.rem(other, n)
        pl.semaphore_signal(
            barrier, inc=1,
            device_id={"segment": other // n, "gx": peer // ny, "gy": lax.rem(peer, ny)},
            device_id_type=mesh_ids,
        )
        return carry

    lax.fori_loop(1, 2 * n, greet, 0)

    def ahead(source, target, send, recv):
        return pltpu.make_async_remote_copy(
            src_ref=source, dst_ref=target, send_sem=send, recv_sem=recv,
            device_id={"segment": 1 - seg}, device_id_type=mesh_ids,
        )

    def row_copy(x):
        return ahead(act_hbm.at[:, x], act1.at[:, x], row_send.at[x], row_recv.at[x])

    def send_rows(start, stop):
        for x in range(start, stop):
            row_copy(x).start()

    def modes_copy(k):
        return ahead(mt_send.at[k], mt_recv.at[k], small_send.at[k], small_recv.at[k])

    small = [
        ahead(mix_hbm, mixv1, small_send.at[2], small_recv.at[2]),
        ahead(bias_hbm, biasv1, small_send.at[3], small_recv.at[3]),
    ]

    def send(source, target, sends, receives):
        def begin(k, carry):
            peer = lax.rem(me + k, n)
            d, h = peer // ny, lax.rem(peer, ny)
            pltpu.make_async_remote_copy(
                src_ref=source(d, h), dst_ref=target, send_sem=sends, recv_sem=receives,
                device_id={"gx": d, "gy": h}, device_id_type=mesh_ids,
            ).start()
            return carry

        lax.fori_loop(1, n, begin, 0)
        target[...] = source(gx, gy)[...]

    def send_half(source, e, half):
        send(source, r_ref.at[e, half, mine], send_sem.at[e, half], recv_sem.at[e, half])

    def send_along(source, e, half):
        def begin(k, carry):
            d = lax.rem(gx + k, nx)
            pltpu.make_async_remote_copy(
                src_ref=source(d), dst_ref=r_ref.at[e, half, mine],
                send_sem=send_sem.at[e, half], recv_sem=recv_sem.at[e, half],
                device_id={"gx": d}, device_id_type=mesh_ids,
            ).start()
            return carry

        lax.fori_loop(1, nx, begin, 0)
        r_ref[e, half, mine] = source(gx)[...]

    def pair_copy(e, half):
        block = r_ref.at[e, half, pl.ds(gy * nx, nx)]
        return pltpu.make_async_remote_copy(
            src_ref=block, dst_ref=block,
            send_sem=pair_send.at[e, half], recv_sem=pair_recv.at[e, half],
            device_id={"gy": 1 - gy}, device_id_type=mesh_ids,
        )

    def forward(e, halves):
        for half in halves:
            await_block(r_ref.at[e, half, pl.ds(0, nx - 1)], recv_sem.at[e, half])
            pair_copy(e, half).start()

    def land(e, half):
        await_block(r_ref.at[e, half, pl.ds(0, nx)], pair_recv.at[e, half])

    def sent_along(e, half):
        await_block(r_ref.at[e, half, pl.ds(0, nx - 1)], send_sem.at[e, half])
        await_block(r_ref.at[e, half, pl.ds(0, nx)], pair_send.at[e, half])

    def send_tail(k, carry):
        peer = lax.rem(me + k, n)
        d, h = peer // ny, lax.rem(peer, ny)
        pltpu.make_async_remote_copy(
            src_ref=s_ref.at[2, nh - 1, h * nx + d], dst_ref=r_ref.at[4, nh - 1, mine],
            send_sem=tail_send.at[0], recv_sem=tail_recv.at[0],
            device_id={"segment": 0, "gx": d, "gy": h}, device_id_type=mesh_ids,
        ).start()
        return carry

    def await_block(block, sem):
        pltpu.make_async_copy(block, block, sem).wait()

    def arrive(e, half):
        await_block(r_ref.at[e, half, pl.ds(0, n - 1)], recv_sem.at[e, half])

    def sent(e, half):
        await_block(r_ref.at[e, half, pl.ds(0, n - 1)], send_sem.at[e, half])

    def to_modes(blocks, k, half):
        parts = []
        for block in blocks:
            g = dot(block, bzf[...])
            parts.append(g[:, : nx * 16] + g[:, nx * 16 :])
        top, rest = split(jnp.concatenate(parts, axis=1))
        t = dot(kyt[0], top) + dot(kyt[1], top) + dot(kyt[0], rest)
        t = t.T.astype(bf16)
        for q in range(len(blocks)):
            for h in range(ny):
                part = t[q * nx * 16 : (q + 1) * nx * 16, h * lanes : (h + 1) * lanes]
                s_ref[k, half, h * nx : (h + 1) * nx, q] = part.reshape(nx, 16, lanes)

    def to_field(e, half, q):
        return field_of(lambda h: r_ref[e, half, h * nx : (h + 1) * nx, q], ny, ky, bzi)

    def row(field, x):
        return field[:, x * zr : (x + 1) * zr].reshape(channels, yr, zr)

    def send_modes(k, e, half):
        send_half(lambda d, h: s_ref.at[k, half, h * nx + d], e, half)

    def own_modes(e, await_half):
        own = None
        for half in range(nh):
            await_half(half)
            block = r_ref[e, half].reshape(n * hq * 16, lanes)
            part = slice(half * n * hq * 16, (half + 1) * n * hq * 16)
            term = dot(bx[0, :, part], block) + dot(bx[1, :, part], block)
            own = term if own is None else own + term
        return own.T.reshape(jl, channels, cl * MODES)

    def send_cells(mt, k, e, halves):
        top, rest = split(mt)
        for half in halves:
            table = [sp[i, half].reshape(nx * hq * 16, cl * MODES) for i in range(2)]
            cells = dot(table[0], top) + dot(table[1], top) + dot(table[0], rest)
            p_ref[k, half] = cells.astype(bf16).reshape(nx, hq, 16, lanes)
            send_along(lambda d: p_ref.at[k, half, d], e, half)

    def mixed():
        return m_ref[...].reshape(lanes, cl * MODES).T

    def mix_back(e, await_half):
        grad_modes[...] = own_modes(e, await_half)

        def step(j, carry):
            m_ref[j] = jnp.sum(wd[j] * grad_modes[j][None], axis=1)
            return carry

        lax.fori_loop(0, jl, step, 0)

    def blend(mixing, values, o, back):
        total = (mixing[0, o] if back else mixing[o, 0]) * values[0]
        for i in range(1, channels):
            total = total + (mixing[i, o] if back else mixing[o, i]) * values[i]
        return total

    def fetch_small():
        for copy in small:
            copy.wait_recv()
        for k, (source, target) in enumerate([(mixv1, mix1), (biasv1, bias1)]):
            copy = pltpu.make_async_copy(source, target, store_sem.at[k])
            copy.start()
            copy.wait()

    def back_block(half, q, offset):
        field = to_field(3, half, q)
        x0 = (half * hq + q) * xq
        block = []
        for k in range(xq):
            incoming = (row(field, k) + offset[:, x0 + k]).astype(bf16).astype(f32)
            signal = incoming * slope[:, x0 + k]
            block.append((x0 + k, signal))
        return block

    def packed(block):
        return jnp.concatenate([s.astype(bf16).reshape(rows, zr) for _, s in block], axis=1)

    def blend_back(start, stop):
        def step(x, carry):
            values = [sig[i, x] for i in range(channels)]
            for o in range(channels):
                u[o, x] = blend(mix_ref, values, o, True)
            return carry

        lax.fori_loop(start, stop, step, 0)

    pl.semaphore_wait(barrier, 2 * n - 1)
    for copy in small:
        copy.start()

    @pl.when(last)
    def _():
        send_rows(0, cuts[0])

    @pl.when(first)
    def _():
        send_rows(tail, xr)

    for load in loads[:3]:
        load.wait()
    for half in range(nh):
        blocks = []
        for q in range(hq):
            x = (half * hq + q) * xq
            block = [act[:, x + k].reshape(rows, zr) for k in range(xq)]
            blocks.append(jnp.concatenate(block, axis=1))
        to_modes(blocks, 0, half)
        send_modes(0, 0, half)

    for load in loads[3:]:
        load.wait()

    def dense(j, carry):
        for i in range(channels):
            wd[j, i] = jnp.concatenate([w[j, c, i] for c in range(cl)], axis=1)
        return carry

    lax.fori_loop(0, jl, dense, 0)

    def pointwise(x, carry):
        values = [act[i, x].astype(f32) for i in range(channels)]
        for o in range(channels):
            u[o, x] = blend(mix_ref, values, o, False) + bias_ref[0, o]
        return carry

    lax.fori_loop(0, xr, pointwise, 0)

    in_modes[...] = own_modes(0, lambda half: arrive(0, half))

    def mix(j, carry):
        own = in_modes[j]
        m_ref[j] = jnp.sum(wd[j] * own[:, None, :], axis=0)
        return carry

    lax.fori_loop(0, jl, mix, 0)
    mt_send[0] = mixed()
    modes_copy(0).start()

    @pl.when(last)
    def _():
        send_rows(cuts[0], cuts[1])

    send_cells(mt_send[0], 0, 1, range(nh))

    @pl.when(last)
    def _():
        forward(1, range(nh))
        for half in range(nh):
            land(1, half)
            blocks = []
            for q in range(hq):
                field = to_field(1, half, q)
                x0 = (half * hq + q) * xq
                block = []
                for k in range(xq):
                    signal = cot[:, x0 + k].astype(f32) * slope_of(row(field, k) + u[:, x0 + k])
                    sig[:, x0 + k] = signal
                    block.append(signal.astype(bf16).reshape(rows, zr))
                blocks.append(jnp.concatenate(block, axis=1))
            to_modes(blocks, 1, half)
            send_modes(1, 2, half)

        modes_copy(0).wait_recv()
        send_cells(mt_recv[0], 3, 5, [nh - 1])
        fetch_small()

        mix_back(2, lambda half: arrive(2, half))
        mt_send[1] = mixed()
        modes_copy(1).start()
        send_rows(cuts[1], cuts[2])
        send_cells(mt_send[1], 1, 3, reversed(range(nh)))

        blend_back(0, xr)
        for x in range(tail, xr):
            row_copy(x).wait_recv()
        forward(5, [nh - 1])
        land(5, nh - 1)
        for q in range(hq):
            field = to_field(5, nh - 1, q)
            x0 = tail + q * xq
            for k in range(xq):
                values = [act1[i, x0 + k].astype(f32) for i in range(channels)]
                here = row(field, k)
                for o in range(channels):
                    pre = here[o] + blend(mix1, values, o, False) + bias1[0, o]
                    slope[o, x0 + k] = slope_of(pre)
        forward(3, reversed(range(nh)))
        land(3, nh - 1)
        to_modes([packed(back_block(nh - 1, q, u)) for q in range(hq)], 2, nh - 1)
        lax.fori_loop(0, n, send_tail, 0)
        send_rows(cuts[2], xr)

    def ahead_quarter(half, q):
        field = to_field(2, half, q)
        x0 = (half * hq + q) * xq
        for k in range(xq):
            row_copy(x0 + k).wait_recv()
            values = [act1[i, x0 + k].astype(f32) for i in range(channels)]
            here = row(field, k)
            signals = []
            for o in range(channels):
                pre = here[o] + blend(mix1, values, o, False) + bias1[0, o]
                signals.append(cot[o, x0 + k].astype(f32) * slope_of(pre))
            for i in range(channels):
                v[i, x0 + k] = blend(mix1, signals, i, True)

    def kept(block):
        for x, signal in block:
            sig[:, x] = signal
        return block

    @pl.when(first)
    def _():
        modes_copy(0).wait_recv()
        send_cells(mt_recv[0], 1, 2, range(nh))
        fetch_small()
        forward(1, range(nh))
        for half in range(nh):
            land(1, half)

            def step(q, carry):
                field = to_field(1, half, q)
                x0 = (half * hq + q) * xq
                for k in range(xq):
                    slope[:, x0 + k] = slope_of(row(field, k) + u[:, x0 + k])
                return carry

            lax.fori_loop(0, hq, step, 0)

        forward(2, range(nh))
        for half in range(nh):
            land(2, half)
        for half in range(nh - 1):
            for q in range(hq):
                ahead_quarter(half, q)
        modes_copy(1).wait_recv()
        send_cells(mt_recv[1], 2, 3, range(nh))
        forward(3, range(nh))
        for half in range(nh - 1):
            land(3, half)
            to_modes([packed(kept(back_block(half, q, v))) for q in range(hq)], 1, half)
            send_modes(1, 4, half)
        blend_back(0, tail)
        land(3, nh - 1)
        for q in range(hq - 1):
            ahead_quarter(nh - 1, q)
            kept(back_block(nh - 1, q, v))

        def await_half(half):
            if half < nh - 1:
                arrive(4, half)
            else:
                await_block(r_ref.at[4, half], tail_recv.at[0])

        mix_back(4, await_half)
        send_cells(mixed(), 3, 5, range(nh))
        if hq > 1:
            blend_back(tail, late)
        for target, e in ((v, 2), (u, 3)):
            field = to_field(e, nh - 1, hq - 1)
            for k in range(xq):
                target[:, late + k] = row(field, k)

    def weight_grad(j, carry):
        for c in range(cl):
            part = slice(c * MODES, (c + 1) * MODES)
            wgrad[j, c] = in_modes[j][:, None, part] * grad_modes[j][None, :, part]
        return carry

    lax.fori_loop(0, jl, weight_grad, 0)
    e = 3 + 2 * (1 - seg)

    @pl.when(last)
    def _():
        for half in range(nh - 1):
            land(3, half)

    @pl.when(first)
    def _():
        forward(5, range(nh))
        for half in range(nh):
            land(5, half)

    for half in range(nh):
        for q in range(hq if half < nh - 1 else hq - 1):
            field = to_field(e, half, q)
            x0 = (half * hq + q) * xq
            for k in range(xq):
                out[:, x0 + k] = (row(field, k) + u[:, x0 + k]).astype(bf16)
    cells_ref[...] = r_ref[e, nh - 1, :, hq - 1 :]

    @pl.when(first)
    def _():
        def step(k, carry):
            x = late + k
            row_copy(x).wait_recv()
            values = [act1[i, x].astype(f32) for i in range(channels)]
            signals = []
            for o in range(channels):
                pre = v[o, x] + blend(mix1, values, o, False) + bias1[0, o]
                signals.append(cot[o, x].astype(f32) * slope_of(pre))
            here = []
            for i in range(channels):
                incoming = u[i, x] + blend(mix1, signals, i, True)
                here.append(incoming.astype(bf16).astype(f32) * slope[i, x])
            for o in range(channels):
                rest_ref[o, k] = blend(mix_ref, here, o, True)
            return carry

        lax.fori_loop(0, xq, step, 0)

    @pl.when(last)
    def _():
        rest_ref[...] = u[:, late:]

    for half in range(nh):
        sent(0, half)
        sent_along(1, half)
        sent_along(3, half)
    for copy in small:
        copy.wait_send()
    modes_copy(0).wait_send()

    @pl.when(first)
    def _():
        for half in range(nh - 1):
            sent(4, half)
        for half in range(nh):
            sent_along(2, half)
            sent_along(5, half)
        for x in range(tail, xr):
            row_copy(x).wait_send()

    @pl.when(last)
    def _():
        for half in range(nh):
            sent(2, half)
        sent_along(5, nh - 1)
        modes_copy(1).wait_send()
        await_block(r_ref.at[4, nh - 1], tail_send.at[0])
        for x in range(xr):
            row_copy(x).wait_send()


def finish_kernel(
    nx, ny, xq, done_ref, rest_ref, cells_ref, wgrad, ky, bzi, grad_hbm, wgrad_hbm, out, sem
):
    channels, done, yr, zr = done_ref.shape
    hq = cells_ref.shape[1]
    stores = [
        pltpu.make_async_copy(wgrad, wgrad_hbm, sem.at[0]),
        pltpu.make_async_copy(done_ref, grad_hbm.at[:, pl.ds(0, done)], sem.at[1]),
    ]
    for store in stores:
        store.start()
    for q in range(hq):
        field = field_of(lambda h: cells_ref[h * nx : (h + 1) * nx, q], ny, ky, bzi)
        for k in range(xq):
            x = q * xq + k
            here = field[:, k * zr : (k + 1) * zr].reshape(channels, yr, zr)
            out[:, x] = (here + rest_ref[:, x]).astype(bf16)
        part = pl.ds(q * xq, xq)
        store = pltpu.make_async_copy(
            out.at[:, part], grad_hbm.at[:, pl.ds(done + q * xq, xq)], sem.at[2 + q]
        )
        store.start()
        stores.append(store)
    for store in stores:
        store.wait()


def two_section_body(activations, cotangent, spectral_weights, pointwise, channel_bias):
    inputs = activations[0]
    channels, xr, yr, zr = inputs.shape
    nx, ny = lax.axis_size("gx"), lax.axis_size("gy")
    n = nx * ny
    cl, jl = MODES // nx, MODES // ny
    xq = 16 // cl
    nh = 2
    hq = xr // (nh * xq)
    lanes, rows = jl * channels, channels * yr
    bz = trig_basis(zr).reshape(nx, cl, zr)
    eye_x, eye_c = np.eye(xq), np.eye(cl)
    bzf = np.einsum("dcz,xX->xzdXc", bz, eye_x).reshape(xq * zr, nx * 16)
    bzi = halves(bzf.reshape(xq, zr, nx * 16).transpose(2, 0, 1).reshape(nx * 16, xq * zr))
    by = trig_basis(yr * ny).reshape(MODES, ny, yr)
    ky = np.einsum("jgy,ik->giyjk", by, np.eye(channels)).reshape(ny, rows, ny * lanes)
    ky = halves(ky)
    bx = trig_basis(xr * nx).reshape(MODES, nx, nh, hq, xq)
    sp = np.einsum("adtqx,cC->tdqxCca", bx, eye_c).reshape(nh * nx * hq * 16, cl * MODES)
    bxf = np.broadcast_to(
        sp.reshape(nh, 1, nx * hq * 16, cl * MODES), (nh, ny, nx * hq * 16, cl * MODES)
    )
    bxf = bxf.reshape(nh * n * hq * 16, cl * MODES).T
    bzf = halves(bzf)
    tables = [
        np.ascontiguousarray(ky.transpose(1, 0, 3, 2)),
        np.ascontiguousarray(ky.transpose(1, 0, 2, 3)),
        np.concatenate([bzf[0], bzf[1]], axis=1),
        np.concatenate([bzi[0], bzi[0], bzi[1]], axis=0),
        halves(bxf),
        halves(sp).reshape(2, nh, nx, hq, 16, cl * MODES),
    ]
    weights, mixing = spectral_weights[0], pointwise[0]
    vmem = pl.BlockSpec(memory_space=pltpu.VMEM)
    smem = pl.BlockSpec(memory_space=pltpu.SMEM)
    hbm = pl.BlockSpec(memory_space=pl.ANY)
    dma = pltpu.SemaphoreType.DMA
    grid = inputs.shape
    done = grid[:1] + (xr - xq,) + grid[2:]
    left = grid[:1] + (xq,) + grid[2:]
    scratch = [
        pltpu.VMEM(grid, bf16), pltpu.VMEM(grid, bf16), pltpu.VMEM(grid, bf16),
        pltpu.VMEM(weights.shape, f32),
        pltpu.VMEM((jl, channels, channels, cl * MODES), f32),
        pltpu.VMEM((2, ny * lanes, rows), bf16),
        pltpu.VMEM((xq * zr, 2 * nx * 16), bf16),
        pltpu.VMEM((2, cl * MODES, nh * n * hq * 16), bf16),
        pltpu.VMEM((2, nh, nx, hq, 16, cl * MODES), bf16),
        pltpu.VMEM(grid, f32), pltpu.VMEM(grid, f32), pltpu.VMEM(grid, f32), pltpu.VMEM(grid, f32),
        pltpu.VMEM((jl, channels, cl * MODES), f32),
        pltpu.VMEM((jl, channels, cl * MODES), f32),
        pltpu.VMEM((jl, channels, cl * MODES), f32),
        pltpu.VMEM((2, cl * MODES, lanes), f32),
        pltpu.VMEM((2, cl * MODES, lanes), f32),
        pltpu.VMEM(mixing.shape, f32), pltpu.VMEM(channel_bias.shape, f32),
        pltpu.SMEM(mixing.shape, f32), pltpu.SMEM(channel_bias.shape, f32),
        pltpu.VMEM((3, nh, n, hq, 16, lanes), bf16),
        pltpu.VMEM((4, nh, nx, hq, 16, lanes), bf16),
        pltpu.VMEM((6, nh, n, hq, 16, lanes), bf16),
        dma((9,)), dma((6, nh)), dma((6, nh)),
        dma((xr,)), dma((xr,)), dma((4,)), dma((4,)), dma((2,)), dma((1,)), dma((1,)), dma((6, nh)), dma((6, nh)),
    ]
    parts = pl.pallas_call(
        functools.partial(relay_kernel, nx, ny, xq, (3, 9, 12)),
        out_shape=(
            jax.ShapeDtypeStruct(done, bf16),
            jax.ShapeDtypeStruct(left, f32),
            jax.ShapeDtypeStruct((n, 1, 16, lanes), bf16),
            pltpu.VMEM(weights.shape, f32),
            jax.ShapeDtypeStruct((2, rows, ny * lanes), bf16),
            jax.ShapeDtypeStruct((3 * nx * 16, xq * zr), bf16),
        ),
        in_specs=[hbm, hbm, hbm, smem, smem] + [hbm] * (2 + len(tables)),
        out_specs=[vmem] * 6,
        scratch_shapes=scratch,
        compiler_params=pltpu.CompilerParams(
            collective_id=0, has_side_effects=True, vmem_limit_bytes=46 * 2**20
        ),
        cost_estimate=pl.CostEstimate(
            flops=4 * 10**9, bytes_accessed=2 * 10**7, transcendentals=10**7
        ),
    )(
        inputs, cotangent, weights, mixing, channel_bias,
        *[
            pltpu.with_memory_space_constraint(jnp.asarray(table), pltpu.HBM)
            for table in [mixing, channel_bias] + tables
        ],
    )
    input_grad, weight_grad = pl.pallas_call(
        functools.partial(finish_kernel, nx, ny, xq),
        out_shape=(
            jax.ShapeDtypeStruct(grid, bf16),
            jax.ShapeDtypeStruct(weights.shape, f32),
        ),
        in_specs=[vmem] * 6,
        out_specs=(hbm, hbm),
        scratch_shapes=[pltpu.VMEM(left, bf16), dma((3,))],
        compiler_params=pltpu.CompilerParams(vmem_limit_bytes=24 * 2**20),
        cost_estimate=pl.CostEstimate(flops=10**9, bytes_accessed=10**7, transcendentals=0),
    )(*parts)
    return (input_grad[None], weight_grad[None])


def fits(mesh):
    nx = mesh.shape["gx"]
    return mesh.shape["segment"] == 2 and mesh.shape["gy"] == 2 and nx == 8


def solution(mesh):
    return jax.shard_map(
        two_section_body if fits(mesh) else body,
        mesh=mesh,
        in_specs=(
            P("segment", "groups", "gx", "gy", None),
            P("groups", "gx", "gy", None),
            P("segment", "gy", "gx", None, None, None),
            P("segment", None, None),
            P("segment", None),
        ),
        out_specs=(
            P("segment", "groups", "gx", "gy", None),
            P("segment", "gy", "gx", "groups", None, None),
        ),
        check_vma=False,
    )
```

```python
import functools
import math

import jax
import jax.numpy as jnp
import ml_dtypes
import numpy as np
from jax import lax
from jax.experimental import pallas as pl
from jax.experimental.pallas import tpu as pltpu
from jax.sharding import PartitionSpec as P

MODES = 32
f32, bf16 = jnp.float32, jnp.bfloat16


def from_behind(block, axis, distance):
    devices = range(lax.axis_size(axis))
    route = [(i - distance, i) for i in devices if i - distance in devices]
    return lax.ppermute(block, axis, route)


def trig_basis(length):
    half = MODES // 2
    freqs = np.arange(half)[:, None]
    points = np.arange(length)[None, :]
    step = 2.0 * math.pi / length
    rows = np.concatenate(
        [np.cos((freqs * points % length) * step), np.sin(((freqs + 1) * points % length) * step)]
    )
    scales = np.where(np.arange(MODES) == 0, 1.0 / math.sqrt(length), math.sqrt(2.0 / length))
    return rows * scales[:, None]


def halves(matrix):
    matrix = np.asarray(matrix, np.float32)
    top = matrix.astype(ml_dtypes.bfloat16)
    rest = (matrix - top.astype(np.float32)).astype(ml_dtypes.bfloat16)
    return np.stack([top, rest])


def split(value):
    top = value.astype(bf16)
    return top, (value - top.astype(f32)).astype(bf16)


def dot(a, b, ca=1, cb=0):
    return lax.dot_general(a, b, (((ca,), (cb,)), ((), ())), preferred_element_type=f32)


def kernel(
    back, nx, ny, xr, *refs
):
    if back:
        (inc_ref, slope_ref, w_hbm, mix_ref, bz_ref, bzs_ref, ky_ref, kyt_ref, bx_ref, bxr_ref,
         out_ref, modes_ref, got_ref, *scratch) = refs
    else:
        (inc_ref, w_hbm, mix_ref, bias_ref, bz_ref, bzs_ref, ky_ref, kyt_ref, bx_ref, bxr_ref,
         out_ref, modes_ref, got_ref, *scratch) = refs
    (w_ref, sig_ref, ghi_ref, glo_ref, s_ref, r_ref, m_ref, p_ref, q_ref, qs_ref,
     send1, recv1, send2, recv2, wsem) = scratch
    channels, _, yr, zr = inc_ref.shape
    cl, jl, xp = MODES // nx, MODES // ny, r_ref.shape[2]
    n = nx * ny
    lanes = jl * channels
    gx, gy = lax.axis_index("gx"), lax.axis_index("gy")
    me = gx * ny + gy

    wcopy = pltpu.make_async_copy(w_hbm, w_ref, wsem)
    wcopy.start()

    barrier = pltpu.get_barrier_semaphore()

    def greet(k, carry):
        peer = lax.rem(me + k, n)
        pl.semaphore_signal(
            barrier, inc=1,
            device_id={"gx": peer // ny, "gy": lax.rem(peer, ny)},
            device_id_type=pl.DeviceIdType.MESH,
        )
        return carry

    lax.fori_loop(1, n, greet, 0)

    def along_z(x, carry):
        if back:
            signal = inc_ref[:, x].astype(f32) * slope_ref[:, x]
            sig_ref[:, x] = signal
            block = signal.astype(bf16)
        else:
            block = inc_ref[:, x]
        block = block.reshape(channels * yr, zr)
        g = dot(bz_ref[0], block, 1, 1) + dot(bz_ref[1], block, 1, 1)
        ghi, glo = split(g)
        rows = pl.ds(pl.multiple_of(x * MODES, MODES), MODES)
        ghi_ref[rows, :] = ghi
        glo_ref[rows, :] = glo
        return carry

    lax.fori_loop(0, xr, along_z, 0)
    ghi = ghi_ref[...]
    t = dot(ghi, ky_ref[0]) + dot(ghi, ky_ref[1]) + dot(glo_ref[...], ky_ref[0])
    t = jnp.swapaxes(t.reshape(xr, MODES, ny * lanes), 0, 1)
    if xp > xr:
        t = jnp.concatenate([t, jnp.zeros((MODES, xp - xr, ny * lanes), f32)], axis=1)
    t = t.astype(bf16)
    for h in range(ny):
        s_ref[h] = t[:, :, h * lanes : (h + 1) * lanes].reshape(nx, cl, xp, lanes)

    pl.semaphore_wait(barrier, n - 1)

    def exchange(source, target, send, recv):
        def copy_to(peer, slot_of):
            return pltpu.make_async_remote_copy(
                src_ref=source(peer // ny, lax.rem(peer, ny)),
                dst_ref=target.at[lax.rem(slot_of, ny) * nx + slot_of // ny],
                send_sem=send.at[peer],
                recv_sem=recv.at[slot_of],
                device_id={"gx": peer // ny, "gy": lax.rem(peer, ny)},
                device_id_type=pl.DeviceIdType.MESH,
            )

        def begin(k, carry):
            copy_to(lax.rem(me + k, n), me).start()
            return carry

        def finish(k, carry):
            copy_to(lax.rem(me + k, n), me).wait_send()
            peer = lax.rem(me + n - k, n)
            copy_to(peer, peer).wait_recv()
            return carry

        lax.fori_loop(1, n, begin, 0)
        target[gy * nx + gx] = source(gx, gy)[...]
        lax.fori_loop(1, n, finish, 0)

    exchange(lambda d, h: s_ref.at[h, d], r_ref, send1, recv1)

    for c in range(cl):
        part = r_ref[:, c].reshape(n * xp, lanes)
        own = dot(bx_ref[0], part) + dot(bx_ref[1], part)
        modes_ref[c] = own.T.reshape(jl, channels, MODES)
    wcopy.wait()

    def mix(j, carry):
        for c in range(cl):
            own = modes_ref[c, j]
            weight = w_ref[j, c]
            if back:
                m_ref[c, j] = jnp.sum(weight * own[None], axis=1)
            else:
                m_ref[c, j] = jnp.sum(weight * own[:, None, :], axis=0)
        return carry

    lax.fori_loop(0, jl, mix, 0)
    for c in range(cl):
        top, rest = split(m_ref[c].reshape(lanes, MODES))
        spread = (
            dot(bxr_ref[0], top, 1, 1) + dot(bxr_ref[1], top, 1, 1) + dot(bxr_ref[0], rest, 1, 1)
        )
        p_ref[:, c] = spread.astype(bf16).reshape(nx, xp, lanes)

    exchange(lambda d, h: p_ref.at[d], q_ref, send2, recv2)

    got = [q_ref[h * nx : (h + 1) * nx].reshape(MODES, xp, lanes) for h in range(ny)]
    got = jnp.concatenate(got, axis=2).astype(f32)
    got = jnp.swapaxes(got, 0, 1)[:xr].reshape(xr * MODES, ny * lanes).astype(bf16)
    got_ref[...] = got
    qs_ref[...] = dot(got, kyt_ref[0]) + dot(got, kyt_ref[1])

    def finish_field(x, carry):
        rows = pl.ds(pl.multiple_of(x * MODES, MODES), MODES)
        top, rest = split(qs_ref[rows, :])
        stack = jnp.concatenate([top, rest, top], axis=0)
        field = dot(stack, bzs_ref[...], 0, 0).reshape(channels, yr, zr)
        if back:
            values = [sig_ref[i, x] for i in range(channels)]
        else:
            values = [inc_ref[i, x].astype(f32) for i in range(channels)]
        for o in range(channels):
            total = field[o]
            for i in range(channels):
                total = total + (mix_ref[i, o] if back else mix_ref[o, i]) * values[i]
            if back:
                out_ref[o, x] = total.astype(bf16)
            else:
                total = total + bias_ref[0, o]
                cdf = 0.5 * (1.0 + lax.erf(total * 0.7071067811865476))
                out_ref[o, x] = cdf + total * jnp.exp(-0.5 * total * total) * 0.3989422804014327
        return carry

    lax.fori_loop(0, xr, finish_field, 0)


def ahead_kernel(
    act_ref, cot_ref, got_ref, got_back_ref, mix_ref, bias_ref, bzs_ref, kyt_ref, out_ref,
    pre_ref, back_ref,
):
    channels, xr, yr, zr = act_ref.shape
    pre_ref[...] = dot(got_ref[...], kyt_ref[0]) + dot(got_ref[...], kyt_ref[1])
    back_ref[...] = dot(got_back_ref[...], kyt_ref[0]) + dot(got_back_ref[...], kyt_ref[1])

    def field_of(ref, x):
        rows = pl.ds(pl.multiple_of(x * MODES, MODES), MODES)
        top, rest = split(ref[rows, :])
        stack = jnp.concatenate([top, rest, top], axis=0)
        return dot(stack, bzs_ref[...], 0, 0).reshape(channels, yr, zr)

    def step(x, carry):
        field = field_of(pre_ref, x)
        values = [act_ref[i, x].astype(f32) for i in range(channels)]
        signals = []
        for o in range(channels):
            total = field[o]
            for i in range(channels):
                total = total + mix_ref[o, i] * values[i]
            total = total + bias_ref[0, o]
            cdf = 0.5 * (1.0 + lax.erf(total * 0.7071067811865476))
            slope = cdf + total * jnp.exp(-0.5 * total * total) * 0.3989422804014327
            signals.append(cot_ref[o, x].astype(f32) * slope)
        field = field_of(back_ref, x)
        for o in range(channels):
            total = field[o]
            for i in range(channels):
                total = total + mix_ref[i, o] * signals[i]
            out_ref[o, x] = total.astype(bf16)
        return carry

    lax.fori_loop(0, xr, step, 0)


def ahead(activations, cotangent, got, got_back, mixing, bias, bzs, kyt):
    channels, xr, yr, zr = activations.shape
    vmem = pl.BlockSpec(memory_space=pltpu.VMEM)
    smem = pl.BlockSpec(memory_space=pltpu.SMEM)
    return pl.pallas_call(
        ahead_kernel,
        out_shape=jax.ShapeDtypeStruct(activations.shape, bf16),
        in_specs=[vmem] * 4 + [smem] * 2 + [vmem] * 2,
        out_specs=vmem,
        scratch_shapes=[pltpu.VMEM((xr * MODES, channels * yr), f32)] * 2,
        compiler_params=pltpu.CompilerParams(vmem_limit_bytes=50 * 2**20),
        cost_estimate=pl.CostEstimate(flops=10**9, bytes_accessed=10**7, transcendentals=10**6),
    )(activations, cotangent, got, got_back, mixing, bias, bzs, kyt)


def block_turn(back, nx, ny, collective, field, slope, weights, mixing, bias, tables):
    channels, xr, yr, zr = field.shape
    xp = -(-xr // 16) * 16
    cl, jl, n = MODES // nx, MODES // ny, nx * ny
    lanes = jl * channels
    vmem = pl.BlockSpec(memory_space=pltpu.VMEM)
    smem = pl.BlockSpec(memory_space=pltpu.SMEM)
    hbm = pl.BlockSpec(memory_space=pl.ANY)
    if back:
        args = (field, slope, weights, mixing, *tables)
        specs = [vmem, vmem, hbm, smem] + [vmem] * len(tables)
    else:
        args = (field, weights, mixing, bias, *tables)
        specs = [vmem, hbm, smem, smem] + [vmem] * len(tables)
    dma = pltpu.SemaphoreType.DMA
    return pl.pallas_call(
        functools.partial(kernel, back, nx, ny, xr),
        out_shape=(
            jax.ShapeDtypeStruct(field.shape, bf16 if back else f32),
            jax.ShapeDtypeStruct((cl, jl, channels, MODES), f32),
            jax.ShapeDtypeStruct((xr * MODES, ny * lanes), bf16),
        ),
        in_specs=specs,
        out_specs=(vmem, vmem, vmem),
        scratch_shapes=[
            pltpu.VMEM(weights.shape, f32),
            pltpu.VMEM(field.shape if back else (8, 128), f32),
            pltpu.VMEM((xr * MODES, channels * yr), bf16),
            pltpu.VMEM((xr * MODES, channels * yr), bf16),
            pltpu.VMEM((ny, nx, cl, xp, lanes), bf16),
            pltpu.VMEM((n, cl, xp, lanes), bf16),
            pltpu.VMEM((cl, jl, channels, MODES), f32),
            pltpu.VMEM((nx, cl, xp, lanes), bf16),
            pltpu.VMEM((n, cl, xp, lanes), bf16),
            pltpu.VMEM((xr * MODES, channels * yr), f32),
            dma((n,)), dma((n,)), dma((n,)), dma((n,)), dma,
        ],
        compiler_params=pltpu.CompilerParams(
            collective_id=collective, has_side_effects=True, vmem_limit_bytes=50 * 2**20
        ),
        cost_estimate=pl.CostEstimate(flops=10**9, bytes_accessed=2 * 10**7, transcendentals=10**6),
    )(*args)


def body(activations, cotangent, spectral_weights, pointwise, channel_bias):
    inputs = activations[0]
    channels, xr, yr, zr = inputs.shape
    nx, ny = lax.axis_size("gx"), lax.axis_size("gy")
    xp = -(-xr // 16) * 16
    bz = trig_basis(zr)
    bx = trig_basis(xr * nx).reshape(MODES, nx, xr)
    bx = np.concatenate([bx, np.zeros((MODES, nx, xp - xr))], axis=2).reshape(MODES, nx * xp)
    by = trig_basis(yr * ny).reshape(MODES, ny, yr)
    kron = np.einsum("jgy,ik->giyjk", by, np.eye(channels)).reshape(
        ny, channels * yr, MODES * channels
    )
    bzh = halves(bz)
    kh = halves(kron)
    gy = lax.axis_index("gy")
    ky = lax.dynamic_index_in_dim(jnp.asarray(np.swapaxes(kh, 0, 1)), gy, 0, False)
    kyt = lax.dynamic_index_in_dim(
        jnp.asarray(np.ascontiguousarray(np.transpose(kh, (1, 0, 3, 2)))), gy, 0, False
    )
    tables = (
        jnp.asarray(bzh),
        jnp.asarray(np.concatenate([bzh[0], bzh[0], bzh[1]], axis=0)),
        ky,
        kyt,
        jnp.asarray(halves(np.concatenate([bx] * ny, axis=1))),
        jnp.asarray(halves(bx.T)),
    )
    weights = spectral_weights[0]
    mixing = pointwise[0]
    following = [from_behind(v, "segment", -1) for v in (inputs, mixing, channel_bias)]
    slope, input_modes, got = block_turn(
        False, nx, ny, 0, inputs, None, weights, mixing, channel_bias, tables
    )
    next_got = from_behind(got, "segment", -1)
    segment_index = lax.axis_index("segment")
    segment_count = lax.axis_size("segment")
    incoming = cotangent
    kept_grad = jnp.zeros(cotangent.shape, bf16)
    kept_modes = jnp.zeros(input_modes.shape, f32)
    for turn_index in range(segment_count):
        active = segment_index == segment_count - 1 - turn_index
        input_grad, grad_modes, got_back = block_turn(
            True, nx, ny, 1 + turn_index, incoming, slope, weights, mixing, None, tables
        )
        kept_grad = jnp.where(active, input_grad, kept_grad)
        kept_modes = jnp.where(active, grad_modes, kept_modes)
        if turn_index == 0 and segment_count > 1:
            next_back = from_behind(got_back, "segment", -1)
            incoming = ahead(
                following[0], cotangent, next_got, next_back, following[1], following[2],
                tables[1], tables[3],
            )
        elif turn_index + 1 < segment_count:
            incoming = from_behind(input_grad, "segment", -1)
    input_modes = jnp.swapaxes(input_modes, 0, 1)
    kept_modes = jnp.swapaxes(kept_modes, 0, 1)
    weight_grad = input_modes[:, :, :, None, :] * kept_modes[:, :, None, :, :]
    return (kept_grad[None], weight_grad[None])


def slope_of(value):
    cdf = 0.5 * (1.0 + lax.erf(value * 0.7071067811865476))
    return cdf + value * jnp.exp(-0.5 * value * value) * 0.3989422804014327


def field_of(cells, ny, ky, bzi):
    blocks = []
    for h in range(ny):
        block = cells(h)
        blocks.append(block.reshape(block.shape[0] * block.shape[1], block.shape[2]))
    block = jnp.concatenate(blocks, axis=1)
    top, rest = split(dot(ky[0], block, 1, 1) + dot(ky[1], block, 1, 1))
    return dot(jnp.concatenate([top, rest, top], axis=1), bzi[...])


def relay_kernel(
    nx, ny, xq, cuts,
    act_hbm, cot_hbm, w_hbm, mix_ref, bias_ref, mix_hbm, bias_hbm,
    kyt_hbm, ky_hbm, bzf_hbm, bzi_hbm, bx_hbm, sp_hbm,
    out, rest_ref, cells_ref, wgrad, ky, bzi,
    act, act1, cot, w, wd, kyt, bzf, bx, sp,
    u, v, slope, sig, in_modes, grad_modes, m_ref, mt_send, mt_recv,
    mixv1, biasv1, mix1, bias1, s_ref, p_ref, r_ref,
    load_sem, send_sem, recv_sem, row_send, row_recv, small_send, small_recv, store_sem,
    tail_send, tail_recv, pair_send, pair_recv,
):
    channels, xr, yr, zr = act.shape
    n = nx * ny
    cl, jl = MODES // nx, MODES // ny
    nh, hq = r_ref.shape[1], r_ref.shape[3]
    lanes = jl * channels
    rows = channels * yr
    tail = xr - hq * xq
    late = xr - xq
    gx, gy, seg = lax.axis_index("gx"), lax.axis_index("gy"), lax.axis_index("segment")
    me = gx * ny + gy
    mine = gy * nx + gx
    first, last = seg == 0, seg == 1
    mesh_ids = pl.DeviceIdType.MESH

    loads = [
        pltpu.make_async_copy(source, target, load_sem.at[k])
        for k, (source, target) in enumerate(
            [
                (act_hbm, act), (bzf_hbm, bzf), (kyt_hbm.at[gy], kyt), (w_hbm, w), (bx_hbm, bx),
                (sp_hbm, sp), (ky_hbm.at[gy], ky), (bzi_hbm, bzi), (cot_hbm, cot),
            ]
        )
    ]
    for load in loads[:3]:
        load.start()

    barrier = pltpu.get_barrier_semaphore()

    def greet(k, carry):
        other = lax.rem(seg * n + me + k, 2 * n)
        peer = lax.rem(other, n)
        pl.semaphore_signal(
            barrier, inc=1,
            device_id={"segment": other // n, "gx": peer // ny, "gy": lax.rem(peer, ny)},
            device_id_type=mesh_ids,
        )
        return carry

    lax.fori_loop(1, 2 * n, greet, 0)

    def ahead(source, target, send, recv):
        return pltpu.make_async_remote_copy(
            src_ref=source, dst_ref=target, send_sem=send, recv_sem=recv,
            device_id={"segment": 1 - seg}, device_id_type=mesh_ids,
        )

    def row_copy(x):
        return ahead(act_hbm.at[:, x], act1.at[:, x], row_send.at[x], row_recv.at[x])

    def send_rows(start, stop):
        for x in range(start, stop):
            row_copy(x).start()

    def modes_copy(k):
        return ahead(mt_send.at[k], mt_recv.at[k], small_send.at[k], small_recv.at[k])

    small = [
        ahead(mix_hbm, mixv1, small_send.at[2], small_recv.at[2]),
        ahead(bias_hbm, biasv1, small_send.at[3], small_recv.at[3]),
    ]

    def send(source, target, sends, receives):
        def begin(k, carry):
            peer = lax.rem(me + k, n)
            d, h = peer // ny, lax.rem(peer, ny)
            pltpu.make_async_remote_copy(
                src_ref=source(d, h), dst_ref=target, send_sem=sends, recv_sem=receives,
                device_id={"gx": d, "gy": h}, device_id_type=mesh_ids,
            ).start()
            return carry

        lax.fori_loop(1, n, begin, 0)
        target[...] = source(gx, gy)[...]

    def send_half(source, e, half):
        send(source, r_ref.at[e, half, mine], send_sem.at[e, half], recv_sem.at[e, half])

    def send_along(source, e, half):
        def begin(k, carry):
            d = lax.rem(gx + k, nx)
            pltpu.make_async_remote_copy(
                src_ref=source(d), dst_ref=r_ref.at[e, half, mine],
                send_sem=send_sem.at[e, half], recv_sem=recv_sem.at[e, half],
                device_id={"gx": d}, device_id_type=mesh_ids,
            ).start()
            return carry

        lax.fori_loop(1, nx, begin, 0)
        r_ref[e, half, mine] = source(gx)[...]

    def pair_copy(e, half):
        block = r_ref.at[e, half, pl.ds(gy * nx, nx)]
        return pltpu.make_async_remote_copy(
            src_ref=block, dst_ref=block,
            send_sem=pair_send.at[e, half], recv_sem=pair_recv.at[e, half],
            device_id={"gy": 1 - gy}, device_id_type=mesh_ids,
        )

    def forward(e, halves):
        for half in halves:
            await_block(r_ref.at[e, half, pl.ds(0, nx - 1)], recv_sem.at[e, half])
            pair_copy(e, half).start()

    def land(e, half):
        await_block(r_ref.at[e, half, pl.ds(0, nx)], pair_recv.at[e, half])

    def sent_along(e, half):
        await_block(r_ref.at[e, half, pl.ds(0, nx - 1)], send_sem.at[e, half])
        await_block(r_ref.at[e, half, pl.ds(0, nx)], pair_send.at[e, half])

    def send_tail(k, carry):
        peer = lax.rem(me + k, n)
        d, h = peer // ny, lax.rem(peer, ny)
        pltpu.make_async_remote_copy(
            src_ref=s_ref.at[2, nh - 1, h * nx + d], dst_ref=r_ref.at[4, nh - 1, mine],
            send_sem=tail_send.at[0], recv_sem=tail_recv.at[0],
            device_id={"segment": 0, "gx": d, "gy": h}, device_id_type=mesh_ids,
        ).start()
        return carry

    def await_block(block, sem):
        pltpu.make_async_copy(block, block, sem).wait()

    def arrive(e, half):
        await_block(r_ref.at[e, half, pl.ds(0, n - 1)], recv_sem.at[e, half])

    def sent(e, half):
        await_block(r_ref.at[e, half, pl.ds(0, n - 1)], send_sem.at[e, half])

    def to_modes(blocks, k, half):
        parts = []
        for block in blocks:
            g = dot(block, bzf[...])
            parts.append(g[:, : nx * 16] + g[:, nx * 16 :])
        top, rest = split(jnp.concatenate(parts, axis=1))
        t = dot(kyt[0], top) + dot(kyt[1], top) + dot(kyt[0], rest)
        t = t.T.astype(bf16)
        for q in range(len(blocks)):
            for h in range(ny):
                part = t[q * nx * 16 : (q + 1) * nx * 16, h * lanes : (h + 1) * lanes]
                s_ref[k, half, h * nx : (h + 1) * nx, q] = part.reshape(nx, 16, lanes)

    def to_field(e, half, q):
        return field_of(lambda h: r_ref[e, half, h * nx : (h + 1) * nx, q], ny, ky, bzi)

    def row(field, x):
        return field[:, x * zr : (x + 1) * zr].reshape(channels, yr, zr)

    def send_modes(k, e, half):
        send_half(lambda d, h: s_ref.at[k, half, h * nx + d], e, half)

    def own_modes(e, await_half):
        own = None
        for half in range(nh):
            await_half(half)
            block = r_ref[e, half].reshape(n * hq * 16, lanes)
            part = slice(half * n * hq * 16, (half + 1) * n * hq * 16)
            term = dot(bx[0, :, part], block) + dot(bx[1, :, part], block)
            own = term if own is None else own + term
        return own.T.reshape(jl, channels, cl * MODES)

    def send_cells(mt, k, e, halves):
        top, rest = split(mt)
        for half in halves:
            table = [sp[i, half].reshape(nx * hq * 16, cl * MODES) for i in range(2)]
            cells = dot(table[0], top) + dot(table[1], top) + dot(table[0], rest)
            p_ref[k, half] = cells.astype(bf16).reshape(nx, hq, 16, lanes)
            send_along(lambda d: p_ref.at[k, half, d], e, half)

    def mixed():
        return m_ref[...].reshape(lanes, cl * MODES).T

    def mix_back(e, await_half):
        grad_modes[...] = own_modes(e, await_half)

        def step(j, carry):
            m_ref[j] = jnp.sum(wd[j] * grad_modes[j][None], axis=1)
            return carry

        lax.fori_loop(0, jl, step, 0)

    def blend(mixing, values, o, back):
        total = (mixing[0, o] if back else mixing[o, 0]) * values[0]
        for i in range(1, channels):
            total = total + (mixing[i, o] if back else mixing[o, i]) * values[i]
        return total

    def fetch_small():
        for copy in small:
            copy.wait_recv()
        for k, (source, target) in enumerate([(mixv1, mix1), (biasv1, bias1)]):
            copy = pltpu.make_async_copy(source, target, store_sem.at[k])
            copy.start()
            copy.wait()

    def back_block(half, q, offset):
        field = to_field(3, half, q)
        x0 = (half * hq + q) * xq
        block = []
        for k in range(xq):
            incoming = (row(field, k) + offset[:, x0 + k]).astype(bf16).astype(f32)
            signal = incoming * slope[:, x0 + k]
            block.append((x0 + k, signal))
        return block

    def packed(block):
        return jnp.concatenate([s.astype(bf16).reshape(rows, zr) for _, s in block], axis=1)

    def blend_back(start, stop):
        def step(x, carry):
            values = [sig[i, x] for i in range(channels)]
            for o in range(channels):
                u[o, x] = blend(mix_ref, values, o, True)
            return carry

        lax.fori_loop(start, stop, step, 0)

    pl.semaphore_wait(barrier, 2 * n - 1)
    for copy in small:
        copy.start()

    @pl.when(last)
    def _():
        send_rows(0, cuts[0])

    @pl.when(first)
    def _():
        send_rows(tail, xr)

    for load in loads[:3]:
        load.wait()
    for load in loads[3:]:
        load.start()
    for half in range(nh):
        blocks = []
        for q in range(hq):
            x = (half * hq + q) * xq
            block = [act[:, x + k].reshape(rows, zr) for k in range(xq)]
            blocks.append(jnp.concatenate(block, axis=1))
        to_modes(blocks, 0, half)
        send_modes(0, 0, half)

    for load in loads[3:]:
        load.wait()

    def dense(j, carry):
        for i in range(channels):
            wd[j, i] = jnp.concatenate([w[j, c, i] for c in range(cl)], axis=1)
        return carry

    lax.fori_loop(0, jl, dense, 0)

    def pointwise(x, carry):
        values = [act[i, x].astype(f32) for i in range(channels)]
        for o in range(channels):
            u[o, x] = blend(mix_ref, values, o, False) + bias_ref[0, o]
        return carry

    lax.fori_loop(0, xr, pointwise, 0)

    in_modes[...] = own_modes(0, lambda half: arrive(0, half))

    def mix(j, carry):
        own = in_modes[j]
        m_ref[j] = jnp.sum(wd[j] * own[:, None, :], axis=0)
        return carry

    lax.fori_loop(0, jl, mix, 0)
    mt_send[0] = mixed()
    modes_copy(0).start()

    @pl.when(last)
    def _():
        send_rows(cuts[0], cuts[1])

    send_cells(mt_send[0], 0, 1, range(nh))

    @pl.when(last)
    def _():
        forward(1, range(nh))
        for half in range(nh):
            land(1, half)
            blocks = []
            for q in range(hq):
                field = to_field(1, half, q)
                x0 = (half * hq + q) * xq
                block = []
                for k in range(xq):
                    signal = cot[:, x0 + k].astype(f32) * slope_of(row(field, k) + u[:, x0 + k])
                    sig[:, x0 + k] = signal
                    block.append(signal.astype(bf16).reshape(rows, zr))
                blocks.append(jnp.concatenate(block, axis=1))
            to_modes(blocks, 1, half)
            send_modes(1, 2, half)

        modes_copy(0).wait_recv()
        send_cells(mt_recv[0], 3, 5, [nh - 1])
        fetch_small()

        mix_back(2, lambda half: arrive(2, half))
        mt_send[1] = mixed()
        modes_copy(1).start()
        send_rows(cuts[1], cuts[2])
        send_cells(mt_send[1], 1, 3, reversed(range(nh)))

        blend_back(0, xr)
        for x in range(tail, xr):
            row_copy(x).wait_recv()
        forward(5, [nh - 1])
        land(5, nh - 1)
        for q in range(hq):
            field = to_field(5, nh - 1, q)
            x0 = tail + q * xq
            for k in range(xq):
                values = [act1[i, x0 + k].astype(f32) for i in range(channels)]
                here = row(field, k)
                for o in range(channels):
                    pre = here[o] + blend(mix1, values, o, False) + bias1[0, o]
                    slope[o, x0 + k] = slope_of(pre)
        forward(3, reversed(range(nh)))
        land(3, nh - 1)
        to_modes([packed(back_block(nh - 1, q, u)) for q in range(hq)], 2, nh - 1)
        lax.fori_loop(0, n, send_tail, 0)
        send_rows(cuts[2], xr)

    def ahead_quarter(half, q):
        field = to_field(2, half, q)
        x0 = (half * hq + q) * xq
        for k in range(xq):
            row_copy(x0 + k).wait_recv()
            values = [act1[i, x0 + k].astype(f32) for i in range(channels)]
            here = row(field, k)
            signals = []
            for o in range(channels):
                pre = here[o] + blend(mix1, values, o, False) + bias1[0, o]
                signals.append(cot[o, x0 + k].astype(f32) * slope_of(pre))
            for i in range(channels):
                v[i, x0 + k] = blend(mix1, signals, i, True)

    def kept(block):
        for x, signal in block:
            sig[:, x] = signal
        return block

    @pl.when(first)
    def _():
        modes_copy(0).wait_recv()
        send_cells(mt_recv[0], 1, 2, range(nh))
        fetch_small()
        forward(1, range(nh))
        for half in range(nh):
            land(1, half)

            def step(q, carry):
                field = to_field(1, half, q)
                x0 = (half * hq + q) * xq
                for k in range(xq):
                    slope[:, x0 + k] = slope_of(row(field, k) + u[:, x0 + k])
                return carry

            lax.fori_loop(0, hq, step, 0)

        forward(2, range(nh))
        for half in range(nh):
            land(2, half)
        for half in range(nh - 1):
            for q in range(hq):
                ahead_quarter(half, q)
        modes_copy(1).wait_recv()
        send_cells(mt_recv[1], 2, 3, range(nh))
        forward(3, range(nh))
        for half in range(nh - 1):
            land(3, half)
            to_modes([packed(kept(back_block(half, q, v))) for q in range(hq)], 1, half)
            send_modes(1, 4, half)
        blend_back(0, tail)
        land(3, nh - 1)
        for q in range(hq - 1):
            ahead_quarter(nh - 1, q)
            kept(back_block(nh - 1, q, v))

        def await_half(half):
            if half < nh - 1:
                arrive(4, half)
            else:
                await_block(r_ref.at[4, half], tail_recv.at[0])

        mix_back(4, await_half)
        send_cells(mixed(), 3, 5, range(nh))
        if hq > 1:
            blend_back(tail, late)
        for target, e in ((v, 2), (u, 3)):
            field = to_field(e, nh - 1, hq - 1)
            for k in range(xq):
                target[:, late + k] = row(field, k)

    def weight_grad(j, carry):
        for c in range(cl):
            part = slice(c * MODES, (c + 1) * MODES)
            wgrad[j, c] = in_modes[j][:, None, part] * grad_modes[j][None, :, part]
        return carry

    lax.fori_loop(0, jl, weight_grad, 0)
    e = 3 + 2 * (1 - seg)

    @pl.when(last)
    def _():
        for half in range(nh - 1):
            land(3, half)

    @pl.when(first)
    def _():
        forward(5, range(nh))
        for half in range(nh - 1):
            land(5, half)

    for half in range(nh - 1):
        for q in range(hq):
            field = to_field(e, half, q)
            x0 = (half * hq + q) * xq
            for k in range(xq):
                out[:, x0 + k] = (row(field, k) + u[:, x0 + k]).astype(bf16)

    @pl.when(first)
    def _():
        land(5, nh - 1)
        rest_ref[:, : late - tail] = u[:, tail:late]

    cells_ref[...] = r_ref[e, nh - 1]

    @pl.when(first)
    def _():
        def step(k, carry):
            x = late + k
            row_copy(x).wait_recv()
            values = [act1[i, x].astype(f32) for i in range(channels)]
            signals = []
            for o in range(channels):
                pre = v[o, x] + blend(mix1, values, o, False) + bias1[0, o]
                signals.append(cot[o, x].astype(f32) * slope_of(pre))
            here = []
            for i in range(channels):
                incoming = u[i, x] + blend(mix1, signals, i, True)
                here.append(incoming.astype(bf16).astype(f32) * slope[i, x])
            for o in range(channels):
                rest_ref[o, late - tail + k] = blend(mix_ref, here, o, True)
            return carry

        lax.fori_loop(0, xq, step, 0)

    @pl.when(last)
    def _():
        rest_ref[...] = u[:, tail:]

    for half in range(nh):
        sent(0, half)
        sent_along(1, half)
        sent_along(3, half)
    for copy in small:
        copy.wait_send()
    modes_copy(0).wait_send()

    @pl.when(first)
    def _():
        for half in range(nh - 1):
            sent(4, half)
        for half in range(nh):
            sent_along(2, half)
            sent_along(5, half)
        for x in range(tail, xr):
            row_copy(x).wait_send()

    @pl.when(last)
    def _():
        for half in range(nh):
            sent(2, half)
        sent_along(5, nh - 1)
        modes_copy(1).wait_send()
        await_block(r_ref.at[4, nh - 1], tail_send.at[0])
        for x in range(xr):
            row_copy(x).wait_send()


def finish_kernel(
    nx, ny, xq, done_ref, rest_ref, cells_ref, wgrad, ky, bzi, grad_hbm, wgrad_hbm, out, sem
):
    channels, done, yr, zr = done_ref.shape
    hq = cells_ref.shape[1]
    stores = [
        pltpu.make_async_copy(wgrad, wgrad_hbm, sem.at[0]),
        pltpu.make_async_copy(done_ref, grad_hbm.at[:, pl.ds(0, done)], sem.at[1]),
    ]
    for store in stores:
        store.start()
    for q in range(hq):
        field = field_of(lambda h: cells_ref[h * nx : (h + 1) * nx, q], ny, ky, bzi)
        for k in range(xq):
            x = q * xq + k
            here = field[:, k * zr : (k + 1) * zr].reshape(channels, yr, zr)
            out[:, x] = (here + rest_ref[:, x]).astype(bf16)
        part = pl.ds(q * xq, xq)
        store = pltpu.make_async_copy(
            out.at[:, part], grad_hbm.at[:, pl.ds(done + q * xq, xq)], sem.at[2 + q]
        )
        store.start()
        stores.append(store)
    for store in stores:
        store.wait()


def in_hbm(value):
    return pltpu.with_memory_space_constraint(jnp.asarray(value), pltpu.HBM)


def two_section_body(activations, cotangent, spectral_weights, pointwise, channel_bias):
    inputs = activations[0]
    channels, xr, yr, zr = inputs.shape
    nx, ny = lax.axis_size("gx"), lax.axis_size("gy")
    n = nx * ny
    cl, jl = MODES // nx, MODES // ny
    xq = 16 // cl
    nh = 2
    hq = xr // (nh * xq)
    lanes, rows = jl * channels, channels * yr
    bz = trig_basis(zr).reshape(nx, cl, zr)
    eye_x, eye_c = np.eye(xq), np.eye(cl)
    bzf = np.einsum("dcz,xX->xzdXc", bz, eye_x).reshape(xq * zr, nx * 16)
    bzi = halves(bzf.reshape(xq, zr, nx * 16).transpose(2, 0, 1).reshape(nx * 16, xq * zr))
    by = trig_basis(yr * ny).reshape(MODES, ny, yr)
    ky = np.einsum("jgy,ik->giyjk", by, np.eye(channels)).reshape(ny, rows, ny * lanes)
    ky = halves(ky)
    bx = trig_basis(xr * nx).reshape(MODES, nx, nh, hq, xq)
    sp = np.einsum("adtqx,cC->tdqxCca", bx, eye_c).reshape(nh * nx * hq * 16, cl * MODES)
    bxf = np.broadcast_to(
        sp.reshape(nh, 1, nx * hq * 16, cl * MODES), (nh, ny, nx * hq * 16, cl * MODES)
    )
    bxf = bxf.reshape(nh * n * hq * 16, cl * MODES).T
    bzf = halves(bzf)
    tables = [
        np.ascontiguousarray(ky.transpose(1, 0, 3, 2)),
        np.ascontiguousarray(ky.transpose(1, 0, 2, 3)),
        np.concatenate([bzf[0], bzf[1]], axis=1),
        np.concatenate([bzi[0], bzi[0], bzi[1]], axis=0),
        halves(bxf),
        halves(sp).reshape(2, nh, nx, hq, 16, cl * MODES),
    ]
    weights, mixing = spectral_weights[0], pointwise[0]
    vmem = pl.BlockSpec(memory_space=pltpu.VMEM)
    smem = pl.BlockSpec(memory_space=pltpu.SMEM)
    hbm = pl.BlockSpec(memory_space=pl.ANY)
    dma = pltpu.SemaphoreType.DMA
    grid = inputs.shape
    done = grid[:1] + ((nh - 1) * hq * xq,) + grid[2:]
    left = grid[:1] + (hq * xq,) + grid[2:]
    scratch = [
        pltpu.VMEM(grid, bf16), pltpu.VMEM(grid, bf16), pltpu.VMEM(grid, bf16),
        pltpu.VMEM(weights.shape, f32),
        pltpu.VMEM((jl, channels, channels, cl * MODES), f32),
        pltpu.VMEM((2, ny * lanes, rows), bf16),
        pltpu.VMEM((xq * zr, 2 * nx * 16), bf16),
        pltpu.VMEM((2, cl * MODES, nh * n * hq * 16), bf16),
        pltpu.VMEM((2, nh, nx, hq, 16, cl * MODES), bf16),
        pltpu.VMEM(grid, f32), pltpu.VMEM(grid, f32), pltpu.VMEM(grid, f32), pltpu.VMEM(grid, f32),
        pltpu.VMEM((jl, channels, cl * MODES), f32),
        pltpu.VMEM((jl, channels, cl * MODES), f32),
        pltpu.VMEM((jl, channels, cl * MODES), f32),
        pltpu.VMEM((2, cl * MODES, lanes), f32),
        pltpu.VMEM((2, cl * MODES, lanes), f32),
        pltpu.VMEM(mixing.shape, f32), pltpu.VMEM(channel_bias.shape, f32),
        pltpu.SMEM(mixing.shape, f32), pltpu.SMEM(channel_bias.shape, f32),
        pltpu.VMEM((3, nh, n, hq, 16, lanes), bf16),
        pltpu.VMEM((4, nh, nx, hq, 16, lanes), bf16),
        pltpu.VMEM((6, nh, n, hq, 16, lanes), bf16),
        dma((9,)), dma((6, nh)), dma((6, nh)),
        dma((xr,)), dma((xr,)), dma((4,)), dma((4,)), dma((2,)), dma((1,)), dma((1,)), dma((6, nh)), dma((6, nh)),
    ]
    parts = pl.pallas_call(
        functools.partial(relay_kernel, nx, ny, xq, (3, 9, 12)),
        out_shape=(
            jax.ShapeDtypeStruct(done, bf16),
            jax.ShapeDtypeStruct(left, f32),
            jax.ShapeDtypeStruct((n, hq, 16, lanes), bf16),
            pltpu.VMEM(weights.shape, f32),
            jax.ShapeDtypeStruct((2, rows, ny * lanes), bf16),
            jax.ShapeDtypeStruct((3 * nx * 16, xq * zr), bf16),
        ),
        in_specs=[hbm, hbm, hbm, smem, smem] + [hbm] * (2 + len(tables)),
        out_specs=[vmem] * 6,
        scratch_shapes=scratch,
        compiler_params=pltpu.CompilerParams(
            collective_id=0, has_side_effects=True, vmem_limit_bytes=46 * 2**20
        ),
        cost_estimate=pl.CostEstimate(
            flops=4 * 10**9, bytes_accessed=2 * 10**7, transcendentals=10**7
        ),
    )(
        *[in_hbm(v) for v in (inputs, cotangent, weights)],
        mixing, channel_bias,
        *[in_hbm(v) for v in [mixing, channel_bias] + tables],
    )
    input_grad, weight_grad = pl.pallas_call(
        functools.partial(finish_kernel, nx, ny, xq),
        out_shape=(
            jax.ShapeDtypeStruct(grid, bf16),
            jax.ShapeDtypeStruct(weights.shape, f32),
        ),
        in_specs=[vmem] * 6,
        out_specs=(hbm, hbm),
        scratch_shapes=[pltpu.VMEM(left, bf16), dma((2 + hq,))],
        compiler_params=pltpu.CompilerParams(vmem_limit_bytes=24 * 2**20),
        cost_estimate=pl.CostEstimate(flops=10**9, bytes_accessed=10**7, transcendentals=0),
    )(*parts)
    return (input_grad[None], weight_grad[None])


def fits(mesh):
    nx = mesh.shape["gx"]
    return mesh.shape["segment"] == 2 and mesh.shape["gy"] == 2 and nx == 8


def solution(mesh):
    return jax.shard_map(
        two_section_body if fits(mesh) else body,
        mesh=mesh,
        in_specs=(
            P("segment", "groups", "gx", "gy", None),
            P("groups", "gx", "gy", None),
            P("segment", "gy", "gx", None, None, None),
            P("segment", None, None),
            P("segment", None),
        ),
        out_specs=(
            P("segment", "groups", "gx", "gy", None),
            P("segment", "gy", "gx", "groups", None, None),
        ),
        check_vma=False,
    )
```

```python
import functools
import math

import jax
import jax.numpy as jnp
import ml_dtypes
import numpy as np
from jax import lax
from jax.experimental import pallas as pl
from jax.experimental.pallas import tpu as pltpu
from jax.sharding import PartitionSpec as P

MODES = 32
f32, bf16 = jnp.float32, jnp.bfloat16


def from_behind(block, axis, distance):
    devices = range(lax.axis_size(axis))
    route = [(i - distance, i) for i in devices if i - distance in devices]
    return lax.ppermute(block, axis, route)


def trig_basis(length):
    half = MODES // 2
    freqs = np.arange(half)[:, None]
    points = np.arange(length)[None, :]
    step = 2.0 * math.pi / length
    rows = np.concatenate(
        [np.cos((freqs * points % length) * step), np.sin(((freqs + 1) * points % length) * step)]
    )
    scales = np.where(np.arange(MODES) == 0, 1.0 / math.sqrt(length), math.sqrt(2.0 / length))
    return rows * scales[:, None]


def halves(matrix):
    matrix = np.asarray(matrix, np.float32)
    top = matrix.astype(ml_dtypes.bfloat16)
    rest = (matrix - top.astype(np.float32)).astype(ml_dtypes.bfloat16)
    return np.stack([top, rest])


def split(value):
    top = value.astype(bf16)
    return top, (value - top.astype(f32)).astype(bf16)


def dot(a, b, ca=1, cb=0):
    return lax.dot_general(a, b, (((ca,), (cb,)), ((), ())), preferred_element_type=f32)


def kernel(
    back, nx, ny, xr, *refs
):
    if back:
        (inc_ref, slope_ref, w_hbm, mix_ref, bz_ref, bzs_ref, ky_ref, kyt_ref, bx_ref, bxr_ref,
         out_ref, modes_ref, got_ref, *scratch) = refs
    else:
        (inc_ref, w_hbm, mix_ref, bias_ref, bz_ref, bzs_ref, ky_ref, kyt_ref, bx_ref, bxr_ref,
         out_ref, modes_ref, got_ref, *scratch) = refs
    (w_ref, sig_ref, ghi_ref, glo_ref, s_ref, r_ref, m_ref, p_ref, q_ref, qs_ref,
     send1, recv1, send2, recv2, wsem) = scratch
    channels, _, yr, zr = inc_ref.shape
    cl, jl, xp = MODES // nx, MODES // ny, r_ref.shape[2]
    n = nx * ny
    lanes = jl * channels
    gx, gy = lax.axis_index("gx"), lax.axis_index("gy")
    me = gx * ny + gy

    wcopy = pltpu.make_async_copy(w_hbm, w_ref, wsem)
    wcopy.start()

    barrier = pltpu.get_barrier_semaphore()

    def greet(k, carry):
        peer = lax.rem(me + k, n)
        pl.semaphore_signal(
            barrier, inc=1,
            device_id={"gx": peer // ny, "gy": lax.rem(peer, ny)},
            device_id_type=pl.DeviceIdType.MESH,
        )
        return carry

    lax.fori_loop(1, n, greet, 0)

    def along_z(x, carry):
        if back:
            signal = inc_ref[:, x].astype(f32) * slope_ref[:, x]
            sig_ref[:, x] = signal
            block = signal.astype(bf16)
        else:
            block = inc_ref[:, x]
        block = block.reshape(channels * yr, zr)
        g = dot(bz_ref[0], block, 1, 1) + dot(bz_ref[1], block, 1, 1)
        ghi, glo = split(g)
        rows = pl.ds(pl.multiple_of(x * MODES, MODES), MODES)
        ghi_ref[rows, :] = ghi
        glo_ref[rows, :] = glo
        return carry

    lax.fori_loop(0, xr, along_z, 0)
    ghi = ghi_ref[...]
    t = dot(ghi, ky_ref[0]) + dot(ghi, ky_ref[1]) + dot(glo_ref[...], ky_ref[0])
    t = jnp.swapaxes(t.reshape(xr, MODES, ny * lanes), 0, 1)
    if xp > xr:
        t = jnp.concatenate([t, jnp.zeros((MODES, xp - xr, ny * lanes), f32)], axis=1)
    t = t.astype(bf16)
    for h in range(ny):
        s_ref[h] = t[:, :, h * lanes : (h + 1) * lanes].reshape(nx, cl, xp, lanes)

    pl.semaphore_wait(barrier, n - 1)

    def exchange(source, target, send, recv):
        def copy_to(peer, slot_of):
            return pltpu.make_async_remote_copy(
                src_ref=source(peer // ny, lax.rem(peer, ny)),
                dst_ref=target.at[lax.rem(slot_of, ny) * nx + slot_of // ny],
                send_sem=send.at[peer],
                recv_sem=recv.at[slot_of],
                device_id={"gx": peer // ny, "gy": lax.rem(peer, ny)},
                device_id_type=pl.DeviceIdType.MESH,
            )

        def begin(k, carry):
            copy_to(lax.rem(me + k, n), me).start()
            return carry

        def finish(k, carry):
            copy_to(lax.rem(me + k, n), me).wait_send()
            peer = lax.rem(me + n - k, n)
            copy_to(peer, peer).wait_recv()
            return carry

        lax.fori_loop(1, n, begin, 0)
        target[gy * nx + gx] = source(gx, gy)[...]
        lax.fori_loop(1, n, finish, 0)

    exchange(lambda d, h: s_ref.at[h, d], r_ref, send1, recv1)

    for c in range(cl):
        part = r_ref[:, c].reshape(n * xp, lanes)
        own = dot(bx_ref[0], part) + dot(bx_ref[1], part)
        modes_ref[c] = own.T.reshape(jl, channels, MODES)
    wcopy.wait()

    def mix(j, carry):
        for c in range(cl):
            own = modes_ref[c, j]
            weight = w_ref[j, c]
            if back:
                m_ref[c, j] = jnp.sum(weight * own[None], axis=1)
            else:
                m_ref[c, j] = jnp.sum(weight * own[:, None, :], axis=0)
        return carry

    lax.fori_loop(0, jl, mix, 0)
    for c in range(cl):
        top, rest = split(m_ref[c].reshape(lanes, MODES))
        spread = (
            dot(bxr_ref[0], top, 1, 1) + dot(bxr_ref[1], top, 1, 1) + dot(bxr_ref[0], rest, 1, 1)
        )
        p_ref[:, c] = spread.astype(bf16).reshape(nx, xp, lanes)

    exchange(lambda d, h: p_ref.at[d], q_ref, send2, recv2)

    got = [q_ref[h * nx : (h + 1) * nx].reshape(MODES, xp, lanes) for h in range(ny)]
    got = jnp.concatenate(got, axis=2).astype(f32)
    got = jnp.swapaxes(got, 0, 1)[:xr].reshape(xr * MODES, ny * lanes).astype(bf16)
    got_ref[...] = got
    qs_ref[...] = dot(got, kyt_ref[0]) + dot(got, kyt_ref[1])

    def finish_field(x, carry):
        rows = pl.ds(pl.multiple_of(x * MODES, MODES), MODES)
        top, rest = split(qs_ref[rows, :])
        stack = jnp.concatenate([top, rest, top], axis=0)
        field = dot(stack, bzs_ref[...], 0, 0).reshape(channels, yr, zr)
        if back:
            values = [sig_ref[i, x] for i in range(channels)]
        else:
            values = [inc_ref[i, x].astype(f32) for i in range(channels)]
        for o in range(channels):
            total = field[o]
            for i in range(channels):
                total = total + (mix_ref[i, o] if back else mix_ref[o, i]) * values[i]
            if back:
                out_ref[o, x] = total.astype(bf16)
            else:
                total = total + bias_ref[0, o]
                cdf = 0.5 * (1.0 + lax.erf(total * 0.7071067811865476))
                out_ref[o, x] = cdf + total * jnp.exp(-0.5 * total * total) * 0.3989422804014327
        return carry

    lax.fori_loop(0, xr, finish_field, 0)


def ahead_kernel(
    act_ref, cot_ref, got_ref, got_back_ref, mix_ref, bias_ref, bzs_ref, kyt_ref, out_ref,
    pre_ref, back_ref,
):
    channels, xr, yr, zr = act_ref.shape
    pre_ref[...] = dot(got_ref[...], kyt_ref[0]) + dot(got_ref[...], kyt_ref[1])
    back_ref[...] = dot(got_back_ref[...], kyt_ref[0]) + dot(got_back_ref[...], kyt_ref[1])

    def field_of(ref, x):
        rows = pl.ds(pl.multiple_of(x * MODES, MODES), MODES)
        top, rest = split(ref[rows, :])
        stack = jnp.concatenate([top, rest, top], axis=0)
        return dot(stack, bzs_ref[...], 0, 0).reshape(channels, yr, zr)

    def step(x, carry):
        field = field_of(pre_ref, x)
        values = [act_ref[i, x].astype(f32) for i in range(channels)]
        signals = []
        for o in range(channels):
            total = field[o]
            for i in range(channels):
                total = total + mix_ref[o, i] * values[i]
            total = total + bias_ref[0, o]
            cdf = 0.5 * (1.0 + lax.erf(total * 0.7071067811865476))
            slope = cdf + total * jnp.exp(-0.5 * total * total) * 0.3989422804014327
            signals.append(cot_ref[o, x].astype(f32) * slope)
        field = field_of(back_ref, x)
        for o in range(channels):
            total = field[o]
            for i in range(channels):
                total = total + mix_ref[i, o] * signals[i]
            out_ref[o, x] = total.astype(bf16)
        return carry

    lax.fori_loop(0, xr, step, 0)


def ahead(activations, cotangent, got, got_back, mixing, bias, bzs, kyt):
    channels, xr, yr, zr = activations.shape
    vmem = pl.BlockSpec(memory_space=pltpu.VMEM)
    smem = pl.BlockSpec(memory_space=pltpu.SMEM)
    return pl.pallas_call(
        ahead_kernel,
        out_shape=jax.ShapeDtypeStruct(activations.shape, bf16),
        in_specs=[vmem] * 4 + [smem] * 2 + [vmem] * 2,
        out_specs=vmem,
        scratch_shapes=[pltpu.VMEM((xr * MODES, channels * yr), f32)] * 2,
        compiler_params=pltpu.CompilerParams(vmem_limit_bytes=50 * 2**20),
        cost_estimate=pl.CostEstimate(flops=10**9, bytes_accessed=10**7, transcendentals=10**6),
    )(activations, cotangent, got, got_back, mixing, bias, bzs, kyt)


def block_turn(back, nx, ny, collective, field, slope, weights, mixing, bias, tables):
    channels, xr, yr, zr = field.shape
    xp = -(-xr // 16) * 16
    cl, jl, n = MODES // nx, MODES // ny, nx * ny
    lanes = jl * channels
    vmem = pl.BlockSpec(memory_space=pltpu.VMEM)
    smem = pl.BlockSpec(memory_space=pltpu.SMEM)
    hbm = pl.BlockSpec(memory_space=pl.ANY)
    if back:
        args = (field, slope, weights, mixing, *tables)
        specs = [vmem, vmem, hbm, smem] + [vmem] * len(tables)
    else:
        args = (field, weights, mixing, bias, *tables)
        specs = [vmem, hbm, smem, smem] + [vmem] * len(tables)
    dma = pltpu.SemaphoreType.DMA
    return pl.pallas_call(
        functools.partial(kernel, back, nx, ny, xr),
        out_shape=(
            jax.ShapeDtypeStruct(field.shape, bf16 if back else f32),
            jax.ShapeDtypeStruct((cl, jl, channels, MODES), f32),
            jax.ShapeDtypeStruct((xr * MODES, ny * lanes), bf16),
        ),
        in_specs=specs,
        out_specs=(vmem, vmem, vmem),
        scratch_shapes=[
            pltpu.VMEM(weights.shape, f32),
            pltpu.VMEM(field.shape if back else (8, 128), f32),
            pltpu.VMEM((xr * MODES, channels * yr), bf16),
            pltpu.VMEM((xr * MODES, channels * yr), bf16),
            pltpu.VMEM((ny, nx, cl, xp, lanes), bf16),
            pltpu.VMEM((n, cl, xp, lanes), bf16),
            pltpu.VMEM((cl, jl, channels, MODES), f32),
            pltpu.VMEM((nx, cl, xp, lanes), bf16),
            pltpu.VMEM((n, cl, xp, lanes), bf16),
            pltpu.VMEM((xr * MODES, channels * yr), f32),
            dma((n,)), dma((n,)), dma((n,)), dma((n,)), dma,
        ],
        compiler_params=pltpu.CompilerParams(
            collective_id=collective, has_side_effects=True, vmem_limit_bytes=50 * 2**20
        ),
        cost_estimate=pl.CostEstimate(flops=10**9, bytes_accessed=2 * 10**7, transcendentals=10**6),
    )(*args)


def body(activations, cotangent, spectral_weights, pointwise, channel_bias):
    inputs = activations[0]
    channels, xr, yr, zr = inputs.shape
    nx, ny = lax.axis_size("gx"), lax.axis_size("gy")
    xp = -(-xr // 16) * 16
    bz = trig_basis(zr)
    bx = trig_basis(xr * nx).reshape(MODES, nx, xr)
    bx = np.concatenate([bx, np.zeros((MODES, nx, xp - xr))], axis=2).reshape(MODES, nx * xp)
    by = trig_basis(yr * ny).reshape(MODES, ny, yr)
    kron = np.einsum("jgy,ik->giyjk", by, np.eye(channels)).reshape(
        ny, channels * yr, MODES * channels
    )
    bzh = halves(bz)
    kh = halves(kron)
    gy = lax.axis_index("gy")
    ky = lax.dynamic_index_in_dim(jnp.asarray(np.swapaxes(kh, 0, 1)), gy, 0, False)
    kyt = lax.dynamic_index_in_dim(
        jnp.asarray(np.ascontiguousarray(np.transpose(kh, (1, 0, 3, 2)))), gy, 0, False
    )
    tables = (
        jnp.asarray(bzh),
        jnp.asarray(np.concatenate([bzh[0], bzh[0], bzh[1]], axis=0)),
        ky,
        kyt,
        jnp.asarray(halves(np.concatenate([bx] * ny, axis=1))),
        jnp.asarray(halves(bx.T)),
    )
    weights = spectral_weights[0]
    mixing = pointwise[0]
    following = [from_behind(v, "segment", -1) for v in (inputs, mixing, channel_bias)]
    slope, input_modes, got = block_turn(
        False, nx, ny, 0, inputs, None, weights, mixing, channel_bias, tables
    )
    next_got = from_behind(got, "segment", -1)
    segment_index = lax.axis_index("segment")
    segment_count = lax.axis_size("segment")
    incoming = cotangent
    kept_grad = jnp.zeros(cotangent.shape, bf16)
    kept_modes = jnp.zeros(input_modes.shape, f32)
    for turn_index in range(segment_count):
        active = segment_index == segment_count - 1 - turn_index
        input_grad, grad_modes, got_back = block_turn(
            True, nx, ny, 1 + turn_index, incoming, slope, weights, mixing, None, tables
        )
        kept_grad = jnp.where(active, input_grad, kept_grad)
        kept_modes = jnp.where(active, grad_modes, kept_modes)
        if turn_index == 0 and segment_count > 1:
            next_back = from_behind(got_back, "segment", -1)
            incoming = ahead(
                following[0], cotangent, next_got, next_back, following[1], following[2],
                tables[1], tables[3],
            )
        elif turn_index + 1 < segment_count:
            incoming = from_behind(input_grad, "segment", -1)
    input_modes = jnp.swapaxes(input_modes, 0, 1)
    kept_modes = jnp.swapaxes(kept_modes, 0, 1)
    weight_grad = input_modes[:, :, :, None, :] * kept_modes[:, :, None, :, :]
    return (kept_grad[None], weight_grad[None])


def slope_of(value):
    cdf = 0.5 * (1.0 + lax.erf(value * 0.7071067811865476))
    return cdf + value * jnp.exp(-0.5 * value * value) * 0.3989422804014327


def field_of(cells, ny, ky, bzi):
    blocks = []
    for h in range(ny):
        block = cells(h)
        blocks.append(block.reshape(block.shape[0] * block.shape[1], block.shape[2]))
    block = jnp.concatenate(blocks, axis=1)
    top, rest = split(dot(ky[0], block, 1, 1) + dot(ky[1], block, 1, 1))
    return dot(jnp.concatenate([top, rest, top], axis=1), bzi[...])


def relay_kernel(
    nx, ny, xq, cuts,
    act_hbm, cot_hbm, w_hbm, mix_ref, bias_ref, mix_hbm, bias_hbm,
    kyt_hbm, ky_hbm, bzf_hbm, bzi_hbm, bx_hbm, sp_hbm,
    out, rest_ref, cells_ref, wgrad, ky, bzi,
    act, act1, cot, w, wd, kyt, bzf, bx, sp,
    u, v, slope, sig, in_modes, grad_modes, m_ref, mt_send, mt_recv,
    mixv1, biasv1, mix1, bias1, s_ref, p_ref, r_ref,
    load_sem, send_sem, recv_sem, row_send, row_recv, small_send, small_recv, store_sem,
    tail_send, tail_recv, pair_send, pair_recv, across_send,
):
    channels, xr, yr, zr = act.shape
    n = nx * ny
    cl, jl = MODES // nx, MODES // ny
    nh, hq = r_ref.shape[1], r_ref.shape[3]
    lanes = jl * channels
    rows = channels * yr
    tail = xr - hq * xq
    late = xr - xq
    gx, gy, seg = lax.axis_index("gx"), lax.axis_index("gy"), lax.axis_index("segment")
    me = gx * ny + gy
    mine = gy * nx + gx
    first, last = seg == 0, seg == 1
    mesh_ids = pl.DeviceIdType.MESH

    loads = [
        pltpu.make_async_copy(source, target, load_sem.at[k])
        for k, (source, target) in enumerate(
            [
                (act_hbm, act), (bzf_hbm, bzf), (kyt_hbm.at[gy], kyt), (w_hbm, w), (bx_hbm, bx),
                (sp_hbm, sp), (ky_hbm.at[gy], ky), (bzi_hbm, bzi), (cot_hbm, cot),
            ]
        )
    ]
    for load in loads[:3]:
        load.start()

    barrier = pltpu.get_barrier_semaphore()

    def greet(k, carry):
        other = lax.rem(seg * n + me + k, 2 * n)
        peer = lax.rem(other, n)
        pl.semaphore_signal(
            barrier, inc=1,
            device_id={"segment": other // n, "gx": peer // ny, "gy": lax.rem(peer, ny)},
            device_id_type=mesh_ids,
        )
        return carry

    lax.fori_loop(1, 2 * n, greet, 0)

    def ahead(source, target, send, recv):
        return pltpu.make_async_remote_copy(
            src_ref=source, dst_ref=target, send_sem=send, recv_sem=recv,
            device_id={"segment": 1 - seg}, device_id_type=mesh_ids,
        )

    def row_copy(x):
        return ahead(act_hbm.at[:, x], act1.at[:, x], row_send.at[x], row_recv.at[x])

    def send_rows(start, stop):
        for x in range(start, stop):
            row_copy(x).start()

    def modes_copy(k):
        return ahead(mt_send.at[k], mt_recv.at[k], small_send.at[k], small_recv.at[k])

    small = [
        ahead(mix_hbm, mixv1, small_send.at[2], small_recv.at[2]),
        ahead(bias_hbm, biasv1, small_send.at[3], small_recv.at[3]),
    ]

    def send(source, target, sends, receives):
        def begin(k, carry):
            peer = lax.rem(me + k, n)
            d, h = peer // ny, lax.rem(peer, ny)
            pltpu.make_async_remote_copy(
                src_ref=source(d, h), dst_ref=target, send_sem=sends, recv_sem=receives,
                device_id={"gx": d, "gy": h}, device_id_type=mesh_ids,
            ).start()
            return carry

        lax.fori_loop(1, n, begin, 0)
        target[...] = source(gx, gy)[...]

    def send_half(source, e, half):
        send(source, r_ref.at[e, half, mine], send_sem.at[e, half], recv_sem.at[e, half])

    def send_along(source, e, half):
        def begin(k, carry):
            d = lax.rem(gx + k, nx)
            pltpu.make_async_remote_copy(
                src_ref=source(d), dst_ref=r_ref.at[e, half, mine],
                send_sem=send_sem.at[e, half], recv_sem=recv_sem.at[e, half],
                device_id={"gx": d}, device_id_type=mesh_ids,
            ).start()
            return carry

        lax.fori_loop(1, nx, begin, 0)
        r_ref[e, half, mine] = source(gx)[...]

    def send_across(half):
        def begin(k, carry):
            d = lax.rem(gx + k, nx)
            pltpu.make_async_remote_copy(
                src_ref=p_ref.at[1, half, d], dst_ref=r_ref.at[3, half, mine],
                send_sem=across_send.at[half], recv_sem=recv_sem.at[3, half],
                device_id={"segment": 0, "gx": d}, device_id_type=mesh_ids,
            ).start()
            return carry

        lax.fori_loop(0, nx, begin, 0)

    def pair_copy(e, half):
        block = r_ref.at[e, half, pl.ds(gy * nx, nx)]
        return pltpu.make_async_remote_copy(
            src_ref=block, dst_ref=block,
            send_sem=pair_send.at[e, half], recv_sem=pair_recv.at[e, half],
            device_id={"gy": 1 - gy}, device_id_type=mesh_ids,
        )

    def forward(e, halves):
        for half in halves:
            await_block(r_ref.at[e, half, pl.ds(0, nx - 1)], recv_sem.at[e, half])
            pair_copy(e, half).start()

    def forward_across(half):
        await_block(r_ref.at[3, half, pl.ds(0, nx)], recv_sem.at[3, half])
        pair_copy(3, half).start()

    def land(e, half):
        await_block(r_ref.at[e, half, pl.ds(0, nx)], pair_recv.at[e, half])

    def sent_along(e, half):
        await_block(r_ref.at[e, half, pl.ds(0, nx - 1)], send_sem.at[e, half])
        await_block(r_ref.at[e, half, pl.ds(0, nx)], pair_send.at[e, half])

    def send_tail(k, carry):
        peer = lax.rem(me + k, n)
        d, h = peer // ny, lax.rem(peer, ny)
        pltpu.make_async_remote_copy(
            src_ref=s_ref.at[2, nh - 1, h * nx + d], dst_ref=r_ref.at[4, nh - 1, mine],
            send_sem=tail_send.at[0], recv_sem=tail_recv.at[0],
            device_id={"segment": 0, "gx": d, "gy": h}, device_id_type=mesh_ids,
        ).start()
        return carry

    def await_block(block, sem):
        pltpu.make_async_copy(block, block, sem).wait()

    def arrive(e, half):
        await_block(r_ref.at[e, half, pl.ds(0, n - 1)], recv_sem.at[e, half])

    def sent(e, half):
        await_block(r_ref.at[e, half, pl.ds(0, n - 1)], send_sem.at[e, half])

    def to_modes(blocks, k, half):
        parts = []
        for block in blocks:
            g = dot(block, bzf[...])
            parts.append(g[:, : nx * 16] + g[:, nx * 16 :])
        top, rest = split(jnp.concatenate(parts, axis=1))
        t = dot(kyt[0], top) + dot(kyt[1], top) + dot(kyt[0], rest)
        t = t.T.astype(bf16)
        for q in range(len(blocks)):
            for h in range(ny):
                part = t[q * nx * 16 : (q + 1) * nx * 16, h * lanes : (h + 1) * lanes]
                s_ref[k, half, h * nx : (h + 1) * nx, q] = part.reshape(nx, 16, lanes)

    def to_field(e, half, q):
        return field_of(lambda h: r_ref[e, half, h * nx : (h + 1) * nx, q], ny, ky, bzi)

    def row(field, x):
        return field[:, x * zr : (x + 1) * zr].reshape(channels, yr, zr)

    def send_modes(k, e, half):
        send_half(lambda d, h: s_ref.at[k, half, h * nx + d], e, half)

    def own_modes(e, await_half):
        own = None
        for half in range(nh):
            await_half(half)
            block = r_ref[e, half].reshape(n * hq * 16, lanes)
            part = slice(half * n * hq * 16, (half + 1) * n * hq * 16)
            term = dot(bx[0, :, part], block) + dot(bx[1, :, part], block)
            own = term if own is None else own + term
        return own.T.reshape(jl, channels, cl * MODES)

    def spread(mt, k, half):
        top, rest = split(mt)
        table = [sp[i, half].reshape(nx * hq * 16, cl * MODES) for i in range(2)]
        cells = dot(table[0], top) + dot(table[1], top) + dot(table[0], rest)
        p_ref[k, half] = cells.astype(bf16).reshape(nx, hq, 16, lanes)

    def send_spread(k, e, half):
        send_along(lambda d: p_ref.at[k, half, d], e, half)

    def send_cells(mt, k, e, halves):
        for half in halves:
            spread(mt, k, half)
            send_spread(k, e, half)

    def mixed():
        return m_ref[...].reshape(lanes, cl * MODES).T

    def mix_back(e, await_half):
        grad_modes[...] = own_modes(e, await_half)

        def step(j, carry):
            m_ref[j] = jnp.sum(wd[j] * grad_modes[j][None], axis=1)
            return carry

        lax.fori_loop(0, jl, step, 0)

    def blend(mixing, values, o, back):
        total = (mixing[0, o] if back else mixing[o, 0]) * values[0]
        for i in range(1, channels):
            total = total + (mixing[i, o] if back else mixing[o, i]) * values[i]
        return total

    def fetch_small():
        for copy in small:
            copy.wait_recv()
        for k, (source, target) in enumerate([(mixv1, mix1), (biasv1, bias1)]):
            copy = pltpu.make_async_copy(source, target, store_sem.at[k])
            copy.start()
            copy.wait()

    def back_block(half, q, offset):
        field = to_field(3, half, q)
        x0 = (half * hq + q) * xq
        block = []
        for k in range(xq):
            incoming = (row(field, k) + offset[:, x0 + k]).astype(bf16).astype(f32)
            signal = incoming * slope[:, x0 + k]
            block.append((x0 + k, signal))
        return block

    def packed(block):
        return jnp.concatenate([s.astype(bf16).reshape(rows, zr) for _, s in block], axis=1)

    def blend_back(start, stop):
        def step(x, carry):
            values = [sig[i, x] for i in range(channels)]
            for o in range(channels):
                u[o, x] = blend(mix_ref, values, o, True)
            return carry

        lax.fori_loop(start, stop, step, 0)

    pl.semaphore_wait(barrier, 2 * n - 1)
    for copy in small:
        copy.start()

    @pl.when(last)
    def _():
        send_rows(0, cuts[0])

    @pl.when(first)
    def _():
        send_rows(tail, xr)

    for load in loads[:3]:
        load.wait()
    for load in loads[3:]:
        load.start()
    for half in range(nh):
        blocks = []
        for q in range(hq):
            x = (half * hq + q) * xq
            block = [act[:, x + k].reshape(rows, zr) for k in range(xq)]
            blocks.append(jnp.concatenate(block, axis=1))
        to_modes(blocks, 0, half)
        send_modes(0, 0, half)

    for load in loads[3:]:
        load.wait()

    def dense(j, carry):
        for i in range(channels):
            wd[j, i] = jnp.concatenate([w[j, c, i] for c in range(cl)], axis=1)
        return carry

    lax.fori_loop(0, jl, dense, 0)

    def pointwise(x, carry):
        values = [act[i, x].astype(f32) for i in range(channels)]
        for o in range(channels):
            u[o, x] = blend(mix_ref, values, o, False) + bias_ref[0, o]
        return carry

    lax.fori_loop(0, xr, pointwise, 0)

    in_modes[...] = own_modes(0, lambda half: arrive(0, half))

    def mix(j, carry):
        own = in_modes[j]
        m_ref[j] = jnp.sum(wd[j] * own[:, None, :], axis=0)
        return carry

    lax.fori_loop(0, jl, mix, 0)
    mt_send[0] = mixed()
    modes_copy(0).start()

    @pl.when(last)
    def _():
        send_rows(cuts[0], cuts[1])

    send_cells(mt_send[0], 0, 1, range(nh))

    @pl.when(last)
    def _():
        forward(1, range(nh))
        for half in range(nh):
            land(1, half)
            blocks = []
            for q in range(hq):
                field = to_field(1, half, q)
                x0 = (half * hq + q) * xq
                block = []
                for k in range(xq):
                    signal = cot[:, x0 + k].astype(f32) * slope_of(row(field, k) + u[:, x0 + k])
                    sig[:, x0 + k] = signal
                    block.append(signal.astype(bf16).reshape(rows, zr))
                blocks.append(jnp.concatenate(block, axis=1))
            to_modes(blocks, 1, half)
            send_modes(1, 2, half)

        modes_copy(0).wait_recv()
        send_cells(mt_recv[0], 3, 5, [nh - 1])
        fetch_small()

        mix_back(2, lambda half: arrive(2, half))
        mt_send[1] = mixed()
        for half in range(nh - 1):
            spread(mt_send[1], 1, half)
            send_across(half)
        send_rows(cuts[1], cuts[2])
        spread(mt_send[1], 1, nh - 1)
        for half in reversed(range(nh)):
            send_spread(1, 3, half)

        blend_back(0, xr)
        for x in range(tail, xr):
            row_copy(x).wait_recv()
        forward(5, [nh - 1])
        land(5, nh - 1)
        for q in range(hq):
            field = to_field(5, nh - 1, q)
            x0 = tail + q * xq
            for k in range(xq):
                values = [act1[i, x0 + k].astype(f32) for i in range(channels)]
                here = row(field, k)
                for o in range(channels):
                    pre = here[o] + blend(mix1, values, o, False) + bias1[0, o]
                    slope[o, x0 + k] = slope_of(pre)
        forward(3, reversed(range(nh)))
        land(3, nh - 1)
        to_modes([packed(back_block(nh - 1, q, u)) for q in range(hq)], 2, nh - 1)
        lax.fori_loop(0, n, send_tail, 0)
        send_across(nh - 1)
        send_rows(cuts[2], xr)

    def ahead_quarter(half, q):
        field = to_field(2, half, q)
        x0 = (half * hq + q) * xq
        for k in range(xq):
            row_copy(x0 + k).wait_recv()
            values = [act1[i, x0 + k].astype(f32) for i in range(channels)]
            here = row(field, k)
            signals = []
            for o in range(channels):
                pre = here[o] + blend(mix1, values, o, False) + bias1[0, o]
                signals.append(cot[o, x0 + k].astype(f32) * slope_of(pre))
            for i in range(channels):
                v[i, x0 + k] = blend(mix1, signals, i, True)

    def kept(block):
        for x, signal in block:
            sig[:, x] = signal
        return block

    @pl.when(first)
    def _():
        modes_copy(0).wait_recv()
        send_cells(mt_recv[0], 1, 2, range(nh))
        fetch_small()
        forward(1, range(nh))
        for half in range(nh):
            land(1, half)

            def step(q, carry):
                field = to_field(1, half, q)
                x0 = (half * hq + q) * xq
                for k in range(xq):
                    slope[:, x0 + k] = slope_of(row(field, k) + u[:, x0 + k])
                return carry

            lax.fori_loop(0, hq, step, 0)

        forward(2, range(nh))
        for half in range(nh):
            land(2, half)
        for half in range(nh - 1):
            for q in range(hq):
                ahead_quarter(half, q)
        for half in range(nh - 1):
            forward_across(half)
            land(3, half)
            to_modes([packed(kept(back_block(half, q, v))) for q in range(hq)], 1, half)
            send_modes(1, 4, half)
        blend_back(0, tail)
        for q in range(hq - 1):
            ahead_quarter(nh - 1, q)

        def await_half(half):
            if half < nh - 1:
                arrive(4, half)
            else:
                await_block(r_ref.at[4, half], tail_recv.at[0])

        mix_back(4, await_half)
        send_cells(mixed(), 3, 5, range(nh))
        forward_across(nh - 1)
        land(3, nh - 1)
        for q in range(hq - 1):
            kept(back_block(nh - 1, q, v))
        if hq > 1:
            blend_back(tail, late)
        for target, e in ((v, 2), (u, 3)):
            field = to_field(e, nh - 1, hq - 1)
            for k in range(xq):
                target[:, late + k] = row(field, k)

    def weight_grad(j, carry):
        for c in range(cl):
            part = slice(c * MODES, (c + 1) * MODES)
            wgrad[j, c] = in_modes[j][:, None, part] * grad_modes[j][None, :, part]
        return carry

    lax.fori_loop(0, jl, weight_grad, 0)
    e = 3 + 2 * (1 - seg)

    @pl.when(last)
    def _():
        for half in range(nh - 1):
            land(3, half)

    @pl.when(first)
    def _():
        forward(5, range(nh))
        for half in range(nh - 1):
            land(5, half)

    for half in range(nh - 1):
        for q in range(hq):
            field = to_field(e, half, q)
            x0 = (half * hq + q) * xq
            for k in range(xq):
                out[:, x0 + k] = (row(field, k) + u[:, x0 + k]).astype(bf16)

    @pl.when(first)
    def _():
        land(5, nh - 1)
        rest_ref[:, : late - tail] = u[:, tail:late]

    cells_ref[...] = r_ref[e, nh - 1]

    @pl.when(first)
    def _():
        def step(k, carry):
            x = late + k
            row_copy(x).wait_recv()
            values = [act1[i, x].astype(f32) for i in range(channels)]
            signals = []
            for o in range(channels):
                pre = v[o, x] + blend(mix1, values, o, False) + bias1[0, o]
                signals.append(cot[o, x].astype(f32) * slope_of(pre))
            here = []
            for i in range(channels):
                incoming = u[i, x] + blend(mix1, signals, i, True)
                here.append(incoming.astype(bf16).astype(f32) * slope[i, x])
            for o in range(channels):
                rest_ref[o, late - tail + k] = blend(mix_ref, here, o, True)
            return carry

        lax.fori_loop(0, xq, step, 0)

    @pl.when(last)
    def _():
        rest_ref[...] = u[:, tail:]

    for half in range(nh):
        sent(0, half)
        sent_along(1, half)
        await_block(r_ref.at[3, half, pl.ds(0, nx)], pair_send.at[3, half])
    for copy in small:
        copy.wait_send()
    modes_copy(0).wait_send()

    @pl.when(first)
    def _():
        for half in range(nh - 1):
            sent(4, half)
        for half in range(nh):
            sent_along(2, half)
            sent_along(5, half)
        for x in range(tail, xr):
            row_copy(x).wait_send()

    @pl.when(last)
    def _():
        for half in range(nh):
            sent(2, half)
            await_block(r_ref.at[3, half, pl.ds(0, nx - 1)], send_sem.at[3, half])
            await_block(r_ref.at[3, half, pl.ds(0, nx)], across_send.at[half])
        sent_along(5, nh - 1)
        await_block(r_ref.at[4, nh - 1], tail_send.at[0])
        for x in range(xr):
            row_copy(x).wait_send()


def finish_kernel(
    nx, ny, xq, done_ref, rest_ref, cells_ref, wgrad, ky, bzi, grad_hbm, wgrad_hbm, out, sem
):
    channels, done, yr, zr = done_ref.shape
    hq = cells_ref.shape[1]
    stores = [
        pltpu.make_async_copy(wgrad, wgrad_hbm, sem.at[0]),
        pltpu.make_async_copy(done_ref, grad_hbm.at[:, pl.ds(0, done)], sem.at[1]),
    ]
    for store in stores:
        store.start()
    for q in range(hq):
        field = field_of(lambda h: cells_ref[h * nx : (h + 1) * nx, q], ny, ky, bzi)
        for k in range(xq):
            x = q * xq + k
            here = field[:, k * zr : (k + 1) * zr].reshape(channels, yr, zr)
            out[:, x] = (here + rest_ref[:, x]).astype(bf16)
        part = pl.ds(q * xq, xq)
        store = pltpu.make_async_copy(
            out.at[:, part], grad_hbm.at[:, pl.ds(done + q * xq, xq)], sem.at[2 + q]
        )
        store.start()
        stores.append(store)
    for store in stores:
        store.wait()


def in_hbm(value):
    return pltpu.with_memory_space_constraint(jnp.asarray(value), pltpu.HBM)


def two_section_body(activations, cotangent, spectral_weights, pointwise, channel_bias):
    inputs = activations[0]
    channels, xr, yr, zr = inputs.shape
    nx, ny = lax.axis_size("gx"), lax.axis_size("gy")
    n = nx * ny
    cl, jl = MODES // nx, MODES // ny
    xq = 16 // cl
    nh = 2
    hq = xr // (nh * xq)
    lanes, rows = jl * channels, channels * yr
    bz = trig_basis(zr).reshape(nx, cl, zr)
    eye_x, eye_c = np.eye(xq), np.eye(cl)
    bzf = np.einsum("dcz,xX->xzdXc", bz, eye_x).reshape(xq * zr, nx * 16)
    bzi = halves(bzf.reshape(xq, zr, nx * 16).transpose(2, 0, 1).reshape(nx * 16, xq * zr))
    by = trig_basis(yr * ny).reshape(MODES, ny, yr)
    ky = np.einsum("jgy,ik->giyjk", by, np.eye(channels)).reshape(ny, rows, ny * lanes)
    ky = halves(ky)
    bx = trig_basis(xr * nx).reshape(MODES, nx, nh, hq, xq)
    sp = np.einsum("adtqx,cC->tdqxCca", bx, eye_c).reshape(nh * nx * hq * 16, cl * MODES)
    bxf = np.broadcast_to(
        sp.reshape(nh, 1, nx * hq * 16, cl * MODES), (nh, ny, nx * hq * 16, cl * MODES)
    )
    bxf = bxf.reshape(nh * n * hq * 16, cl * MODES).T
    bzf = halves(bzf)
    tables = [
        np.ascontiguousarray(ky.transpose(1, 0, 3, 2)),
        np.ascontiguousarray(ky.transpose(1, 0, 2, 3)),
        np.concatenate([bzf[0], bzf[1]], axis=1),
        np.concatenate([bzi[0], bzi[0], bzi[1]], axis=0),
        halves(bxf),
        halves(sp).reshape(2, nh, nx, hq, 16, cl * MODES),
    ]
    weights, mixing = spectral_weights[0], pointwise[0]
    vmem = pl.BlockSpec(memory_space=pltpu.VMEM)
    smem = pl.BlockSpec(memory_space=pltpu.SMEM)
    hbm = pl.BlockSpec(memory_space=pl.ANY)
    dma = pltpu.SemaphoreType.DMA
    grid = inputs.shape
    done = grid[:1] + ((nh - 1) * hq * xq,) + grid[2:]
    left = grid[:1] + (hq * xq,) + grid[2:]
    scratch = [
        pltpu.VMEM(grid, bf16), pltpu.VMEM(grid, bf16), pltpu.VMEM(grid, bf16),
        pltpu.VMEM(weights.shape, f32),
        pltpu.VMEM((jl, channels, channels, cl * MODES), f32),
        pltpu.VMEM((2, ny * lanes, rows), bf16),
        pltpu.VMEM((xq * zr, 2 * nx * 16), bf16),
        pltpu.VMEM((2, cl * MODES, nh * n * hq * 16), bf16),
        pltpu.VMEM((2, nh, nx, hq, 16, cl * MODES), bf16),
        pltpu.VMEM(grid, f32), pltpu.VMEM(grid, f32), pltpu.VMEM(grid, f32), pltpu.VMEM(grid, f32),
        pltpu.VMEM((jl, channels, cl * MODES), f32),
        pltpu.VMEM((jl, channels, cl * MODES), f32),
        pltpu.VMEM((jl, channels, cl * MODES), f32),
        pltpu.VMEM((2, cl * MODES, lanes), f32),
        pltpu.VMEM((2, cl * MODES, lanes), f32),
        pltpu.VMEM(mixing.shape, f32), pltpu.VMEM(channel_bias.shape, f32),
        pltpu.SMEM(mixing.shape, f32), pltpu.SMEM(channel_bias.shape, f32),
        pltpu.VMEM((3, nh, n, hq, 16, lanes), bf16),
        pltpu.VMEM((4, nh, nx, hq, 16, lanes), bf16),
        pltpu.VMEM((6, nh, n, hq, 16, lanes), bf16),
        dma((9,)), dma((6, nh)), dma((6, nh)),
        dma((xr,)), dma((xr,)), dma((4,)), dma((4,)), dma((2,)), dma((1,)), dma((1,)), dma((6, nh)), dma((6, nh)), dma((nh,)),
    ]
    parts = pl.pallas_call(
        functools.partial(relay_kernel, nx, ny, xq, (3, 9, 12)),
        out_shape=(
            jax.ShapeDtypeStruct(done, bf16),
            jax.ShapeDtypeStruct(left, f32),
            jax.ShapeDtypeStruct((n, hq, 16, lanes), bf16),
            pltpu.VMEM(weights.shape, f32),
            jax.ShapeDtypeStruct((2, rows, ny * lanes), bf16),
            jax.ShapeDtypeStruct((3 * nx * 16, xq * zr), bf16),
        ),
        in_specs=[hbm, hbm, hbm, smem, smem] + [hbm] * (2 + len(tables)),
        out_specs=[vmem] * 6,
        scratch_shapes=scratch,
        compiler_params=pltpu.CompilerParams(
            collective_id=0, has_side_effects=True, vmem_limit_bytes=46 * 2**20
        ),
        cost_estimate=pl.CostEstimate(
            flops=4 * 10**9, bytes_accessed=2 * 10**7, transcendentals=10**7
        ),
    )(
        *[in_hbm(v) for v in (inputs, cotangent, weights)],
        mixing, channel_bias,
        *[in_hbm(v) for v in [mixing, channel_bias] + tables],
    )
    input_grad, weight_grad = pl.pallas_call(
        functools.partial(finish_kernel, nx, ny, xq),
        out_shape=(
            jax.ShapeDtypeStruct(grid, bf16),
            jax.ShapeDtypeStruct(weights.shape, f32),
        ),
        in_specs=[vmem] * 6,
        out_specs=(hbm, hbm),
        scratch_shapes=[pltpu.VMEM(left, bf16), dma((2 + hq,))],
        compiler_params=pltpu.CompilerParams(vmem_limit_bytes=24 * 2**20),
        cost_estimate=pl.CostEstimate(flops=10**9, bytes_accessed=10**7, transcendentals=0),
    )(*parts)
    return (input_grad[None], weight_grad[None])


def fits(mesh):
    nx = mesh.shape["gx"]
    return mesh.shape["segment"] == 2 and mesh.shape["gy"] == 2 and nx == 8


def solution(mesh):
    return jax.shard_map(
        two_section_body if fits(mesh) else body,
        mesh=mesh,
        in_specs=(
            P("segment", "groups", "gx", "gy", None),
            P("groups", "gx", "gy", None),
            P("segment", "gy", "gx", None, None, None),
            P("segment", None, None),
            P("segment", None),
        ),
        out_specs=(
            P("segment", "groups", "gx", "gy", None),
            P("segment", "gy", "gx", "groups", None, None),
        ),
        check_vma=False,
    )
```

```python
import functools
import math

import jax
import jax.numpy as jnp
import ml_dtypes
import numpy as np
from jax import lax
from jax.experimental import pallas as pl
from jax.experimental.pallas import tpu as pltpu
from jax.sharding import PartitionSpec as P

MODES = 32
f32, bf16 = jnp.float32, jnp.bfloat16


def from_behind(block, axis, distance):
    devices = range(lax.axis_size(axis))
    route = [(i - distance, i) for i in devices if i - distance in devices]
    return lax.ppermute(block, axis, route)


def trig_basis(length):
    half = MODES // 2
    freqs = np.arange(half)[:, None]
    points = np.arange(length)[None, :]
    step = 2.0 * math.pi / length
    rows = np.concatenate(
        [np.cos((freqs * points % length) * step), np.sin(((freqs + 1) * points % length) * step)]
    )
    scales = np.where(np.arange(MODES) == 0, 1.0 / math.sqrt(length), math.sqrt(2.0 / length))
    return rows * scales[:, None]


def halves(matrix):
    matrix = np.asarray(matrix, np.float32)
    top = matrix.astype(ml_dtypes.bfloat16)
    rest = (matrix - top.astype(np.float32)).astype(ml_dtypes.bfloat16)
    return np.stack([top, rest])


def split(value):
    top = value.astype(bf16)
    return top, (value - top.astype(f32)).astype(bf16)


def dot(a, b, ca=1, cb=0):
    return lax.dot_general(a, b, (((ca,), (cb,)), ((), ())), preferred_element_type=f32)


def kernel(
    back, nx, ny, xr, *refs
):
    if back:
        (inc_ref, slope_ref, w_hbm, mix_ref, bz_ref, bzs_ref, ky_ref, kyt_ref, bx_ref, bxr_ref,
         out_ref, modes_ref, got_ref, *scratch) = refs
    else:
        (inc_ref, w_hbm, mix_ref, bias_ref, bz_ref, bzs_ref, ky_ref, kyt_ref, bx_ref, bxr_ref,
         out_ref, modes_ref, got_ref, *scratch) = refs
    (w_ref, sig_ref, ghi_ref, glo_ref, s_ref, r_ref, m_ref, p_ref, q_ref, qs_ref,
     send1, recv1, send2, recv2, wsem) = scratch
    channels, _, yr, zr = inc_ref.shape
    cl, jl, xp = MODES // nx, MODES // ny, r_ref.shape[2]
    n = nx * ny
    lanes = jl * channels
    gx, gy = lax.axis_index("gx"), lax.axis_index("gy")
    me = gx * ny + gy

    wcopy = pltpu.make_async_copy(w_hbm, w_ref, wsem)
    wcopy.start()

    barrier = pltpu.get_barrier_semaphore()

    def greet(k, carry):
        peer = lax.rem(me + k, n)
        pl.semaphore_signal(
            barrier, inc=1,
            device_id={"gx": peer // ny, "gy": lax.rem(peer, ny)},
            device_id_type=pl.DeviceIdType.MESH,
        )
        return carry

    lax.fori_loop(1, n, greet, 0)

    def along_z(x, carry):
        if back:
            signal = inc_ref[:, x].astype(f32) * slope_ref[:, x]
            sig_ref[:, x] = signal
            block = signal.astype(bf16)
        else:
            block = inc_ref[:, x]
        block = block.reshape(channels * yr, zr)
        g = dot(bz_ref[0], block, 1, 1) + dot(bz_ref[1], block, 1, 1)
        ghi, glo = split(g)
        rows = pl.ds(pl.multiple_of(x * MODES, MODES), MODES)
        ghi_ref[rows, :] = ghi
        glo_ref[rows, :] = glo
        return carry

    lax.fori_loop(0, xr, along_z, 0)
    ghi = ghi_ref[...]
    t = dot(ghi, ky_ref[0]) + dot(ghi, ky_ref[1]) + dot(glo_ref[...], ky_ref[0])
    t = jnp.swapaxes(t.reshape(xr, MODES, ny * lanes), 0, 1)
    if xp > xr:
        t = jnp.concatenate([t, jnp.zeros((MODES, xp - xr, ny * lanes), f32)], axis=1)
    t = t.astype(bf16)
    for h in range(ny):
        s_ref[h] = t[:, :, h * lanes : (h + 1) * lanes].reshape(nx, cl, xp, lanes)

    pl.semaphore_wait(barrier, n - 1)

    def exchange(source, target, send, recv):
        def copy_to(peer, slot_of):
            return pltpu.make_async_remote_copy(
                src_ref=source(peer // ny, lax.rem(peer, ny)),
                dst_ref=target.at[lax.rem(slot_of, ny) * nx + slot_of // ny],
                send_sem=send.at[peer],
                recv_sem=recv.at[slot_of],
                device_id={"gx": peer // ny, "gy": lax.rem(peer, ny)},
                device_id_type=pl.DeviceIdType.MESH,
            )

        def begin(k, carry):
            copy_to(lax.rem(me + k, n), me).start()
            return carry

        def finish(k, carry):
            copy_to(lax.rem(me + k, n), me).wait_send()
            peer = lax.rem(me + n - k, n)
            copy_to(peer, peer).wait_recv()
            return carry

        lax.fori_loop(1, n, begin, 0)
        target[gy * nx + gx] = source(gx, gy)[...]
        lax.fori_loop(1, n, finish, 0)

    exchange(lambda d, h: s_ref.at[h, d], r_ref, send1, recv1)

    for c in range(cl):
        part = r_ref[:, c].reshape(n * xp, lanes)
        own = dot(bx_ref[0], part) + dot(bx_ref[1], part)
        modes_ref[c] = own.T.reshape(jl, channels, MODES)
    wcopy.wait()

    def mix(j, carry):
        for c in range(cl):
            own = modes_ref[c, j]
            weight = w_ref[j, c]
            if back:
                m_ref[c, j] = jnp.sum(weight * own[None], axis=1)
            else:
                m_ref[c, j] = jnp.sum(weight * own[:, None, :], axis=0)
        return carry

    lax.fori_loop(0, jl, mix, 0)
    for c in range(cl):
        top, rest = split(m_ref[c].reshape(lanes, MODES))
        spread = (
            dot(bxr_ref[0], top, 1, 1) + dot(bxr_ref[1], top, 1, 1) + dot(bxr_ref[0], rest, 1, 1)
        )
        p_ref[:, c] = spread.astype(bf16).reshape(nx, xp, lanes)

    exchange(lambda d, h: p_ref.at[d], q_ref, send2, recv2)

    got = [q_ref[h * nx : (h + 1) * nx].reshape(MODES, xp, lanes) for h in range(ny)]
    got = jnp.concatenate(got, axis=2).astype(f32)
    got = jnp.swapaxes(got, 0, 1)[:xr].reshape(xr * MODES, ny * lanes).astype(bf16)
    got_ref[...] = got
    qs_ref[...] = dot(got, kyt_ref[0]) + dot(got, kyt_ref[1])

    def finish_field(x, carry):
        rows = pl.ds(pl.multiple_of(x * MODES, MODES), MODES)
        top, rest = split(qs_ref[rows, :])
        stack = jnp.concatenate([top, rest, top], axis=0)
        field = dot(stack, bzs_ref[...], 0, 0).reshape(channels, yr, zr)
        if back:
            values = [sig_ref[i, x] for i in range(channels)]
        else:
            values = [inc_ref[i, x].astype(f32) for i in range(channels)]
        for o in range(channels):
            total = field[o]
            for i in range(channels):
                total = total + (mix_ref[i, o] if back else mix_ref[o, i]) * values[i]
            if back:
                out_ref[o, x] = total.astype(bf16)
            else:
                total = total + bias_ref[0, o]
                cdf = 0.5 * (1.0 + lax.erf(total * 0.7071067811865476))
                out_ref[o, x] = cdf + total * jnp.exp(-0.5 * total * total) * 0.3989422804014327
        return carry

    lax.fori_loop(0, xr, finish_field, 0)


def ahead_kernel(
    act_ref, cot_ref, got_ref, got_back_ref, mix_ref, bias_ref, bzs_ref, kyt_ref, out_ref,
    pre_ref, back_ref,
):
    channels, xr, yr, zr = act_ref.shape
    pre_ref[...] = dot(got_ref[...], kyt_ref[0]) + dot(got_ref[...], kyt_ref[1])
    back_ref[...] = dot(got_back_ref[...], kyt_ref[0]) + dot(got_back_ref[...], kyt_ref[1])

    def field_of(ref, x):
        rows = pl.ds(pl.multiple_of(x * MODES, MODES), MODES)
        top, rest = split(ref[rows, :])
        stack = jnp.concatenate([top, rest, top], axis=0)
        return dot(stack, bzs_ref[...], 0, 0).reshape(channels, yr, zr)

    def step(x, carry):
        field = field_of(pre_ref, x)
        values = [act_ref[i, x].astype(f32) for i in range(channels)]
        signals = []
        for o in range(channels):
            total = field[o]
            for i in range(channels):
                total = total + mix_ref[o, i] * values[i]
            total = total + bias_ref[0, o]
            cdf = 0.5 * (1.0 + lax.erf(total * 0.7071067811865476))
            slope = cdf + total * jnp.exp(-0.5 * total * total) * 0.3989422804014327
            signals.append(cot_ref[o, x].astype(f32) * slope)
        field = field_of(back_ref, x)
        for o in range(channels):
            total = field[o]
            for i in range(channels):
                total = total + mix_ref[i, o] * signals[i]
            out_ref[o, x] = total.astype(bf16)
        return carry

    lax.fori_loop(0, xr, step, 0)


def ahead(activations, cotangent, got, got_back, mixing, bias, bzs, kyt):
    channels, xr, yr, zr = activations.shape
    vmem = pl.BlockSpec(memory_space=pltpu.VMEM)
    smem = pl.BlockSpec(memory_space=pltpu.SMEM)
    return pl.pallas_call(
        ahead_kernel,
        out_shape=jax.ShapeDtypeStruct(activations.shape, bf16),
        in_specs=[vmem] * 4 + [smem] * 2 + [vmem] * 2,
        out_specs=vmem,
        scratch_shapes=[pltpu.VMEM((xr * MODES, channels * yr), f32)] * 2,
        compiler_params=pltpu.CompilerParams(vmem_limit_bytes=50 * 2**20),
        cost_estimate=pl.CostEstimate(flops=10**9, bytes_accessed=10**7, transcendentals=10**6),
    )(activations, cotangent, got, got_back, mixing, bias, bzs, kyt)


def block_turn(back, nx, ny, collective, field, slope, weights, mixing, bias, tables):
    channels, xr, yr, zr = field.shape
    xp = -(-xr // 16) * 16
    cl, jl, n = MODES // nx, MODES // ny, nx * ny
    lanes = jl * channels
    vmem = pl.BlockSpec(memory_space=pltpu.VMEM)
    smem = pl.BlockSpec(memory_space=pltpu.SMEM)
    hbm = pl.BlockSpec(memory_space=pl.ANY)
    if back:
        args = (field, slope, weights, mixing, *tables)
        specs = [vmem, vmem, hbm, smem] + [vmem] * len(tables)
    else:
        args = (field, weights, mixing, bias, *tables)
        specs = [vmem, hbm, smem, smem] + [vmem] * len(tables)
    dma = pltpu.SemaphoreType.DMA
    return pl.pallas_call(
        functools.partial(kernel, back, nx, ny, xr),
        out_shape=(
            jax.ShapeDtypeStruct(field.shape, bf16 if back else f32),
            jax.ShapeDtypeStruct((cl, jl, channels, MODES), f32),
            jax.ShapeDtypeStruct((xr * MODES, ny * lanes), bf16),
        ),
        in_specs=specs,
        out_specs=(vmem, vmem, vmem),
        scratch_shapes=[
            pltpu.VMEM(weights.shape, f32),
            pltpu.VMEM(field.shape if back else (8, 128), f32),
            pltpu.VMEM((xr * MODES, channels * yr), bf16),
            pltpu.VMEM((xr * MODES, channels * yr), bf16),
            pltpu.VMEM((ny, nx, cl, xp, lanes), bf16),
            pltpu.VMEM((n, cl, xp, lanes), bf16),
            pltpu.VMEM((cl, jl, channels, MODES), f32),
            pltpu.VMEM((nx, cl, xp, lanes), bf16),
            pltpu.VMEM((n, cl, xp, lanes), bf16),
            pltpu.VMEM((xr * MODES, channels * yr), f32),
            dma((n,)), dma((n,)), dma((n,)), dma((n,)), dma,
        ],
        compiler_params=pltpu.CompilerParams(
            collective_id=collective, has_side_effects=True, vmem_limit_bytes=50 * 2**20
        ),
        cost_estimate=pl.CostEstimate(flops=10**9, bytes_accessed=2 * 10**7, transcendentals=10**6),
    )(*args)


def body(activations, cotangent, spectral_weights, pointwise, channel_bias):
    inputs = activations[0]
    channels, xr, yr, zr = inputs.shape
    nx, ny = lax.axis_size("gx"), lax.axis_size("gy")
    xp = -(-xr // 16) * 16
    bz = trig_basis(zr)
    bx = trig_basis(xr * nx).reshape(MODES, nx, xr)
    bx = np.concatenate([bx, np.zeros((MODES, nx, xp - xr))], axis=2).reshape(MODES, nx * xp)
    by = trig_basis(yr * ny).reshape(MODES, ny, yr)
    kron = np.einsum("jgy,ik->giyjk", by, np.eye(channels)).reshape(
        ny, channels * yr, MODES * channels
    )
    bzh = halves(bz)
    kh = halves(kron)
    gy = lax.axis_index("gy")
    ky = lax.dynamic_index_in_dim(jnp.asarray(np.swapaxes(kh, 0, 1)), gy, 0, False)
    kyt = lax.dynamic_index_in_dim(
        jnp.asarray(np.ascontiguousarray(np.transpose(kh, (1, 0, 3, 2)))), gy, 0, False
    )
    tables = (
        jnp.asarray(bzh),
        jnp.asarray(np.concatenate([bzh[0], bzh[0], bzh[1]], axis=0)),
        ky,
        kyt,
        jnp.asarray(halves(np.concatenate([bx] * ny, axis=1))),
        jnp.asarray(halves(bx.T)),
    )
    weights = spectral_weights[0]
    mixing = pointwise[0]
    following = [from_behind(v, "segment", -1) for v in (inputs, mixing, channel_bias)]
    slope, input_modes, got = block_turn(
        False, nx, ny, 0, inputs, None, weights, mixing, channel_bias, tables
    )
    next_got = from_behind(got, "segment", -1)
    segment_index = lax.axis_index("segment")
    segment_count = lax.axis_size("segment")
    incoming = cotangent
    kept_grad = jnp.zeros(cotangent.shape, bf16)
    kept_modes = jnp.zeros(input_modes.shape, f32)
    for turn_index in range(segment_count):
        active = segment_index == segment_count - 1 - turn_index
        input_grad, grad_modes, got_back = block_turn(
            True, nx, ny, 1 + turn_index, incoming, slope, weights, mixing, None, tables
        )
        kept_grad = jnp.where(active, input_grad, kept_grad)
        kept_modes = jnp.where(active, grad_modes, kept_modes)
        if turn_index == 0 and segment_count > 1:
            next_back = from_behind(got_back, "segment", -1)
            incoming = ahead(
                following[0], cotangent, next_got, next_back, following[1], following[2],
                tables[1], tables[3],
            )
        elif turn_index + 1 < segment_count:
            incoming = from_behind(input_grad, "segment", -1)
    input_modes = jnp.swapaxes(input_modes, 0, 1)
    kept_modes = jnp.swapaxes(kept_modes, 0, 1)
    weight_grad = input_modes[:, :, :, None, :] * kept_modes[:, :, None, :, :]
    return (kept_grad[None], weight_grad[None])


def slope_of(value):
    cdf = 0.5 * (1.0 + lax.erf(value * 0.7071067811865476))
    return cdf + value * jnp.exp(-0.5 * value * value) * 0.3989422804014327


def field_of(cells, ny, ky, bzi):
    blocks = []
    for h in range(ny):
        block = cells(h)
        blocks.append(block.reshape(block.shape[0] * block.shape[1], block.shape[2]))
    block = jnp.concatenate(blocks, axis=1)
    top, rest = split(dot(ky[0], block, 1, 1) + dot(ky[1], block, 1, 1))
    return dot(jnp.concatenate([top, rest, top], axis=1), bzi[...])


def relay_kernel(
    nx, ny, xq, cuts,
    act_hbm, cot_hbm, w_hbm, mix_ref, bias_ref, mix_hbm, bias_hbm,
    kyt_hbm, ky_hbm, bzf_hbm, bzi_hbm, bx_hbm, sp_hbm,
    out, rest_ref, cells_ref, wgrad, ky, bzi,
    act, act1, cot, w, wd, kyt, bzf, bx, sp,
    u, v, slope, sig, in_modes, grad_modes, m_ref, mt_send, mt_recv,
    mixv1, biasv1, mix1, bias1, s_ref, p_ref, r_ref,
    load_sem, send_sem, recv_sem, row_send, row_recv, small_send, small_recv, store_sem,
    tail_send, tail_recv, pair_send, pair_recv, across_send,
):
    channels, xr, yr, zr = act.shape
    n = nx * ny
    cl, jl = MODES // nx, MODES // ny
    nh, hq = r_ref.shape[1], r_ref.shape[3]
    lanes = jl * channels
    rows = channels * yr
    tail = xr - hq * xq
    late = xr - xq
    gx, gy, seg = lax.axis_index("gx"), lax.axis_index("gy"), lax.axis_index("segment")
    me = gx * ny + gy
    mine = gy * nx + gx
    first, last = seg == 0, seg == 1
    mesh_ids = pl.DeviceIdType.MESH

    loads = [
        pltpu.make_async_copy(source, target, load_sem.at[k])
        for k, (source, target) in enumerate(
            [
                (act_hbm, act), (bzf_hbm, bzf), (kyt_hbm.at[gy], kyt), (w_hbm, w), (bx_hbm, bx),
                (sp_hbm, sp), (ky_hbm.at[gy], ky), (bzi_hbm, bzi), (cot_hbm, cot),
            ]
        )
    ]
    for load in loads[:3]:
        load.start()

    barrier = pltpu.get_barrier_semaphore()

    def greet(k, carry):
        other = lax.rem(seg * n + me + k, 2 * n)
        peer = lax.rem(other, n)
        pl.semaphore_signal(
            barrier, inc=1,
            device_id={"segment": other // n, "gx": peer // ny, "gy": lax.rem(peer, ny)},
            device_id_type=mesh_ids,
        )
        return carry

    lax.fori_loop(1, 2 * n, greet, 0)

    def ahead(source, target, send, recv):
        return pltpu.make_async_remote_copy(
            src_ref=source, dst_ref=target, send_sem=send, recv_sem=recv,
            device_id={"segment": 1 - seg}, device_id_type=mesh_ids,
        )

    def row_copy(x):
        return ahead(act_hbm.at[:, x], act1.at[:, x], row_send.at[x], row_recv.at[x])

    def send_rows(start, stop):
        for x in range(start, stop):
            row_copy(x).start()

    def modes_copy(k):
        return ahead(mt_send.at[k], mt_recv.at[k], small_send.at[k], small_recv.at[k])

    small = [
        ahead(mix_hbm, mixv1, small_send.at[2], small_recv.at[2]),
        ahead(bias_hbm, biasv1, small_send.at[3], small_recv.at[3]),
    ]

    def send(source, target, sends, receives):
        def begin(k, carry):
            peer = lax.rem(me + k, n)
            d, h = peer // ny, lax.rem(peer, ny)
            pltpu.make_async_remote_copy(
                src_ref=source(d, h), dst_ref=target, send_sem=sends, recv_sem=receives,
                device_id={"gx": d, "gy": h}, device_id_type=mesh_ids,
            ).start()
            return carry

        lax.fori_loop(1, n, begin, 0)
        target[...] = source(gx, gy)[...]

    def send_half(source, e, half):
        send(source, r_ref.at[e, half, mine], send_sem.at[e, half], recv_sem.at[e, half])

    def send_along(source, e, half):
        def begin(k, carry):
            d = lax.rem(gx + k, nx)
            pltpu.make_async_remote_copy(
                src_ref=source(d), dst_ref=r_ref.at[e, half, mine],
                send_sem=send_sem.at[e, half], recv_sem=recv_sem.at[e, half],
                device_id={"gx": d}, device_id_type=mesh_ids,
            ).start()
            return carry

        lax.fori_loop(1, nx, begin, 0)
        r_ref[e, half, mine] = source(gx)[...]

    def send_across(half):
        def begin(k, carry):
            d = lax.rem(gx + k, nx)
            pltpu.make_async_remote_copy(
                src_ref=p_ref.at[1, half, d], dst_ref=r_ref.at[3, half, mine],
                send_sem=across_send.at[half], recv_sem=recv_sem.at[3, half],
                device_id={"segment": 0, "gx": d}, device_id_type=mesh_ids,
            ).start()
            return carry

        lax.fori_loop(0, nx, begin, 0)

    def pair_copy(e, half):
        block = r_ref.at[e, half, pl.ds(gy * nx, nx)]
        return pltpu.make_async_remote_copy(
            src_ref=block, dst_ref=block,
            send_sem=pair_send.at[e, half], recv_sem=pair_recv.at[e, half],
            device_id={"gy": 1 - gy}, device_id_type=mesh_ids,
        )

    def forward(e, halves):
        for half in halves:
            await_block(r_ref.at[e, half, pl.ds(0, nx - 1)], recv_sem.at[e, half])
            pair_copy(e, half).start()

    def forward_across(half):
        await_block(r_ref.at[3, half, pl.ds(0, nx)], recv_sem.at[3, half])
        pair_copy(3, half).start()

    def land(e, half):
        await_block(r_ref.at[e, half, pl.ds(0, nx)], pair_recv.at[e, half])

    def sent_along(e, half):
        await_block(r_ref.at[e, half, pl.ds(0, nx - 1)], send_sem.at[e, half])
        await_block(r_ref.at[e, half, pl.ds(0, nx)], pair_send.at[e, half])

    def send_tail(k, carry):
        peer = lax.rem(me + k, n)
        d, h = peer // ny, lax.rem(peer, ny)
        pltpu.make_async_remote_copy(
            src_ref=s_ref.at[2, nh - 1, h * nx + d], dst_ref=r_ref.at[4, nh - 1, mine],
            send_sem=tail_send.at[0], recv_sem=tail_recv.at[0],
            device_id={"segment": 0, "gx": d, "gy": h}, device_id_type=mesh_ids,
        ).start()
        return carry

    def await_block(block, sem):
        pltpu.make_async_copy(block, block, sem).wait()

    def arrive(e, half):
        await_block(r_ref.at[e, half, pl.ds(0, n - 1)], recv_sem.at[e, half])

    def sent(e, half):
        await_block(r_ref.at[e, half, pl.ds(0, n - 1)], send_sem.at[e, half])

    def to_modes(blocks, k, half):
        parts = []
        for block in blocks:
            g = dot(block, bzf[...])
            parts.append(g[:, : nx * 16] + g[:, nx * 16 :])
        top, rest = split(jnp.concatenate(parts, axis=1))
        t = dot(kyt[0], top) + dot(kyt[1], top) + dot(kyt[0], rest)
        t = t.T.astype(bf16)
        for q in range(len(blocks)):
            for h in range(ny):
                part = t[q * nx * 16 : (q + 1) * nx * 16, h * lanes : (h + 1) * lanes]
                s_ref[k, half, h * nx : (h + 1) * nx, q] = part.reshape(nx, 16, lanes)

    def to_field(e, half, q):
        return field_of(lambda h: r_ref[e, half, h * nx : (h + 1) * nx, q], ny, ky, bzi)

    def row(field, x):
        return field[:, x * zr : (x + 1) * zr].reshape(channels, yr, zr)

    def send_modes(k, e, half):
        send_half(lambda d, h: s_ref.at[k, half, h * nx + d], e, half)

    def own_modes(e, await_half):
        own = None
        for half in range(nh):
            await_half(half)
            block = r_ref[e, half].reshape(n * hq * 16, lanes)
            part = slice(half * n * hq * 16, (half + 1) * n * hq * 16)
            term = dot(bx[0, :, part], block) + dot(bx[1, :, part], block)
            own = term if own is None else own + term
        return own.T.reshape(jl, channels, cl * MODES)

    def spread(mt, k, half):
        top, rest = split(mt)
        table = [sp[i, half].reshape(nx * hq * 16, cl * MODES) for i in range(2)]
        cells = dot(table[0], top) + dot(table[1], top) + dot(table[0], rest)
        p_ref[k, half] = cells.astype(bf16).reshape(nx, hq, 16, lanes)

    def send_spread(k, e, half):
        send_along(lambda d: p_ref.at[k, half, d], e, half)

    def send_cells(mt, k, e, halves):
        for half in halves:
            spread(mt, k, half)
            send_spread(k, e, half)

    def mixed():
        return m_ref[...].reshape(lanes, cl * MODES).T

    def mix_back(e, await_half):
        grad_modes[...] = own_modes(e, await_half)

        def step(j, carry):
            m_ref[j] = jnp.sum(wd[j] * grad_modes[j][None], axis=1)
            return carry

        lax.fori_loop(0, jl, step, 0)

    def blend(mixing, values, o, back):
        total = (mixing[0, o] if back else mixing[o, 0]) * values[0]
        for i in range(1, channels):
            total = total + (mixing[i, o] if back else mixing[o, i]) * values[i]
        return total

    def fetch_small():
        for copy in small:
            copy.wait_recv()
        for k, (source, target) in enumerate([(mixv1, mix1), (biasv1, bias1)]):
            copy = pltpu.make_async_copy(source, target, store_sem.at[k])
            copy.start()
            copy.wait()

    def back_block(half, q, offset):
        field = to_field(3, half, q)
        x0 = (half * hq + q) * xq
        block = []
        for k in range(xq):
            incoming = (row(field, k) + offset[:, x0 + k]).astype(bf16).astype(f32)
            signal = incoming * slope[:, x0 + k]
            block.append((x0 + k, signal))
        return block

    def packed(block):
        return jnp.concatenate([s.astype(bf16).reshape(rows, zr) for _, s in block], axis=1)

    def blend_back(start, stop):
        def step(x, carry):
            values = [sig[i, x] for i in range(channels)]
            for o in range(channels):
                u[o, x] = blend(mix_ref, values, o, True)
            return carry

        lax.fori_loop(start, stop, step, 0)

    pl.semaphore_wait(barrier, 2 * n - 1)
    for copy in small:
        copy.start()

    @pl.when(last)
    def _():
        send_rows(0, cuts[0])

    @pl.when(first)
    def _():
        send_rows(tail, tail + cuts[0])

    for load in loads[:3]:
        load.wait()
    for load in loads[3:]:
        load.start()
    for half in range(nh):
        blocks = []
        for q in range(hq):
            x = (half * hq + q) * xq
            block = [act[:, x + k].reshape(rows, zr) for k in range(xq)]
            blocks.append(jnp.concatenate(block, axis=1))
        to_modes(blocks, 0, half)
        send_modes(0, 0, half)

    for load in loads[3:]:
        load.wait()

    def dense(j, carry):
        for i in range(channels):
            wd[j, i] = jnp.concatenate([w[j, c, i] for c in range(cl)], axis=1)
        return carry

    lax.fori_loop(0, jl, dense, 0)

    def pointwise(x, carry):
        values = [act[i, x].astype(f32) for i in range(channels)]
        for o in range(channels):
            u[o, x] = blend(mix_ref, values, o, False) + bias_ref[0, o]
        return carry

    lax.fori_loop(0, xr, pointwise, 0)

    in_modes[...] = own_modes(0, lambda half: arrive(0, half))

    def mix(j, carry):
        own = in_modes[j]
        m_ref[j] = jnp.sum(wd[j] * own[:, None, :], axis=0)
        return carry

    lax.fori_loop(0, jl, mix, 0)
    mt_send[0] = mixed()
    modes_copy(0).start()

    @pl.when(last)
    def _():
        send_rows(cuts[0], cuts[1])

    @pl.when(first)
    def _():
        send_rows(tail + cuts[0], xr)

    send_cells(mt_send[0], 0, 1, range(nh))

    @pl.when(last)
    def _():
        forward(1, range(nh))
        for half in range(nh):
            land(1, half)
            blocks = []
            for q in range(hq):
                field = to_field(1, half, q)
                x0 = (half * hq + q) * xq
                block = []
                for k in range(xq):
                    signal = cot[:, x0 + k].astype(f32) * slope_of(row(field, k) + u[:, x0 + k])
                    sig[:, x0 + k] = signal
                    block.append(signal.astype(bf16).reshape(rows, zr))
                blocks.append(jnp.concatenate(block, axis=1))
            to_modes(blocks, 1, half)
            send_modes(1, 2, half)
            if half == 0:
                modes_copy(0).wait_recv()
                send_cells(mt_recv[0], 3, 5, [nh - 1])

        fetch_small()
        forward(5, [nh - 1])
        land(5, nh - 1)
        for q in range(hq):
            field = to_field(5, nh - 1, q)
            for k in range(xq):
                v[:, tail + q * xq + k] = row(field, k)

        mix_back(2, lambda half: arrive(2, half))
        mt_send[1] = mixed()
        for half in range(nh - 1):
            spread(mt_send[1], 1, half)
            send_across(half)
        send_rows(cuts[1], cuts[2])
        spread(mt_send[1], 1, nh - 1)
        for half in reversed(range(nh)):
            send_spread(1, 3, half)

        blend_back(tail, xr)

        def step(x, carry):
            row_copy(x).wait_recv()
            values = [act1[i, x].astype(f32) for i in range(channels)]
            for o in range(channels):
                pre = v[o, x] + blend(mix1, values, o, False) + bias1[0, o]
                slope[o, x] = slope_of(pre)
            return carry

        lax.fori_loop(tail, xr, step, 0)
        forward(3, reversed(range(nh)))
        land(3, nh - 1)
        to_modes([packed(back_block(nh - 1, q, u)) for q in range(hq)], 2, nh - 1)
        lax.fori_loop(0, n, send_tail, 0)
        send_across(nh - 1)
        send_rows(cuts[2], xr)
        blend_back(0, tail)

    def ahead_quarter(half, q):
        field = to_field(2, half, q)
        x0 = (half * hq + q) * xq
        for k in range(xq):
            row_copy(x0 + k).wait_recv()
            values = [act1[i, x0 + k].astype(f32) for i in range(channels)]
            here = row(field, k)
            signals = []
            for o in range(channels):
                pre = here[o] + blend(mix1, values, o, False) + bias1[0, o]
                signals.append(cot[o, x0 + k].astype(f32) * slope_of(pre))
            for i in range(channels):
                v[i, x0 + k] = blend(mix1, signals, i, True)

    def kept(block):
        for x, signal in block:
            sig[:, x] = signal
        return block

    @pl.when(first)
    def _():
        modes_copy(0).wait_recv()
        send_cells(mt_recv[0], 1, 2, range(nh))
        fetch_small()
        forward(1, range(nh))
        for half in range(nh):
            land(1, half)

            def step(q, carry):
                field = to_field(1, half, q)
                x0 = (half * hq + q) * xq
                for k in range(xq):
                    slope[:, x0 + k] = slope_of(row(field, k) + u[:, x0 + k])
                return carry

            lax.fori_loop(0, hq, step, 0)

        forward(2, range(nh))
        for half in range(nh):
            land(2, half)
        for half in range(nh - 1):
            for q in range(hq):
                ahead_quarter(half, q)
        for half in range(nh - 1):
            forward_across(half)
            land(3, half)
            to_modes([packed(kept(back_block(half, q, v))) for q in range(hq)], 1, half)
            send_modes(1, 4, half)
        blend_back(0, tail)
        for q in range(hq - 1):
            ahead_quarter(nh - 1, q)

        def await_half(half):
            if half < nh - 1:
                arrive(4, half)
            else:
                await_block(r_ref.at[4, half], tail_recv.at[0])

        mix_back(4, await_half)
        send_cells(mixed(), 3, 5, range(nh))
        forward_across(nh - 1)
        land(3, nh - 1)
        for q in range(hq - 1):
            kept(back_block(nh - 1, q, v))
        if hq > 1:
            blend_back(tail, late)
        for target, e in ((v, 2), (u, 3)):
            field = to_field(e, nh - 1, hq - 1)
            for k in range(xq):
                target[:, late + k] = row(field, k)

    def weight_grad(j, carry):
        for c in range(cl):
            part = slice(c * MODES, (c + 1) * MODES)
            wgrad[j, c] = in_modes[j][:, None, part] * grad_modes[j][None, :, part]
        return carry

    lax.fori_loop(0, jl, weight_grad, 0)
    e = 3 + 2 * (1 - seg)

    @pl.when(last)
    def _():
        for half in range(nh - 1):
            land(3, half)

    @pl.when(first)
    def _():
        forward(5, range(nh))
        for half in range(nh - 1):
            land(5, half)

    for half in range(nh - 1):
        for q in range(hq):
            field = to_field(e, half, q)
            x0 = (half * hq + q) * xq
            for k in range(xq):
                out[:, x0 + k] = (row(field, k) + u[:, x0 + k]).astype(bf16)

    @pl.when(first)
    def _():
        land(5, nh - 1)
        rest_ref[:, : late - tail] = u[:, tail:late]

    cells_ref[...] = r_ref[e, nh - 1]

    @pl.when(first)
    def _():
        def step(k, carry):
            x = late + k
            row_copy(x).wait_recv()
            values = [act1[i, x].astype(f32) for i in range(channels)]
            signals = []
            for o in range(channels):
                pre = v[o, x] + blend(mix1, values, o, False) + bias1[0, o]
                signals.append(cot[o, x].astype(f32) * slope_of(pre))
            here = []
            for i in range(channels):
                incoming = u[i, x] + blend(mix1, signals, i, True)
                here.append(incoming.astype(bf16).astype(f32) * slope[i, x])
            for o in range(channels):
                rest_ref[o, late - tail + k] = blend(mix_ref, here, o, True)
            return carry

        lax.fori_loop(0, xq, step, 0)

    @pl.when(last)
    def _():
        rest_ref[...] = u[:, tail:]

    for half in range(nh):
        sent(0, half)
        sent_along(1, half)
        await_block(r_ref.at[3, half, pl.ds(0, nx)], pair_send.at[3, half])
    for copy in small:
        copy.wait_send()
    modes_copy(0).wait_send()

    @pl.when(first)
    def _():
        for half in range(nh - 1):
            sent(4, half)
        for half in range(nh):
            sent_along(2, half)
            sent_along(5, half)
        for x in range(tail, xr):
            row_copy(x).wait_send()

    @pl.when(last)
    def _():
        for half in range(nh):
            sent(2, half)
            await_block(r_ref.at[3, half, pl.ds(0, nx - 1)], send_sem.at[3, half])
            await_block(r_ref.at[3, half, pl.ds(0, nx)], across_send.at[half])
        sent_along(5, nh - 1)
        await_block(r_ref.at[4, nh - 1], tail_send.at[0])
        for x in range(xr):
            row_copy(x).wait_send()


def finish_kernel(
    nx, ny, xq, done_ref, rest_ref, cells_ref, wgrad, ky, bzi, grad_hbm, wgrad_hbm, out, sem
):
    channels, done, yr, zr = done_ref.shape
    hq = cells_ref.shape[1]
    stores = [
        pltpu.make_async_copy(wgrad, wgrad_hbm, sem.at[0]),
        pltpu.make_async_copy(done_ref, grad_hbm.at[:, pl.ds(0, done)], sem.at[1]),
    ]
    for store in stores:
        store.start()
    for q in range(hq):
        field = field_of(lambda h: cells_ref[h * nx : (h + 1) * nx, q], ny, ky, bzi)
        for k in range(xq):
            x = q * xq + k
            here = field[:, k * zr : (k + 1) * zr].reshape(channels, yr, zr)
            out[:, x] = (here + rest_ref[:, x]).astype(bf16)
        part = pl.ds(q * xq, xq)
        store = pltpu.make_async_copy(
            out.at[:, part], grad_hbm.at[:, pl.ds(done + q * xq, xq)], sem.at[2 + q]
        )
        store.start()
        stores.append(store)
    for store in stores:
        store.wait()


def in_hbm(value):
    return pltpu.with_memory_space_constraint(jnp.asarray(value), pltpu.HBM)


def two_section_body(activations, cotangent, spectral_weights, pointwise, channel_bias):
    inputs = activations[0]
    channels, xr, yr, zr = inputs.shape
    nx, ny = lax.axis_size("gx"), lax.axis_size("gy")
    n = nx * ny
    cl, jl = MODES // nx, MODES // ny
    xq = 16 // cl
    nh = 2
    hq = xr // (nh * xq)
    lanes, rows = jl * channels, channels * yr
    bz = trig_basis(zr).reshape(nx, cl, zr)
    eye_x, eye_c = np.eye(xq), np.eye(cl)
    bzf = np.einsum("dcz,xX->xzdXc", bz, eye_x).reshape(xq * zr, nx * 16)
    bzi = halves(bzf.reshape(xq, zr, nx * 16).transpose(2, 0, 1).reshape(nx * 16, xq * zr))
    by = trig_basis(yr * ny).reshape(MODES, ny, yr)
    ky = np.einsum("jgy,ik->giyjk", by, np.eye(channels)).reshape(ny, rows, ny * lanes)
    ky = halves(ky)
    bx = trig_basis(xr * nx).reshape(MODES, nx, nh, hq, xq)
    sp = np.einsum("adtqx,cC->tdqxCca", bx, eye_c).reshape(nh * nx * hq * 16, cl * MODES)
    bxf = np.broadcast_to(
        sp.reshape(nh, 1, nx * hq * 16, cl * MODES), (nh, ny, nx * hq * 16, cl * MODES)
    )
    bxf = bxf.reshape(nh * n * hq * 16, cl * MODES).T
    bzf = halves(bzf)
    tables = [
        np.ascontiguousarray(ky.transpose(1, 0, 3, 2)),
        np.ascontiguousarray(ky.transpose(1, 0, 2, 3)),
        np.concatenate([bzf[0], bzf[1]], axis=1),
        np.concatenate([bzi[0], bzi[0], bzi[1]], axis=0),
        halves(bxf),
        halves(sp).reshape(2, nh, nx, hq, 16, cl * MODES),
    ]
    weights, mixing = spectral_weights[0], pointwise[0]
    vmem = pl.BlockSpec(memory_space=pltpu.VMEM)
    smem = pl.BlockSpec(memory_space=pltpu.SMEM)
    hbm = pl.BlockSpec(memory_space=pl.ANY)
    dma = pltpu.SemaphoreType.DMA
    grid = inputs.shape
    done = grid[:1] + ((nh - 1) * hq * xq,) + grid[2:]
    left = grid[:1] + (hq * xq,) + grid[2:]
    scratch = [
        pltpu.VMEM(grid, bf16), pltpu.VMEM(grid, bf16), pltpu.VMEM(grid, bf16),
        pltpu.VMEM(weights.shape, f32),
        pltpu.VMEM((jl, channels, channels, cl * MODES), f32),
        pltpu.VMEM((2, ny * lanes, rows), bf16),
        pltpu.VMEM((xq * zr, 2 * nx * 16), bf16),
        pltpu.VMEM((2, cl * MODES, nh * n * hq * 16), bf16),
        pltpu.VMEM((2, nh, nx, hq, 16, cl * MODES), bf16),
        pltpu.VMEM(grid, f32), pltpu.VMEM(grid, f32), pltpu.VMEM(grid, f32), pltpu.VMEM(grid, f32),
        pltpu.VMEM((jl, channels, cl * MODES), f32),
        pltpu.VMEM((jl, channels, cl * MODES), f32),
        pltpu.VMEM((jl, channels, cl * MODES), f32),
        pltpu.VMEM((2, cl * MODES, lanes), f32),
        pltpu.VMEM((2, cl * MODES, lanes), f32),
        pltpu.VMEM(mixing.shape, f32), pltpu.VMEM(channel_bias.shape, f32),
        pltpu.SMEM(mixing.shape, f32), pltpu.SMEM(channel_bias.shape, f32),
        pltpu.VMEM((3, nh, n, hq, 16, lanes), bf16),
        pltpu.VMEM((4, nh, nx, hq, 16, lanes), bf16),
        pltpu.VMEM((6, nh, n, hq, 16, lanes), bf16),
        dma((9,)), dma((6, nh)), dma((6, nh)),
        dma((xr,)), dma((xr,)), dma((4,)), dma((4,)), dma((2,)), dma((1,)), dma((1,)), dma((6, nh)), dma((6, nh)), dma((nh,)),
    ]
    parts = pl.pallas_call(
        functools.partial(relay_kernel, nx, ny, xq, (3, 9, 12)),
        out_shape=(
            jax.ShapeDtypeStruct(done, bf16),
            jax.ShapeDtypeStruct(left, f32),
            jax.ShapeDtypeStruct((n, hq, 16, lanes), bf16),
            pltpu.VMEM(weights.shape, f32),
            jax.ShapeDtypeStruct((2, rows, ny * lanes), bf16),
            jax.ShapeDtypeStruct((3 * nx * 16, xq * zr), bf16),
        ),
        in_specs=[hbm, hbm, hbm, smem, smem] + [hbm] * (2 + len(tables)),
        out_specs=[vmem] * 6,
        scratch_shapes=scratch,
        compiler_params=pltpu.CompilerParams(
            collective_id=0, has_side_effects=True, vmem_limit_bytes=46 * 2**20
        ),
        cost_estimate=pl.CostEstimate(
            flops=4 * 10**9, bytes_accessed=2 * 10**7, transcendentals=10**7
        ),
    )(
        *[in_hbm(v) for v in (inputs, cotangent, weights)],
        mixing, channel_bias,
        *[in_hbm(v) for v in [mixing, channel_bias] + tables],
    )
    input_grad, weight_grad = pl.pallas_call(
        functools.partial(finish_kernel, nx, ny, xq),
        out_shape=(
            jax.ShapeDtypeStruct(grid, bf16),
            jax.ShapeDtypeStruct(weights.shape, f32),
        ),
        in_specs=[vmem] * 6,
        out_specs=(hbm, hbm),
        scratch_shapes=[pltpu.VMEM(left, bf16), dma((2 + hq,))],
        compiler_params=pltpu.CompilerParams(vmem_limit_bytes=24 * 2**20),
        cost_estimate=pl.CostEstimate(flops=10**9, bytes_accessed=10**7, transcendentals=0),
    )(*parts)
    return (input_grad[None], weight_grad[None])


def fits(mesh):
    nx = mesh.shape["gx"]
    return mesh.shape["segment"] == 2 and mesh.shape["gy"] == 2 and nx == 8


def solution(mesh):
    return jax.shard_map(
        two_section_body if fits(mesh) else body,
        mesh=mesh,
        in_specs=(
            P("segment", "groups", "gx", "gy", None),
            P("groups", "gx", "gy", None),
            P("segment", "gy", "gx", None, None, None),
            P("segment", None, None),
            P("segment", None),
        ),
        out_specs=(
            P("segment", "groups", "gx", "gy", None),
            P("segment", "gy", "gx", "groups", None, None),
        ),
        check_vma=False,
    )
```

```python
import functools
import math

import jax
import jax.numpy as jnp
import ml_dtypes
import numpy as np
from jax import lax
from jax.experimental import pallas as pl
from jax.experimental.pallas import tpu as pltpu
from jax.sharding import PartitionSpec as P

MODES = 32
f32, bf16 = jnp.float32, jnp.bfloat16


def from_behind(block, axis, distance):
    devices = range(lax.axis_size(axis))
    route = [(i - distance, i) for i in devices if i - distance in devices]
    return lax.ppermute(block, axis, route)


def trig_basis(length):
    half = MODES // 2
    freqs = np.arange(half)[:, None]
    points = np.arange(length)[None, :]
    step = 2.0 * math.pi / length
    rows = np.concatenate(
        [np.cos((freqs * points % length) * step), np.sin(((freqs + 1) * points % length) * step)]
    )
    scales = np.where(np.arange(MODES) == 0, 1.0 / math.sqrt(length), math.sqrt(2.0 / length))
    return rows * scales[:, None]


def halves(matrix):
    matrix = np.asarray(matrix, np.float32)
    top = matrix.astype(ml_dtypes.bfloat16)
    rest = (matrix - top.astype(np.float32)).astype(ml_dtypes.bfloat16)
    return np.stack([top, rest])


def split(value):
    top = value.astype(bf16)
    return top, (value - top.astype(f32)).astype(bf16)


def dot(a, b, ca=1, cb=0):
    return lax.dot_general(a, b, (((ca,), (cb,)), ((), ())), preferred_element_type=f32)


def kernel(
    back, nx, ny, xr, *refs
):
    if back:
        (inc_ref, slope_ref, w_hbm, mix_ref, bz_ref, bzs_ref, ky_ref, kyt_ref, bx_ref, bxr_ref,
         out_ref, modes_ref, got_ref, *scratch) = refs
    else:
        (inc_ref, w_hbm, mix_ref, bias_ref, bz_ref, bzs_ref, ky_ref, kyt_ref, bx_ref, bxr_ref,
         out_ref, modes_ref, got_ref, *scratch) = refs
    (w_ref, sig_ref, ghi_ref, glo_ref, s_ref, r_ref, m_ref, p_ref, q_ref, qs_ref,
     send1, recv1, send2, recv2, wsem) = scratch
    channels, _, yr, zr = inc_ref.shape
    cl, jl, xp = MODES // nx, MODES // ny, r_ref.shape[2]
    n = nx * ny
    lanes = jl * channels
    gx, gy = lax.axis_index("gx"), lax.axis_index("gy")
    me = gx * ny + gy

    wcopy = pltpu.make_async_copy(w_hbm, w_ref, wsem)
    wcopy.start()

    barrier = pltpu.get_barrier_semaphore()

    def greet(k, carry):
        peer = lax.rem(me + k, n)
        pl.semaphore_signal(
            barrier, inc=1,
            device_id={"gx": peer // ny, "gy": lax.rem(peer, ny)},
            device_id_type=pl.DeviceIdType.MESH,
        )
        return carry

    lax.fori_loop(1, n, greet, 0)

    def along_z(x, carry):
        if back:
            signal = inc_ref[:, x].astype(f32) * slope_ref[:, x]
            sig_ref[:, x] = signal
            block = signal.astype(bf16)
        else:
            block = inc_ref[:, x]
        block = block.reshape(channels * yr, zr)
        g = dot(bz_ref[0], block, 1, 1) + dot(bz_ref[1], block, 1, 1)
        ghi, glo = split(g)
        rows = pl.ds(pl.multiple_of(x * MODES, MODES), MODES)
        ghi_ref[rows, :] = ghi
        glo_ref[rows, :] = glo
        return carry

    lax.fori_loop(0, xr, along_z, 0)
    ghi = ghi_ref[...]
    t = dot(ghi, ky_ref[0]) + dot(ghi, ky_ref[1]) + dot(glo_ref[...], ky_ref[0])
    t = jnp.swapaxes(t.reshape(xr, MODES, ny * lanes), 0, 1)
    if xp > xr:
        t = jnp.concatenate([t, jnp.zeros((MODES, xp - xr, ny * lanes), f32)], axis=1)
    t = t.astype(bf16)
    for h in range(ny):
        s_ref[h] = t[:, :, h * lanes : (h + 1) * lanes].reshape(nx, cl, xp, lanes)

    pl.semaphore_wait(barrier, n - 1)

    def exchange(source, target, send, recv):
        def copy_to(peer, slot_of):
            return pltpu.make_async_remote_copy(
                src_ref=source(peer // ny, lax.rem(peer, ny)),
                dst_ref=target.at[lax.rem(slot_of, ny) * nx + slot_of // ny],
                send_sem=send.at[peer],
                recv_sem=recv.at[slot_of],
                device_id={"gx": peer // ny, "gy": lax.rem(peer, ny)},
                device_id_type=pl.DeviceIdType.MESH,
            )

        def begin(k, carry):
            copy_to(lax.rem(me + k, n), me).start()
            return carry

        def finish(k, carry):
            copy_to(lax.rem(me + k, n), me).wait_send()
            peer = lax.rem(me + n - k, n)
            copy_to(peer, peer).wait_recv()
            return carry

        lax.fori_loop(1, n, begin, 0)
        target[gy * nx + gx] = source(gx, gy)[...]
        lax.fori_loop(1, n, finish, 0)

    exchange(lambda d, h: s_ref.at[h, d], r_ref, send1, recv1)

    for c in range(cl):
        part = r_ref[:, c].reshape(n * xp, lanes)
        own = dot(bx_ref[0], part) + dot(bx_ref[1], part)
        modes_ref[c] = own.T.reshape(jl, channels, MODES)
    wcopy.wait()

    def mix(j, carry):
        for c in range(cl):
            own = modes_ref[c, j]
            weight = w_ref[j, c]
            if back:
                m_ref[c, j] = jnp.sum(weight * own[None], axis=1)
            else:
                m_ref[c, j] = jnp.sum(weight * own[:, None, :], axis=0)
        return carry

    lax.fori_loop(0, jl, mix, 0)
    for c in range(cl):
        top, rest = split(m_ref[c].reshape(lanes, MODES))
        spread = (
            dot(bxr_ref[0], top, 1, 1) + dot(bxr_ref[1], top, 1, 1) + dot(bxr_ref[0], rest, 1, 1)
        )
        p_ref[:, c] = spread.astype(bf16).reshape(nx, xp, lanes)

    exchange(lambda d, h: p_ref.at[d], q_ref, send2, recv2)

    got = [q_ref[h * nx : (h + 1) * nx].reshape(MODES, xp, lanes) for h in range(ny)]
    got = jnp.concatenate(got, axis=2).astype(f32)
    got = jnp.swapaxes(got, 0, 1)[:xr].reshape(xr * MODES, ny * lanes).astype(bf16)
    got_ref[...] = got
    qs_ref[...] = dot(got, kyt_ref[0]) + dot(got, kyt_ref[1])

    def finish_field(x, carry):
        rows = pl.ds(pl.multiple_of(x * MODES, MODES), MODES)
        top, rest = split(qs_ref[rows, :])
        stack = jnp.concatenate([top, rest, top], axis=0)
        field = dot(stack, bzs_ref[...], 0, 0).reshape(channels, yr, zr)
        if back:
            values = [sig_ref[i, x] for i in range(channels)]
        else:
            values = [inc_ref[i, x].astype(f32) for i in range(channels)]
        for o in range(channels):
            total = field[o]
            for i in range(channels):
                total = total + (mix_ref[i, o] if back else mix_ref[o, i]) * values[i]
            if back:
                out_ref[o, x] = total.astype(bf16)
            else:
                total = total + bias_ref[0, o]
                cdf = 0.5 * (1.0 + lax.erf(total * 0.7071067811865476))
                out_ref[o, x] = cdf + total * jnp.exp(-0.5 * total * total) * 0.3989422804014327
        return carry

    lax.fori_loop(0, xr, finish_field, 0)


def ahead_kernel(
    act_ref, cot_ref, got_ref, got_back_ref, mix_ref, bias_ref, bzs_ref, kyt_ref, out_ref,
    pre_ref, back_ref,
):
    channels, xr, yr, zr = act_ref.shape
    pre_ref[...] = dot(got_ref[...], kyt_ref[0]) + dot(got_ref[...], kyt_ref[1])
    back_ref[...] = dot(got_back_ref[...], kyt_ref[0]) + dot(got_back_ref[...], kyt_ref[1])

    def field_of(ref, x):
        rows = pl.ds(pl.multiple_of(x * MODES, MODES), MODES)
        top, rest = split(ref[rows, :])
        stack = jnp.concatenate([top, rest, top], axis=0)
        return dot(stack, bzs_ref[...], 0, 0).reshape(channels, yr, zr)

    def step(x, carry):
        field = field_of(pre_ref, x)
        values = [act_ref[i, x].astype(f32) for i in range(channels)]
        signals = []
        for o in range(channels):
            total = field[o]
            for i in range(channels):
                total = total + mix_ref[o, i] * values[i]
            total = total + bias_ref[0, o]
            cdf = 0.5 * (1.0 + lax.erf(total * 0.7071067811865476))
            slope = cdf + total * jnp.exp(-0.5 * total * total) * 0.3989422804014327
            signals.append(cot_ref[o, x].astype(f32) * slope)
        field = field_of(back_ref, x)
        for o in range(channels):
            total = field[o]
            for i in range(channels):
                total = total + mix_ref[i, o] * signals[i]
            out_ref[o, x] = total.astype(bf16)
        return carry

    lax.fori_loop(0, xr, step, 0)


def ahead(activations, cotangent, got, got_back, mixing, bias, bzs, kyt):
    channels, xr, yr, zr = activations.shape
    vmem = pl.BlockSpec(memory_space=pltpu.VMEM)
    smem = pl.BlockSpec(memory_space=pltpu.SMEM)
    return pl.pallas_call(
        ahead_kernel,
        out_shape=jax.ShapeDtypeStruct(activations.shape, bf16),
        in_specs=[vmem] * 4 + [smem] * 2 + [vmem] * 2,
        out_specs=vmem,
        scratch_shapes=[pltpu.VMEM((xr * MODES, channels * yr), f32)] * 2,
        compiler_params=pltpu.CompilerParams(vmem_limit_bytes=50 * 2**20),
        cost_estimate=pl.CostEstimate(flops=10**9, bytes_accessed=10**7, transcendentals=10**6),
    )(activations, cotangent, got, got_back, mixing, bias, bzs, kyt)


def block_turn(back, nx, ny, collective, field, slope, weights, mixing, bias, tables):
    channels, xr, yr, zr = field.shape
    xp = -(-xr // 16) * 16
    cl, jl, n = MODES // nx, MODES // ny, nx * ny
    lanes = jl * channels
    vmem = pl.BlockSpec(memory_space=pltpu.VMEM)
    smem = pl.BlockSpec(memory_space=pltpu.SMEM)
    hbm = pl.BlockSpec(memory_space=pl.ANY)
    if back:
        args = (field, slope, weights, mixing, *tables)
        specs = [vmem, vmem, hbm, smem] + [vmem] * len(tables)
    else:
        args = (field, weights, mixing, bias, *tables)
        specs = [vmem, hbm, smem, smem] + [vmem] * len(tables)
    dma = pltpu.SemaphoreType.DMA
    return pl.pallas_call(
        functools.partial(kernel, back, nx, ny, xr),
        out_shape=(
            jax.ShapeDtypeStruct(field.shape, bf16 if back else f32),
            jax.ShapeDtypeStruct((cl, jl, channels, MODES), f32),
            jax.ShapeDtypeStruct((xr * MODES, ny * lanes), bf16),
        ),
        in_specs=specs,
        out_specs=(vmem, vmem, vmem),
        scratch_shapes=[
            pltpu.VMEM(weights.shape, f32),
            pltpu.VMEM(field.shape if back else (8, 128), f32),
            pltpu.VMEM((xr * MODES, channels * yr), bf16),
            pltpu.VMEM((xr * MODES, channels * yr), bf16),
            pltpu.VMEM((ny, nx, cl, xp, lanes), bf16),
            pltpu.VMEM((n, cl, xp, lanes), bf16),
            pltpu.VMEM((cl, jl, channels, MODES), f32),
            pltpu.VMEM((nx, cl, xp, lanes), bf16),
            pltpu.VMEM((n, cl, xp, lanes), bf16),
            pltpu.VMEM((xr * MODES, channels * yr), f32),
            dma((n,)), dma((n,)), dma((n,)), dma((n,)), dma,
        ],
        compiler_params=pltpu.CompilerParams(
            collective_id=collective, has_side_effects=True, vmem_limit_bytes=50 * 2**20
        ),
        cost_estimate=pl.CostEstimate(flops=10**9, bytes_accessed=2 * 10**7, transcendentals=10**6),
    )(*args)


def body(activations, cotangent, spectral_weights, pointwise, channel_bias):
    inputs = activations[0]
    channels, xr, yr, zr = inputs.shape
    nx, ny = lax.axis_size("gx"), lax.axis_size("gy")
    xp = -(-xr // 16) * 16
    bz = trig_basis(zr)
    bx = trig_basis(xr * nx).reshape(MODES, nx, xr)
    bx = np.concatenate([bx, np.zeros((MODES, nx, xp - xr))], axis=2).reshape(MODES, nx * xp)
    by = trig_basis(yr * ny).reshape(MODES, ny, yr)
    kron = np.einsum("jgy,ik->giyjk", by, np.eye(channels)).reshape(
        ny, channels * yr, MODES * channels
    )
    bzh = halves(bz)
    kh = halves(kron)
    gy = lax.axis_index("gy")
    ky = lax.dynamic_index_in_dim(jnp.asarray(np.swapaxes(kh, 0, 1)), gy, 0, False)
    kyt = lax.dynamic_index_in_dim(
        jnp.asarray(np.ascontiguousarray(np.transpose(kh, (1, 0, 3, 2)))), gy, 0, False
    )
    tables = (
        jnp.asarray(bzh),
        jnp.asarray(np.concatenate([bzh[0], bzh[0], bzh[1]], axis=0)),
        ky,
        kyt,
        jnp.asarray(halves(np.concatenate([bx] * ny, axis=1))),
        jnp.asarray(halves(bx.T)),
    )
    weights = spectral_weights[0]
    mixing = pointwise[0]
    following = [from_behind(v, "segment", -1) for v in (inputs, mixing, channel_bias)]
    slope, input_modes, got = block_turn(
        False, nx, ny, 0, inputs, None, weights, mixing, channel_bias, tables
    )
    next_got = from_behind(got, "segment", -1)
    segment_index = lax.axis_index("segment")
    segment_count = lax.axis_size("segment")
    incoming = cotangent
    kept_grad = jnp.zeros(cotangent.shape, bf16)
    kept_modes = jnp.zeros(input_modes.shape, f32)
    for turn_index in range(segment_count):
        active = segment_index == segment_count - 1 - turn_index
        input_grad, grad_modes, got_back = block_turn(
            True, nx, ny, 1 + turn_index, incoming, slope, weights, mixing, None, tables
        )
        kept_grad = jnp.where(active, input_grad, kept_grad)
        kept_modes = jnp.where(active, grad_modes, kept_modes)
        if turn_index == 0 and segment_count > 1:
            next_back = from_behind(got_back, "segment", -1)
            incoming = ahead(
                following[0], cotangent, next_got, next_back, following[1], following[2],
                tables[1], tables[3],
            )
        elif turn_index + 1 < segment_count:
            incoming = from_behind(input_grad, "segment", -1)
    input_modes = jnp.swapaxes(input_modes, 0, 1)
    kept_modes = jnp.swapaxes(kept_modes, 0, 1)
    weight_grad = input_modes[:, :, :, None, :] * kept_modes[:, :, None, :, :]
    return (kept_grad[None], weight_grad[None])


def slope_of(value):
    cdf = 0.5 * (1.0 + lax.erf(value * 0.7071067811865476))
    return cdf + value * jnp.exp(-0.5 * value * value) * 0.3989422804014327


def field_of(cells, ny, ky, bzi):
    blocks = []
    for h in range(ny):
        block = cells(h)
        blocks.append(block.reshape(block.shape[0] * block.shape[1], block.shape[2]))
    block = jnp.concatenate(blocks, axis=1)
    top, rest = split(dot(ky[0], block, 1, 1) + dot(ky[1], block, 1, 1))
    return dot(jnp.concatenate([top, rest, top], axis=1), bzi[...])


def relay_kernel(
    nx, ny, xq, cuts,
    act_hbm, cot_hbm, w_hbm, mix_ref, bias_ref, mix_hbm, bias_hbm,
    kyt_hbm, ky_hbm, bzf_hbm, bzi_hbm, bx_hbm, sp_hbm,
    out, rest_ref, cells_ref, wgrad, ky, bzi,
    act, act1, cot, w, wd, kyt, bzf, bx, sp,
    u, v, slope, sig, in_modes, grad_modes, m_ref, mt_send, mt_recv,
    mixv1, biasv1, mix1, bias1, s_ref, p_ref, r_ref,
    load_sem, send_sem, recv_sem, row_send, row_recv, small_send, small_recv, store_sem,
    tail_send, tail_recv, pair_send, pair_recv, across_send,
):
    channels, xr, yr, zr = act.shape
    n = nx * ny
    cl, jl = MODES // nx, MODES // ny
    nh, hq = r_ref.shape[1], r_ref.shape[3]
    lanes = jl * channels
    rows = channels * yr
    tail = xr - hq * xq
    late = xr - xq
    gx, gy, seg = lax.axis_index("gx"), lax.axis_index("gy"), lax.axis_index("segment")
    me = gx * ny + gy
    mine = gy * nx + gx
    first, last = seg == 0, seg == 1
    mesh_ids = pl.DeviceIdType.MESH

    loads = [
        pltpu.make_async_copy(source, target, load_sem.at[k])
        for k, (source, target) in enumerate(
            [
                (act_hbm, act), (bzf_hbm, bzf), (kyt_hbm.at[gy], kyt), (w_hbm, w), (bx_hbm, bx),
                (sp_hbm, sp), (ky_hbm.at[gy], ky), (bzi_hbm, bzi), (cot_hbm, cot),
            ]
        )
    ]
    for load in loads[:3]:
        load.start()

    barrier = pltpu.get_barrier_semaphore()

    def greet(k, carry):
        other = lax.rem(seg * n + me + k, 2 * n)
        peer = lax.rem(other, n)
        pl.semaphore_signal(
            barrier, inc=1,
            device_id={"segment": other // n, "gx": peer // ny, "gy": lax.rem(peer, ny)},
            device_id_type=mesh_ids,
        )
        return carry

    lax.fori_loop(1, 2 * n, greet, 0)

    def ahead(source, target, send, recv):
        return pltpu.make_async_remote_copy(
            src_ref=source, dst_ref=target, send_sem=send, recv_sem=recv,
            device_id={"segment": 1 - seg}, device_id_type=mesh_ids,
        )

    def row_copy(x):
        return ahead(act_hbm.at[:, x], act1.at[:, x], row_send.at[x], row_recv.at[x])

    def send_rows(start, stop):
        for x in range(start, stop):
            row_copy(x).start()

    def modes_copy(k):
        return ahead(mt_send.at[k], mt_recv.at[k], small_send.at[k], small_recv.at[k])

    small = [
        ahead(mix_hbm, mixv1, small_send.at[2], small_recv.at[2]),
        ahead(bias_hbm, biasv1, small_send.at[3], small_recv.at[3]),
    ]

    def send(source, target, sends, receives):
        def begin(k, carry):
            peer = lax.rem(me + k, n)
            d, h = peer // ny, lax.rem(peer, ny)
            pltpu.make_async_remote_copy(
                src_ref=source(d, h), dst_ref=target, send_sem=sends, recv_sem=receives,
                device_id={"gx": d, "gy": h}, device_id_type=mesh_ids,
            ).start()
            return carry

        lax.fori_loop(1, n, begin, 0)
        target[...] = source(gx, gy)[...]

    def send_half(source, e, half):
        send(source, r_ref.at[e, half, mine], send_sem.at[e, half], recv_sem.at[e, half])

    def send_along(source, e, half):
        def begin(k, carry):
            d = lax.rem(gx + k, nx)
            pltpu.make_async_remote_copy(
                src_ref=source(d), dst_ref=r_ref.at[e, half, mine],
                send_sem=send_sem.at[e, half], recv_sem=recv_sem.at[e, half],
                device_id={"gx": d}, device_id_type=mesh_ids,
            ).start()
            return carry

        lax.fori_loop(1, nx, begin, 0)
        r_ref[e, half, mine] = source(gx)[...]

    def send_across(half):
        def begin(k, carry):
            d = lax.rem(gx + k, nx)
            pltpu.make_async_remote_copy(
                src_ref=p_ref.at[1, half, d], dst_ref=r_ref.at[3, half, mine],
                send_sem=across_send.at[half], recv_sem=recv_sem.at[3, half],
                device_id={"segment": 0, "gx": d}, device_id_type=mesh_ids,
            ).start()
            return carry

        lax.fori_loop(0, nx, begin, 0)

    def pair_copy(e, half):
        block = r_ref.at[e, half, pl.ds(gy * nx, nx)]
        return pltpu.make_async_remote_copy(
            src_ref=block, dst_ref=block,
            send_sem=pair_send.at[e, half], recv_sem=pair_recv.at[e, half],
            device_id={"gy": 1 - gy}, device_id_type=mesh_ids,
        )

    def forward(e, halves):
        for half in halves:
            await_block(r_ref.at[e, half, pl.ds(0, nx - 1)], recv_sem.at[e, half])
            pair_copy(e, half).start()

    def forward_across(half):
        await_block(r_ref.at[3, half, pl.ds(0, nx)], recv_sem.at[3, half])
        pair_copy(3, half).start()

    def land(e, half):
        await_block(r_ref.at[e, half, pl.ds(0, nx)], pair_recv.at[e, half])

    def sent_along(e, half):
        await_block(r_ref.at[e, half, pl.ds(0, nx - 1)], send_sem.at[e, half])
        await_block(r_ref.at[e, half, pl.ds(0, nx)], pair_send.at[e, half])

    def send_tail(k, carry):
        peer = lax.rem(me + k, n)
        d, h = peer // ny, lax.rem(peer, ny)
        pltpu.make_async_remote_copy(
            src_ref=s_ref.at[2, nh - 1, h * nx + d], dst_ref=r_ref.at[4, nh - 1, mine],
            send_sem=tail_send.at[0], recv_sem=tail_recv.at[0],
            device_id={"segment": 0, "gx": d, "gy": h}, device_id_type=mesh_ids,
        ).start()
        return carry

    def await_block(block, sem):
        pltpu.make_async_copy(block, block, sem).wait()

    def arrive(e, half):
        await_block(r_ref.at[e, half, pl.ds(0, n - 1)], recv_sem.at[e, half])

    def sent(e, half):
        await_block(r_ref.at[e, half, pl.ds(0, n - 1)], send_sem.at[e, half])

    def to_modes(blocks, k, half):
        parts = []
        for block in blocks:
            g = dot(block, bzf[...])
            parts.append(g[:, : nx * 16] + g[:, nx * 16 :])
        top, rest = split(jnp.concatenate(parts, axis=1))
        t = dot(kyt[0], top) + dot(kyt[1], top) + dot(kyt[0], rest)
        t = t.T.astype(bf16)
        for q in range(len(blocks)):
            for h in range(ny):
                part = t[q * nx * 16 : (q + 1) * nx * 16, h * lanes : (h + 1) * lanes]
                s_ref[k, half, h * nx : (h + 1) * nx, q] = part.reshape(nx, 16, lanes)

    def to_field(e, half, q):
        return field_of(lambda h: r_ref[e, half, h * nx : (h + 1) * nx, q], ny, ky, bzi)

    def row(field, x):
        return field[:, x * zr : (x + 1) * zr].reshape(channels, yr, zr)

    def stash(e, half, target):
        def step(q, carry):
            field = to_field(e, half, q)
            x0 = (half * hq + q) * xq
            for k in range(xq):
                target[:, x0 + k] = row(field, k)
            return carry

        lax.fori_loop(0, hq, step, 0)

    def ahead_rows(start, stop):
        def step(x, carry):
            row_copy(x).wait_recv()
            values = [act1[i, x].astype(f32) for i in range(channels)]
            signals = []
            for o in range(channels):
                pre = v[o, x] + blend(mix1, values, o, False) + bias1[0, o]
                signals.append(cot[o, x].astype(f32) * slope_of(pre))
            for i in range(channels):
                v[i, x] = blend(mix1, signals, i, True)
            return carry

        lax.fori_loop(start, stop, step, 0)

    def send_modes(k, e, half):
        send_half(lambda d, h: s_ref.at[k, half, h * nx + d], e, half)

    def own_modes(e, await_half):
        own = None
        for half in range(nh):
            await_half(half)
            block = r_ref[e, half].reshape(n * hq * 16, lanes)
            part = slice(half * n * hq * 16, (half + 1) * n * hq * 16)
            term = dot(bx[0, :, part], block) + dot(bx[1, :, part], block)
            own = term if own is None else own + term
        return own.T.reshape(jl, channels, cl * MODES)

    def spread(mt, k, half):
        top, rest = split(mt)
        table = [sp[i, half].reshape(nx * hq * 16, cl * MODES) for i in range(2)]
        cells = dot(table[0], top) + dot(table[1], top) + dot(table[0], rest)
        p_ref[k, half] = cells.astype(bf16).reshape(nx, hq, 16, lanes)

    def send_spread(k, e, half):
        send_along(lambda d: p_ref.at[k, half, d], e, half)

    def send_cells(mt, k, e, halves):
        for half in halves:
            spread(mt, k, half)
            send_spread(k, e, half)

    def mixed():
        return m_ref[...].reshape(lanes, cl * MODES).T

    def mix_back(e, await_half):
        grad_modes[...] = own_modes(e, await_half)

        def step(j, carry):
            m_ref[j] = jnp.sum(wd[j] * grad_modes[j][None], axis=1)
            return carry

        lax.fori_loop(0, jl, step, 0)

    def blend(mixing, values, o, back):
        total = (mixing[0, o] if back else mixing[o, 0]) * values[0]
        for i in range(1, channels):
            total = total + (mixing[i, o] if back else mixing[o, i]) * values[i]
        return total

    def fetch_small():
        for copy in small:
            copy.wait_recv()
        for k, (source, target) in enumerate([(mixv1, mix1), (biasv1, bias1)]):
            copy = pltpu.make_async_copy(source, target, store_sem.at[k])
            copy.start()
            copy.wait()

    def back_block(half, q, offset):
        field = to_field(3, half, q)
        x0 = (half * hq + q) * xq
        block = []
        for k in range(xq):
            incoming = (row(field, k) + offset[:, x0 + k]).astype(bf16).astype(f32)
            signal = incoming * slope[:, x0 + k]
            block.append((x0 + k, signal))
        return block

    def packed(block):
        return jnp.concatenate([s.astype(bf16).reshape(rows, zr) for _, s in block], axis=1)

    def blend_back(start, stop):
        def step(x, carry):
            values = [sig[i, x] for i in range(channels)]
            for o in range(channels):
                u[o, x] = blend(mix_ref, values, o, True)
            return carry

        lax.fori_loop(start, stop, step, 0)

    pl.semaphore_wait(barrier, 2 * n - 1)
    for copy in small:
        copy.start()

    @pl.when(last)
    def _():
        send_rows(0, cuts[0])

    @pl.when(first)
    def _():
        send_rows(tail, tail + cuts[0])

    for load in loads[:3]:
        load.wait()
    for load in loads[3:]:
        load.start()
    for half in range(nh):
        blocks = []
        for q in range(hq):
            x = (half * hq + q) * xq
            block = [act[:, x + k].reshape(rows, zr) for k in range(xq)]
            blocks.append(jnp.concatenate(block, axis=1))
        to_modes(blocks, 0, half)
        send_modes(0, 0, half)

    for load in loads[3:]:
        load.wait()

    def dense(j, carry):
        for i in range(channels):
            wd[j, i] = jnp.concatenate([w[j, c, i] for c in range(cl)], axis=1)
        return carry

    lax.fori_loop(0, jl, dense, 0)

    def pointwise(x, carry):
        values = [act[i, x].astype(f32) for i in range(channels)]
        for o in range(channels):
            u[o, x] = blend(mix_ref, values, o, False) + bias_ref[0, o]
        return carry

    lax.fori_loop(0, xr, pointwise, 0)

    in_modes[...] = own_modes(0, lambda half: arrive(0, half))

    def mix(j, carry):
        own = in_modes[j]
        m_ref[j] = jnp.sum(wd[j] * own[:, None, :], axis=0)
        return carry

    lax.fori_loop(0, jl, mix, 0)
    mt_send[0] = mixed()
    modes_copy(0).start()

    @pl.when(last)
    def _():
        send_rows(cuts[0], cuts[1])

    @pl.when(first)
    def _():
        send_rows(tail + cuts[0], xr)

    send_cells(mt_send[0], 0, 1, range(nh))

    @pl.when(last)
    def _():
        forward(1, range(nh))
        for half in range(nh):
            land(1, half)
            stash(1, half, sig)

            def step(x, carry):
                sig[:, x] = cot[:, x].astype(f32) * slope_of(sig[:, x] + u[:, x])
                return carry

            lax.fori_loop(half * hq * xq, (half + 1) * hq * xq, step, 0)
            blocks = []
            for q in range(hq):
                x0 = (half * hq + q) * xq
                block = [sig[:, x0 + k].astype(bf16).reshape(rows, zr) for k in range(xq)]
                blocks.append(jnp.concatenate(block, axis=1))
            to_modes(blocks, 1, half)
            send_modes(1, 2, half)
            if half == 0:
                modes_copy(0).wait_recv()
                send_cells(mt_recv[0], 3, 5, [nh - 1])

        fetch_small()
        forward(5, [nh - 1])
        land(5, nh - 1)
        stash(5, nh - 1, v)

        mix_back(2, lambda half: arrive(2, half))
        mt_send[1] = mixed()
        for half in range(nh - 1):
            spread(mt_send[1], 1, half)
            send_across(half)
        send_rows(cuts[1], cuts[2])
        spread(mt_send[1], 1, nh - 1)
        for half in reversed(range(nh)):
            send_spread(1, 3, half)

        blend_back(tail, xr)

        def step(x, carry):
            row_copy(x).wait_recv()
            values = [act1[i, x].astype(f32) for i in range(channels)]
            for o in range(channels):
                pre = v[o, x] + blend(mix1, values, o, False) + bias1[0, o]
                slope[o, x] = slope_of(pre)
            return carry

        lax.fori_loop(tail, xr, step, 0)
        forward(3, reversed(range(nh)))
        land(3, nh - 1)
        to_modes([packed(back_block(nh - 1, q, u)) for q in range(hq)], 2, nh - 1)
        lax.fori_loop(0, n, send_tail, 0)
        send_across(nh - 1)
        send_rows(cuts[2], xr)
        blend_back(0, tail)

    def kept(block):
        for x, signal in block:
            sig[:, x] = signal
        return block

    @pl.when(first)
    def _():
        modes_copy(0).wait_recv()
        send_cells(mt_recv[0], 1, 2, range(nh))
        fetch_small()
        forward(1, range(nh))
        for half in range(nh):
            land(1, half)
            stash(1, half, slope)

            def step(x, carry):
                slope[:, x] = slope_of(slope[:, x] + u[:, x])
                return carry

            lax.fori_loop(half * hq * xq, (half + 1) * hq * xq, step, 0)

        forward(2, range(nh))
        for half in range(nh):
            land(2, half)
        for half in range(nh - 1):
            stash(2, half, v)
        ahead_rows(0, tail)
        for half in range(nh - 1):
            forward_across(half)
            land(3, half)
            to_modes([packed(kept(back_block(half, q, v))) for q in range(hq)], 1, half)
            send_modes(1, 4, half)
        blend_back(0, tail)
        stash(2, nh - 1, v)
        ahead_rows(tail, late)

        def await_half(half):
            if half < nh - 1:
                arrive(4, half)
            else:
                await_block(r_ref.at[4, half], tail_recv.at[0])

        mix_back(4, await_half)
        send_cells(mixed(), 3, 5, range(nh))
        forward_across(nh - 1)
        land(3, nh - 1)
        for q in range(hq - 1):
            kept(back_block(nh - 1, q, v))
        if hq > 1:
            blend_back(tail, late)
        field = to_field(3, nh - 1, hq - 1)
        for k in range(xq):
            u[:, late + k] = row(field, k)

    def weight_grad(j, carry):
        for c in range(cl):
            part = slice(c * MODES, (c + 1) * MODES)
            wgrad[j, c] = in_modes[j][:, None, part] * grad_modes[j][None, :, part]
        return carry

    lax.fori_loop(0, jl, weight_grad, 0)
    e = 3 + 2 * (1 - seg)

    @pl.when(last)
    def _():
        for half in range(nh - 1):
            land(3, half)

    @pl.when(first)
    def _():
        forward(5, range(nh))
        for half in range(nh - 1):
            land(5, half)

    def finish(q, carry):
        field = to_field(e, q // hq, lax.rem(q, hq))
        for k in range(xq):
            out[:, q * xq + k] = (row(field, k) + u[:, q * xq + k]).astype(bf16)
        return carry

    lax.fori_loop(0, (nh - 1) * hq, finish, 0)

    @pl.when(first)
    def _():
        land(5, nh - 1)
        rest_ref[:, : late - tail] = u[:, tail:late]

    cells_ref[...] = r_ref[e, nh - 1]

    @pl.when(first)
    def _():
        def step(k, carry):
            x = late + k
            row_copy(x).wait_recv()
            values = [act1[i, x].astype(f32) for i in range(channels)]
            signals = []
            for o in range(channels):
                pre = v[o, x] + blend(mix1, values, o, False) + bias1[0, o]
                signals.append(cot[o, x].astype(f32) * slope_of(pre))
            here = []
            for i in range(channels):
                incoming = u[i, x] + blend(mix1, signals, i, True)
                here.append(incoming.astype(bf16).astype(f32) * slope[i, x])
            for o in range(channels):
                rest_ref[o, late - tail + k] = blend(mix_ref, here, o, True)
            return carry

        lax.fori_loop(0, xq, step, 0)

    @pl.when(last)
    def _():
        rest_ref[...] = u[:, tail:]

    for half in range(nh):
        sent(0, half)
        sent_along(1, half)
        await_block(r_ref.at[3, half, pl.ds(0, nx)], pair_send.at[3, half])
    for copy in small:
        copy.wait_send()
    modes_copy(0).wait_send()

    @pl.when(first)
    def _():
        for half in range(nh - 1):
            sent(4, half)
        for half in range(nh):
            sent_along(2, half)
            sent_along(5, half)
        for x in range(tail, xr):
            row_copy(x).wait_send()

    @pl.when(last)
    def _():
        for half in range(nh):
            sent(2, half)
            await_block(r_ref.at[3, half, pl.ds(0, nx - 1)], send_sem.at[3, half])
            await_block(r_ref.at[3, half, pl.ds(0, nx)], across_send.at[half])
        sent_along(5, nh - 1)
        await_block(r_ref.at[4, nh - 1], tail_send.at[0])
        for x in range(xr):
            row_copy(x).wait_send()


def finish_kernel(
    nx, ny, xq, done_ref, rest_ref, cells_ref, wgrad, ky, bzi, grad_hbm, wgrad_hbm, out, sem
):
    channels, done, yr, zr = done_ref.shape
    hq = cells_ref.shape[1]
    stores = [
        pltpu.make_async_copy(wgrad, wgrad_hbm, sem.at[0]),
        pltpu.make_async_copy(done_ref, grad_hbm.at[:, pl.ds(0, done)], sem.at[1]),
    ]
    for store in stores:
        store.start()
    for q in range(hq):
        field = field_of(lambda h: cells_ref[h * nx : (h + 1) * nx, q], ny, ky, bzi)
        for k in range(xq):
            x = q * xq + k
            here = field[:, k * zr : (k + 1) * zr].reshape(channels, yr, zr)
            out[:, x] = (here + rest_ref[:, x]).astype(bf16)
        part = pl.ds(q * xq, xq)
        store = pltpu.make_async_copy(
            out.at[:, part], grad_hbm.at[:, pl.ds(done + q * xq, xq)], sem.at[2 + q]
        )
        store.start()
        stores.append(store)
    for store in stores:
        store.wait()


def in_hbm(value):
    return pltpu.with_memory_space_constraint(jnp.asarray(value), pltpu.HBM)


def two_section_body(activations, cotangent, spectral_weights, pointwise, channel_bias):
    inputs = activations[0]
    channels, xr, yr, zr = inputs.shape
    nx, ny = lax.axis_size("gx"), lax.axis_size("gy")
    n = nx * ny
    cl, jl = MODES // nx, MODES // ny
    xq = 16 // cl
    nh = 2
    hq = xr // (nh * xq)
    lanes, rows = jl * channels, channels * yr
    bz = trig_basis(zr).reshape(nx, cl, zr)
    eye_x, eye_c = np.eye(xq), np.eye(cl)
    bzf = np.einsum("dcz,xX->xzdXc", bz, eye_x).reshape(xq * zr, nx * 16)
    bzi = halves(bzf.reshape(xq, zr, nx * 16).transpose(2, 0, 1).reshape(nx * 16, xq * zr))
    by = trig_basis(yr * ny).reshape(MODES, ny, yr)
    ky = np.einsum("jgy,ik->giyjk", by, np.eye(channels)).reshape(ny, rows, ny * lanes)
    ky = halves(ky)
    bx = trig_basis(xr * nx).reshape(MODES, nx, nh, hq, xq)
    sp = np.einsum("adtqx,cC->tdqxCca", bx, eye_c).reshape(nh * nx * hq * 16, cl * MODES)
    bxf = np.broadcast_to(
        sp.reshape(nh, 1, nx * hq * 16, cl * MODES), (nh, ny, nx * hq * 16, cl * MODES)
    )
    bxf = bxf.reshape(nh * n * hq * 16, cl * MODES).T
    bzf = halves(bzf)
    tables = [
        np.ascontiguousarray(ky.transpose(1, 0, 3, 2)),
        np.ascontiguousarray(ky.transpose(1, 0, 2, 3)),
        np.concatenate([bzf[0], bzf[1]], axis=1),
        np.concatenate([bzi[0], bzi[0], bzi[1]], axis=0),
        halves(bxf),
        halves(sp).reshape(2, nh, nx, hq, 16, cl * MODES),
    ]
    weights, mixing = spectral_weights[0], pointwise[0]
    vmem = pl.BlockSpec(memory_space=pltpu.VMEM)
    smem = pl.BlockSpec(memory_space=pltpu.SMEM)
    hbm = pl.BlockSpec(memory_space=pl.ANY)
    dma = pltpu.SemaphoreType.DMA
    grid = inputs.shape
    done = grid[:1] + ((nh - 1) * hq * xq,) + grid[2:]
    left = grid[:1] + (hq * xq,) + grid[2:]
    scratch = [
        pltpu.VMEM(grid, bf16), pltpu.VMEM(grid, bf16), pltpu.VMEM(grid, bf16),
        pltpu.VMEM(weights.shape, f32),
        pltpu.VMEM((jl, channels, channels, cl * MODES), f32),
        pltpu.VMEM((2, ny * lanes, rows), bf16),
        pltpu.VMEM((xq * zr, 2 * nx * 16), bf16),
        pltpu.VMEM((2, cl * MODES, nh * n * hq * 16), bf16),
        pltpu.VMEM((2, nh, nx, hq, 16, cl * MODES), bf16),
        pltpu.VMEM(grid, f32), pltpu.VMEM(grid, f32), pltpu.VMEM(grid, f32), pltpu.VMEM(grid, f32),
        pltpu.VMEM((jl, channels, cl * MODES), f32),
        pltpu.VMEM((jl, channels, cl * MODES), f32),
        pltpu.VMEM((jl, channels, cl * MODES), f32),
        pltpu.VMEM((2, cl * MODES, lanes), f32),
        pltpu.VMEM((2, cl * MODES, lanes), f32),
        pltpu.VMEM(mixing.shape, f32), pltpu.VMEM(channel_bias.shape, f32),
        pltpu.SMEM(mixing.shape, f32), pltpu.SMEM(channel_bias.shape, f32),
        pltpu.VMEM((3, nh, n, hq, 16, lanes), bf16),
        pltpu.VMEM((4, nh, nx, hq, 16, lanes), bf16),
        pltpu.VMEM((6, nh, n, hq, 16, lanes), bf16),
        dma((9,)), dma((6, nh)), dma((6, nh)),
        dma((xr,)), dma((xr,)), dma((4,)), dma((4,)), dma((2,)), dma((1,)), dma((1,)), dma((6, nh)), dma((6, nh)), dma((nh,)),
    ]
    parts = pl.pallas_call(
        functools.partial(relay_kernel, nx, ny, xq, (4, 10, 12)),
        out_shape=(
            jax.ShapeDtypeStruct(done, bf16),
            jax.ShapeDtypeStruct(left, f32),
            jax.ShapeDtypeStruct((n, hq, 16, lanes), bf16),
            pltpu.VMEM(weights.shape, f32),
            jax.ShapeDtypeStruct((2, rows, ny * lanes), bf16),
            jax.ShapeDtypeStruct((3 * nx * 16, xq * zr), bf16),
        ),
        in_specs=[hbm, hbm, hbm, smem, smem] + [hbm] * (2 + len(tables)),
        out_specs=[vmem] * 6,
        scratch_shapes=scratch,
        compiler_params=pltpu.CompilerParams(
            collective_id=0, has_side_effects=True, vmem_limit_bytes=46 * 2**20
        ),
        cost_estimate=pl.CostEstimate(
            flops=4 * 10**9, bytes_accessed=2 * 10**7, transcendentals=10**7
        ),
    )(
        *[in_hbm(v) for v in (inputs, cotangent, weights)],
        mixing, channel_bias,
        *[in_hbm(v) for v in [mixing, channel_bias] + tables],
    )
    input_grad, weight_grad = pl.pallas_call(
        functools.partial(finish_kernel, nx, ny, xq),
        out_shape=(
            jax.ShapeDtypeStruct(grid, bf16),
            jax.ShapeDtypeStruct(weights.shape, f32),
        ),
        in_specs=[vmem] * 6,
        out_specs=(hbm, hbm),
        scratch_shapes=[pltpu.VMEM(left, bf16), dma((2 + hq,))],
        compiler_params=pltpu.CompilerParams(vmem_limit_bytes=24 * 2**20),
        cost_estimate=pl.CostEstimate(flops=10**9, bytes_accessed=10**7, transcendentals=0),
    )(*parts)
    return (input_grad[None], weight_grad[None])


def fits(mesh):
    nx = mesh.shape["gx"]
    return mesh.shape["segment"] == 2 and mesh.shape["gy"] == 2 and nx == 8


def solution(mesh):
    return jax.shard_map(
        two_section_body if fits(mesh) else body,
        mesh=mesh,
        in_specs=(
            P("segment", "groups", "gx", "gy", None),
            P("groups", "gx", "gy", None),
            P("segment", "gy", "gx", None, None, None),
            P("segment", None, None),
            P("segment", None),
        ),
        out_specs=(
            P("segment", "groups", "gx", "gy", None),
            P("segment", "gy", "gx", "groups", None, None),
        ),
        check_vma=False,
    )
```

```python
import functools
import math

import jax
import jax.numpy as jnp
import ml_dtypes
import numpy as np
from jax import lax
from jax.experimental import pallas as pl
from jax.experimental.pallas import tpu as pltpu
from jax.sharding import PartitionSpec as P

MODES = 32
f32, bf16 = jnp.float32, jnp.bfloat16


def from_behind(block, axis, distance):
    devices = range(lax.axis_size(axis))
    route = [(i - distance, i) for i in devices if i - distance in devices]
    return lax.ppermute(block, axis, route)


def trig_basis(length):
    half = MODES // 2
    freqs = np.arange(half)[:, None]
    points = np.arange(length)[None, :]
    step = 2.0 * math.pi / length
    rows = np.concatenate(
        [np.cos((freqs * points % length) * step), np.sin(((freqs + 1) * points % length) * step)]
    )
    scales = np.where(np.arange(MODES) == 0, 1.0 / math.sqrt(length), math.sqrt(2.0 / length))
    return rows * scales[:, None]


def halves(matrix):
    matrix = np.asarray(matrix, np.float32)
    top = matrix.astype(ml_dtypes.bfloat16)
    rest = (matrix - top.astype(np.float32)).astype(ml_dtypes.bfloat16)
    return np.stack([top, rest])


def split(value):
    top = value.astype(bf16)
    return top, (value - top.astype(f32)).astype(bf16)


def dot(a, b, ca=1, cb=0):
    return lax.dot_general(a, b, (((ca,), (cb,)), ((), ())), preferred_element_type=f32)


def kernel(
    back, nx, ny, xr, *refs
):
    if back:
        (inc_ref, slope_ref, w_hbm, mix_ref, bz_ref, bzs_ref, ky_ref, kyt_ref, bx_ref, bxr_ref,
         out_ref, modes_ref, got_ref, *scratch) = refs
    else:
        (inc_ref, w_hbm, mix_ref, bias_ref, bz_ref, bzs_ref, ky_ref, kyt_ref, bx_ref, bxr_ref,
         out_ref, modes_ref, got_ref, *scratch) = refs
    (w_ref, sig_ref, ghi_ref, glo_ref, s_ref, r_ref, m_ref, p_ref, q_ref, qs_ref,
     send1, recv1, send2, recv2, wsem) = scratch
    channels, _, yr, zr = inc_ref.shape
    cl, jl, xp = MODES // nx, MODES // ny, r_ref.shape[2]
    n = nx * ny
    lanes = jl * channels
    gx, gy = lax.axis_index("gx"), lax.axis_index("gy")
    me = gx * ny + gy

    wcopy = pltpu.make_async_copy(w_hbm, w_ref, wsem)
    wcopy.start()

    barrier = pltpu.get_barrier_semaphore()

    def greet(k, carry):
        peer = lax.rem(me + k, n)
        pl.semaphore_signal(
            barrier, inc=1,
            device_id={"gx": peer // ny, "gy": lax.rem(peer, ny)},
            device_id_type=pl.DeviceIdType.MESH,
        )
        return carry

    lax.fori_loop(1, n, greet, 0)

    def along_z(x, carry):
        if back:
            signal = inc_ref[:, x].astype(f32) * slope_ref[:, x]
            sig_ref[:, x] = signal
            block = signal.astype(bf16)
        else:
            block = inc_ref[:, x]
        block = block.reshape(channels * yr, zr)
        g = dot(bz_ref[0], block, 1, 1) + dot(bz_ref[1], block, 1, 1)
        ghi, glo = split(g)
        rows = pl.ds(pl.multiple_of(x * MODES, MODES), MODES)
        ghi_ref[rows, :] = ghi
        glo_ref[rows, :] = glo
        return carry

    lax.fori_loop(0, xr, along_z, 0)
    ghi = ghi_ref[...]
    t = dot(ghi, ky_ref[0]) + dot(ghi, ky_ref[1]) + dot(glo_ref[...], ky_ref[0])
    t = jnp.swapaxes(t.reshape(xr, MODES, ny * lanes), 0, 1)
    if xp > xr:
        t = jnp.concatenate([t, jnp.zeros((MODES, xp - xr, ny * lanes), f32)], axis=1)
    t = t.astype(bf16)
    for h in range(ny):
        s_ref[h] = t[:, :, h * lanes : (h + 1) * lanes].reshape(nx, cl, xp, lanes)

    pl.semaphore_wait(barrier, n - 1)

    def exchange(source, target, send, recv):
        def copy_to(peer, slot_of):
            return pltpu.make_async_remote_copy(
                src_ref=source(peer // ny, lax.rem(peer, ny)),
                dst_ref=target.at[lax.rem(slot_of, ny) * nx + slot_of // ny],
                send_sem=send.at[peer],
                recv_sem=recv.at[slot_of],
                device_id={"gx": peer // ny, "gy": lax.rem(peer, ny)},
                device_id_type=pl.DeviceIdType.MESH,
            )

        def begin(k, carry):
            copy_to(lax.rem(me + k, n), me).start()
            return carry

        def finish(k, carry):
            copy_to(lax.rem(me + k, n), me).wait_send()
            peer = lax.rem(me + n - k, n)
            copy_to(peer, peer).wait_recv()
            return carry

        lax.fori_loop(1, n, begin, 0)
        target[gy * nx + gx] = source(gx, gy)[...]
        lax.fori_loop(1, n, finish, 0)

    exchange(lambda d, h: s_ref.at[h, d], r_ref, send1, recv1)

    for c in range(cl):
        part = r_ref[:, c].reshape(n * xp, lanes)
        own = dot(bx_ref[0], part) + dot(bx_ref[1], part)
        modes_ref[c] = own.T.reshape(jl, channels, MODES)
    wcopy.wait()

    def mix(j, carry):
        for c in range(cl):
            own = modes_ref[c, j]
            weight = w_ref[j, c]
            if back:
                m_ref[c, j] = jnp.sum(weight * own[None], axis=1)
            else:
                m_ref[c, j] = jnp.sum(weight * own[:, None, :], axis=0)
        return carry

    lax.fori_loop(0, jl, mix, 0)
    for c in range(cl):
        top, rest = split(m_ref[c].reshape(lanes, MODES))
        spread = (
            dot(bxr_ref[0], top, 1, 1) + dot(bxr_ref[1], top, 1, 1) + dot(bxr_ref[0], rest, 1, 1)
        )
        p_ref[:, c] = spread.astype(bf16).reshape(nx, xp, lanes)

    exchange(lambda d, h: p_ref.at[d], q_ref, send2, recv2)

    got = [q_ref[h * nx : (h + 1) * nx].reshape(MODES, xp, lanes) for h in range(ny)]
    got = jnp.concatenate(got, axis=2).astype(f32)
    got = jnp.swapaxes(got, 0, 1)[:xr].reshape(xr * MODES, ny * lanes).astype(bf16)
    got_ref[...] = got
    qs_ref[...] = dot(got, kyt_ref[0]) + dot(got, kyt_ref[1])

    def finish_field(x, carry):
        rows = pl.ds(pl.multiple_of(x * MODES, MODES), MODES)
        top, rest = split(qs_ref[rows, :])
        stack = jnp.concatenate([top, rest, top], axis=0)
        field = dot(stack, bzs_ref[...], 0, 0).reshape(channels, yr, zr)
        if back:
            values = [sig_ref[i, x] for i in range(channels)]
        else:
            values = [inc_ref[i, x].astype(f32) for i in range(channels)]
        for o in range(channels):
            total = field[o]
            for i in range(channels):
                total = total + (mix_ref[i, o] if back else mix_ref[o, i]) * values[i]
            if back:
                out_ref[o, x] = total.astype(bf16)
            else:
                total = total + bias_ref[0, o]
                cdf = 0.5 * (1.0 + lax.erf(total * 0.7071067811865476))
                out_ref[o, x] = cdf + total * jnp.exp(-0.5 * total * total) * 0.3989422804014327
        return carry

    lax.fori_loop(0, xr, finish_field, 0)


def ahead_kernel(
    act_ref, cot_ref, got_ref, got_back_ref, mix_ref, bias_ref, bzs_ref, kyt_ref, out_ref,
    pre_ref, back_ref,
):
    channels, xr, yr, zr = act_ref.shape
    pre_ref[...] = dot(got_ref[...], kyt_ref[0]) + dot(got_ref[...], kyt_ref[1])
    back_ref[...] = dot(got_back_ref[...], kyt_ref[0]) + dot(got_back_ref[...], kyt_ref[1])

    def field_of(ref, x):
        rows = pl.ds(pl.multiple_of(x * MODES, MODES), MODES)
        top, rest = split(ref[rows, :])
        stack = jnp.concatenate([top, rest, top], axis=0)
        return dot(stack, bzs_ref[...], 0, 0).reshape(channels, yr, zr)

    def step(x, carry):
        field = field_of(pre_ref, x)
        values = [act_ref[i, x].astype(f32) for i in range(channels)]
        signals = []
        for o in range(channels):
            total = field[o]
            for i in range(channels):
                total = total + mix_ref[o, i] * values[i]
            total = total + bias_ref[0, o]
            cdf = 0.5 * (1.0 + lax.erf(total * 0.7071067811865476))
            slope = cdf + total * jnp.exp(-0.5 * total * total) * 0.3989422804014327
            signals.append(cot_ref[o, x].astype(f32) * slope)
        field = field_of(back_ref, x)
        for o in range(channels):
            total = field[o]
            for i in range(channels):
                total = total + mix_ref[i, o] * signals[i]
            out_ref[o, x] = total.astype(bf16)
        return carry

    lax.fori_loop(0, xr, step, 0)


def ahead(activations, cotangent, got, got_back, mixing, bias, bzs, kyt):
    channels, xr, yr, zr = activations.shape
    vmem = pl.BlockSpec(memory_space=pltpu.VMEM)
    smem = pl.BlockSpec(memory_space=pltpu.SMEM)
    return pl.pallas_call(
        ahead_kernel,
        out_shape=jax.ShapeDtypeStruct(activations.shape, bf16),
        in_specs=[vmem] * 4 + [smem] * 2 + [vmem] * 2,
        out_specs=vmem,
        scratch_shapes=[pltpu.VMEM((xr * MODES, channels * yr), f32)] * 2,
        compiler_params=pltpu.CompilerParams(vmem_limit_bytes=50 * 2**20),
        cost_estimate=pl.CostEstimate(flops=10**9, bytes_accessed=10**7, transcendentals=10**6),
    )(activations, cotangent, got, got_back, mixing, bias, bzs, kyt)


def block_turn(back, nx, ny, collective, field, slope, weights, mixing, bias, tables):
    channels, xr, yr, zr = field.shape
    xp = -(-xr // 16) * 16
    cl, jl, n = MODES // nx, MODES // ny, nx * ny
    lanes = jl * channels
    vmem = pl.BlockSpec(memory_space=pltpu.VMEM)
    smem = pl.BlockSpec(memory_space=pltpu.SMEM)
    hbm = pl.BlockSpec(memory_space=pl.ANY)
    if back:
        args = (field, slope, weights, mixing, *tables)
        specs = [vmem, vmem, hbm, smem] + [vmem] * len(tables)
    else:
        args = (field, weights, mixing, bias, *tables)
        specs = [vmem, hbm, smem, smem] + [vmem] * len(tables)
    dma = pltpu.SemaphoreType.DMA
    return pl.pallas_call(
        functools.partial(kernel, back, nx, ny, xr),
        out_shape=(
            jax.ShapeDtypeStruct(field.shape, bf16 if back else f32),
            jax.ShapeDtypeStruct((cl, jl, channels, MODES), f32),
            jax.ShapeDtypeStruct((xr * MODES, ny * lanes), bf16),
        ),
        in_specs=specs,
        out_specs=(vmem, vmem, vmem),
        scratch_shapes=[
            pltpu.VMEM(weights.shape, f32),
            pltpu.VMEM(field.shape if back else (8, 128), f32),
            pltpu.VMEM((xr * MODES, channels * yr), bf16),
            pltpu.VMEM((xr * MODES, channels * yr), bf16),
            pltpu.VMEM((ny, nx, cl, xp, lanes), bf16),
            pltpu.VMEM((n, cl, xp, lanes), bf16),
            pltpu.VMEM((cl, jl, channels, MODES), f32),
            pltpu.VMEM((nx, cl, xp, lanes), bf16),
            pltpu.VMEM((n, cl, xp, lanes), bf16),
            pltpu.VMEM((xr * MODES, channels * yr), f32),
            dma((n,)), dma((n,)), dma((n,)), dma((n,)), dma,
        ],
        compiler_params=pltpu.CompilerParams(
            collective_id=collective, has_side_effects=True, vmem_limit_bytes=50 * 2**20
        ),
        cost_estimate=pl.CostEstimate(flops=10**9, bytes_accessed=2 * 10**7, transcendentals=10**6),
    )(*args)


def body(activations, cotangent, spectral_weights, pointwise, channel_bias):
    inputs = activations[0]
    channels, xr, yr, zr = inputs.shape
    nx, ny = lax.axis_size("gx"), lax.axis_size("gy")
    xp = -(-xr // 16) * 16
    bz = trig_basis(zr)
    bx = trig_basis(xr * nx).reshape(MODES, nx, xr)
    bx = np.concatenate([bx, np.zeros((MODES, nx, xp - xr))], axis=2).reshape(MODES, nx * xp)
    by = trig_basis(yr * ny).reshape(MODES, ny, yr)
    kron = np.einsum("jgy,ik->giyjk", by, np.eye(channels)).reshape(
        ny, channels * yr, MODES * channels
    )
    bzh = halves(bz)
    kh = halves(kron)
    gy = lax.axis_index("gy")
    ky = lax.dynamic_index_in_dim(jnp.asarray(np.swapaxes(kh, 0, 1)), gy, 0, False)
    kyt = lax.dynamic_index_in_dim(
        jnp.asarray(np.ascontiguousarray(np.transpose(kh, (1, 0, 3, 2)))), gy, 0, False
    )
    tables = (
        jnp.asarray(bzh),
        jnp.asarray(np.concatenate([bzh[0], bzh[0], bzh[1]], axis=0)),
        ky,
        kyt,
        jnp.asarray(halves(np.concatenate([bx] * ny, axis=1))),
        jnp.asarray(halves(bx.T)),
    )
    weights = spectral_weights[0]
    mixing = pointwise[0]
    following = [from_behind(v, "segment", -1) for v in (inputs, mixing, channel_bias)]
    slope, input_modes, got = block_turn(
        False, nx, ny, 0, inputs, None, weights, mixing, channel_bias, tables
    )
    next_got = from_behind(got, "segment", -1)
    segment_index = lax.axis_index("segment")
    segment_count = lax.axis_size("segment")
    incoming = cotangent
    kept_grad = jnp.zeros(cotangent.shape, bf16)
    kept_modes = jnp.zeros(input_modes.shape, f32)
    for turn_index in range(segment_count):
        active = segment_index == segment_count - 1 - turn_index
        input_grad, grad_modes, got_back = block_turn(
            True, nx, ny, 1 + turn_index, incoming, slope, weights, mixing, None, tables
        )
        kept_grad = jnp.where(active, input_grad, kept_grad)
        kept_modes = jnp.where(active, grad_modes, kept_modes)
        if turn_index == 0 and segment_count > 1:
            next_back = from_behind(got_back, "segment", -1)
            incoming = ahead(
                following[0], cotangent, next_got, next_back, following[1], following[2],
                tables[1], tables[3],
            )
        elif turn_index + 1 < segment_count:
            incoming = from_behind(input_grad, "segment", -1)
    input_modes = jnp.swapaxes(input_modes, 0, 1)
    kept_modes = jnp.swapaxes(kept_modes, 0, 1)
    weight_grad = input_modes[:, :, :, None, :] * kept_modes[:, :, None, :, :]
    return (kept_grad[None], weight_grad[None])


def slope_of(value):
    cdf = 0.5 * (1.0 + lax.erf(value * 0.7071067811865476))
    return cdf + value * jnp.exp(-0.5 * value * value) * 0.3989422804014327


def field_of(cells, ny, ky, bzi):
    blocks = []
    for h in range(ny):
        block = cells(h)
        blocks.append(block.reshape(block.shape[0] * block.shape[1], block.shape[2]))
    block = jnp.concatenate(blocks, axis=1)
    top, rest = split(dot(ky[0], block, 1, 1) + dot(ky[1], block, 1, 1))
    return dot(jnp.concatenate([top, rest, top], axis=1), bzi[...])


def relay_kernel(
    nx, ny, xq, cuts,
    act_hbm, cot_hbm, w_hbm, mix_ref, bias_ref, mix_hbm, bias_hbm,
    kyt_hbm, ky_hbm, bzf_hbm, bzi_hbm, bx_hbm, sp_hbm,
    out, rest_ref, cells_ref, wgrad, ky, bzi,
    act, act1, cot, w, wd, kyt, bzf, bx, sp,
    u, v, slope, sig, in_modes, grad_modes, m_ref, mt_send, mt_recv,
    mixv1, biasv1, mix1, bias1, s_ref, p_ref, r_ref,
    load_sem, send_sem, recv_sem, row_send, row_recv, small_send, small_recv, store_sem,
    tail_send, tail_recv, pair_send, pair_recv,
):
    channels, xr, yr, zr = act.shape
    n = nx * ny
    cl, jl = MODES // nx, MODES // ny
    nh, hq = r_ref.shape[1], r_ref.shape[3]
    lanes = jl * channels
    rows = channels * yr
    tail = xr - hq * xq
    late = xr - xq
    gx, gy, seg = lax.axis_index("gx"), lax.axis_index("gy"), lax.axis_index("segment")
    me = gx * ny + gy
    mine = gy * nx + gx
    first, last = seg == 0, seg == 1
    mesh_ids = pl.DeviceIdType.MESH

    loads = [
        pltpu.make_async_copy(source, target, load_sem.at[k])
        for k, (source, target) in enumerate(
            [
                (act_hbm, act), (bzf_hbm, bzf), (kyt_hbm.at[gy], kyt), (w_hbm, w), (bx_hbm, bx),
                (sp_hbm, sp), (ky_hbm.at[gy], ky), (bzi_hbm, bzi), (cot_hbm, cot),
            ]
        )
    ]
    for load in loads[:3]:
        load.start()

    barrier = pltpu.get_barrier_semaphore()

    def greet(k, carry):
        other = lax.rem(seg * n + me + k, 2 * n)
        peer = lax.rem(other, n)
        pl.semaphore_signal(
            barrier, inc=1,
            device_id={"segment": other // n, "gx": peer // ny, "gy": lax.rem(peer, ny)},
            device_id_type=mesh_ids,
        )
        return carry

    lax.fori_loop(1, 2 * n, greet, 0)

    def ahead(source, target, send, recv):
        return pltpu.make_async_remote_copy(
            src_ref=source, dst_ref=target, send_sem=send, recv_sem=recv,
            device_id={"segment": 1 - seg}, device_id_type=mesh_ids,
        )

    def row_copy(x):
        return ahead(act_hbm.at[:, x], act1.at[:, x], row_send.at[x], row_recv.at[x])

    def send_rows(start, stop):
        for x in range(start, stop):
            row_copy(x).start()

    def modes_copy(k):
        return ahead(mt_send.at[k], mt_recv.at[k], small_send.at[k], small_recv.at[k])

    small = [
        ahead(mix_hbm, mixv1, small_send.at[2], small_recv.at[2]),
        ahead(bias_hbm, biasv1, small_send.at[3], small_recv.at[3]),
    ]

    def send(source, target, sends, receives):
        def begin(k, carry):
            peer = lax.rem(me + k, n)
            d, h = peer // ny, lax.rem(peer, ny)
            pltpu.make_async_remote_copy(
                src_ref=source(d, h), dst_ref=target, send_sem=sends, recv_sem=receives,
                device_id={"gx": d, "gy": h}, device_id_type=mesh_ids,
            ).start()
            return carry

        lax.fori_loop(1, n, begin, 0)
        target[...] = source(gx, gy)[...]

    def send_half(source, e, half):
        send(source, r_ref.at[e, half, mine], send_sem.at[e, half], recv_sem.at[e, half])

    def send_along(source, e, half):
        def begin(k, carry):
            d = lax.rem(gx + k, nx)
            pltpu.make_async_remote_copy(
                src_ref=source(d), dst_ref=r_ref.at[e, half, mine],
                send_sem=send_sem.at[e, half], recv_sem=recv_sem.at[e, half],
                device_id={"gx": d}, device_id_type=mesh_ids,
            ).start()
            return carry

        lax.fori_loop(1, nx, begin, 0)
        r_ref[e, half, mine] = source(gx)[...]

    def pair_copy(e, half):
        block = r_ref.at[e, half, pl.ds(gy * nx, nx)]
        return pltpu.make_async_remote_copy(
            src_ref=block, dst_ref=block,
            send_sem=pair_send.at[e, half], recv_sem=pair_recv.at[e, half],
            device_id={"gy": 1 - gy}, device_id_type=mesh_ids,
        )

    def forward(e, halves):
        for half in halves:
            await_block(r_ref.at[e, half, pl.ds(0, nx - 1)], recv_sem.at[e, half])
            pair_copy(e, half).start()

    def land(e, half):
        await_block(r_ref.at[e, half, pl.ds(0, nx)], pair_recv.at[e, half])

    def sent_along(e, half):
        await_block(r_ref.at[e, half, pl.ds(0, nx - 1)], send_sem.at[e, half])
        await_block(r_ref.at[e, half, pl.ds(0, nx)], pair_send.at[e, half])

    def send_tail(k, carry):
        peer = lax.rem(me + k, n)
        d, h = peer // ny, lax.rem(peer, ny)
        pltpu.make_async_remote_copy(
            src_ref=s_ref.at[2, nh - 1, h * nx + d], dst_ref=r_ref.at[4, nh - 1, mine],
            send_sem=tail_send.at[0], recv_sem=tail_recv.at[0],
            device_id={"segment": 0, "gx": d, "gy": h}, device_id_type=mesh_ids,
        ).start()
        return carry

    def await_block(block, sem):
        pltpu.make_async_copy(block, block, sem).wait()

    def arrive(e, half):
        await_block(r_ref.at[e, half, pl.ds(0, n - 1)], recv_sem.at[e, half])

    def sent(e, half):
        await_block(r_ref.at[e, half, pl.ds(0, n - 1)], send_sem.at[e, half])

    def to_modes(blocks, k, half):
        parts = []
        for block in blocks:
            g = dot(block, bzf[...])
            parts.append(g[:, : nx * 16] + g[:, nx * 16 :])
        top, rest = split(jnp.concatenate(parts, axis=1))
        t = dot(kyt[0], top) + dot(kyt[1], top) + dot(kyt[0], rest)
        t = t.T.astype(bf16)
        for q in range(len(blocks)):
            for h in range(ny):
                part = t[q * nx * 16 : (q + 1) * nx * 16, h * lanes : (h + 1) * lanes]
                s_ref[k, half, h * nx : (h + 1) * nx, q] = part.reshape(nx, 16, lanes)

    def to_field(e, half, q):
        return field_of(lambda h: r_ref[e, half, h * nx : (h + 1) * nx, q], ny, ky, bzi)

    def row(field, x):
        return field[:, x * zr : (x + 1) * zr].reshape(channels, yr, zr)

    def send_modes(k, e, half):
        send_half(lambda d, h: s_ref.at[k, half, h * nx + d], e, half)

    def own_modes(e, await_half):
        own = None
        for half in range(nh):
            await_half(half)
            block = r_ref[e, half].reshape(n * hq * 16, lanes)
            part = slice(half * n * hq * 16, (half + 1) * n * hq * 16)
            term = dot(bx[0, :, part], block) + dot(bx[1, :, part], block)
            own = term if own is None else own + term
        return own.T.reshape(jl, channels, cl * MODES)

    def send_cells(mt, k, e, halves):
        top, rest = split(mt)
        for half in halves:
            table = [sp[i, half].reshape(nx * hq * 16, cl * MODES) for i in range(2)]
            cells = dot(table[0], top) + dot(table[1], top) + dot(table[0], rest)
            p_ref[k, half] = cells.astype(bf16).reshape(nx, hq, 16, lanes)
            send_along(lambda d: p_ref.at[k, half, d], e, half)

    def mixed():
        return m_ref[...].reshape(lanes, cl * MODES).T

    def mix_back(e, await_half):
        grad_modes[...] = own_modes(e, await_half)

        def step(j, carry):
            m_ref[j] = jnp.sum(wd[j] * grad_modes[j][None], axis=1)
            return carry

        lax.fori_loop(0, jl, step, 0)

    def blend(mixing, values, o, back):
        total = (mixing[0, o] if back else mixing[o, 0]) * values[0]
        for i in range(1, channels):
            total = total + (mixing[i, o] if back else mixing[o, i]) * values[i]
        return total

    def fetch_small():
        for copy in small:
            copy.wait_recv()
        for k, (source, target) in enumerate([(mixv1, mix1), (biasv1, bias1)]):
            copy = pltpu.make_async_copy(source, target, store_sem.at[k])
            copy.start()
            copy.wait()

    def back_block(half, q, offset):
        field = to_field(3, half, q)
        x0 = (half * hq + q) * xq
        block = []
        for k in range(xq):
            incoming = (row(field, k) + offset[:, x0 + k]).astype(bf16).astype(f32)
            signal = incoming * slope[:, x0 + k]
            block.append((x0 + k, signal))
        return block

    def packed(block):
        return jnp.concatenate([s.astype(bf16).reshape(rows, zr) for _, s in block], axis=1)

    def blend_back(start, stop):
        def step(x, carry):
            values = [sig[i, x] for i in range(channels)]
            for o in range(channels):
                u[o, x] = blend(mix_ref, values, o, True)
            return carry

        lax.fori_loop(start, stop, step, 0)

    pl.semaphore_wait(barrier, 2 * n - 1)
    for copy in small:
        copy.start()

    @pl.when(last)
    def _():
        send_rows(0, cuts[0])

    @pl.when(first)
    def _():
        send_rows(tail, tail + cuts[0])

    for load in loads[:3]:
        load.wait()
    for load in loads[3:]:
        load.start()
    for half in range(nh):
        blocks = []
        for q in range(hq):
            x = (half * hq + q) * xq
            block = [act[:, x + k].reshape(rows, zr) for k in range(xq)]
            blocks.append(jnp.concatenate(block, axis=1))
        to_modes(blocks, 0, half)
        send_modes(0, 0, half)

    for load in loads[3:]:
        load.wait()

    def dense(j, carry):
        for i in range(channels):
            wd[j, i] = jnp.concatenate([w[j, c, i] for c in range(cl)], axis=1)
        return carry

    lax.fori_loop(0, jl, dense, 0)

    def pointwise(x, carry):
        values = [act[i, x].astype(f32) for i in range(channels)]
        for o in range(channels):
            u[o, x] = blend(mix_ref, values, o, False) + bias_ref[0, o]
        return carry

    lax.fori_loop(0, xr, pointwise, 0)

    in_modes[...] = own_modes(0, lambda half: arrive(0, half))

    def mix(j, carry):
        own = in_modes[j]
        m_ref[j] = jnp.sum(wd[j] * own[:, None, :], axis=0)
        return carry

    lax.fori_loop(0, jl, mix, 0)
    mt_send[0] = mixed()
    modes_copy(0).start()

    @pl.when(last)
    def _():
        send_rows(cuts[0], cuts[1])

    @pl.when(first)
    def _():
        send_rows(tail + cuts[0], xr)

    send_cells(mt_send[0], 0, 1, range(nh))

    @pl.when(last)
    def _():
        forward(1, range(nh))
        for half in range(nh):
            land(1, half)
            blocks = []
            for q in range(hq):
                field = to_field(1, half, q)
                x0 = (half * hq + q) * xq
                block = []
                for k in range(xq):
                    signal = cot[:, x0 + k].astype(f32) * slope_of(row(field, k) + u[:, x0 + k])
                    sig[:, x0 + k] = signal
                    block.append(signal.astype(bf16).reshape(rows, zr))
                blocks.append(jnp.concatenate(block, axis=1))
            to_modes(blocks, 1, half)
            send_modes(1, 2, half)

        modes_copy(0).wait_recv()
        send_cells(mt_recv[0], 3, 5, [nh - 1])
        fetch_small()

        mix_back(2, lambda half: arrive(2, half))
        mt_send[1] = mixed()
        modes_copy(1).start()
        send_rows(cuts[1], cuts[2])
        send_cells(mt_send[1], 1, 3, reversed(range(nh)))

        blend_back(0, xr)
        forward(5, [nh - 1])
        land(5, nh - 1)
        for q in range(hq):
            field = to_field(5, nh - 1, q)
            x0 = tail + q * xq
            for k in range(xq):
                row_copy(x0 + k).wait_recv()
                values = [act1[i, x0 + k].astype(f32) for i in range(channels)]
                here = row(field, k)
                for o in range(channels):
                    pre = here[o] + blend(mix1, values, o, False) + bias1[0, o]
                    slope[o, x0 + k] = slope_of(pre)
        forward(3, reversed(range(nh)))
        land(3, nh - 1)
        to_modes([packed(back_block(nh - 1, q, u)) for q in range(hq)], 2, nh - 1)
        lax.fori_loop(0, n, send_tail, 0)
        send_rows(cuts[2], xr)

    def ahead_quarter(half, q):
        field = to_field(2, half, q)
        x0 = (half * hq + q) * xq
        for k in range(xq):
            row_copy(x0 + k).wait_recv()
            values = [act1[i, x0 + k].astype(f32) for i in range(channels)]
            here = row(field, k)
            signals = []
            for o in range(channels):
                pre = here[o] + blend(mix1, values, o, False) + bias1[0, o]
                signals.append(cot[o, x0 + k].astype(f32) * slope_of(pre))
            for i in range(channels):
                v[i, x0 + k] = blend(mix1, signals, i, True)

    def kept(block):
        for x, signal in block:
            sig[:, x] = signal
        return block

    @pl.when(first)
    def _():
        modes_copy(0).wait_recv()
        send_cells(mt_recv[0], 1, 2, range(nh))
        fetch_small()
        forward(1, range(nh))
        for half in range(nh):
            land(1, half)

            def step(q, carry):
                field = to_field(1, half, q)
                x0 = (half * hq + q) * xq
                for k in range(xq):
                    slope[:, x0 + k] = slope_of(row(field, k) + u[:, x0 + k])
                return carry

            lax.fori_loop(0, hq, step, 0)

        forward(2, range(nh))
        for half in range(nh):
            land(2, half)
        for half in range(nh - 1):
            for q in range(hq):
                ahead_quarter(half, q)
        modes_copy(1).wait_recv()
        send_cells(mt_recv[1], 2, 3, range(nh))
        forward(3, range(nh))
        for half in range(nh - 1):
            land(3, half)
            to_modes([packed(kept(back_block(half, q, v))) for q in range(hq)], 1, half)
            send_modes(1, 4, half)
        blend_back(0, tail)
        land(3, nh - 1)
        for q in range(hq - 1):
            ahead_quarter(nh - 1, q)
            kept(back_block(nh - 1, q, v))

        for target, e in ((v, 2), (u, 3)):
            field = to_field(e, nh - 1, hq - 1)
            for k in range(xq):
                target[:, late + k] = row(field, k)

        def await_half(half):
            if half < nh - 1:
                arrive(4, half)
            else:
                await_block(r_ref.at[4, half], tail_recv.at[0])

        mix_back(4, await_half)
        send_cells(mixed(), 3, 5, range(nh))
        if hq > 1:
            blend_back(tail, late)

    def weight_grad(j, carry):
        for c in range(cl):
            part = slice(c * MODES, (c + 1) * MODES)
            wgrad[j, c] = in_modes[j][:, None, part] * grad_modes[j][None, :, part]
        return carry

    lax.fori_loop(0, jl, weight_grad, 0)
    e = 3 + 2 * (1 - seg)

    @pl.when(last)
    def _():
        for half in range(nh - 1):
            land(3, half)

    @pl.when(first)
    def _():
        forward(5, range(nh))
        for half in range(nh - 1):
            land(5, half)

    for half in range(nh - 1):
        for q in range(hq):
            field = to_field(e, half, q)
            x0 = (half * hq + q) * xq
            for k in range(xq):
                out[:, x0 + k] = (row(field, k) + u[:, x0 + k]).astype(bf16)

    @pl.when(first)
    def _():
        land(5, nh - 1)
        rest_ref[:, : late - tail] = u[:, tail:late]

    cells_ref[...] = r_ref[e, nh - 1]

    @pl.when(first)
    def _():
        def step(k, carry):
            x = late + k
            row_copy(x).wait_recv()
            values = [act1[i, x].astype(f32) for i in range(channels)]
            signals = []
            for o in range(channels):
                pre = v[o, x] + blend(mix1, values, o, False) + bias1[0, o]
                signals.append(cot[o, x].astype(f32) * slope_of(pre))
            here = []
            for i in range(channels):
                incoming = u[i, x] + blend(mix1, signals, i, True)
                here.append(incoming.astype(bf16).astype(f32) * slope[i, x])
            for o in range(channels):
                rest_ref[o, late - tail + k] = blend(mix_ref, here, o, True)
            return carry

        lax.fori_loop(0, xq, step, 0)

    @pl.when(last)
    def _():
        rest_ref[...] = u[:, tail:]

    for half in range(nh):
        sent(0, half)
        sent_along(1, half)
        sent_along(3, half)
    for copy in small:
        copy.wait_send()
    modes_copy(0).wait_send()

    @pl.when(first)
    def _():
        for half in range(nh - 1):
            sent(4, half)
        for half in range(nh):
            sent_along(2, half)
            sent_along(5, half)
        for x in range(tail, xr):
            row_copy(x).wait_send()

    @pl.when(last)
    def _():
        for half in range(nh):
            sent(2, half)
        sent_along(5, nh - 1)
        modes_copy(1).wait_send()
        await_block(r_ref.at[4, nh - 1], tail_send.at[0])
        for x in range(xr):
            row_copy(x).wait_send()


def finish_kernel(
    nx, ny, xq, done_ref, rest_ref, cells_ref, wgrad, ky, bzi, grad_hbm, wgrad_hbm, out, sem
):
    channels, done, yr, zr = done_ref.shape
    hq = cells_ref.shape[1]
    stores = [
        pltpu.make_async_copy(wgrad, wgrad_hbm, sem.at[0]),
        pltpu.make_async_copy(done_ref, grad_hbm.at[:, pl.ds(0, done)], sem.at[1]),
    ]
    for store in stores:
        store.start()
    for q in range(hq):
        field = field_of(lambda h: cells_ref[h * nx : (h + 1) * nx, q], ny, ky, bzi)
        for k in range(xq):
            x = q * xq + k
            here = field[:, k * zr : (k + 1) * zr].reshape(channels, yr, zr)
            out[:, x] = (here + rest_ref[:, x]).astype(bf16)
        part = pl.ds(q * xq, xq)
        store = pltpu.make_async_copy(
            out.at[:, part], grad_hbm.at[:, pl.ds(done + q * xq, xq)], sem.at[2 + q]
        )
        store.start()
        stores.append(store)
    for store in stores:
        store.wait()


def in_hbm(value):
    return pltpu.with_memory_space_constraint(jnp.asarray(value), pltpu.HBM)


def two_section_body(activations, cotangent, spectral_weights, pointwise, channel_bias):
    inputs = activations[0]
    channels, xr, yr, zr = inputs.shape
    nx, ny = lax.axis_size("gx"), lax.axis_size("gy")
    n = nx * ny
    cl, jl = MODES // nx, MODES // ny
    xq = 16 // cl
    nh = 2
    hq = xr // (nh * xq)
    lanes, rows = jl * channels, channels * yr
    bz = trig_basis(zr).reshape(nx, cl, zr)
    eye_x, eye_c = np.eye(xq), np.eye(cl)
    bzf = np.einsum("dcz,xX->xzdXc", bz, eye_x).reshape(xq * zr, nx * 16)
    bzi = halves(bzf.reshape(xq, zr, nx * 16).transpose(2, 0, 1).reshape(nx * 16, xq * zr))
    by = trig_basis(yr * ny).reshape(MODES, ny, yr)
    ky = np.einsum("jgy,ik->giyjk", by, np.eye(channels)).reshape(ny, rows, ny * lanes)
    ky = halves(ky)
    bx = trig_basis(xr * nx).reshape(MODES, nx, nh, hq, xq)
    sp = np.einsum("adtqx,cC->tdqxCca", bx, eye_c).reshape(nh * nx * hq * 16, cl * MODES)
    bxf = np.broadcast_to(
        sp.reshape(nh, 1, nx * hq * 16, cl * MODES), (nh, ny, nx * hq * 16, cl * MODES)
    )
    bxf = bxf.reshape(nh * n * hq * 16, cl * MODES).T
    bzf = halves(bzf)
    tables = [
        np.ascontiguousarray(ky.transpose(1, 0, 3, 2)),
        np.ascontiguousarray(ky.transpose(1, 0, 2, 3)),
        np.concatenate([bzf[0], bzf[1]], axis=1),
        np.concatenate([bzi[0], bzi[0], bzi[1]], axis=0),
        halves(bxf),
        halves(sp).reshape(2, nh, nx, hq, 16, cl * MODES),
    ]
    weights, mixing = spectral_weights[0], pointwise[0]
    vmem = pl.BlockSpec(memory_space=pltpu.VMEM)
    smem = pl.BlockSpec(memory_space=pltpu.SMEM)
    hbm = pl.BlockSpec(memory_space=pl.ANY)
    dma = pltpu.SemaphoreType.DMA
    grid = inputs.shape
    done = grid[:1] + ((nh - 1) * hq * xq,) + grid[2:]
    left = grid[:1] + (hq * xq,) + grid[2:]
    scratch = [
        pltpu.VMEM(grid, bf16), pltpu.VMEM(grid, bf16), pltpu.VMEM(grid, bf16),
        pltpu.VMEM(weights.shape, f32),
        pltpu.VMEM((jl, channels, channels, cl * MODES), f32),
        pltpu.VMEM((2, ny * lanes, rows), bf16),
        pltpu.VMEM((xq * zr, 2 * nx * 16), bf16),
        pltpu.VMEM((2, cl * MODES, nh * n * hq * 16), bf16),
        pltpu.VMEM((2, nh, nx, hq, 16, cl * MODES), bf16),
        pltpu.VMEM(grid, f32), pltpu.VMEM(grid, f32), pltpu.VMEM(grid, f32), pltpu.VMEM(grid, f32),
        pltpu.VMEM((jl, channels, cl * MODES), f32),
        pltpu.VMEM((jl, channels, cl * MODES), f32),
        pltpu.VMEM((jl, channels, cl * MODES), f32),
        pltpu.VMEM((2, cl * MODES, lanes), f32),
        pltpu.VMEM((2, cl * MODES, lanes), f32),
        pltpu.VMEM(mixing.shape, f32), pltpu.VMEM(channel_bias.shape, f32),
        pltpu.SMEM(mixing.shape, f32), pltpu.SMEM(channel_bias.shape, f32),
        pltpu.VMEM((3, nh, n, hq, 16, lanes), bf16),
        pltpu.VMEM((4, nh, nx, hq, 16, lanes), bf16),
        pltpu.VMEM((6, nh, n, hq, 16, lanes), bf16),
        dma((9,)), dma((6, nh)), dma((6, nh)),
        dma((xr,)), dma((xr,)), dma((4,)), dma((4,)), dma((2,)), dma((1,)), dma((1,)), dma((6, nh)), dma((6, nh)),
    ]
    parts = pl.pallas_call(
        functools.partial(relay_kernel, nx, ny, xq, (3, 9, 12)),
        out_shape=(
            jax.ShapeDtypeStruct(done, bf16),
            jax.ShapeDtypeStruct(left, f32),
            jax.ShapeDtypeStruct((n, hq, 16, lanes), bf16),
            pltpu.VMEM(weights.shape, f32),
            jax.ShapeDtypeStruct((2, rows, ny * lanes), bf16),
            jax.ShapeDtypeStruct((3 * nx * 16, xq * zr), bf16),
        ),
        in_specs=[hbm, hbm, hbm, smem, smem] + [hbm] * (2 + len(tables)),
        out_specs=[vmem] * 6,
        scratch_shapes=scratch,
        compiler_params=pltpu.CompilerParams(
            collective_id=0, has_side_effects=True, vmem_limit_bytes=46 * 2**20
        ),
        cost_estimate=pl.CostEstimate(
            flops=4 * 10**9, bytes_accessed=2 * 10**7, transcendentals=10**7
        ),
    )(
        *[in_hbm(v) for v in (inputs, cotangent, weights)],
        mixing, channel_bias,
        *[in_hbm(v) for v in [mixing, channel_bias] + tables],
    )
    input_grad, weight_grad = pl.pallas_call(
        functools.partial(finish_kernel, nx, ny, xq),
        out_shape=(
            jax.ShapeDtypeStruct(grid, bf16),
            jax.ShapeDtypeStruct(weights.shape, f32),
        ),
        in_specs=[vmem] * 6,
        out_specs=(hbm, hbm),
        scratch_shapes=[pltpu.VMEM(left, bf16), dma((2 + hq,))],
        compiler_params=pltpu.CompilerParams(vmem_limit_bytes=24 * 2**20),
        cost_estimate=pl.CostEstimate(flops=10**9, bytes_accessed=10**7, transcendentals=0),
    )(*parts)
    return (input_grad[None], weight_grad[None])


def fits(mesh):
    nx = mesh.shape["gx"]
    return mesh.shape["segment"] == 2 and mesh.shape["gy"] == 2 and nx == 8


def solution(mesh):
    return jax.shard_map(
        two_section_body if fits(mesh) else body,
        mesh=mesh,
        in_specs=(
            P("segment", "groups", "gx", "gy", None),
            P("groups", "gx", "gy", None),
            P("segment", "gy", "gx", None, None, None),
            P("segment", None, None),
            P("segment", None),
        ),
        out_specs=(
            P("segment", "groups", "gx", "gy", None),
            P("segment", "gy", "gx", "groups", None, None),
        ),
        check_vma=False,
    )
```

```python
import functools
import math

import jax
import jax.numpy as jnp
import ml_dtypes
import numpy as np
from jax import lax
from jax.experimental import pallas as pl
from jax.experimental.pallas import tpu as pltpu
from jax.sharding import PartitionSpec as P

MODES = 32
f32, bf16 = jnp.float32, jnp.bfloat16


def from_behind(block, axis, distance):
    devices = range(lax.axis_size(axis))
    route = [(i - distance, i) for i in devices if i - distance in devices]
    return lax.ppermute(block, axis, route)


def trig_basis(length):
    half = MODES // 2
    freqs = np.arange(half)[:, None]
    points = np.arange(length)[None, :]
    step = 2.0 * math.pi / length
    rows = np.concatenate(
        [np.cos((freqs * points % length) * step), np.sin(((freqs + 1) * points % length) * step)]
    )
    scales = np.where(np.arange(MODES) == 0, 1.0 / math.sqrt(length), math.sqrt(2.0 / length))
    return rows * scales[:, None]


def halves(matrix):
    matrix = np.asarray(matrix, np.float32)
    top = matrix.astype(ml_dtypes.bfloat16)
    rest = (matrix - top.astype(np.float32)).astype(ml_dtypes.bfloat16)
    return np.stack([top, rest])


def split(value):
    top = value.astype(bf16)
    return top, (value - top.astype(f32)).astype(bf16)


def dot(a, b, ca=1, cb=0):
    return lax.dot_general(a, b, (((ca,), (cb,)), ((), ())), preferred_element_type=f32)


def kernel(
    back, nx, ny, xr, *refs
):
    if back:
        (inc_ref, slope_ref, w_hbm, mix_ref, bz_ref, bzs_ref, ky_ref, kyt_ref, bx_ref, bxr_ref,
         out_ref, modes_ref, got_ref, *scratch) = refs
    else:
        (inc_ref, w_hbm, mix_ref, bias_ref, bz_ref, bzs_ref, ky_ref, kyt_ref, bx_ref, bxr_ref,
         out_ref, modes_ref, got_ref, *scratch) = refs
    (w_ref, sig_ref, ghi_ref, glo_ref, s_ref, r_ref, m_ref, p_ref, q_ref, qs_ref,
     send1, recv1, send2, recv2, wsem) = scratch
    channels, _, yr, zr = inc_ref.shape
    cl, jl, xp = MODES // nx, MODES // ny, r_ref.shape[2]
    n = nx * ny
    lanes = jl * channels
    gx, gy = lax.axis_index("gx"), lax.axis_index("gy")
    me = gx * ny + gy

    wcopy = pltpu.make_async_copy(w_hbm, w_ref, wsem)
    wcopy.start()

    barrier = pltpu.get_barrier_semaphore()

    def greet(k, carry):
        peer = lax.rem(me + k, n)
        pl.semaphore_signal(
            barrier, inc=1,
            device_id={"gx": peer // ny, "gy": lax.rem(peer, ny)},
            device_id_type=pl.DeviceIdType.MESH,
        )
        return carry

    lax.fori_loop(1, n, greet, 0)

    def along_z(x, carry):
        if back:
            signal = inc_ref[:, x].astype(f32) * slope_ref[:, x]
            sig_ref[:, x] = signal
            block = signal.astype(bf16)
        else:
            block = inc_ref[:, x]
        block = block.reshape(channels * yr, zr)
        g = dot(bz_ref[0], block, 1, 1) + dot(bz_ref[1], block, 1, 1)
        ghi, glo = split(g)
        rows = pl.ds(pl.multiple_of(x * MODES, MODES), MODES)
        ghi_ref[rows, :] = ghi
        glo_ref[rows, :] = glo
        return carry

    lax.fori_loop(0, xr, along_z, 0)
    ghi = ghi_ref[...]
    t = dot(ghi, ky_ref[0]) + dot(ghi, ky_ref[1]) + dot(glo_ref[...], ky_ref[0])
    t = jnp.swapaxes(t.reshape(xr, MODES, ny * lanes), 0, 1)
    if xp > xr:
        t = jnp.concatenate([t, jnp.zeros((MODES, xp - xr, ny * lanes), f32)], axis=1)
    t = t.astype(bf16)
    for h in range(ny):
        s_ref[h] = t[:, :, h * lanes : (h + 1) * lanes].reshape(nx, cl, xp, lanes)

    pl.semaphore_wait(barrier, n - 1)

    def exchange(source, target, send, recv):
        def copy_to(peer, slot_of):
            return pltpu.make_async_remote_copy(
                src_ref=source(peer // ny, lax.rem(peer, ny)),
                dst_ref=target.at[lax.rem(slot_of, ny) * nx + slot_of // ny],
                send_sem=send.at[peer],
                recv_sem=recv.at[slot_of],
                device_id={"gx": peer // ny, "gy": lax.rem(peer, ny)},
                device_id_type=pl.DeviceIdType.MESH,
            )

        def begin(k, carry):
            copy_to(lax.rem(me + k, n), me).start()
            return carry

        def finish(k, carry):
            copy_to(lax.rem(me + k, n), me).wait_send()
            peer = lax.rem(me + n - k, n)
            copy_to(peer, peer).wait_recv()
            return carry

        lax.fori_loop(1, n, begin, 0)
        target[gy * nx + gx] = source(gx, gy)[...]
        lax.fori_loop(1, n, finish, 0)

    exchange(lambda d, h: s_ref.at[h, d], r_ref, send1, recv1)

    for c in range(cl):
        part = r_ref[:, c].reshape(n * xp, lanes)
        own = dot(bx_ref[0], part) + dot(bx_ref[1], part)
        modes_ref[c] = own.T.reshape(jl, channels, MODES)
    wcopy.wait()

    def mix(j, carry):
        for c in range(cl):
            own = modes_ref[c, j]
            weight = w_ref[j, c]
            if back:
                m_ref[c, j] = jnp.sum(weight * own[None], axis=1)
            else:
                m_ref[c, j] = jnp.sum(weight * own[:, None, :], axis=0)
        return carry

    lax.fori_loop(0, jl, mix, 0)
    for c in range(cl):
        top, rest = split(m_ref[c].reshape(lanes, MODES))
        spread = (
            dot(bxr_ref[0], top, 1, 1) + dot(bxr_ref[1], top, 1, 1) + dot(bxr_ref[0], rest, 1, 1)
        )
        p_ref[:, c] = spread.astype(bf16).reshape(nx, xp, lanes)

    exchange(lambda d, h: p_ref.at[d], q_ref, send2, recv2)

    got = [q_ref[h * nx : (h + 1) * nx].reshape(MODES, xp, lanes) for h in range(ny)]
    got = jnp.concatenate(got, axis=2).astype(f32)
    got = jnp.swapaxes(got, 0, 1)[:xr].reshape(xr * MODES, ny * lanes).astype(bf16)
    got_ref[...] = got
    qs_ref[...] = dot(got, kyt_ref[0]) + dot(got, kyt_ref[1])

    def finish_field(x, carry):
        rows = pl.ds(pl.multiple_of(x * MODES, MODES), MODES)
        top, rest = split(qs_ref[rows, :])
        stack = jnp.concatenate([top, rest, top], axis=0)
        field = dot(stack, bzs_ref[...], 0, 0).reshape(channels, yr, zr)
        if back:
            values = [sig_ref[i, x] for i in range(channels)]
        else:
            values = [inc_ref[i, x].astype(f32) for i in range(channels)]
        for o in range(channels):
            total = field[o]
            for i in range(channels):
                total = total + (mix_ref[i, o] if back else mix_ref[o, i]) * values[i]
            if back:
                out_ref[o, x] = total.astype(bf16)
            else:
                total = total + bias_ref[0, o]
                cdf = 0.5 * (1.0 + lax.erf(total * 0.7071067811865476))
                out_ref[o, x] = cdf + total * jnp.exp(-0.5 * total * total) * 0.3989422804014327
        return carry

    lax.fori_loop(0, xr, finish_field, 0)


def ahead_kernel(
    act_ref, cot_ref, got_ref, got_back_ref, mix_ref, bias_ref, bzs_ref, kyt_ref, out_ref,
    pre_ref, back_ref,
):
    channels, xr, yr, zr = act_ref.shape
    pre_ref[...] = dot(got_ref[...], kyt_ref[0]) + dot(got_ref[...], kyt_ref[1])
    back_ref[...] = dot(got_back_ref[...], kyt_ref[0]) + dot(got_back_ref[...], kyt_ref[1])

    def field_of(ref, x):
        rows = pl.ds(pl.multiple_of(x * MODES, MODES), MODES)
        top, rest = split(ref[rows, :])
        stack = jnp.concatenate([top, rest, top], axis=0)
        return dot(stack, bzs_ref[...], 0, 0).reshape(channels, yr, zr)

    def step(x, carry):
        field = field_of(pre_ref, x)
        values = [act_ref[i, x].astype(f32) for i in range(channels)]
        signals = []
        for o in range(channels):
            total = field[o]
            for i in range(channels):
                total = total + mix_ref[o, i] * values[i]
            total = total + bias_ref[0, o]
            cdf = 0.5 * (1.0 + lax.erf(total * 0.7071067811865476))
            slope = cdf + total * jnp.exp(-0.5 * total * total) * 0.3989422804014327
            signals.append(cot_ref[o, x].astype(f32) * slope)
        field = field_of(back_ref, x)
        for o in range(channels):
            total = field[o]
            for i in range(channels):
                total = total + mix_ref[i, o] * signals[i]
            out_ref[o, x] = total.astype(bf16)
        return carry

    lax.fori_loop(0, xr, step, 0)


def ahead(activations, cotangent, got, got_back, mixing, bias, bzs, kyt):
    channels, xr, yr, zr = activations.shape
    vmem = pl.BlockSpec(memory_space=pltpu.VMEM)
    smem = pl.BlockSpec(memory_space=pltpu.SMEM)
    return pl.pallas_call(
        ahead_kernel,
        out_shape=jax.ShapeDtypeStruct(activations.shape, bf16),
        in_specs=[vmem] * 4 + [smem] * 2 + [vmem] * 2,
        out_specs=vmem,
        scratch_shapes=[pltpu.VMEM((xr * MODES, channels * yr), f32)] * 2,
        compiler_params=pltpu.CompilerParams(vmem_limit_bytes=50 * 2**20),
        cost_estimate=pl.CostEstimate(flops=10**9, bytes_accessed=10**7, transcendentals=10**6),
    )(activations, cotangent, got, got_back, mixing, bias, bzs, kyt)


def block_turn(back, nx, ny, collective, field, slope, weights, mixing, bias, tables):
    channels, xr, yr, zr = field.shape
    xp = -(-xr // 16) * 16
    cl, jl, n = MODES // nx, MODES // ny, nx * ny
    lanes = jl * channels
    vmem = pl.BlockSpec(memory_space=pltpu.VMEM)
    smem = pl.BlockSpec(memory_space=pltpu.SMEM)
    hbm = pl.BlockSpec(memory_space=pl.ANY)
    if back:
        args = (field, slope, weights, mixing, *tables)
        specs = [vmem, vmem, hbm, smem] + [vmem] * len(tables)
    else:
        args = (field, weights, mixing, bias, *tables)
        specs = [vmem, hbm, smem, smem] + [vmem] * len(tables)
    dma = pltpu.SemaphoreType.DMA
    return pl.pallas_call(
        functools.partial(kernel, back, nx, ny, xr),
        out_shape=(
            jax.ShapeDtypeStruct(field.shape, bf16 if back else f32),
            jax.ShapeDtypeStruct((cl, jl, channels, MODES), f32),
            jax.ShapeDtypeStruct((xr * MODES, ny * lanes), bf16),
        ),
        in_specs=specs,
        out_specs=(vmem, vmem, vmem),
        scratch_shapes=[
            pltpu.VMEM(weights.shape, f32),
            pltpu.VMEM(field.shape if back else (8, 128), f32),
            pltpu.VMEM((xr * MODES, channels * yr), bf16),
            pltpu.VMEM((xr * MODES, channels * yr), bf16),
            pltpu.VMEM((ny, nx, cl, xp, lanes), bf16),
            pltpu.VMEM((n, cl, xp, lanes), bf16),
            pltpu.VMEM((cl, jl, channels, MODES), f32),
            pltpu.VMEM((nx, cl, xp, lanes), bf16),
            pltpu.VMEM((n, cl, xp, lanes), bf16),
            pltpu.VMEM((xr * MODES, channels * yr), f32),
            dma((n,)), dma((n,)), dma((n,)), dma((n,)), dma,
        ],
        compiler_params=pltpu.CompilerParams(
            collective_id=collective, has_side_effects=True, vmem_limit_bytes=50 * 2**20
        ),
        cost_estimate=pl.CostEstimate(flops=10**9, bytes_accessed=2 * 10**7, transcendentals=10**6),
    )(*args)


def body(activations, cotangent, spectral_weights, pointwise, channel_bias):
    inputs = activations[0]
    channels, xr, yr, zr = inputs.shape
    nx, ny = lax.axis_size("gx"), lax.axis_size("gy")
    xp = -(-xr // 16) * 16
    bz = trig_basis(zr)
    bx = trig_basis(xr * nx).reshape(MODES, nx, xr)
    bx = np.concatenate([bx, np.zeros((MODES, nx, xp - xr))], axis=2).reshape(MODES, nx * xp)
    by = trig_basis(yr * ny).reshape(MODES, ny, yr)
    kron = np.einsum("jgy,ik->giyjk", by, np.eye(channels)).reshape(
        ny, channels * yr, MODES * channels
    )
    bzh = halves(bz)
    kh = halves(kron)
    gy = lax.axis_index("gy")
    ky = lax.dynamic_index_in_dim(jnp.asarray(np.swapaxes(kh, 0, 1)), gy, 0, False)
    kyt = lax.dynamic_index_in_dim(
        jnp.asarray(np.ascontiguousarray(np.transpose(kh, (1, 0, 3, 2)))), gy, 0, False
    )
    tables = (
        jnp.asarray(bzh),
        jnp.asarray(np.concatenate([bzh[0], bzh[0], bzh[1]], axis=0)),
        ky,
        kyt,
        jnp.asarray(halves(np.concatenate([bx] * ny, axis=1))),
        jnp.asarray(halves(bx.T)),
    )
    weights = spectral_weights[0]
    mixing = pointwise[0]
    following = [from_behind(v, "segment", -1) for v in (inputs, mixing, channel_bias)]
    slope, input_modes, got = block_turn(
        False, nx, ny, 0, inputs, None, weights, mixing, channel_bias, tables
    )
    next_got = from_behind(got, "segment", -1)
    segment_index = lax.axis_index("segment")
    segment_count = lax.axis_size("segment")
    incoming = cotangent
    kept_grad = jnp.zeros(cotangent.shape, bf16)
    kept_modes = jnp.zeros(input_modes.shape, f32)
    for turn_index in range(segment_count):
        active = segment_index == segment_count - 1 - turn_index
        input_grad, grad_modes, got_back = block_turn(
            True, nx, ny, 1 + turn_index, incoming, slope, weights, mixing, None, tables
        )
        kept_grad = jnp.where(active, input_grad, kept_grad)
        kept_modes = jnp.where(active, grad_modes, kept_modes)
        if turn_index == 0 and segment_count > 1:
            next_back = from_behind(got_back, "segment", -1)
            incoming = ahead(
                following[0], cotangent, next_got, next_back, following[1], following[2],
                tables[1], tables[3],
            )
        elif turn_index + 1 < segment_count:
            incoming = from_behind(input_grad, "segment", -1)
    input_modes = jnp.swapaxes(input_modes, 0, 1)
    kept_modes = jnp.swapaxes(kept_modes, 0, 1)
    weight_grad = input_modes[:, :, :, None, :] * kept_modes[:, :, None, :, :]
    return (kept_grad[None], weight_grad[None])


def slope_of(value):
    cdf = 0.5 * (1.0 + lax.erf(value * 0.7071067811865476))
    return cdf + value * jnp.exp(-0.5 * value * value) * 0.3989422804014327


def field_of(cells, ny, ky, bzi):
    blocks = []
    for h in range(ny):
        block = cells(h)
        blocks.append(block.reshape(block.shape[0] * block.shape[1], block.shape[2]))
    block = jnp.concatenate(blocks, axis=1)
    top, rest = split(dot(ky[0], block, 1, 1) + dot(ky[1], block, 1, 1))
    return dot(jnp.concatenate([top, rest, top], axis=1), bzi[...])


def relay_kernel(
    nx, ny, xq, cuts,
    act_hbm, cot_hbm, w_hbm, mix_ref, bias_ref, mix_hbm, bias_hbm,
    kyt_hbm, ky_hbm, bzf_hbm, bzi_hbm, bx_hbm, sp_hbm,
    out, rest_ref, cells_ref, wgrad, ky, bzi,
    act, act1, cot, w, wd, kyt, bzf, bx, sp,
    u, v, slope, sig, in_modes, grad_modes, m_ref, mt_send, mt_recv,
    mixv1, biasv1, mix1, bias1, s_ref, p_ref, r_ref,
    load_sem, send_sem, recv_sem, row_send, row_recv, small_send, small_recv, store_sem,
    tail_send, tail_recv, pair_send, pair_recv,
):
    channels, xr, yr, zr = act.shape
    n = nx * ny
    cl, jl = MODES // nx, MODES // ny
    nh, hq = r_ref.shape[1], r_ref.shape[3]
    lanes = jl * channels
    rows = channels * yr
    tail = xr - hq * xq
    late = xr - xq
    gx, gy, seg = lax.axis_index("gx"), lax.axis_index("gy"), lax.axis_index("segment")
    me = gx * ny + gy
    mine = gy * nx + gx
    first, last = seg == 0, seg == 1
    mesh_ids = pl.DeviceIdType.MESH

    loads = [
        pltpu.make_async_copy(source, target, load_sem.at[k])
        for k, (source, target) in enumerate(
            [
                (act_hbm, act), (bzf_hbm, bzf), (kyt_hbm.at[gy], kyt), (w_hbm, w), (bx_hbm, bx),
                (sp_hbm, sp), (ky_hbm.at[gy], ky), (bzi_hbm, bzi), (cot_hbm, cot),
            ]
        )
    ]
    for load in loads[:3]:
        load.start()

    barrier = pltpu.get_barrier_semaphore()

    def greet(k, carry):
        other = lax.rem(seg * n + me + k, 2 * n)
        peer = lax.rem(other, n)
        pl.semaphore_signal(
            barrier, inc=1,
            device_id={"segment": other // n, "gx": peer // ny, "gy": lax.rem(peer, ny)},
            device_id_type=mesh_ids,
        )
        return carry

    lax.fori_loop(1, 2 * n, greet, 0)

    def ahead(source, target, send, recv):
        return pltpu.make_async_remote_copy(
            src_ref=source, dst_ref=target, send_sem=send, recv_sem=recv,
            device_id={"segment": 1 - seg}, device_id_type=mesh_ids,
        )

    def row_copy(x):
        return ahead(act_hbm.at[:, x], act1.at[:, x], row_send.at[x], row_recv.at[x])

    def send_rows(start, stop):
        for x in range(start, stop):
            row_copy(x).start()

    def modes_copy(k):
        return ahead(mt_send.at[k], mt_recv.at[k], small_send.at[k], small_recv.at[k])

    small = [
        ahead(mix_hbm, mixv1, small_send.at[2], small_recv.at[2]),
        ahead(bias_hbm, biasv1, small_send.at[3], small_recv.at[3]),
    ]

    def send(source, target, sends, receives):
        def begin(k, carry):
            peer = lax.rem(me + k, n)
            d, h = peer // ny, lax.rem(peer, ny)
            pltpu.make_async_remote_copy(
                src_ref=source(d, h), dst_ref=target, send_sem=sends, recv_sem=receives,
                device_id={"gx": d, "gy": h}, device_id_type=mesh_ids,
            ).start()
            return carry

        lax.fori_loop(1, n, begin, 0)
        target[...] = source(gx, gy)[...]

    def send_half(source, e, half):
        send(source, r_ref.at[e, half, mine], send_sem.at[e, half], recv_sem.at[e, half])

    def send_along(source, e, half):
        def begin(k, carry):
            d = lax.rem(gx + k, nx)
            pltpu.make_async_remote_copy(
                src_ref=source(d), dst_ref=r_ref.at[e, half, mine],
                send_sem=send_sem.at[e, half], recv_sem=recv_sem.at[e, half],
                device_id={"gx": d}, device_id_type=mesh_ids,
            ).start()
            return carry

        lax.fori_loop(1, nx, begin, 0)
        r_ref[e, half, mine] = source(gx)[...]

    def pair_copy(e, half):
        block = r_ref.at[e, half, pl.ds(gy * nx, nx)]
        return pltpu.make_async_remote_copy(
            src_ref=block, dst_ref=block,
            send_sem=pair_send.at[e, half], recv_sem=pair_recv.at[e, half],
            device_id={"gy": 1 - gy}, device_id_type=mesh_ids,
        )

    def forward(e, halves):
        for half in halves:
            await_block(r_ref.at[e, half, pl.ds(0, nx - 1)], recv_sem.at[e, half])
            pair_copy(e, half).start()

    def land(e, half):
        await_block(r_ref.at[e, half, pl.ds(0, nx)], pair_recv.at[e, half])

    def sent_along(e, half):
        await_block(r_ref.at[e, half, pl.ds(0, nx - 1)], send_sem.at[e, half])
        await_block(r_ref.at[e, half, pl.ds(0, nx)], pair_send.at[e, half])

    def send_tail(k, carry):
        peer = lax.rem(me + k, n)
        d, h = peer // ny, lax.rem(peer, ny)
        pltpu.make_async_remote_copy(
            src_ref=s_ref.at[2, nh - 1, h * nx + d], dst_ref=r_ref.at[4, nh - 1, mine],
            send_sem=tail_send.at[0], recv_sem=tail_recv.at[0],
            device_id={"segment": 0, "gx": d, "gy": h}, device_id_type=mesh_ids,
        ).start()
        return carry

    def await_block(block, sem):
        pltpu.make_async_copy(block, block, sem).wait()

    def arrive(e, half):
        await_block(r_ref.at[e, half, pl.ds(0, n - 1)], recv_sem.at[e, half])

    def sent(e, half):
        await_block(r_ref.at[e, half, pl.ds(0, n - 1)], send_sem.at[e, half])

    def to_modes(blocks, k, half):
        parts = []
        for block in blocks:
            g = dot(block, bzf[...])
            parts.append(g[:, : nx * 16] + g[:, nx * 16 :])
        top, rest = split(jnp.concatenate(parts, axis=1))
        t = dot(kyt[0], top) + dot(kyt[1], top) + dot(kyt[0], rest)
        t = t.T.astype(bf16)
        for q in range(len(blocks)):
            for h in range(ny):
                part = t[q * nx * 16 : (q + 1) * nx * 16, h * lanes : (h + 1) * lanes]
                s_ref[k, half, h * nx : (h + 1) * nx, q] = part.reshape(nx, 16, lanes)

    def to_field(e, half, q):
        return field_of(lambda h: r_ref[e, half, h * nx : (h + 1) * nx, q], ny, ky, bzi)

    def row(field, x):
        return field[:, x * zr : (x + 1) * zr].reshape(channels, yr, zr)

    def send_modes(k, e, half):
        send_half(lambda d, h: s_ref.at[k, half, h * nx + d], e, half)

    def own_modes(e, await_half):
        own = None
        for half in range(nh):
            await_half(half)
            block = r_ref[e, half].reshape(n * hq * 16, lanes)
            part = slice(half * n * hq * 16, (half + 1) * n * hq * 16)
            term = dot(bx[0, :, part], block) + dot(bx[1, :, part], block)
            own = term if own is None else own + term
        return own.T.reshape(jl, channels, cl * MODES)

    def send_cells(mt, k, e, halves):
        top, rest = split(mt)
        for half in halves:
            table = [sp[i, half].reshape(nx * hq * 16, cl * MODES) for i in range(2)]
            cells = dot(table[0], top) + dot(table[1], top) + dot(table[0], rest)
            p_ref[k, half] = cells.astype(bf16).reshape(nx, hq, 16, lanes)
            send_along(lambda d: p_ref.at[k, half, d], e, half)

    def mixed():
        return m_ref[...].reshape(lanes, cl * MODES).T

    def mix_back(e, await_half):
        grad_modes[...] = own_modes(e, await_half)

        def step(j, carry):
            m_ref[j] = jnp.sum(wd[j] * grad_modes[j][None], axis=1)
            return carry

        lax.fori_loop(0, jl, step, 0)

    def blend(mixing, values, o, back):
        total = (mixing[0, o] if back else mixing[o, 0]) * values[0]
        for i in range(1, channels):
            total = total + (mixing[i, o] if back else mixing[o, i]) * values[i]
        return total

    def fetch_small():
        for copy in small:
            copy.wait_recv()
        fetches = [
            pltpu.make_async_copy(source, target, store_sem.at[k])
            for k, (source, target) in enumerate([(mixv1, mix1), (biasv1, bias1)])
        ]
        for fetch in fetches:
            fetch.start()
        for fetch in fetches:
            fetch.wait()

    def back_block(half, q, offset):
        field = to_field(3, half, q)
        x0 = (half * hq + q) * xq
        block = []
        for k in range(xq):
            incoming = (row(field, k) + offset[:, x0 + k]).astype(bf16).astype(f32)
            signal = incoming * slope[:, x0 + k]
            block.append((x0 + k, signal))
        return block

    def packed(block):
        return jnp.concatenate([s.astype(bf16).reshape(rows, zr) for _, s in block], axis=1)

    def blend_back(start, stop):
        def step(x, carry):
            values = [sig[i, x] for i in range(channels)]
            for o in range(channels):
                u[o, x] = blend(mix_ref, values, o, True)
            return carry

        lax.fori_loop(start, stop, step, 0)

    pl.semaphore_wait(barrier, 2 * n - 1)
    for copy in small:
        copy.start()

    @pl.when(last)
    def _():
        send_rows(0, cuts[0])

    @pl.when(first)
    def _():
        send_rows(tail, tail + cuts[0])

    for load in loads[:3]:
        load.wait()
    for load in loads[3:]:
        load.start()
    for half in range(nh):
        blocks = []
        for q in range(hq):
            x = (half * hq + q) * xq
            block = [act[:, x + k].reshape(rows, zr) for k in range(xq)]
            blocks.append(jnp.concatenate(block, axis=1))
        to_modes(blocks, 0, half)
        send_modes(0, 0, half)

    for load in loads[3:]:
        load.wait()

    def dense(j, carry):
        for i in range(channels):
            wd[j, i] = jnp.concatenate([w[j, c, i] for c in range(cl)], axis=1)
        return carry

    lax.fori_loop(0, jl, dense, 0)

    def pointwise(x, carry):
        values = [act[i, x].astype(f32) for i in range(channels)]
        for o in range(channels):
            u[o, x] = blend(mix_ref, values, o, False) + bias_ref[0, o]
        return carry

    lax.fori_loop(0, xr, pointwise, 0)

    in_modes[...] = own_modes(0, lambda half: arrive(0, half))

    def mix(j, carry):
        own = in_modes[j]
        m_ref[j] = jnp.sum(wd[j] * own[:, None, :], axis=0)
        return carry

    lax.fori_loop(0, jl, mix, 0)
    mt_send[0] = mixed()
    modes_copy(0).start()

    @pl.when(last)
    def _():
        send_rows(cuts[0], cuts[1])

    @pl.when(first)
    def _():
        send_rows(tail + cuts[0], xr)

    send_cells(mt_send[0], 0, 1, range(nh))

    @pl.when(last)
    def _():
        forward(1, range(nh))
        for half in range(nh):
            land(1, half)
            blocks = []
            for q in range(hq):
                field = to_field(1, half, q)
                x0 = (half * hq + q) * xq
                block = []
                for k in range(xq):
                    signal = cot[:, x0 + k].astype(f32) * slope_of(row(field, k) + u[:, x0 + k])
                    sig[:, x0 + k] = signal
                    block.append(signal.astype(bf16).reshape(rows, zr))
                blocks.append(jnp.concatenate(block, axis=1))
            to_modes(blocks, 1, half)
            send_modes(1, 2, half)

        modes_copy(0).wait_recv()
        send_cells(mt_recv[0], 3, 5, [nh - 1])
        fetch_small()

        mix_back(2, lambda half: arrive(2, half))
        mt_send[1] = mixed()
        modes_copy(1).start()
        send_rows(cuts[1], cuts[2])
        send_cells(mt_send[1], 1, 3, reversed(range(nh)))

        blend_back(0, xr)
        forward(5, [nh - 1])
        land(5, nh - 1)
        for q in range(hq):
            field = to_field(5, nh - 1, q)
            x0 = tail + q * xq
            for k in range(xq):
                row_copy(x0 + k).wait_recv()
                values = [act1[i, x0 + k].astype(f32) for i in range(channels)]
                here = row(field, k)
                for o in range(channels):
                    pre = here[o] + blend(mix1, values, o, False) + bias1[0, o]
                    slope[o, x0 + k] = slope_of(pre)
        forward(3, reversed(range(nh)))
        land(3, nh - 1)
        to_modes([packed(back_block(nh - 1, q, u)) for q in range(hq)], 2, nh - 1)
        lax.fori_loop(0, n, send_tail, 0)
        send_rows(cuts[2], xr)

    def ahead_quarter(half, q):
        field = to_field(2, half, q)
        x0 = (half * hq + q) * xq
        for k in range(xq):
            row_copy(x0 + k).wait_recv()
            values = [act1[i, x0 + k].astype(f32) for i in range(channels)]
            here = row(field, k)
            signals = []
            for o in range(channels):
                pre = here[o] + blend(mix1, values, o, False) + bias1[0, o]
                signals.append(cot[o, x0 + k].astype(f32) * slope_of(pre))
            for i in range(channels):
                v[i, x0 + k] = blend(mix1, signals, i, True)

    def kept(block):
        for x, signal in block:
            sig[:, x] = signal
        return block

    @pl.when(first)
    def _():
        modes_copy(0).wait_recv()
        send_cells(mt_recv[0], 1, 2, range(nh))
        forward(1, range(nh))
        for half in range(nh):
            land(1, half)

            def step(q, carry):
                field = to_field(1, half, q)
                x0 = (half * hq + q) * xq
                for k in range(xq):
                    slope[:, x0 + k] = slope_of(row(field, k) + u[:, x0 + k])
                return carry

            lax.fori_loop(0, hq, step, 0)

        forward(2, range(nh))
        fetch_small()
        for half in range(nh):
            land(2, half)
        for half in range(nh - 1):
            for q in range(hq):
                ahead_quarter(half, q)
        modes_copy(1).wait_recv()
        send_cells(mt_recv[1], 2, 3, range(nh))
        forward(3, range(nh))
        for half in range(nh - 1):
            land(3, half)
            to_modes([packed(kept(back_block(half, q, v))) for q in range(hq)], 1, half)
            send_modes(1, 4, half)
        blend_back(0, tail)
        land(3, nh - 1)
        for q in range(hq - 1):
            ahead_quarter(nh - 1, q)
            kept(back_block(nh - 1, q, v))

        for target, e in ((v, 2), (u, 3)):
            field = to_field(e, nh - 1, hq - 1)
            for k in range(xq):
                target[:, late + k] = row(field, k)

        def await_half(half):
            if half < nh - 1:
                arrive(4, half)
            else:
                await_block(r_ref.at[4, half], tail_recv.at[0])

        mix_back(4, await_half)
        send_cells(mixed(), 3, 5, range(nh))
        if hq > 1:
            blend_back(tail, late)

    def weight_grad(j, carry):
        for c in range(cl):
            part = slice(c * MODES, (c + 1) * MODES)
            wgrad[j, c] = in_modes[j][:, None, part] * grad_modes[j][None, :, part]
        return carry

    lax.fori_loop(0, jl, weight_grad, 0)
    e = 3 + 2 * (1 - seg)

    @pl.when(last)
    def _():
        for half in range(nh - 1):
            land(3, half)

    @pl.when(first)
    def _():
        forward(5, range(nh))
        for half in range(nh - 1):
            land(5, half)

    for half in range(nh - 1):
        for q in range(hq):
            field = to_field(e, half, q)
            x0 = (half * hq + q) * xq
            for k in range(xq):
                out[:, x0 + k] = (row(field, k) + u[:, x0 + k]).astype(bf16)

    @pl.when(first)
    def _():
        land(5, nh - 1)
        rest_ref[:, : late - tail] = u[:, tail:late]

    cells_ref[...] = r_ref[e, nh - 1]

    @pl.when(first)
    def _():
        def step(k, carry):
            x = late + k
            row_copy(x).wait_recv()
            values = [act1[i, x].astype(f32) for i in range(channels)]
            signals = []
            for o in range(channels):
                pre = v[o, x] + blend(mix1, values, o, False) + bias1[0, o]
                signals.append(cot[o, x].astype(f32) * slope_of(pre))
            here = []
            for i in range(channels):
                incoming = u[i, x] + blend(mix1, signals, i, True)
                here.append(incoming.astype(bf16).astype(f32) * slope[i, x])
            for o in range(channels):
                rest_ref[o, late - tail + k] = blend(mix_ref, here, o, True)
            return carry

        lax.fori_loop(0, xq, step, 0)

    @pl.when(last)
    def _():
        rest_ref[...] = u[:, tail:]

    for half in range(nh):
        sent(0, half)
        sent_along(1, half)
        sent_along(3, half)
    for copy in small:
        copy.wait_send()
    modes_copy(0).wait_send()

    @pl.when(first)
    def _():
        for half in range(nh - 1):
            sent(4, half)
        for half in range(nh):
            sent_along(2, half)
            sent_along(5, half)
        for x in range(tail, xr):
            row_copy(x).wait_send()

    @pl.when(last)
    def _():
        for half in range(nh):
            sent(2, half)
        sent_along(5, nh - 1)
        modes_copy(1).wait_send()
        await_block(r_ref.at[4, nh - 1], tail_send.at[0])
        for x in range(xr):
            row_copy(x).wait_send()


def finish_kernel(
    nx, ny, xq, done_ref, rest_ref, cells_ref, wgrad, ky, bzi, grad_hbm, wgrad_hbm, out, sem
):
    channels, done, yr, zr = done_ref.shape
    hq = cells_ref.shape[1]
    stores = [
        pltpu.make_async_copy(wgrad, wgrad_hbm, sem.at[0]),
        pltpu.make_async_copy(done_ref, grad_hbm.at[:, pl.ds(0, done)], sem.at[1]),
    ]
    for store in stores:
        store.start()
    for q in range(hq):
        field = field_of(lambda h: cells_ref[h * nx : (h + 1) * nx, q], ny, ky, bzi)
        for k in range(xq):
            x = q * xq + k
            here = field[:, k * zr : (k + 1) * zr].reshape(channels, yr, zr)
            out[:, x] = (here + rest_ref[:, x]).astype(bf16)
        part = pl.ds(q * xq, xq)
        store = pltpu.make_async_copy(
            out.at[:, part], grad_hbm.at[:, pl.ds(done + q * xq, xq)], sem.at[2 + q]
        )
        store.start()
        stores.append(store)
    for store in stores:
        store.wait()


def in_hbm(value):
    return pltpu.with_memory_space_constraint(jnp.asarray(value), pltpu.HBM)


def two_section_body(activations, cotangent, spectral_weights, pointwise, channel_bias):
    inputs = activations[0]
    channels, xr, yr, zr = inputs.shape
    nx, ny = lax.axis_size("gx"), lax.axis_size("gy")
    n = nx * ny
    cl, jl = MODES // nx, MODES // ny
    xq = 16 // cl
    nh = 2
    hq = xr // (nh * xq)
    lanes, rows = jl * channels, channels * yr
    bz = trig_basis(zr).reshape(nx, cl, zr)
    eye_x, eye_c = np.eye(xq), np.eye(cl)
    bzf = np.einsum("dcz,xX->xzdXc", bz, eye_x).reshape(xq * zr, nx * 16)
    bzi = halves(bzf.reshape(xq, zr, nx * 16).transpose(2, 0, 1).reshape(nx * 16, xq * zr))
    by = trig_basis(yr * ny).reshape(MODES, ny, yr)
    ky = np.einsum("jgy,ik->giyjk", by, np.eye(channels)).reshape(ny, rows, ny * lanes)
    ky = halves(ky)
    bx = trig_basis(xr * nx).reshape(MODES, nx, nh, hq, xq)
    sp = np.einsum("adtqx,cC->tdqxCca", bx, eye_c).reshape(nh * nx * hq * 16, cl * MODES)
    bxf = np.broadcast_to(
        sp.reshape(nh, 1, nx * hq * 16, cl * MODES), (nh, ny, nx * hq * 16, cl * MODES)
    )
    bxf = bxf.reshape(nh * n * hq * 16, cl * MODES).T
    bzf = halves(bzf)
    tables = [
        np.ascontiguousarray(ky.transpose(1, 0, 3, 2)),
        np.ascontiguousarray(ky.transpose(1, 0, 2, 3)),
        np.concatenate([bzf[0], bzf[1]], axis=1),
        np.concatenate([bzi[0], bzi[0], bzi[1]], axis=0),
        halves(bxf),
        halves(sp).reshape(2, nh, nx, hq, 16, cl * MODES),
    ]
    weights, mixing = spectral_weights[0], pointwise[0]
    vmem = pl.BlockSpec(memory_space=pltpu.VMEM)
    smem = pl.BlockSpec(memory_space=pltpu.SMEM)
    hbm = pl.BlockSpec(memory_space=pl.ANY)
    dma = pltpu.SemaphoreType.DMA
    grid = inputs.shape
    done = grid[:1] + ((nh - 1) * hq * xq,) + grid[2:]
    left = grid[:1] + (hq * xq,) + grid[2:]
    scratch = [
        pltpu.VMEM(grid, bf16), pltpu.VMEM(grid, bf16), pltpu.VMEM(grid, bf16),
        pltpu.VMEM(weights.shape, f32),
        pltpu.VMEM((jl, channels, channels, cl * MODES), f32),
        pltpu.VMEM((2, ny * lanes, rows), bf16),
        pltpu.VMEM((xq * zr, 2 * nx * 16), bf16),
        pltpu.VMEM((2, cl * MODES, nh * n * hq * 16), bf16),
        pltpu.VMEM((2, nh, nx, hq, 16, cl * MODES), bf16),
        pltpu.VMEM(grid, f32), pltpu.VMEM(grid, f32), pltpu.VMEM(grid, f32), pltpu.VMEM(grid, f32),
        pltpu.VMEM((jl, channels, cl * MODES), f32),
        pltpu.VMEM((jl, channels, cl * MODES), f32),
        pltpu.VMEM((jl, channels, cl * MODES), f32),
        pltpu.VMEM((2, cl * MODES, lanes), f32),
        pltpu.VMEM((2, cl * MODES, lanes), f32),
        pltpu.VMEM(mixing.shape, f32), pltpu.VMEM(channel_bias.shape, f32),
        pltpu.SMEM(mixing.shape, f32), pltpu.SMEM(channel_bias.shape, f32),
        pltpu.VMEM((3, nh, n, hq, 16, lanes), bf16),
        pltpu.VMEM((4, nh, nx, hq, 16, lanes), bf16),
        pltpu.VMEM((6, nh, n, hq, 16, lanes), bf16),
        dma((9,)), dma((6, nh)), dma((6, nh)),
        dma((xr,)), dma((xr,)), dma((4,)), dma((4,)), dma((2,)), dma((1,)), dma((1,)), dma((6, nh)), dma((6, nh)),
    ]
    parts = pl.pallas_call(
        functools.partial(relay_kernel, nx, ny, xq, (3, 9, 12)),
        out_shape=(
            jax.ShapeDtypeStruct(done, bf16),
            jax.ShapeDtypeStruct(left, f32),
            jax.ShapeDtypeStruct((n, hq, 16, lanes), bf16),
            pltpu.VMEM(weights.shape, f32),
            jax.ShapeDtypeStruct((2, rows, ny * lanes), bf16),
            jax.ShapeDtypeStruct((3 * nx * 16, xq * zr), bf16),
        ),
        in_specs=[hbm, hbm, hbm, smem, smem] + [hbm] * (2 + len(tables)),
        out_specs=[vmem] * 6,
        scratch_shapes=scratch,
        compiler_params=pltpu.CompilerParams(
            collective_id=0, has_side_effects=True, vmem_limit_bytes=46 * 2**20
        ),
        cost_estimate=pl.CostEstimate(
            flops=4 * 10**9, bytes_accessed=2 * 10**7, transcendentals=10**7
        ),
    )(
        *[in_hbm(v) for v in (inputs, cotangent, weights)],
        mixing, channel_bias,
        *[in_hbm(v) for v in [mixing, channel_bias] + tables],
    )
    input_grad, weight_grad = pl.pallas_call(
        functools.partial(finish_kernel, nx, ny, xq),
        out_shape=(
            jax.ShapeDtypeStruct(grid, bf16),
            jax.ShapeDtypeStruct(weights.shape, f32),
        ),
        in_specs=[vmem] * 6,
        out_specs=(hbm, hbm),
        scratch_shapes=[pltpu.VMEM(left, bf16), dma((2 + hq,))],
        compiler_params=pltpu.CompilerParams(vmem_limit_bytes=24 * 2**20),
        cost_estimate=pl.CostEstimate(flops=10**9, bytes_accessed=10**7, transcendentals=0),
    )(*parts)
    return (input_grad[None], weight_grad[None])


def fits(mesh):
    nx = mesh.shape["gx"]
    return mesh.shape["segment"] == 2 and mesh.shape["gy"] == 2 and nx == 8


def solution(mesh):
    return jax.shard_map(
        two_section_body if fits(mesh) else body,
        mesh=mesh,
        in_specs=(
            P("segment", "groups", "gx", "gy", None),
            P("groups", "gx", "gy", None),
            P("segment", "gy", "gx", None, None, None),
            P("segment", None, None),
            P("segment", None),
        ),
        out_specs=(
            P("segment", "groups", "gx", "gy", None),
            P("segment", "gy", "gx", "groups", None, None),
        ),
        check_vma=False,
    )
```

```python
import functools
import math

import jax
import jax.numpy as jnp
import ml_dtypes
import numpy as np
from jax import lax
from jax.experimental import pallas as pl
from jax.experimental.pallas import tpu as pltpu
from jax.sharding import PartitionSpec as P

MODES = 32
f32, bf16 = jnp.float32, jnp.bfloat16


def from_behind(block, axis, distance):
    devices = range(lax.axis_size(axis))
    route = [(i - distance, i) for i in devices if i - distance in devices]
    return lax.ppermute(block, axis, route)


def trig_basis(length):
    half = MODES // 2
    freqs = np.arange(half)[:, None]
    points = np.arange(length)[None, :]
    step = 2.0 * math.pi / length
    rows = np.concatenate(
        [np.cos((freqs * points % length) * step), np.sin(((freqs + 1) * points % length) * step)]
    )
    scales = np.where(np.arange(MODES) == 0, 1.0 / math.sqrt(length), math.sqrt(2.0 / length))
    return rows * scales[:, None]


def halves(matrix):
    matrix = np.asarray(matrix, np.float32)
    top = matrix.astype(ml_dtypes.bfloat16)
    rest = (matrix - top.astype(np.float32)).astype(ml_dtypes.bfloat16)
    return np.stack([top, rest])


def split(value):
    top = value.astype(bf16)
    return top, (value - top.astype(f32)).astype(bf16)


def dot(a, b, ca=1, cb=0):
    return lax.dot_general(a, b, (((ca,), (cb,)), ((), ())), preferred_element_type=f32)


def kernel(
    back, nx, ny, xr, *refs
):
    if back:
        (inc_ref, slope_ref, w_hbm, mix_ref, bz_ref, bzs_ref, ky_ref, kyt_ref, bx_ref, bxr_ref,
         out_ref, modes_ref, got_ref, *scratch) = refs
    else:
        (inc_ref, w_hbm, mix_ref, bias_ref, bz_ref, bzs_ref, ky_ref, kyt_ref, bx_ref, bxr_ref,
         out_ref, modes_ref, got_ref, *scratch) = refs
    (w_ref, sig_ref, ghi_ref, glo_ref, s_ref, r_ref, m_ref, p_ref, q_ref, qs_ref,
     send1, recv1, send2, recv2, wsem) = scratch
    channels, _, yr, zr = inc_ref.shape
    cl, jl, xp = MODES // nx, MODES // ny, r_ref.shape[2]
    n = nx * ny
    lanes = jl * channels
    gx, gy = lax.axis_index("gx"), lax.axis_index("gy")
    me = gx * ny + gy

    wcopy = pltpu.make_async_copy(w_hbm, w_ref, wsem)
    wcopy.start()

    barrier = pltpu.get_barrier_semaphore()

    def greet(k, carry):
        peer = lax.rem(me + k, n)
        pl.semaphore_signal(
            barrier, inc=1,
            device_id={"gx": peer // ny, "gy": lax.rem(peer, ny)},
            device_id_type=pl.DeviceIdType.MESH,
        )
        return carry

    lax.fori_loop(1, n, greet, 0)

    def along_z(x, carry):
        if back:
            signal = inc_ref[:, x].astype(f32) * slope_ref[:, x]
            sig_ref[:, x] = signal
            block = signal.astype(bf16)
        else:
            block = inc_ref[:, x]
        block = block.reshape(channels * yr, zr)
        g = dot(bz_ref[0], block, 1, 1) + dot(bz_ref[1], block, 1, 1)
        ghi, glo = split(g)
        rows = pl.ds(pl.multiple_of(x * MODES, MODES), MODES)
        ghi_ref[rows, :] = ghi
        glo_ref[rows, :] = glo
        return carry

    lax.fori_loop(0, xr, along_z, 0)
    ghi = ghi_ref[...]
    t = dot(ghi, ky_ref[0]) + dot(ghi, ky_ref[1]) + dot(glo_ref[...], ky_ref[0])
    t = jnp.swapaxes(t.reshape(xr, MODES, ny * lanes), 0, 1)
    if xp > xr:
        t = jnp.concatenate([t, jnp.zeros((MODES, xp - xr, ny * lanes), f32)], axis=1)
    t = t.astype(bf16)
    for h in range(ny):
        s_ref[h] = t[:, :, h * lanes : (h + 1) * lanes].reshape(nx, cl, xp, lanes)

    pl.semaphore_wait(barrier, n - 1)

    def exchange(source, target, send, recv):
        def copy_to(peer, slot_of):
            return pltpu.make_async_remote_copy(
                src_ref=source(peer // ny, lax.rem(peer, ny)),
                dst_ref=target.at[lax.rem(slot_of, ny) * nx + slot_of // ny],
                send_sem=send.at[peer],
                recv_sem=recv.at[slot_of],
                device_id={"gx": peer // ny, "gy": lax.rem(peer, ny)},
                device_id_type=pl.DeviceIdType.MESH,
            )

        def begin(k, carry):
            copy_to(lax.rem(me + k, n), me).start()
            return carry

        def finish(k, carry):
            copy_to(lax.rem(me + k, n), me).wait_send()
            peer = lax.rem(me + n - k, n)
            copy_to(peer, peer).wait_recv()
            return carry

        lax.fori_loop(1, n, begin, 0)
        target[gy * nx + gx] = source(gx, gy)[...]
        lax.fori_loop(1, n, finish, 0)

    exchange(lambda d, h: s_ref.at[h, d], r_ref, send1, recv1)

    for c in range(cl):
        part = r_ref[:, c].reshape(n * xp, lanes)
        own = dot(bx_ref[0], part) + dot(bx_ref[1], part)
        modes_ref[c] = own.T.reshape(jl, channels, MODES)
    wcopy.wait()

    def mix(j, carry):
        for c in range(cl):
            own = modes_ref[c, j]
            weight = w_ref[j, c]
            if back:
                m_ref[c, j] = jnp.sum(weight * own[None], axis=1)
            else:
                m_ref[c, j] = jnp.sum(weight * own[:, None, :], axis=0)
        return carry

    lax.fori_loop(0, jl, mix, 0)
    for c in range(cl):
        top, rest = split(m_ref[c].reshape(lanes, MODES))
        spread = (
            dot(bxr_ref[0], top, 1, 1) + dot(bxr_ref[1], top, 1, 1) + dot(bxr_ref[0], rest, 1, 1)
        )
        p_ref[:, c] = spread.astype(bf16).reshape(nx, xp, lanes)

    exchange(lambda d, h: p_ref.at[d], q_ref, send2, recv2)

    got = [q_ref[h * nx : (h + 1) * nx].reshape(MODES, xp, lanes) for h in range(ny)]
    got = jnp.concatenate(got, axis=2).astype(f32)
    got = jnp.swapaxes(got, 0, 1)[:xr].reshape(xr * MODES, ny * lanes).astype(bf16)
    got_ref[...] = got
    qs_ref[...] = dot(got, kyt_ref[0]) + dot(got, kyt_ref[1])

    def finish_field(x, carry):
        rows = pl.ds(pl.multiple_of(x * MODES, MODES), MODES)
        top, rest = split(qs_ref[rows, :])
        stack = jnp.concatenate([top, rest, top], axis=0)
        field = dot(stack, bzs_ref[...], 0, 0).reshape(channels, yr, zr)
        if back:
            values = [sig_ref[i, x] for i in range(channels)]
        else:
            values = [inc_ref[i, x].astype(f32) for i in range(channels)]
        for o in range(channels):
            total = field[o]
            for i in range(channels):
                total = total + (mix_ref[i, o] if back else mix_ref[o, i]) * values[i]
            if back:
                out_ref[o, x] = total.astype(bf16)
            else:
                total = total + bias_ref[0, o]
                cdf = 0.5 * (1.0 + lax.erf(total * 0.7071067811865476))
                out_ref[o, x] = cdf + total * jnp.exp(-0.5 * total * total) * 0.3989422804014327
        return carry

    lax.fori_loop(0, xr, finish_field, 0)


def ahead_kernel(
    act_ref, cot_ref, got_ref, got_back_ref, mix_ref, bias_ref, bzs_ref, kyt_ref, out_ref,
    pre_ref, back_ref,
):
    channels, xr, yr, zr = act_ref.shape
    pre_ref[...] = dot(got_ref[...], kyt_ref[0]) + dot(got_ref[...], kyt_ref[1])
    back_ref[...] = dot(got_back_ref[...], kyt_ref[0]) + dot(got_back_ref[...], kyt_ref[1])

    def field_of(ref, x):
        rows = pl.ds(pl.multiple_of(x * MODES, MODES), MODES)
        top, rest = split(ref[rows, :])
        stack = jnp.concatenate([top, rest, top], axis=0)
        return dot(stack, bzs_ref[...], 0, 0).reshape(channels, yr, zr)

    def step(x, carry):
        field = field_of(pre_ref, x)
        values = [act_ref[i, x].astype(f32) for i in range(channels)]
        signals = []
        for o in range(channels):
            total = field[o]
            for i in range(channels):
                total = total + mix_ref[o, i] * values[i]
            total = total + bias_ref[0, o]
            cdf = 0.5 * (1.0 + lax.erf(total * 0.7071067811865476))
            slope = cdf + total * jnp.exp(-0.5 * total * total) * 0.3989422804014327
            signals.append(cot_ref[o, x].astype(f32) * slope)
        field = field_of(back_ref, x)
        for o in range(channels):
            total = field[o]
            for i in range(channels):
                total = total + mix_ref[i, o] * signals[i]
            out_ref[o, x] = total.astype(bf16)
        return carry

    lax.fori_loop(0, xr, step, 0)


def ahead(activations, cotangent, got, got_back, mixing, bias, bzs, kyt):
    channels, xr, yr, zr = activations.shape
    vmem = pl.BlockSpec(memory_space=pltpu.VMEM)
    smem = pl.BlockSpec(memory_space=pltpu.SMEM)
    return pl.pallas_call(
        ahead_kernel,
        out_shape=jax.ShapeDtypeStruct(activations.shape, bf16),
        in_specs=[vmem] * 4 + [smem] * 2 + [vmem] * 2,
        out_specs=vmem,
        scratch_shapes=[pltpu.VMEM((xr * MODES, channels * yr), f32)] * 2,
        compiler_params=pltpu.CompilerParams(vmem_limit_bytes=50 * 2**20),
        cost_estimate=pl.CostEstimate(flops=10**9, bytes_accessed=10**7, transcendentals=10**6),
    )(activations, cotangent, got, got_back, mixing, bias, bzs, kyt)


def block_turn(back, nx, ny, collective, field, slope, weights, mixing, bias, tables):
    channels, xr, yr, zr = field.shape
    xp = -(-xr // 16) * 16
    cl, jl, n = MODES // nx, MODES // ny, nx * ny
    lanes = jl * channels
    vmem = pl.BlockSpec(memory_space=pltpu.VMEM)
    smem = pl.BlockSpec(memory_space=pltpu.SMEM)
    hbm = pl.BlockSpec(memory_space=pl.ANY)
    if back:
        args = (field, slope, weights, mixing, *tables)
        specs = [vmem, vmem, hbm, smem] + [vmem] * len(tables)
    else:
        args = (field, weights, mixing, bias, *tables)
        specs = [vmem, hbm, smem, smem] + [vmem] * len(tables)
    dma = pltpu.SemaphoreType.DMA
    return pl.pallas_call(
        functools.partial(kernel, back, nx, ny, xr),
        out_shape=(
            jax.ShapeDtypeStruct(field.shape, bf16 if back else f32),
            jax.ShapeDtypeStruct((cl, jl, channels, MODES), f32),
            jax.ShapeDtypeStruct((xr * MODES, ny * lanes), bf16),
        ),
        in_specs=specs,
        out_specs=(vmem, vmem, vmem),
        scratch_shapes=[
            pltpu.VMEM(weights.shape, f32),
            pltpu.VMEM(field.shape if back else (8, 128), f32),
            pltpu.VMEM((xr * MODES, channels * yr), bf16),
            pltpu.VMEM((xr * MODES, channels * yr), bf16),
            pltpu.VMEM((ny, nx, cl, xp, lanes), bf16),
            pltpu.VMEM((n, cl, xp, lanes), bf16),
            pltpu.VMEM((cl, jl, channels, MODES), f32),
            pltpu.VMEM((nx, cl, xp, lanes), bf16),
            pltpu.VMEM((n, cl, xp, lanes), bf16),
            pltpu.VMEM((xr * MODES, channels * yr), f32),
            dma((n,)), dma((n,)), dma((n,)), dma((n,)), dma,
        ],
        compiler_params=pltpu.CompilerParams(
            collective_id=collective, has_side_effects=True, vmem_limit_bytes=50 * 2**20
        ),
        cost_estimate=pl.CostEstimate(flops=10**9, bytes_accessed=2 * 10**7, transcendentals=10**6),
    )(*args)


def body(activations, cotangent, spectral_weights, pointwise, channel_bias):
    inputs = activations[0]
    channels, xr, yr, zr = inputs.shape
    nx, ny = lax.axis_size("gx"), lax.axis_size("gy")
    xp = -(-xr // 16) * 16
    bz = trig_basis(zr)
    bx = trig_basis(xr * nx).reshape(MODES, nx, xr)
    bx = np.concatenate([bx, np.zeros((MODES, nx, xp - xr))], axis=2).reshape(MODES, nx * xp)
    by = trig_basis(yr * ny).reshape(MODES, ny, yr)
    kron = np.einsum("jgy,ik->giyjk", by, np.eye(channels)).reshape(
        ny, channels * yr, MODES * channels
    )
    bzh = halves(bz)
    kh = halves(kron)
    gy = lax.axis_index("gy")
    ky = lax.dynamic_index_in_dim(jnp.asarray(np.swapaxes(kh, 0, 1)), gy, 0, False)
    kyt = lax.dynamic_index_in_dim(
        jnp.asarray(np.ascontiguousarray(np.transpose(kh, (1, 0, 3, 2)))), gy, 0, False
    )
    tables = (
        jnp.asarray(bzh),
        jnp.asarray(np.concatenate([bzh[0], bzh[0], bzh[1]], axis=0)),
        ky,
        kyt,
        jnp.asarray(halves(np.concatenate([bx] * ny, axis=1))),
        jnp.asarray(halves(bx.T)),
    )
    weights = spectral_weights[0]
    mixing = pointwise[0]
    following = [from_behind(v, "segment", -1) for v in (inputs, mixing, channel_bias)]
    slope, input_modes, got = block_turn(
        False, nx, ny, 0, inputs, None, weights, mixing, channel_bias, tables
    )
    next_got = from_behind(got, "segment", -1)
    segment_index = lax.axis_index("segment")
    segment_count = lax.axis_size("segment")
    incoming = cotangent
    kept_grad = jnp.zeros(cotangent.shape, bf16)
    kept_modes = jnp.zeros(input_modes.shape, f32)
    for turn_index in range(segment_count):
        active = segment_index == segment_count - 1 - turn_index
        input_grad, grad_modes, got_back = block_turn(
            True, nx, ny, 1 + turn_index, incoming, slope, weights, mixing, None, tables
        )
        kept_grad = jnp.where(active, input_grad, kept_grad)
        kept_modes = jnp.where(active, grad_modes, kept_modes)
        if turn_index == 0 and segment_count > 1:
            next_back = from_behind(got_back, "segment", -1)
            incoming = ahead(
                following[0], cotangent, next_got, next_back, following[1], following[2],
                tables[1], tables[3],
            )
        elif turn_index + 1 < segment_count:
            incoming = from_behind(input_grad, "segment", -1)
    input_modes = jnp.swapaxes(input_modes, 0, 1)
    kept_modes = jnp.swapaxes(kept_modes, 0, 1)
    weight_grad = input_modes[:, :, :, None, :] * kept_modes[:, :, None, :, :]
    return (kept_grad[None], weight_grad[None])


def slope_of(value):
    cdf = 0.5 * (1.0 + lax.erf(value * 0.7071067811865476))
    return cdf + value * jnp.exp(-0.5 * value * value) * 0.3989422804014327


def field_of(cells, ny, ky, bzi):
    blocks = []
    for h in range(ny):
        block = cells(h)
        blocks.append(block.reshape(block.shape[0] * block.shape[1], block.shape[2]))
    block = jnp.concatenate(blocks, axis=1)
    top, rest = split(dot(ky[0], block, 1, 1) + dot(ky[1], block, 1, 1))
    return dot(jnp.concatenate([top, rest, top], axis=1), bzi[...])


def relay_kernel(
    nx, ny, xq, cuts,
    act_hbm, cot_hbm, w_hbm, mix_ref, bias_ref, mix_hbm, bias_hbm,
    kyt_hbm, ky_hbm, bzf_hbm, bzi_hbm, bx_hbm, sp_hbm,
    out, rest_ref, cells_ref, wgrad, ky, bzi,
    act, act1, cot, w, wd, kyt, bzf, bx, sp,
    u, v, slope, sig, in_modes, grad_modes, m_ref, mt_send, mt_recv,
    mixv1, biasv1, mix1, bias1, s_ref, p_ref, r_ref,
    load_sem, send_sem, recv_sem, row_send, row_recv, small_send, small_recv, store_sem,
    tail_send, tail_recv, pair_send, pair_recv,
):
    channels, xr, yr, zr = act.shape
    n = nx * ny
    cl, jl = MODES // nx, MODES // ny
    nh, hq = r_ref.shape[1], r_ref.shape[3]
    lanes = jl * channels
    rows = channels * yr
    tail = xr - hq * xq
    late = xr - xq
    gx, gy, seg = lax.axis_index("gx"), lax.axis_index("gy"), lax.axis_index("segment")
    me = gx * ny + gy
    mine = gy * nx + gx
    first, last = seg == 0, seg == 1
    mesh_ids = pl.DeviceIdType.MESH

    loads = [
        pltpu.make_async_copy(source, target, load_sem.at[k])
        for k, (source, target) in enumerate(
            [
                (act_hbm, act), (bzf_hbm, bzf), (kyt_hbm.at[gy], kyt), (w_hbm, w), (bx_hbm, bx),
                (sp_hbm, sp), (ky_hbm.at[gy], ky), (bzi_hbm, bzi), (cot_hbm, cot),
            ]
        )
    ]
    for load in loads[:3]:
        load.start()

    barrier = pltpu.get_barrier_semaphore()

    def greet(k, carry):
        other = lax.rem(seg * n + me + k, 2 * n)
        peer = lax.rem(other, n)
        pl.semaphore_signal(
            barrier, inc=1,
            device_id={"segment": other // n, "gx": peer // ny, "gy": lax.rem(peer, ny)},
            device_id_type=mesh_ids,
        )
        return carry

    lax.fori_loop(1, 2 * n, greet, 0)

    def ahead(source, target, send, recv):
        return pltpu.make_async_remote_copy(
            src_ref=source, dst_ref=target, send_sem=send, recv_sem=recv,
            device_id={"segment": 1 - seg}, device_id_type=mesh_ids,
        )

    def row_copy(x):
        return ahead(act_hbm.at[:, x], act1.at[:, x], row_send.at[x], row_recv.at[x])

    def send_rows(start, stop):
        for x in range(start, stop):
            row_copy(x).start()

    def modes_copy(k):
        return ahead(mt_send.at[k], mt_recv.at[k], small_send.at[k], small_recv.at[k])

    small = [
        ahead(mix_hbm, mixv1, small_send.at[2], small_recv.at[2]),
        ahead(bias_hbm, biasv1, small_send.at[3], small_recv.at[3]),
    ]

    def send(source, target, sends, receives):
        def begin(k, carry):
            peer = lax.rem(me + k, n)
            d, h = peer // ny, lax.rem(peer, ny)
            pltpu.make_async_remote_copy(
                src_ref=source(d, h), dst_ref=target, send_sem=sends, recv_sem=receives,
                device_id={"gx": d, "gy": h}, device_id_type=mesh_ids,
            ).start()
            return carry

        lax.fori_loop(1, n, begin, 0)
        target[...] = source(gx, gy)[...]

    def send_half(source, e, half):
        send(source, r_ref.at[e, half, mine], send_sem.at[e, half], recv_sem.at[e, half])

    def send_along(source, e, half):
        def begin(k, carry):
            d = lax.rem(gx + k, nx)
            pltpu.make_async_remote_copy(
                src_ref=source(d), dst_ref=r_ref.at[e, half, mine],
                send_sem=send_sem.at[e, half], recv_sem=recv_sem.at[e, half],
                device_id={"gx": d}, device_id_type=mesh_ids,
            ).start()
            return carry

        lax.fori_loop(1, nx, begin, 0)
        r_ref[e, half, mine] = source(gx)[...]

    def pair_copy(e, half):
        block = r_ref.at[e, half, pl.ds(gy * nx, nx)]
        return pltpu.make_async_remote_copy(
            src_ref=block, dst_ref=block,
            send_sem=pair_send.at[e, half], recv_sem=pair_recv.at[e, half],
            device_id={"gy": 1 - gy}, device_id_type=mesh_ids,
        )

    def forward(e, halves):
        for half in halves:
            await_block(r_ref.at[e, half, pl.ds(0, nx - 1)], recv_sem.at[e, half])
            pair_copy(e, half).start()

    def land(e, half):
        await_block(r_ref.at[e, half, pl.ds(0, nx)], pair_recv.at[e, half])

    def sent_along(e, half):
        await_block(r_ref.at[e, half, pl.ds(0, nx - 1)], send_sem.at[e, half])
        await_block(r_ref.at[e, half, pl.ds(0, nx)], pair_send.at[e, half])

    def send_tail(k, carry):
        peer = lax.rem(me + k, n)
        d, h = peer // ny, lax.rem(peer, ny)
        pltpu.make_async_remote_copy(
            src_ref=s_ref.at[2, nh - 1, h * nx + d], dst_ref=r_ref.at[4, nh - 1, mine],
            send_sem=tail_send.at[0], recv_sem=tail_recv.at[0],
            device_id={"segment": 0, "gx": d, "gy": h}, device_id_type=mesh_ids,
        ).start()
        return carry

    def await_block(block, sem):
        pltpu.make_async_copy(block, block, sem).wait()

    def arrive(e, half):
        await_block(r_ref.at[e, half, pl.ds(0, n - 1)], recv_sem.at[e, half])

    def sent(e, half):
        await_block(r_ref.at[e, half, pl.ds(0, n - 1)], send_sem.at[e, half])

    def to_modes(blocks, k, half):
        parts = []
        for block in blocks:
            g = dot(block, bzf[...])
            parts.append(g[:, : nx * 16] + g[:, nx * 16 :])
        top, rest = split(jnp.concatenate(parts, axis=1))
        t = dot(kyt[0], top) + dot(kyt[1], top) + dot(kyt[0], rest)
        t = t.T.astype(bf16)
        for q in range(len(blocks)):
            for h in range(ny):
                part = t[q * nx * 16 : (q + 1) * nx * 16, h * lanes : (h + 1) * lanes]
                s_ref[k, half, h * nx : (h + 1) * nx, q] = part.reshape(nx, 16, lanes)

    def to_field(e, half, q):
        return field_of(lambda h: r_ref[e, half, h * nx : (h + 1) * nx, q], ny, ky, bzi)

    def row(field, x):
        return field[:, x * zr : (x + 1) * zr].reshape(channels, yr, zr)

    def send_modes(k, e, half):
        send_half(lambda d, h: s_ref.at[k, half, h * nx + d], e, half)

    def own_modes(e, await_half):
        own = None
        for half in range(nh):
            await_half(half)
            block = r_ref[e, half].reshape(n * hq * 16, lanes)
            part = slice(half * n * hq * 16, (half + 1) * n * hq * 16)
            term = dot(bx[0, :, part], block) + dot(bx[1, :, part], block)
            own = term if own is None else own + term
        return own.T.reshape(jl, channels, cl * MODES)

    def send_cells(mt, k, e, halves):
        top, rest = split(mt)
        for half in halves:
            table = [sp[i, half].reshape(nx * hq * 16, cl * MODES) for i in range(2)]
            cells = dot(table[0], top) + dot(table[1], top) + dot(table[0], rest)
            p_ref[k, half] = cells.astype(bf16).reshape(nx, hq, 16, lanes)
            send_along(lambda d: p_ref.at[k, half, d], e, half)

    def mixed():
        return m_ref[...].reshape(lanes, cl * MODES).T

    def mix_back(e, await_half):
        grad_modes[...] = own_modes(e, await_half)

        def step(j, carry):
            m_ref[j] = jnp.sum(wd[j] * grad_modes[j][None], axis=1)
            return carry

        lax.fori_loop(0, jl, step, 0)

    def blend(mixing, values, o, back):
        total = (mixing[0, o] if back else mixing[o, 0]) * values[0]
        for i in range(1, channels):
            total = total + (mixing[i, o] if back else mixing[o, i]) * values[i]
        return total

    def fetch_small():
        for copy in small:
            copy.wait_recv()
        for k, (source, target) in enumerate([(mixv1, mix1), (biasv1, bias1)]):
            copy = pltpu.make_async_copy(source, target, store_sem.at[k])
            copy.start()
            copy.wait()

    def back_block(half, q, offset):
        field = to_field(3, half, q)
        x0 = (half * hq + q) * xq
        block = []
        for k in range(xq):
            incoming = (row(field, k) + offset[:, x0 + k]).astype(bf16).astype(f32)
            signal = incoming * slope[:, x0 + k]
            block.append((x0 + k, signal))
        return block

    def packed(block):
        return jnp.concatenate([s.astype(bf16).reshape(rows, zr) for _, s in block], axis=1)

    def blend_back(start, stop):
        def step(x, carry):
            values = [sig[i, x] for i in range(channels)]
            for o in range(channels):
                u[o, x] = blend(mix_ref, values, o, True)
            return carry

        lax.fori_loop(start, stop, step, 0)

    pl.semaphore_wait(barrier, 2 * n - 1)
    for copy in small:
        copy.start()

    @pl.when(last)
    def _():
        send_rows(0, cuts[0])

    @pl.when(first)
    def _():
        send_rows(tail, tail + cuts[0])

    for load in loads[:3]:
        load.wait()
    for load in loads[3:]:
        load.start()
    for half in range(nh):
        blocks = []
        for q in range(hq):
            x = (half * hq + q) * xq
            block = [act[:, x + k].reshape(rows, zr) for k in range(xq)]
            blocks.append(jnp.concatenate(block, axis=1))
        to_modes(blocks, 0, half)
        send_modes(0, 0, half)

    for load in loads[3:]:
        load.wait()

    def dense(j, carry):
        for i in range(channels):
            wd[j, i] = jnp.concatenate([w[j, c, i] for c in range(cl)], axis=1)
        return carry

    lax.fori_loop(0, jl, dense, 0)

    def pointwise(x, carry):
        values = [act[i, x].astype(f32) for i in range(channels)]
        for o in range(channels):
            u[o, x] = blend(mix_ref, values, o, False) + bias_ref[0, o]
        return carry

    lax.fori_loop(0, xr, pointwise, 0)

    in_modes[...] = own_modes(0, lambda half: arrive(0, half))

    def mix(j, carry):
        own = in_modes[j]
        m_ref[j] = jnp.sum(wd[j] * own[:, None, :], axis=0)
        return carry

    lax.fori_loop(0, jl, mix, 0)
    mt_send[0] = mixed()
    modes_copy(0).start()

    @pl.when(last)
    def _():
        send_rows(cuts[0], cuts[1])

    @pl.when(first)
    def _():
        send_rows(tail + cuts[0], xr)

    send_cells(mt_send[0], 0, 1, range(nh))

    @pl.when(last)
    def _():
        forward(1, range(nh))
        for half in range(nh):
            land(1, half)
            blocks = []
            for q in range(hq):
                field = to_field(1, half, q)
                x0 = (half * hq + q) * xq
                block = []
                for k in range(xq):
                    signal = cot[:, x0 + k].astype(f32) * slope_of(row(field, k) + u[:, x0 + k])
                    sig[:, x0 + k] = signal
                    block.append(signal.astype(bf16).reshape(rows, zr))
                blocks.append(jnp.concatenate(block, axis=1))
            to_modes(blocks, 1, half)
            send_modes(1, 2, half)

        modes_copy(0).wait_recv()
        send_cells(mt_recv[0], 3, 5, [nh - 1])
        fetch_small()

        mix_back(2, lambda half: arrive(2, half))
        mt_send[1] = mixed()
        modes_copy(1).start()
        send_rows(cuts[1], cuts[2])
        send_cells(mt_send[1], 1, 3, reversed(range(nh)))

        blend_back(0, xr)
        forward(5, [nh - 1])
        land(5, nh - 1)
        for q in range(hq):
            field = to_field(5, nh - 1, q)
            x0 = tail + q * xq
            for k in range(xq):
                row_copy(x0 + k).wait_recv()
                values = [act1[i, x0 + k].astype(f32) for i in range(channels)]
                here = row(field, k)
                for o in range(channels):
                    pre = here[o] + blend(mix1, values, o, False) + bias1[0, o]
                    slope[o, x0 + k] = slope_of(pre)
        forward(3, reversed(range(nh)))
        land(3, nh - 1)
        to_modes([packed(back_block(nh - 1, q, u)) for q in range(hq)], 2, nh - 1)
        lax.fori_loop(0, n, send_tail, 0)
        send_rows(cuts[2], xr)

    def ahead_quarter(half, q):
        field = to_field(2, half, q)
        x0 = (half * hq + q) * xq
        for k in range(xq):
            row_copy(x0 + k).wait_recv()
            values = [act1[i, x0 + k].astype(f32) for i in range(channels)]
            here = row(field, k)
            signals = []
            for o in range(channels):
                pre = here[o] + blend(mix1, values, o, False) + bias1[0, o]
                signals.append(cot[o, x0 + k].astype(f32) * slope_of(pre))
            for i in range(channels):
                v[i, x0 + k] = blend(mix1, signals, i, True)

    def kept(block):
        for x, signal in block:
            sig[:, x] = signal
        return block

    @pl.when(first)
    def _():
        modes_copy(0).wait_recv()
        send_cells(mt_recv[0], 1, 2, range(nh))
        fetch_small()
        forward(1, range(nh))
        for half in range(nh):
            land(1, half)

            def step(q, carry):
                field = to_field(1, half, q)
                x0 = (half * hq + q) * xq
                for k in range(xq):
                    slope[:, x0 + k] = slope_of(row(field, k) + u[:, x0 + k])
                return carry

            lax.fori_loop(0, hq, step, 0)

        forward(2, range(nh))
        for half in range(nh):
            land(2, half)
        for half in range(nh - 1):
            for q in range(hq):
                ahead_quarter(half, q)
        modes_copy(1).wait_recv()
        send_cells(mt_recv[1], 2, 3, range(nh))
        forward(3, range(nh))
        for half in range(nh - 1):
            land(3, half)
            to_modes([packed(kept(back_block(half, q, v))) for q in range(hq)], 1, half)
            send_modes(1, 4, half)
        blend_back(0, tail)
        land(3, nh - 1)
        for q in range(hq - 1):
            ahead_quarter(nh - 1, q)
            kept(back_block(nh - 1, q, v))

        for target, e in ((v, 2), (u, 3)):
            field = to_field(e, nh - 1, hq - 1)
            for k in range(xq):
                target[:, late + k] = row(field, k)

        def await_half(half):
            if half < nh - 1:
                arrive(4, half)
            else:
                await_block(r_ref.at[4, half], tail_recv.at[0])

        mix_back(4, await_half)
        send_cells(mixed(), 3, 5, range(nh))
        if hq > 1:
            blend_back(tail, late)

    def weight_grad(j, carry):
        for c in range(cl):
            part = slice(c * MODES, (c + 1) * MODES)
            wgrad[j, c] = in_modes[j][:, None, part] * grad_modes[j][None, :, part]
        return carry

    lax.fori_loop(0, jl // 2, weight_grad, 0)

    @pl.when(first)
    def _():
        forward(5, range(nh))

    lax.fori_loop(jl // 2, jl, weight_grad, 0)
    e = 3 + 2 * (1 - seg)

    @pl.when(last)
    def _():
        for half in range(nh - 1):
            land(3, half)

    @pl.when(first)
    def _():
        for half in range(nh - 1):
            land(5, half)

    for half in range(nh - 1):
        for q in range(hq):
            field = to_field(e, half, q)
            x0 = (half * hq + q) * xq
            for k in range(xq):
                out[:, x0 + k] = (row(field, k) + u[:, x0 + k]).astype(bf16)

    @pl.when(first)
    def _():
        land(5, nh - 1)
        rest_ref[:, : late - tail] = u[:, tail:late]

    cells_ref[...] = r_ref[e, nh - 1]

    @pl.when(first)
    def _():
        def step(k, carry):
            x = late + k
            row_copy(x).wait_recv()
            values = [act1[i, x].astype(f32) for i in range(channels)]
            signals = []
            for o in range(channels):
                pre = v[o, x] + blend(mix1, values, o, False) + bias1[0, o]
                signals.append(cot[o, x].astype(f32) * slope_of(pre))
            here = []
            for i in range(channels):
                incoming = u[i, x] + blend(mix1, signals, i, True)
                here.append(incoming.astype(bf16).astype(f32) * slope[i, x])
            for o in range(channels):
                rest_ref[o, late - tail + k] = blend(mix_ref, here, o, True)
            return carry

        lax.fori_loop(0, xq, step, 0)

    @pl.when(last)
    def _():
        rest_ref[...] = u[:, tail:]

    for half in range(nh):
        sent(0, half)
        sent_along(1, half)
        sent_along(3, half)
    for copy in small:
        copy.wait_send()
    modes_copy(0).wait_send()

    @pl.when(first)
    def _():
        for half in range(nh - 1):
            sent(4, half)
        for half in range(nh):
            sent_along(2, half)
            sent_along(5, half)
        for x in range(tail, xr):
            row_copy(x).wait_send()

    @pl.when(last)
    def _():
        for half in range(nh):
            sent(2, half)
        sent_along(5, nh - 1)
        modes_copy(1).wait_send()
        await_block(r_ref.at[4, nh - 1], tail_send.at[0])
        for x in range(xr):
            row_copy(x).wait_send()


def finish_kernel(
    nx, ny, xq, done_ref, rest_ref, cells_ref, wgrad, ky, bzi, grad_hbm, wgrad_hbm, out, sem
):
    channels, done, yr, zr = done_ref.shape
    hq = cells_ref.shape[1]
    stores = [
        pltpu.make_async_copy(wgrad, wgrad_hbm, sem.at[0]),
        pltpu.make_async_copy(done_ref, grad_hbm.at[:, pl.ds(0, done)], sem.at[1]),
    ]
    for store in stores:
        store.start()
    for q in range(hq):
        field = field_of(lambda h: cells_ref[h * nx : (h + 1) * nx, q], ny, ky, bzi)
        for k in range(xq):
            x = q * xq + k
            here = field[:, k * zr : (k + 1) * zr].reshape(channels, yr, zr)
            out[:, x] = (here + rest_ref[:, x]).astype(bf16)
        part = pl.ds(q * xq, xq)
        store = pltpu.make_async_copy(
            out.at[:, part], grad_hbm.at[:, pl.ds(done + q * xq, xq)], sem.at[2 + q]
        )
        store.start()
        stores.append(store)
    for store in stores:
        store.wait()


def in_hbm(value):
    return pltpu.with_memory_space_constraint(jnp.asarray(value), pltpu.HBM)


def two_section_body(activations, cotangent, spectral_weights, pointwise, channel_bias):
    inputs = activations[0]
    channels, xr, yr, zr = inputs.shape
    nx, ny = lax.axis_size("gx"), lax.axis_size("gy")
    n = nx * ny
    cl, jl = MODES // nx, MODES // ny
    xq = 16 // cl
    nh = 2
    hq = xr // (nh * xq)
    lanes, rows = jl * channels, channels * yr
    bz = trig_basis(zr).reshape(nx, cl, zr)
    eye_x, eye_c = np.eye(xq), np.eye(cl)
    bzf = np.einsum("dcz,xX->xzdXc", bz, eye_x).reshape(xq * zr, nx * 16)
    bzi = halves(bzf.reshape(xq, zr, nx * 16).transpose(2, 0, 1).reshape(nx * 16, xq * zr))
    by = trig_basis(yr * ny).reshape(MODES, ny, yr)
    ky = np.einsum("jgy,ik->giyjk", by, np.eye(channels)).reshape(ny, rows, ny * lanes)
    ky = halves(ky)
    bx = trig_basis(xr * nx).reshape(MODES, nx, nh, hq, xq)
    sp = np.einsum("adtqx,cC->tdqxCca", bx, eye_c).reshape(nh * nx * hq * 16, cl * MODES)
    bxf = np.broadcast_to(
        sp.reshape(nh, 1, nx * hq * 16, cl * MODES), (nh, ny, nx * hq * 16, cl * MODES)
    )
    bxf = bxf.reshape(nh * n * hq * 16, cl * MODES).T
    bzf = halves(bzf)
    tables = [
        np.ascontiguousarray(ky.transpose(1, 0, 3, 2)),
        np.ascontiguousarray(ky.transpose(1, 0, 2, 3)),
        np.concatenate([bzf[0], bzf[1]], axis=1),
        np.concatenate([bzi[0], bzi[0], bzi[1]], axis=0),
        halves(bxf),
        halves(sp).reshape(2, nh, nx, hq, 16, cl * MODES),
    ]
    weights, mixing = spectral_weights[0], pointwise[0]
    vmem = pl.BlockSpec(memory_space=pltpu.VMEM)
    smem = pl.BlockSpec(memory_space=pltpu.SMEM)
    hbm = pl.BlockSpec(memory_space=pl.ANY)
    dma = pltpu.SemaphoreType.DMA
    grid = inputs.shape
    done = grid[:1] + ((nh - 1) * hq * xq,) + grid[2:]
    left = grid[:1] + (hq * xq,) + grid[2:]
    scratch = [
        pltpu.VMEM(grid, bf16), pltpu.VMEM(grid, bf16), pltpu.VMEM(grid, bf16),
        pltpu.VMEM(weights.shape, f32),
        pltpu.VMEM((jl, channels, channels, cl * MODES), f32),
        pltpu.VMEM((2, ny * lanes, rows), bf16),
        pltpu.VMEM((xq * zr, 2 * nx * 16), bf16),
        pltpu.VMEM((2, cl * MODES, nh * n * hq * 16), bf16),
        pltpu.VMEM((2, nh, nx, hq, 16, cl * MODES), bf16),
        pltpu.VMEM(grid, f32), pltpu.VMEM(grid, f32), pltpu.VMEM(grid, f32), pltpu.VMEM(grid, f32),
        pltpu.VMEM((jl, channels, cl * MODES), f32),
        pltpu.VMEM((jl, channels, cl * MODES), f32),
        pltpu.VMEM((jl, channels, cl * MODES), f32),
        pltpu.VMEM((2, cl * MODES, lanes), f32),
        pltpu.VMEM((2, cl * MODES, lanes), f32),
        pltpu.VMEM(mixing.shape, f32), pltpu.VMEM(channel_bias.shape, f32),
        pltpu.SMEM(mixing.shape, f32), pltpu.SMEM(channel_bias.shape, f32),
        pltpu.VMEM((3, nh, n, hq, 16, lanes), bf16),
        pltpu.VMEM((4, nh, nx, hq, 16, lanes), bf16),
        pltpu.VMEM((6, nh, n, hq, 16, lanes), bf16),
        dma((9,)), dma((6, nh)), dma((6, nh)),
        dma((xr,)), dma((xr,)), dma((4,)), dma((4,)), dma((2,)), dma((1,)), dma((1,)), dma((6, nh)), dma((6, nh)),
    ]
    parts = pl.pallas_call(
        functools.partial(relay_kernel, nx, ny, xq, (3, 9, 12)),
        out_shape=(
            jax.ShapeDtypeStruct(done, bf16),
            jax.ShapeDtypeStruct(left, f32),
            jax.ShapeDtypeStruct((n, hq, 16, lanes), bf16),
            pltpu.VMEM(weights.shape, f32),
            jax.ShapeDtypeStruct((2, rows, ny * lanes), bf16),
            jax.ShapeDtypeStruct((3 * nx * 16, xq * zr), bf16),
        ),
        in_specs=[hbm, hbm, hbm, smem, smem] + [hbm] * (2 + len(tables)),
        out_specs=[vmem] * 6,
        scratch_shapes=scratch,
        compiler_params=pltpu.CompilerParams(
            collective_id=0, has_side_effects=True, vmem_limit_bytes=46 * 2**20
        ),
        cost_estimate=pl.CostEstimate(
            flops=4 * 10**9, bytes_accessed=2 * 10**7, transcendentals=10**7
        ),
    )(
        *[in_hbm(v) for v in (inputs, cotangent, weights)],
        mixing, channel_bias,
        *[in_hbm(v) for v in [mixing, channel_bias] + tables],
    )
    input_grad, weight_grad = pl.pallas_call(
        functools.partial(finish_kernel, nx, ny, xq),
        out_shape=(
            jax.ShapeDtypeStruct(grid, bf16),
            jax.ShapeDtypeStruct(weights.shape, f32),
        ),
        in_specs=[vmem] * 6,
        out_specs=(hbm, hbm),
        scratch_shapes=[pltpu.VMEM(left, bf16), dma((2 + hq,))],
        compiler_params=pltpu.CompilerParams(vmem_limit_bytes=24 * 2**20),
        cost_estimate=pl.CostEstimate(flops=10**9, bytes_accessed=10**7, transcendentals=0),
    )(*parts)
    return (input_grad[None], weight_grad[None])


def fits(mesh):
    nx = mesh.shape["gx"]
    return mesh.shape["segment"] == 2 and mesh.shape["gy"] == 2 and nx == 8


def solution(mesh):
    return jax.shard_map(
        two_section_body if fits(mesh) else body,
        mesh=mesh,
        in_specs=(
            P("segment", "groups", "gx", "gy", None),
            P("groups", "gx", "gy", None),
            P("segment", "gy", "gx", None, None, None),
            P("segment", None, None),
            P("segment", None),
        ),
        out_specs=(
            P("segment", "groups", "gx", "gy", None),
            P("segment", "gy", "gx", "groups", None, None),
        ),
        check_vma=False,
    )
```
